32 devices in a mesh: clip: 4 (over x, core), row: 8 (over z, y).
Axes of the slice: x: 2, y: 2, z: 4, core: 2. Of those that a mesh axis runs over, the one named last changes fastest.
Arguments:
- features: bfloat16 [4, 16, 128, 48, 128], P('clip', None, 'row'), may hold values from -6 to 6
- target: bfloat16 [4, 16, 128, 3, 48], P('clip', None, 'row'), may hold values from -6 to 6
- conv_weight: bfloat16 [3, 3, 3, 128], replicated, may hold values from -0.4375 to 0.4375
- disc_first: bfloat16 [4, 4, 3, 64], replicated, may hold values from -0.875 to 0.875
- disc_second: bfloat16 [4, 4, 64, 128], replicated, may hold values from -0.1875 to 0.1875
- disc_third: bfloat16 [4, 4, 128, 256], replicated, may hold values from -0.125 to 0.125
- disc_fourth: bfloat16 [4, 4, 256, 512], replicated, may hold values from -0.09375 to 0.09375
- disc_head: bfloat16 [4, 4, 512, 1], replicated, may hold values from -0.0625 to 0.0625
Outputs:
- feature_grad: bfloat16 [4, 16, 128, 48, 128], P('clip', None, 'row')
- gan_grad: bfloat16 [4, 16, 128, 3, 48], P('clip', None, 'row')
- weight_grad: float32 [3, 3, 3, 128], replicated
- adaptive: float32 [], replicated
The draws below stay inside these ranges and needn't reach their ends.
All inputs are finite; a program needn't handle non-finite values.
Results may differ from the reference program's by a relative error of at most 0.015.
Values may be sent and summed in bfloat16 or wider, within the bound.
No kernel may reach another device: no remote copies, remote signals or barrier semaphores. Data moves between devices by JAX's collectives and lax.ppermute only.
A program may use at most 64 MiB of HBM per device.

```python
import jax
import jax.numpy as jnp
from jax import lax

C = 128
D1 = 64
D2 = 128
D3 = 256
D4 = 512
FRAMES = 16
WIDTH = 48
HEIGHT = 128
CLIPS = 4


def block_scale(stream_key, extent, split, smallest, top_value):
    loudness, own = 1.0, jax.random.fold_in(stream_key, 6)
    for dim, parts in split:
        steps = jnp.exp(jax.random.uniform(jax.random.fold_in(own, dim), (parts,), jnp.float32, smallest / len(split), top_value / len(split)))
        loudness = loudness * jnp.repeat(steps, extent[dim] // parts).reshape([-1 if axis == dim else 1 for axis in range(len(extent))])
    return loudness


def scatter_about(key, shape, scale, limit, split=(), kind=jnp.bfloat16):
    entries = scale * jax.random.normal(key, shape, jnp.float32)
    if split:
        entries = entries * block_scale(key, shape, split, -0.22, 0.18)
    return jnp.clip(entries, -limit, limit).astype(kind)


def setup_inputs(seed: int = 0) -> dict:
    seeds = jax.random.split(jax.random.key(seed), 9)
    features = scatter_about(seeds[0], (CLIPS, FRAMES, HEIGHT, WIDTH, C), 1.0, 6.0, ((0, 4), (2, 8)))
    target = scatter_about(seeds[1], (CLIPS, FRAMES, HEIGHT, 3, WIDTH), 1.0, 6.0, ((0, 4), (2, 8)))
    conv_weight = scatter_about(seeds[2], (3, 3, 3, C), 0.03, 0.4375)
    disc_first = scatter_about(seeds[3], (4, 4, 3, D1), 48 ** -0.5, 0.875)
    disc_second = scatter_about(seeds[4], (4, 4, D1, D2), (16 * D1) ** -0.5, 0.1875)
    disc_third = scatter_about(seeds[5], (4, 4, D2, D3), (16 * D2) ** -0.5, 0.125)
    disc_fourth = scatter_about(seeds[6], (4, 4, D3, D4), (16 * D3) ** -0.5, 0.09375)
    disc_head = scatter_about(seeds[7], (4, 4, D4, 1), (16 * D4) ** -0.5, 0.0625)
    return {"features": features, "target": target, "conv_weight": conv_weight, "disc_first": disc_first, "disc_second": disc_second, "disc_third": disc_third, "disc_fourth": disc_fourth, "disc_head": disc_head}


loss_scale = 64.0
epsilon = 0.0001

def forward_conv(padded, conv_weight):
    return lax.conv_general_dilated(padded, conv_weight, (1, 1), 'VALID', dimension_numbers=('NHWC', 'HWOI', 'NHCW'), preferred_element_type=jnp.float32)

def weight_terms(padded, grads):
    return lax.conv_general_dilated(padded, grads, (1, 1), 'VALID', dimension_numbers=('CHWN', 'IHOW', 'HWCN'), preferred_element_type=jnp.float32)

def input_grad(grad_rows, conv_weight):
    flipped = conv_weight[::-1, ::-1]
    result = lax.conv_general_dilated(grad_rows, flipped, (1, 1), ((0, 0), (1, 1)), dimension_numbers=('NHCW', 'HWIO', 'NHWC'), preferred_element_type=jnp.float32)
    return result.astype(jnp.bfloat16)

def down_conv(values, weight, stride, layout_spec):
    return lax.conv_general_dilated(values, weight, (stride, stride), ((1, 1), (1, 1)), dimension_numbers=layout_spec, preferred_element_type=jnp.float32)

def back_conv(cotangent, weight, stride, layout_spec):
    return lax.conv_general_dilated(cotangent, weight[::-1, ::-1], (1, 1), ((2, 2), (2, 2)), lhs_dilation=(stride, stride), dimension_numbers=layout_spec, preferred_element_type=jnp.float32)

def silu_slope(values):
    logistic = jax.nn.sigmoid(values)
    return logistic * (1.0 + values * (1.0 - logistic))

def disc_gradient(images, layer_one, layer_two, layer_three, layer_four, layer_head):
    plain = ('NHWC', 'HWIO', 'NHWC')
    pre_one = down_conv(images, layer_one, 2, ('NHCW', 'HWIO', 'NHWC'))
    act_one = jax.nn.silu(pre_one).astype(jnp.bfloat16)
    pre_two = down_conv(act_one, layer_two, 2, plain)
    act_two = jax.nn.silu(pre_two).astype(jnp.bfloat16)
    pre_three = down_conv(act_two, layer_three, 2, plain)
    act_three = jax.nn.silu(pre_three).astype(jnp.bfloat16)
    pre_four = down_conv(act_three, layer_four, 1, plain)
    act_four = jax.nn.silu(pre_four).astype(jnp.bfloat16)
    back_spec = ('NHWC', 'HWOI', 'NHWC')
    cot_head = jnp.full((act_four.shape[0], act_four.shape[1] - 1, act_four.shape[2] - 1, 1), -loss_scale, jnp.bfloat16)
    cot_four = (back_conv(cot_head, layer_head, 1, back_spec) * silu_slope(pre_four)).astype(jnp.bfloat16)
    cot_three = (back_conv(cot_four, layer_four, 1, back_spec) * silu_slope(pre_three)).astype(jnp.bfloat16)
    cot_two = (back_conv(cot_three, layer_three, 2, back_spec) * silu_slope(pre_two)).astype(jnp.bfloat16)
    cot_one = (back_conv(cot_two, layer_two, 2, back_spec) * silu_slope(pre_one)).astype(jnp.bfloat16)
    return back_conv(cot_one, layer_one, 2, ('NHWC', 'HWOI', 'NHCW')).astype(jnp.bfloat16)

def reference(features, target, conv_weight, disc_first, disc_second, disc_third, disc_fourth, disc_head):
    pixels = CLIPS * FRAMES * HEIGHT * WIDTH

    def first_pass(clip_index):
        clip_features = lax.dynamic_index_in_dim(features, clip_index, 0, keepdims=False)
        wanted = lax.dynamic_index_in_dim(target, clip_index, 0, keepdims=False)
        padded = jnp.pad(clip_features, ((0, 0), (1, 1), (1, 1), (0, 0)))
        rebuilt = forward_conv(padded, conv_weight)
        rec_grad = loss_scale * (rebuilt - wanted.astype(jnp.float32))
        rec_part = weight_terms(padded, rec_grad.astype(jnp.bfloat16))
        gan_grad = disc_gradient(rebuilt.astype(jnp.bfloat16), disc_first, disc_second, disc_third, disc_fourth, disc_head)
        gan_part = weight_terms(padded, gan_grad)
        return (rec_part, gan_part, rec_grad, gan_grad)
    rec_parts, gan_parts, rec_grads, gan_grads = lax.map(first_pass, jnp.arange(CLIPS, dtype=jnp.int32))
    rec_weight = lax.optimization_barrier(jnp.sum(rec_parts, axis=0))
    gan_weight = lax.optimization_barrier(jnp.sum(gan_parts, axis=0))
    adaptive = jnp.sqrt(jnp.sum(rec_weight * rec_weight)) / (jnp.sqrt(jnp.sum(gan_weight * gan_weight)) + epsilon)
    weight_grad = (rec_weight + adaptive * gan_weight) / pixels
    combined = (rec_grads + adaptive * gan_grads.astype(jnp.float32)).astype(jnp.bfloat16)

    def second_pass(clip_grads):
        grad_rows = jnp.pad(clip_grads, ((0, 0), (1, 1), (0, 0), (0, 0)))
        return input_grad(grad_rows, conv_weight)
    feature_grad = lax.map(second_pass, combined)
    return (feature_grad, gan_grads, weight_grad, adaptive)
```

```python
import functools

import jax
import jax.numpy as jnp
import numpy as np
from jax import lax
from jax.experimental import pallas as pl
from jax.experimental.pallas import tpu as pltpu
from jax.sharding import PartitionSpec as P

loss_scale = 64.0
epsilon = 0.0001
F32 = jnp.float32
BF16 = jnp.bfloat16
LANES = 128
NN = (((1,), (0,)), ((), ()))
NT = (((1,), (1,)), ((), ()))
TN = (((0,), (0,)), ((), ()))


def up_to(value, step):
    return -(-value // step) * step


def mat(left, right, dims=NN):
    return lax.dot_general(left, right, dims, preferred_element_type=F32)


def slot_of(frame, devices, group):
    return (frame % group) * devices + frame // group


def forward_kernel(feat_ref, weight_ref, pay_ref, own_ref, taps_ref, out_ref, *, frames, devices, group, cols, lanes):
    pixels = feat_ref.shape[0] // frames
    pieces = pixels // LANES
    pitch = out_ref.shape[1] // devices
    taps = weight_ref.shape[0]
    weight = weight_ref[...]
    for frame in range(frames):
        product = mat(weight, feat_ref[frame * pixels : (frame + 1) * pixels, :], NT)
        slot = slot_of(frame, devices, group)
        for k in range(pieces):
            taps_ref[k, pl.ds(slot, taps, stride=frames), :] = product[:, k * LANES : (k + 1) * LANES]
    column = lax.broadcasted_iota(jnp.int32, (frames, pixels), 1) % cols
    out_ref[...] = jnp.zeros_like(out_ref)

    def tap(a, b, o):
        rows = pl.ds(((a * 3 + b) * 3 + o) * frames, frames)
        return jnp.concatenate([taps_ref[k, rows, :] for k in range(pieces)], axis=1)

    for o in range(3):
        total = None
        for a in range(3):
            part = tap(a, 1, o)
            part = part + jnp.where(column == 0, 0.0, pltpu.roll(tap(a, 0, o), 1, 1))
            part = part + jnp.where(column == cols - 1, 0.0, pltpu.roll(tap(a, 2, o), pixels - 1, 1))
            part = jnp.concatenate([part, jnp.zeros((frames, lanes - pixels), F32)], axis=1)
            if a < 2:
                part = pltpu.roll(part, (2 - a) * cols, 1)
            total = part if total is None else total + part
        own_ref[o * frames : (o + 1) * frames, :] = total
        for part in range(group):
            rows = total[part * devices : (part + 1) * devices, :]
            for k in range(lanes // LANES):
                out_ref[k, pl.ds(o * group + part, devices, stride=pitch), :] = rows[:, k * LANES : (k + 1) * LANES]
    for k in range(lanes // LANES):
        pay_ref[:, k * LANES : (k + 1) * LANES] = out_ref[k].astype(BF16)


def forward_call(features, weight, frames, devices, group, cols, lanes, pitch):
    pixels = features.shape[0] // frames
    return pl.pallas_call(
        functools.partial(forward_kernel, frames=frames, devices=devices, group=group, cols=cols, lanes=lanes),
        out_shape=(
            jax.ShapeDtypeStruct((devices * pitch, lanes), BF16),
            jax.ShapeDtypeStruct((3 * frames, lanes), F32),
        ),
        in_specs=[pl.BlockSpec(memory_space=pltpu.VMEM)] * 2,
        out_specs=(pl.BlockSpec(memory_space=pltpu.VMEM),) * 2,
        scratch_shapes=[
            pltpu.VMEM((pixels // LANES, weight.shape[0] * frames, LANES), F32),
            pltpu.VMEM((lanes // LANES, devices * pitch, LANES), F32),
        ],
        compiler_params=pltpu.CompilerParams(vmem_limit_bytes=24 * 2**20),
        cost_estimate=pl.CostEstimate(flops=2 * features.size * 27, bytes_accessed=2 * features.size, transcendentals=0),
        name="forward_taps",
    )(features, weight)


def shift_rows(values, step, period):
    size = values.shape[0]
    row = lax.broadcasted_iota(jnp.int32, values.shape, 0) % period
    rolled = pltpu.roll(values, step % size, 0)
    source = row - step
    return jnp.where((source >= 0) & (source < period), rolled, 0.0)


def gate_of(values):
    logistic = 1.0 / (1.0 + jnp.exp(-values))
    return (values * logistic).astype(BF16), logistic * (1.0 + values * (1.0 - logistic))


def disc_kernel(
    pay_ref, gather_ref, scatter_ref, band_hbm, second_hbm, third_hbm, fourth_hbm, head_ref, out_ref,
    zin, band, second, third, fourth, rows_in, act_one, slope_one, cols_two, act_two, slope_two, act_three, cols_four,
    pull_four, pull_three, pull_two, zout, sems, *, devices, group, cols, block_rows, period,
):
    lanes = pay_ref.shape[1]
    pitch = pay_ref.shape[0] // devices
    span = block_rows + 2
    unit = group * period
    wide = 3 * cols
    d1 = (act_one.shape[1]) // (cols // 2 + 2)
    d2, d3, d4 = second.shape[1], third.shape[1], fourth.shape[1]
    x1, x2, x3 = cols // 2, cols // 4, cols // 8
    x4 = x3 - 1
    copies = [
        pltpu.make_async_copy(source, target, sems.at[i])
        for i, (source, target) in enumerate(
            ((band_hbm, band), (second_hbm, second), (third_hbm, third), (fourth_hbm, fourth))
        )
    ]
    for copy in copies:
        copy.start()
    for k in range(lanes // LANES):
        zin[k] = pay_ref[:, k * LANES : (k + 1) * LANES].astype(F32)
    for part in range(group):
        planes = []
        for o in range(3):
            pieces = [zin[k, pl.ds(o * group + part, devices, stride=pitch), :] for k in range(lanes // LANES)]
            planes.append(jnp.concatenate(pieces, axis=1))
        for i in range(span):
            row = jnp.concatenate([plane[:, i * cols : (i + 1) * cols] for plane in planes], axis=1)
            rows_in[pl.ds((i * group + part) * devices, devices), :] = row
    image = mat(gather_ref[...], rows_in[...].astype(BF16)).astype(BF16).astype(F32)
    ext = [image[r * unit : (r + 1) * unit] for r in range(8)]
    ext = [shift_rows(ext[7], 1, period)] + ext + [shift_rows(ext[0], -1, period)]
    ext = [piece.astype(BF16) for piece in ext]
    copies[0].wait()
    left = [jnp.concatenate([ext[a + 2 * p] for p in range(4)], axis=0) for a in range(4)]
    width_one = act_one.shape[1]
    step = 256
    for start in range(0, width_one, step):
        end = min(start + step, width_one)
        pre = mat(left[0], band[0:wide, start:end])
        for a in range(1, 4):
            pre = pre + mat(left[a], band[a * wide : (a + 1) * wide, start:end])
        act, slope = gate_of(pre)
        slope_one[:, start:end] = slope
        act_one[unit : 5 * unit, start:end] = act
        actual = act.astype(F32)
        act_one[0:unit, start:end] = shift_rows(actual[3 * unit :], 1, period).astype(BF16)
        act_one[5 * unit :, start:end] = shift_rows(actual[:unit], -1, period).astype(BF16)
    copies[1].wait()
    for x in range(x2):
        for a in range(4):
            for p in range(2):
                cols_two[(x * 2 + p) * unit : (x * 2 + p + 1) * unit, a * 4 * d1 : (a + 1) * 4 * d1] = act_one[
                    (2 * p + a) * unit : (2 * p + a + 1) * unit, 2 * x * d1 : (2 * x + 4) * d1
                ]
    pre = mat(cols_two[...], second[...])
    act, slope = gate_of(pre)
    slope_two[...] = slope
    act_two[:, 0:d2] = jnp.zeros((4 * unit, d2), BF16)
    act_two[:, (x2 + 1) * d2 :] = jnp.zeros((4 * unit, d2), BF16)
    for x in range(x2):
        block = act[x * 2 * unit : (x + 1) * 2 * unit]
        actual = block.astype(F32)
        at = slice((x + 1) * d2, (x + 2) * d2)
        act_two[unit : 3 * unit, at] = block
        act_two[0:unit, at] = shift_rows(actual[unit:], 1, period).astype(BF16)
        act_two[3 * unit :, at] = shift_rows(actual[:unit], -1, period).astype(BF16)
    copies[2].wait()
    left = jnp.concatenate(
        [
            jnp.concatenate([act_two[a * unit : (a + 1) * unit, 2 * x * d2 : (2 * x + 4) * d2] for a in range(4)], axis=1)
            for x in range(x3)
        ],
        axis=0,
    )
    act, slope_three = gate_of(mat(left, third[...]))
    act_three[:, 0:d3] = jnp.zeros((4 * unit, d3), BF16)
    act_three[:, (x3 + 1) * d3 :] = jnp.zeros((4 * unit, d3), BF16)
    for x in range(x3):
        block = act[x * unit : (x + 1) * unit]
        actual = block.astype(F32)
        at = slice((x + 1) * d3, (x + 2) * d3)
        act_three[unit : 2 * unit, at] = block
        for a in (0, 2, 3):
            act_three[a * unit : (a + 1) * unit, at] = shift_rows(actual, 1 - a, period).astype(BF16)
    for x in range(x4):
        for a in range(4):
            cols_four[x * unit : (x + 1) * unit, a * 4 * d3 : (a + 1) * 4 * d3] = act_three[
                a * unit : (a + 1) * unit, x * d3 : (x + 4) * d3
            ]
    copies[3].wait()
    pre = mat(cols_four[...], fourth[...])
    _, slope = gate_of(pre)
    row = lax.broadcasted_iota(jnp.int32, (unit, d4), 0) % period
    head = head_ref[...].astype(F32) * -loss_scale
    heads = []
    for x in range(x4):
        total = None
        for a in range(4):
            taps = [head[a * 4 + b : a * 4 + b + 1, :] for b in range(4) if 0 <= x - b + 1 < x4 - 1]
            tap = functools.reduce(lambda u, v: u + v, taps)
            inside = (row - a + 1 >= 0) & (row - a + 1 < period - 2) & (row < period - 1)
            term = jnp.where(inside, jnp.broadcast_to(tap, (unit, d4)), 0.0)
            total = term if total is None else total + term
        heads.append(total)
    cot = (jnp.concatenate(heads, axis=0) * slope).astype(BF16)
    pull_four[...] = mat(cot, fourth[...], NT)
    cots = []
    for x in range(x3):
        total = None
        for a in range(4):
            term = None
            for b in range(4):
                source = x - b + 1
                if 0 <= source < x4:
                    piece = pull_four[source * unit : (source + 1) * unit, (a * 4 + b) * d3 : (a * 4 + b + 1) * d3]
                    term = piece if term is None else term + piece
            if a != 1:
                term = shift_rows(term, a - 1, period)
            total = term if total is None else total + term
        cots.append((total * slope_three[x * unit : (x + 1) * unit]).astype(BF16))
    pull_three[...] = mat(jnp.concatenate(cots, axis=0), third[...], NT)
    cots = []
    for x in range(x2):
        terms = []
        for a in range(4):
            term = None
            for b in range(4):
                if (x - b + 1) % 2 == 0 and 0 <= (x - b + 1) // 2 < x3:
                    source = (x - b + 1) // 2
                    piece = pull_three[source * unit : (source + 1) * unit, (a * 4 + b) * d2 : (a * 4 + b + 1) * d2]
                    term = piece if term is None else term + piece
            terms.append(term)
        even = terms[1] + shift_rows(terms[3], 1, period)
        odd = terms[2] + shift_rows(terms[0], -1, period)
        both = jnp.concatenate([even, odd], axis=0)
        cots.append((both * slope_two[x * 2 * unit : (x + 1) * 2 * unit]).astype(BF16))
    pull_two[...] = mat(jnp.concatenate(cots, axis=0), second[...], NT)
    strips = []
    for k in range(x2 + 1):
        terms = {}
        for p in range(2):
            for a in range(4):
                term = None
                if k < x2:
                    term = pull_two[(2 * k + p) * unit : (2 * k + p + 1) * unit, a * 4 * d1 : (a * 4 + 2) * d1]
                if k > 0:
                    other = pull_two[(2 * k - 2 + p) * unit : (2 * k - 1 + p) * unit, (a * 4 + 2) * d1 : (a + 1) * 4 * d1]
                    term = other if term is None else term + other
                terms[p, a] = term
        both = jnp.concatenate(
            [
                terms[0, 1] + shift_rows(terms[1, 3], 1, period),
                terms[0, 2] + terms[1, 0],
                terms[0, 3] + terms[1, 1],
                terms[1, 2] + shift_rows(terms[0, 0], -1, period),
            ],
            axis=0,
        )
        strips.append((both * slope_one[:, 2 * k * d1 : (2 * k + 2) * d1]).astype(BF16))
    cot = jnp.concatenate(strips, axis=1)
    pulls = [mat(cot, band[a * wide : (a + 1) * wide, :], NT) for a in range(4)]
    part = lambda p, a: pulls[a][p * unit : (p + 1) * unit]
    phases = []
    for r in range(8):
        terms = [part(p, a) for p in range(4) for a in range(4) if 2 * p + a - 1 == r]
        if r == 0:
            terms.append(shift_rows(part(3, 3), 1, period))
        if r == 7:
            terms.append(shift_rows(part(0, 0), -1, period))
        phases.append(functools.reduce(lambda u, v: u + v, terms))
    image = jnp.concatenate(phases, axis=0).astype(BF16)
    rows = mat(scatter_ref[...], image)
    zout[...] = jnp.zeros_like(zout)
    for part_at in range(group):
        picked = [rows[(i * group + part_at) * devices : (i * group + part_at + 1) * devices] for i in range(span)]
        for o in range(3):
            plane = [piece[:, o * cols : (o + 1) * cols] for piece in picked]
            plane.append(jnp.zeros((devices, lanes - span * cols), F32))
            plane = jnp.concatenate(plane, axis=1)
            for k in range(lanes // LANES):
                zout[k, pl.ds(o * group + part_at, devices, stride=pitch), :] = plane[:, k * LANES : (k + 1) * LANES]
    for k in range(lanes // LANES):
        out_ref[:, k * LANES : (k + 1) * LANES] = zout[k].astype(BF16)


def row_maps(devices, group, block_rows):
    height = devices * block_rows
    period = height // 8
    span = block_rows + 2
    gather = np.zeros((8 * group * period, span * group * devices), np.float32)
    for device in range(devices):
        for i in range(span):
            y = device * block_rows + i - 1
            if 0 <= y < height:
                for part in range(group):
                    gather[((y % 8) * group + part) * period + y // 8, (i * group + part) * devices + device] = 1.0
    return gather


def band_of(first, cols):
    d1 = first.shape[-1]
    width = (cols // 2 + 2) * d1
    x = np.arange(cols)[:, None]
    out_x = np.arange(width)[None, :] // d1 - 1
    tap = x - 2 * out_x + 1
    inside = (out_x >= 0) & (out_x < cols // 2)
    tiled = jnp.tile(first, (1, 1, 1, cols // 2 + 2))
    band = jnp.zeros((4, 3, cols, width), BF16)
    for b in range(4):
        band = jnp.where(jnp.asarray((tap == b) & inside), tiled[:, b, :, None, :], band)
    return band.reshape(4 * 3 * cols, width)


def disc_call(payload, first, second, third, fourth, head, devices, group, cols, block_rows):
    period = devices * block_rows // 8
    unit = group * period
    d1, d2, d3, d4 = first.shape[-1], second.shape[-1], third.shape[-1], fourth.shape[-1]
    x2, x3 = cols // 4, cols // 8
    x4 = x3 - 1
    gather = row_maps(devices, group, block_rows)
    band = band_of(first, cols)
    args = (
        payload,
        jnp.asarray(gather, BF16),
        jnp.asarray(gather.T, BF16),
        band,
        second.reshape(16 * d1, d2),
        third.reshape(16 * d2, d3),
        fourth.reshape(16 * d3, d4),
        head.reshape(16, d4),
    )
    lanes = payload.shape[1]
    vm = pl.BlockSpec(memory_space=pltpu.VMEM)
    hbm = pl.BlockSpec(memory_space=pl.ANY)
    return pl.pallas_call(
        functools.partial(
            disc_kernel, devices=devices, group=group, cols=cols, block_rows=block_rows, period=period
        ),
        out_shape=jax.ShapeDtypeStruct(payload.shape, BF16),
        in_specs=[vm, vm, vm, hbm, hbm, hbm, hbm, vm],
        out_specs=vm,
        scratch_shapes=[
            pltpu.VMEM((lanes // LANES, payload.shape[0], LANES), F32),
            pltpu.VMEM(band.shape, BF16),
            pltpu.VMEM((16 * d1, d2), BF16),
            pltpu.VMEM((16 * d2, d3), BF16),
            pltpu.VMEM((16 * d3, d4), BF16),
            pltpu.VMEM((gather.shape[1], 3 * cols), F32),
            pltpu.VMEM((6 * unit, band.shape[1]), BF16),
            pltpu.VMEM((4 * unit, band.shape[1]), F32),
            pltpu.VMEM((x2 * 2 * unit, 16 * d1), BF16),
            pltpu.VMEM((4 * unit, (x2 + 2) * d2), BF16),
            pltpu.VMEM((x2 * 2 * unit, d2), F32),
            pltpu.VMEM((4 * unit, (x3 + 2) * d3), BF16),
            pltpu.VMEM((x4 * unit, 16 * d3), BF16),
            pltpu.VMEM((x4 * unit, 16 * d3), F32),
            pltpu.VMEM((x3 * unit, 16 * d2), F32),
            pltpu.VMEM((x2 * 2 * unit, 16 * d1), F32),
            pltpu.VMEM((lanes // LANES, payload.shape[0], LANES), F32),
            pltpu.SemaphoreType.DMA((4,)),
        ],
        compiler_params=pltpu.CompilerParams(vmem_limit_bytes=48 * 2**20),
        cost_estimate=pl.CostEstimate(flops=4 * 10**9, bytes_accessed=8 * 10**6, transcendentals=10**6),
        name="disc_rows",
    )(*args)


def taps_kernel(plane_ref, feat_ref, taps_out, part_ref, taps_ref, zin, *, frames, devices, group, cols, packed):
    lanes = plane_ref.shape[1]
    pixels = feat_ref.shape[0] // frames
    pieces = pixels // LANES
    if packed:
        pitch = plane_ref.shape[0] // devices
        for k in range(lanes // LANES):
            zin[k] = plane_ref[:, k * LANES : (k + 1) * LANES].astype(F32)
        blocks = []
        for o in range(3):
            for part in range(group):
                row = pl.ds(o * group + part, devices, stride=pitch)
                blocks.append(jnp.concatenate([zin[k, row, :] for k in range(lanes // LANES)], axis=1))
        plane = jnp.concatenate(blocks, axis=0)
    else:
        plane = plane_ref[...]
    column = lax.broadcasted_iota(jnp.int32, plane.shape, 1) % cols
    for b in range(3):
        moved = plane
        if b == 0:
            moved = jnp.where(column == cols - 1, 0.0, pltpu.roll(plane, lanes - 1, 1))
        if b == 2:
            moved = jnp.where(column == 0, 0.0, pltpu.roll(plane, 1, 1))
        for a in range(3):
            turned = moved if a == 2 else pltpu.roll(moved, lanes - (2 - a) * cols, 1)
            for k in range(pieces):
                taps_ref[k, pl.ds((a * 3 + b) * 3 * frames, 3 * frames), :] = turned[:, k * LANES : (k + 1) * LANES]
    padded = taps_out.shape[1]
    for k in range(pieces):
        taps_ref[k, pl.ds(27 * frames, (padded - 27) * frames), :] = jnp.zeros(((padded - 27) * frames, LANES), F32)
    total = jnp.zeros(part_ref.shape, F32)
    for frame in range(frames):
        rows = pl.ds(slot_of(frame, devices, group), padded, stride=frames)
        taps = jnp.concatenate([taps_ref[k, rows, :] for k in range(pieces)], axis=1).astype(BF16)
        taps_out[frame] = taps
        total = total + mat(taps, feat_ref[frame * pixels : (frame + 1) * pixels, :])
    part_ref[...] = total


def taps_call(plane, features, frames, devices, group, cols, packed, name):
    pixels = features.shape[0] // frames
    channels = features.shape[1]
    vm = pl.BlockSpec(memory_space=pltpu.VMEM)
    return pl.pallas_call(
        functools.partial(
            taps_kernel, frames=frames, devices=devices, group=group, cols=cols, packed=packed
        ),
        out_shape=(
            jax.ShapeDtypeStruct((frames, 32, pixels), BF16),
            jax.ShapeDtypeStruct((32, channels), F32),
        ),
        in_specs=[vm, vm],
        out_specs=(vm, vm),
        scratch_shapes=[
            pltpu.VMEM((pixels // LANES, 32 * frames, LANES), F32),
            pltpu.VMEM((plane.shape[1] // LANES, plane.shape[0], LANES), F32),
        ],
        compiler_params=pltpu.CompilerParams(vmem_limit_bytes=24 * 2**20),
        cost_estimate=pl.CostEstimate(
            flops=2 * features.size * 27, bytes_accessed=2 * features.size, transcendentals=0
        ),
        name=name,
    )(plane, features)


def final_kernel(rec_ref, gan_ref, sums_ref, weight_ref, out_ref, grad_ref, adapt_ref, both_ref, *, pixels):
    half = weight_ref.shape[0]

    @pl.when(pl.program_id(0) == 0)
    def _():
        total = sums_ref[0].astype(F32)
        for i in range(1, sums_ref.shape[0]):
            total = total + sums_ref[i].astype(F32)
        rec, gan = total[:half], total[half:]
        norm = lambda values: jnp.sqrt(jnp.sum(jnp.sum(values * values, axis=1, keepdims=True), axis=0, keepdims=True))
        adaptive = norm(rec) / (norm(gan) + epsilon)
        grad_ref[...] = (rec + adaptive * gan) / pixels
        adapt_ref[...] = jnp.broadcast_to(adaptive, adapt_ref.shape)
        both_ref[:half] = weight_ref[...]
        both_ref[half:] = (adaptive * weight_ref[...].astype(F32)).astype(BF16)

    step_frames, _, block = rec_ref.shape
    for at in range(step_frames):
        left = jnp.concatenate([rec_ref[at], gan_ref[at]], axis=0)
        out_ref[at * block : (at + 1) * block] = mat(left, both_ref[...], TN).astype(BF16)


def final_call(rec_taps, gan_taps, sums, weight, pixels):
    frames, padded, block = rec_taps.shape
    channels = weight.shape[1]
    step = 2
    whole = lambda shape: pl.BlockSpec(shape, lambda i: (0,) * len(shape))
    return pl.pallas_call(
        functools.partial(final_kernel, pixels=pixels),
        grid=(frames // step,),
        out_shape=(
            jax.ShapeDtypeStruct((frames * block, channels), BF16),
            jax.ShapeDtypeStruct((padded, channels), F32),
            jax.ShapeDtypeStruct((8, LANES), F32),
        ),
        in_specs=[
            pl.BlockSpec((step, padded, block), lambda i: (i, 0, 0)),
            pl.BlockSpec((step, padded, block), lambda i: (i, 0, 0)),
            whole(sums.shape),
            whole(weight.shape),
        ],
        out_specs=(
            pl.BlockSpec((step * block, channels), lambda i: (i, 0)),
            whole((padded, channels)),
            whole((8, LANES)),
        ),
        scratch_shapes=[pltpu.VMEM((2 * padded, channels), BF16)],
        compiler_params=pltpu.CompilerParams(vmem_limit_bytes=24 * 2**20),
        cost_estimate=pl.CostEstimate(
            flops=4 * frames * block * channels * padded, bytes_accessed=4 * frames * block * channels, transcendentals=0
        ),
        name="feature_pull",
    )(rec_taps, gan_taps, sums, weight)


def spread(values, axis):
    count = lax.axis_size(axis)
    copies = jnp.broadcast_to(values[None], (count,) + values.shape)
    return lax.all_to_all(copies, axis, split_axis=0, concat_axis=0, tiled=True)


def per_device(
    features, target, conv_weight, disc_first, disc_second, disc_third, disc_fourth, disc_head
):
    devices = lax.axis_size("row")
    _, frames, block_rows, cols, channels = features.shape
    group = frames // devices
    pixels = lax.axis_size("clip") * devices * frames * block_rows * cols
    lanes = up_to((block_rows + 2) * cols, LANES)
    pitch = up_to(3 * group, 8)
    edge = lax.axis_index("row")
    feats = features.reshape(frames * block_rows * cols, channels)
    weight = jnp.pad(conv_weight.reshape(27, channels), ((0, 5), (0, 0)))
    payload, own = forward_call(feats, weight, frames, devices, group, cols, lanes, pitch)
    trade = lambda values: lax.all_to_all(
        values.reshape(devices, pitch, lanes), "row", split_axis=0, concat_axis=0, tiled=True
    ).reshape(devices * pitch, lanes)
    arrived = trade(payload)
    wanted = target[0].reshape(devices, group, block_rows, 3, cols).transpose(3, 1, 0, 2, 4)
    wanted = wanted.reshape(3 * frames, block_rows * cols)
    upward = jnp.concatenate([own[:, : 2 * cols].astype(BF16), wanted[:, :cols]], axis=1)
    downward = jnp.concatenate(
        [own[:, block_rows * cols : (block_rows + 2) * cols].astype(BF16), wanted[:, -cols:]], axis=1
    )
    below = lax.ppermute(upward, "row", [(i + 1, i) for i in range(devices - 1)]).astype(F32)
    above = lax.ppermute(downward, "row", [(i, i + 1) for i in range(devices - 1)]).astype(F32)
    none = lambda count: jnp.zeros((3 * frames, count), F32)
    rest = lanes - (block_rows + 2) * cols
    added = jnp.concatenate(
        [above[:, : 2 * cols], none((block_rows - 2) * cols), below[:, : 2 * cols], none(rest)], axis=1
    )
    asked = jnp.concatenate([above[:, 2 * cols :], wanted.astype(F32), below[:, 2 * cols :], none(rest)], axis=1)
    lane = jnp.arange(lanes)[None, :]
    first = jnp.where(edge == 0, cols, 0)
    last = jnp.where(edge == devices - 1, (block_rows + 1) * cols, (block_rows + 2) * cols)
    rec_plane = jnp.where((lane >= first) & (lane < last), loss_scale * (own + added - asked), 0.0)
    sent = disc_call(
        arrived, disc_first, disc_second, disc_third, disc_fourth, disc_head, devices, group, cols, block_rows
    )
    returned = trade(sent)
    rec_taps, rec_part = taps_call(rec_plane, feats, frames, devices, group, cols, False, "rec_taps")
    gan_taps, gan_part = taps_call(returned, feats, frames, devices, group, cols, True, "gan_taps")
    partial = jnp.concatenate([rec_part, gan_part], axis=0)
    partial = jnp.sum(spread(partial.astype(BF16), "clip").astype(F32), axis=0)
    sums = spread(partial.astype(BF16), "row")
    image_back = returned.reshape(devices, pitch, lanes)[:, : 3 * group, cols : (block_rows + 1) * cols]
    image_back = image_back.reshape(devices, 3, group, block_rows, cols).transpose(0, 2, 3, 1, 4)
    image_back = image_back.reshape(1, frames, block_rows, 3, cols)
    feature_grad, weight_grad, adaptive = final_call(rec_taps, gan_taps, sums, weight, pixels)
    return (
        feature_grad.reshape(features.shape),
        image_back,
        weight_grad[:27].reshape(3, 3, 3, channels),
        adaptive[0, 0],
    )


def solution(mesh):
    rows = P("clip", None, "row", None, None)
    return jax.shard_map(
        per_device,
        mesh=mesh,
        in_specs=(rows, rows, P(), P(), P(), P(), P(), P()),
        out_specs=(rows, rows, P(), P()),
        check_vma=False,
    )
```

```python
import functools

import jax
import jax.numpy as jnp
import numpy as np
from jax import lax
from jax.experimental import pallas as pl
from jax.experimental.pallas import tpu as pltpu
from jax.sharding import PartitionSpec as P

loss_scale = 64.0
epsilon = 0.0001
F32 = jnp.float32
BF16 = jnp.bfloat16
LANES = 128
NN = (((1,), (0,)), ((), ()))
NT = (((1,), (1,)), ((), ()))
TN = (((0,), (0,)), ((), ()))
VM = pl.BlockSpec(memory_space=pltpu.VMEM)
HBM = pl.BlockSpec(memory_space=pl.ANY)
WHOLE = pltpu.CompilerParams(vmem_limit_bytes=60 * 2**20)


def up_to(value, step):
    return -(-value // step) * step


def mat(left, right, dims=NN):
    return lax.dot_general(left, right, dims, preferred_element_type=F32)


def slot_of(frame, devices, group):
    return (frame % group) * devices + frame // group


def forward_kernel(
    feat_hbm, weight_ref, pay_ref, own_ref, flat_ref, feat_ref, weight_scr, taps_ref, out_ref, sems,
    *, frames, devices, group, cols, lanes,
):
    pixels = feat_ref.shape[0] // frames
    pieces = pixels // LANES
    pitch = out_ref.shape[1] // devices
    taps = flat_ref.shape[0]
    copies = [
        pltpu.make_async_copy(
            feat_hbm.at[pl.ds(frame * pixels, pixels), :], feat_ref.at[pl.ds(frame * pixels, pixels), :], sems.at[frame]
        )
        for frame in range(frames)
    ]
    for copy in copies:
        copy.start()
    weight_scr[...] = jnp.zeros_like(weight_scr)
    for a in range(3):
        for b in range(3):
            at = (a * 3 + b) * 3
            weight_scr[at : at + 3, :] = weight_ref[a, b].astype(F32)
    weight = weight_scr[...].astype(BF16)
    flat_ref[...] = weight
    out_ref[...] = jnp.zeros_like(out_ref)
    for frame in range(frames):
        copies[frame].wait()
        product = mat(weight, feat_ref[frame * pixels : (frame + 1) * pixels, :], NT)
        slot = slot_of(frame, devices, group)
        for k in range(pieces):
            taps_ref[k, pl.ds(slot, taps, stride=frames), :] = product[:, k * LANES : (k + 1) * LANES]
    column = lax.broadcasted_iota(jnp.int32, (frames, pixels), 1) % cols

    def tap(a, b, o):
        rows = pl.ds(((a * 3 + b) * 3 + o) * frames, frames)
        return jnp.concatenate([taps_ref[k, rows, :] for k in range(pieces)], axis=1)

    for o in range(3):
        total = None
        for a in range(3):
            part = tap(a, 1, o)
            part = part + jnp.where(column == 0, 0.0, pltpu.roll(tap(a, 0, o), 1, 1))
            part = part + jnp.where(column == cols - 1, 0.0, pltpu.roll(tap(a, 2, o), pixels - 1, 1))
            part = jnp.concatenate([part, jnp.zeros((frames, lanes - pixels), F32)], axis=1)
            if a < 2:
                part = pltpu.roll(part, (2 - a) * cols, 1)
            total = part if total is None else total + part
        own_ref[o * frames : (o + 1) * frames, :] = total
        for part in range(group):
            rows = total[part * devices : (part + 1) * devices, :]
            for k in range(lanes // LANES):
                out_ref[k, pl.ds(o * group + part, devices, stride=pitch), :] = rows[:, k * LANES : (k + 1) * LANES]
    for k in range(lanes // LANES):
        pay_ref[:, k * LANES : (k + 1) * LANES] = out_ref[k].astype(BF16)


def forward_call(features, weight, frames, devices, group, cols, lanes, pitch):
    pixels = features.shape[0] // frames
    channels = features.shape[1]
    return pl.pallas_call(
        functools.partial(forward_kernel, frames=frames, devices=devices, group=group, cols=cols, lanes=lanes),
        out_shape=(
            jax.ShapeDtypeStruct((devices * pitch, lanes), BF16),
            jax.ShapeDtypeStruct((3 * frames, lanes), F32),
            jax.ShapeDtypeStruct((32, channels), BF16),
        ),
        in_specs=[pl.BlockSpec(memory_space=pl.ANY), VM],
        out_specs=(VM,) * 3,
        scratch_shapes=[
            pltpu.VMEM(features.shape, BF16),
            pltpu.VMEM((32, channels), F32),
            pltpu.VMEM((pixels // LANES, 32 * frames, LANES), F32),
            pltpu.VMEM((lanes // LANES, devices * pitch, LANES), F32),
            pltpu.SemaphoreType.DMA((frames,)),
        ],
        compiler_params=WHOLE,
        cost_estimate=pl.CostEstimate(flops=2 * features.size * 27, bytes_accessed=2 * features.size, transcendentals=0),
        name="forward_taps",
    )(features, weight)


def edge_kernel(own_ref, target_ref, wanted_ref, up_ref, down_ref, scr, *, frames, devices, group, block_rows, cols):
    scr[:, 0:cols] = target_ref[...].reshape(scr.shape[0], cols).astype(F32)
    stride = group * 3 * block_rows
    for o in range(3):
        for part in range(group):
            at = o * frames + part * devices
            rows = [
                scr[pl.ds((part * 3 + o) * block_rows + y, devices, stride=stride), :][:, 0:cols]
                for y in range(block_rows)
            ]
            wanted_ref[at : at + devices, :] = jnp.concatenate(rows, axis=1)
    own = own_ref[...]
    wanted = wanted_ref[...]
    up_ref[...] = jnp.concatenate([own[:, 0 : 2 * cols], wanted[:, 0:cols]], axis=1).astype(BF16)
    down_ref[...] = jnp.concatenate(
        [own[:, block_rows * cols : (block_rows + 2) * cols], wanted[:, (block_rows - 1) * cols :]], axis=1
    ).astype(BF16)


def edge_call(own, target, frames, devices, group, block_rows, cols):
    return pl.pallas_call(
        functools.partial(
            edge_kernel, frames=frames, devices=devices, group=group, block_rows=block_rows, cols=cols
        ),
        out_shape=(
            jax.ShapeDtypeStruct((3 * frames, block_rows * cols), F32),
            jax.ShapeDtypeStruct((3 * frames, 3 * cols), BF16),
            jax.ShapeDtypeStruct((3 * frames, 3 * cols), BF16),
        ),
        in_specs=[VM, VM],
        out_specs=(VM,) * 3,
        scratch_shapes=[pltpu.VMEM((frames * 3 * block_rows, LANES), F32)],
        compiler_params=WHOLE,
        cost_estimate=pl.CostEstimate(flops=10**9, bytes_accessed=10**7, transcendentals=0),
        name="edge_rows",
    )(own, target)


def shift_rows(values, step, period):
    size = values.shape[0]
    row = lax.broadcasted_iota(jnp.int32, values.shape, 0) % period
    rolled = pltpu.roll(values, step % size, 0)
    source = row - step
    return jnp.where((source >= 0) & (source < period), rolled, 0.0)


def gate_of(values):
    logistic = 1.0 / (1.0 + jnp.exp(-values))
    return (values * logistic).astype(BF16), logistic * (1.0 + values * (1.0 - logistic))


def disc_kernel(
    pay_ref, gather_ref, scatter_ref, band_hbm, second_hbm, third_hbm, fourth_hbm, head_ref, out_ref,
    zin, band, second, third, fourth, rows_in, act_one, slope_one, cols_two, act_two, slope_two, act_three, cols_four,
    pull_four, pull_three, pull_two, zout, sems, *, devices, group, cols, block_rows, period,
):
    lanes = pay_ref.shape[1]
    pitch = pay_ref.shape[0] // devices
    span = block_rows + 2
    unit = group * period
    wide = 3 * cols
    d1 = (act_one.shape[1]) // (cols // 2 + 2)
    d2, d3, d4 = second.shape[1], third.shape[1], fourth.shape[1]
    x1, x2, x3 = cols // 2, cols // 4, cols // 8
    x4 = x3 - 1
    copies = [
        pltpu.make_async_copy(source, target, sems.at[i])
        for i, (source, target) in enumerate(
            ((band_hbm, band), (second_hbm, second), (third_hbm, third), (fourth_hbm, fourth))
        )
    ]
    for copy in copies:
        copy.start()
    for k in range(lanes // LANES):
        zin[k] = pay_ref[:, k * LANES : (k + 1) * LANES].astype(F32)
    for part in range(group):
        planes = []
        for o in range(3):
            pieces = [zin[k, pl.ds(o * group + part, devices, stride=pitch), :] for k in range(lanes // LANES)]
            planes.append(jnp.concatenate(pieces, axis=1))
        for i in range(span):
            row = jnp.concatenate([plane[:, i * cols : (i + 1) * cols] for plane in planes], axis=1)
            rows_in[pl.ds((i * group + part) * devices, devices), :] = row
    image = mat(gather_ref[...], rows_in[...].astype(BF16)).astype(BF16).astype(F32)
    ext = [image[r * unit : (r + 1) * unit] for r in range(8)]
    ext = [shift_rows(ext[7], 1, period)] + ext + [shift_rows(ext[0], -1, period)]
    ext = [piece.astype(BF16) for piece in ext]
    copies[0].wait()
    left = [jnp.concatenate([ext[a + 2 * p] for p in range(4)], axis=0) for a in range(4)]
    width_one = act_one.shape[1]
    step = 256
    for start in range(0, width_one, step):
        end = min(start + step, width_one)
        pre = mat(left[0], band[0:wide, start:end])
        for a in range(1, 4):
            pre = pre + mat(left[a], band[a * wide : (a + 1) * wide, start:end])
        act, slope = gate_of(pre)
        slope_one[:, start:end] = slope
        act_one[unit : 5 * unit, start:end] = act
        actual = act.astype(F32)
        act_one[0:unit, start:end] = shift_rows(actual[3 * unit :], 1, period).astype(BF16)
        act_one[5 * unit :, start:end] = shift_rows(actual[:unit], -1, period).astype(BF16)
    copies[1].wait()
    for x in range(x2):
        for a in range(4):
            for p in range(2):
                cols_two[(x * 2 + p) * unit : (x * 2 + p + 1) * unit, a * 4 * d1 : (a + 1) * 4 * d1] = act_one[
                    (2 * p + a) * unit : (2 * p + a + 1) * unit, 2 * x * d1 : (2 * x + 4) * d1
                ]
    pre = mat(cols_two[...], second[...])
    act, slope = gate_of(pre)
    slope_two[...] = slope
    act_two[:, 0:d2] = jnp.zeros((4 * unit, d2), BF16)
    act_two[:, (x2 + 1) * d2 :] = jnp.zeros((4 * unit, d2), BF16)
    for x in range(x2):
        block = act[x * 2 * unit : (x + 1) * 2 * unit]
        actual = block.astype(F32)
        at = slice((x + 1) * d2, (x + 2) * d2)
        act_two[unit : 3 * unit, at] = block
        act_two[0:unit, at] = shift_rows(actual[unit:], 1, period).astype(BF16)
        act_two[3 * unit :, at] = shift_rows(actual[:unit], -1, period).astype(BF16)
    copies[2].wait()
    left = jnp.concatenate(
        [
            jnp.concatenate([act_two[a * unit : (a + 1) * unit, 2 * x * d2 : (2 * x + 4) * d2] for a in range(4)], axis=1)
            for x in range(x3)
        ],
        axis=0,
    )
    act, slope_three = gate_of(mat(left, third[...]))
    act_three[:, 0:d3] = jnp.zeros((4 * unit, d3), BF16)
    act_three[:, (x3 + 1) * d3 :] = jnp.zeros((4 * unit, d3), BF16)
    for x in range(x3):
        block = act[x * unit : (x + 1) * unit]
        actual = block.astype(F32)
        at = slice((x + 1) * d3, (x + 2) * d3)
        act_three[unit : 2 * unit, at] = block
        for a in (0, 2, 3):
            act_three[a * unit : (a + 1) * unit, at] = shift_rows(actual, 1 - a, period).astype(BF16)
    for x in range(x4):
        for a in range(4):
            cols_four[x * unit : (x + 1) * unit, a * 4 * d3 : (a + 1) * 4 * d3] = act_three[
                a * unit : (a + 1) * unit, x * d3 : (x + 4) * d3
            ]
    copies[3].wait()
    pre = mat(cols_four[...], fourth[...])
    _, slope = gate_of(pre)
    row = lax.broadcasted_iota(jnp.int32, (unit, d4), 0) % period
    head = head_ref[...].astype(F32) * -loss_scale
    heads = []
    for x in range(x4):
        total = None
        for a in range(4):
            taps = [head[a * 4 + b : a * 4 + b + 1, :] for b in range(4) if 0 <= x - b + 1 < x4 - 1]
            tap = functools.reduce(lambda u, v: u + v, taps)
            inside = (row - a + 1 >= 0) & (row - a + 1 < period - 2) & (row < period - 1)
            term = jnp.where(inside, jnp.broadcast_to(tap, (unit, d4)), 0.0)
            total = term if total is None else total + term
        heads.append(total)
    cot = (jnp.concatenate(heads, axis=0) * slope).astype(BF16)
    pull_four[...] = mat(cot, fourth[...], NT)
    cots = []
    for x in range(x3):
        total = None
        for a in range(4):
            term = None
            for b in range(4):
                source = x - b + 1
                if 0 <= source < x4:
                    piece = pull_four[source * unit : (source + 1) * unit, (a * 4 + b) * d3 : (a * 4 + b + 1) * d3]
                    term = piece if term is None else term + piece
            if a != 1:
                term = shift_rows(term, a - 1, period)
            total = term if total is None else total + term
        cots.append((total * slope_three[x * unit : (x + 1) * unit]).astype(BF16))
    pull_three[...] = mat(jnp.concatenate(cots, axis=0), third[...], NT)
    cots = []
    for x in range(x2):
        terms = []
        for a in range(4):
            term = None
            for b in range(4):
                if (x - b + 1) % 2 == 0 and 0 <= (x - b + 1) // 2 < x3:
                    source = (x - b + 1) // 2
                    piece = pull_three[source * unit : (source + 1) * unit, (a * 4 + b) * d2 : (a * 4 + b + 1) * d2]
                    term = piece if term is None else term + piece
            terms.append(term)
        even = terms[1] + shift_rows(terms[3], 1, period)
        odd = terms[2] + shift_rows(terms[0], -1, period)
        both = jnp.concatenate([even, odd], axis=0)
        cots.append((both * slope_two[x * 2 * unit : (x + 1) * 2 * unit]).astype(BF16))
    pull_two[...] = mat(jnp.concatenate(cots, axis=0), second[...], NT)
    strips = []
    for k in range(x2 + 1):
        terms = {}
        for p in range(2):
            for a in range(4):
                term = None
                if k < x2:
                    term = pull_two[(2 * k + p) * unit : (2 * k + p + 1) * unit, a * 4 * d1 : (a * 4 + 2) * d1]
                if k > 0:
                    other = pull_two[(2 * k - 2 + p) * unit : (2 * k - 1 + p) * unit, (a * 4 + 2) * d1 : (a + 1) * 4 * d1]
                    term = other if term is None else term + other
                terms[p, a] = term
        both = jnp.concatenate(
            [
                terms[0, 1] + shift_rows(terms[1, 3], 1, period),
                terms[0, 2] + terms[1, 0],
                terms[0, 3] + terms[1, 1],
                terms[1, 2] + shift_rows(terms[0, 0], -1, period),
            ],
            axis=0,
        )
        strips.append((both * slope_one[:, 2 * k * d1 : (2 * k + 2) * d1]).astype(BF16))
    cot = jnp.concatenate(strips, axis=1)
    pulls = [mat(cot, band[a * wide : (a + 1) * wide, :], NT) for a in range(4)]
    part = lambda p, a: pulls[a][p * unit : (p + 1) * unit]
    phases = []
    for r in range(8):
        terms = [part(p, a) for p in range(4) for a in range(4) if 2 * p + a - 1 == r]
        if r == 0:
            terms.append(shift_rows(part(3, 3), 1, period))
        if r == 7:
            terms.append(shift_rows(part(0, 0), -1, period))
        phases.append(functools.reduce(lambda u, v: u + v, terms))
    image = jnp.concatenate(phases, axis=0).astype(BF16)
    rows = mat(scatter_ref[...], image)
    zout[...] = jnp.zeros_like(zout)
    for part_at in range(group):
        picked = [rows[(i * group + part_at) * devices : (i * group + part_at + 1) * devices] for i in range(span)]
        for o in range(3):
            plane = [piece[:, o * cols : (o + 1) * cols] for piece in picked]
            plane.append(jnp.zeros((devices, lanes - span * cols), F32))
            plane = jnp.concatenate(plane, axis=1)
            for k in range(lanes // LANES):
                zout[k, pl.ds(o * group + part_at, devices, stride=pitch), :] = plane[:, k * LANES : (k + 1) * LANES]
    for k in range(lanes // LANES):
        out_ref[:, k * LANES : (k + 1) * LANES] = zout[k].astype(BF16)


def row_maps(devices, group, block_rows):
    height = devices * block_rows
    period = height // 8
    span = block_rows + 2
    gather = np.zeros((8 * group * period, span * group * devices), np.float32)
    for device in range(devices):
        for i in range(span):
            y = device * block_rows + i - 1
            if 0 <= y < height:
                for part in range(group):
                    gather[((y % 8) * group + part) * period + y // 8, (i * group + part) * devices + device] = 1.0
    return gather


def band_of(first, cols):
    d1 = first.shape[-1]
    width = (cols // 2 + 2) * d1
    x = np.arange(cols)[:, None]
    out_x = np.arange(width)[None, :] // d1 - 1
    tap = x - 2 * out_x + 1
    inside = (out_x >= 0) & (out_x < cols // 2)
    tiled = jnp.tile(first, (1, 1, 1, cols // 2 + 2))
    band = jnp.zeros((4, 3, cols, width), BF16)
    for b in range(4):
        band = jnp.where(jnp.asarray((tap == b) & inside), tiled[:, b, :, None, :], band)
    return band.reshape(4 * 3 * cols, width)


def disc_call(payload, first, second, third, fourth, head, devices, group, cols, block_rows):
    period = devices * block_rows // 8
    unit = group * period
    d1, d2, d3, d4 = first.shape[-1], second.shape[-1], third.shape[-1], fourth.shape[-1]
    x2, x3 = cols // 4, cols // 8
    x4 = x3 - 1
    gather = row_maps(devices, group, block_rows)
    band = band_of(first, cols)
    args = (
        payload,
        jnp.asarray(gather, BF16),
        jnp.asarray(gather.T, BF16),
        band,
        second.reshape(16 * d1, d2),
        third.reshape(16 * d2, d3),
        fourth.reshape(16 * d3, d4),
        head.reshape(16, d4),
    )
    lanes = payload.shape[1]
    return pl.pallas_call(
        functools.partial(
            disc_kernel, devices=devices, group=group, cols=cols, block_rows=block_rows, period=period
        ),
        out_shape=jax.ShapeDtypeStruct(payload.shape, BF16),
        in_specs=[VM, VM, VM, HBM, HBM, HBM, HBM, VM],
        out_specs=VM,
        scratch_shapes=[
            pltpu.VMEM((lanes // LANES, payload.shape[0], LANES), F32),
            pltpu.VMEM(band.shape, BF16),
            pltpu.VMEM((16 * d1, d2), BF16),
            pltpu.VMEM((16 * d2, d3), BF16),
            pltpu.VMEM((16 * d3, d4), BF16),
            pltpu.VMEM((gather.shape[1], 3 * cols), F32),
            pltpu.VMEM((6 * unit, band.shape[1]), BF16),
            pltpu.VMEM((4 * unit, band.shape[1]), F32),
            pltpu.VMEM((x2 * 2 * unit, 16 * d1), BF16),
            pltpu.VMEM((4 * unit, (x2 + 2) * d2), BF16),
            pltpu.VMEM((x2 * 2 * unit, d2), F32),
            pltpu.VMEM((4 * unit, (x3 + 2) * d3), BF16),
            pltpu.VMEM((x4 * unit, 16 * d3), BF16),
            pltpu.VMEM((x4 * unit, 16 * d3), F32),
            pltpu.VMEM((x3 * unit, 16 * d2), F32),
            pltpu.VMEM((x2 * 2 * unit, 16 * d1), F32),
            pltpu.VMEM((lanes // LANES, payload.shape[0], LANES), F32),
            pltpu.SemaphoreType.DMA((4,)),
        ],
        compiler_params=WHOLE,
        cost_estimate=pl.CostEstimate(flops=4 * 10**9, bytes_accessed=8 * 10**6, transcendentals=10**6),
        name="disc_rows",
    )(*args)


def put_taps(plane, taps_ref, frames, cols, pieces, padded):
    lanes = plane.shape[1]
    column = lax.broadcasted_iota(jnp.int32, plane.shape, 1) % cols
    for b in range(3):
        moved = plane
        if b == 0:
            moved = jnp.where(column == cols - 1, 0.0, pltpu.roll(plane, lanes - 1, 1))
        if b == 2:
            moved = jnp.where(column == 0, 0.0, pltpu.roll(plane, 1, 1))
        for a in range(3):
            turned = moved if a == 2 else pltpu.roll(moved, lanes - (2 - a) * cols, 1)
            for k in range(pieces):
                taps_ref[k, pl.ds((a * 3 + b) * 3 * frames, 3 * frames), :] = turned[:, k * LANES : (k + 1) * LANES]
    for k in range(pieces):
        taps_ref[k, pl.ds(27 * frames, (padded - 27) * frames), :] = jnp.zeros(((padded - 27) * frames, LANES), F32)


def weigh(taps_ref, taps_out, feat_ref, copies, frames, devices, group, pieces, padded):
    pixels = pieces * LANES
    total = jnp.zeros((padded, feat_ref.shape[1]), F32)
    for frame in range(frames):
        rows = pl.ds(slot_of(frame, devices, group), padded, stride=frames)
        taps = jnp.concatenate([taps_ref[k, rows, :] for k in range(pieces)], axis=1).astype(BF16)
        taps_out[frame] = taps
        copies[frame].wait()
        total = total + mat(taps, feat_ref[frame * pixels : (frame + 1) * pixels, :])
    return total


def fetch(feat_hbm, feat_ref, sems, frames):
    pixels = feat_ref.shape[0] // frames
    copies = [
        pltpu.make_async_copy(
            feat_hbm.at[pl.ds(frame * pixels, pixels), :], feat_ref.at[pl.ds(frame * pixels, pixels), :], sems.at[frame]
        )
        for frame in range(frames)
    ]
    for copy in copies:
        copy.start()
    return copies


def rec_kernel(
    ends_ref, own_ref, wanted_ref, above_ref, below_ref, feat_hbm, taps_out, part_ref, feat_ref, taps_ref, sems,
    *, frames, devices, group, cols, block_rows,
):
    copies = fetch(feat_hbm, feat_ref, sems, frames)
    lanes = own_ref.shape[1]
    pieces = block_rows * cols // LANES
    none = lambda count: jnp.zeros((3 * frames, count), F32)
    rest = none(lanes - (block_rows + 2) * cols)
    above, below = above_ref[...].astype(F32), below_ref[...].astype(F32)
    added = jnp.concatenate(
        [above[:, : 2 * cols], none((block_rows - 2) * cols), below[:, : 2 * cols], rest], axis=1
    )
    asked = jnp.concatenate([above[:, 2 * cols :], wanted_ref[...], below[:, 2 * cols :], rest], axis=1)
    lane = lax.broadcasted_iota(jnp.int32, (3 * frames, lanes), 1)
    plane = loss_scale * (own_ref[...] + added - asked)
    plane = jnp.where((lane >= ends_ref[0]) & (lane < ends_ref[1]), plane, 0.0)
    put_taps(plane, taps_ref, frames, cols, pieces, taps_out.shape[1])
    part_ref[...] = weigh(taps_ref, taps_out, feat_ref, copies, frames, devices, group, pieces, taps_out.shape[1])


def gan_kernel(
    plane_ref, feat_hbm, taps_out, part_ref, feat_ref, taps_ref, zin, sems, *, frames, devices, group, cols, block_rows
):
    copies = fetch(feat_hbm, feat_ref, sems, frames)
    lanes = plane_ref.shape[1]
    pieces = block_rows * cols // LANES
    pitch = plane_ref.shape[0] // devices
    for k in range(lanes // LANES):
        zin[k] = plane_ref[:, k * LANES : (k + 1) * LANES].astype(F32)
    blocks = []
    for o in range(3):
        for part in range(group):
            row = pl.ds(o * group + part, devices, stride=pitch)
            blocks.append(jnp.concatenate([zin[k, row, :] for k in range(lanes // LANES)], axis=1))
    plane = jnp.concatenate(blocks, axis=0)
    put_taps(plane, taps_ref, frames, cols, pieces, taps_out.shape[1])
    total = weigh(taps_ref, taps_out, feat_ref, copies, frames, devices, group, pieces, taps_out.shape[1])
    total = total.astype(BF16)
    for i in range(part_ref.shape[0]):
        part_ref[i] = total


def taps_call(kernel, specs, operands, features, part, extra, frames, devices, group, cols, block_rows, name):
    return pl.pallas_call(
        functools.partial(kernel, frames=frames, devices=devices, group=group, cols=cols, block_rows=block_rows),
        out_shape=(jax.ShapeDtypeStruct((frames, 32, block_rows * cols), BF16), part),
        in_specs=specs + [HBM],
        out_specs=(VM, VM),
        scratch_shapes=[
            pltpu.VMEM(features.shape, BF16),
            pltpu.VMEM((block_rows * cols // LANES, 32 * frames, LANES), F32),
            *extra,
            pltpu.SemaphoreType.DMA((frames,)),
        ],
        compiler_params=WHOLE,
        cost_estimate=pl.CostEstimate(
            flops=2 * features.size * 27, bytes_accessed=2 * features.size, transcendentals=0
        ),
        name=name,
    )(*operands, features)


def final_kernel(
    rec_hbm, gan_hbm, rec_sum, gan_sums, weight_ref, out_hbm, grad_ref, adapt_ref, rec_ref, gan_ref, both_ref, out_ref,
    in_sems, out_sems, *, pixels, chunk,
):
    frames, padded, block = rec_ref.shape
    loads = []
    for at in range(0, frames, chunk):
        part = pl.ds(at, chunk)
        loads.append(pltpu.make_async_copy(rec_hbm.at[part], rec_ref.at[part], in_sems.at[0, at // chunk]))
        loads.append(pltpu.make_async_copy(gan_hbm.at[part], gan_ref.at[part], in_sems.at[1, at // chunk]))
    for copy in loads:
        copy.start()
    gan = gan_sums[0].astype(F32)
    for i in range(1, gan_sums.shape[0]):
        gan = gan + gan_sums[i].astype(F32)
    rec = rec_sum[...]
    norm = lambda values: jnp.sqrt(jnp.sum(jnp.sum(values * values, axis=1, keepdims=True), axis=0, keepdims=True))
    adaptive = norm(rec) / (norm(gan) + epsilon)
    grad = (rec + adaptive * gan) / pixels
    for a in range(3):
        for b in range(3):
            at = (a * 3 + b) * 3
            grad_ref[a, b] = grad[at : at + 3, :]
    adapt_ref[...] = adaptive
    weight = weight_ref[...]
    both_ref[:padded] = weight
    both_ref[padded:] = (adaptive * weight.astype(F32)).astype(BF16)
    stores = []
    for frame in range(frames):
        if frame % chunk == 0:
            loads[frame // chunk * 2].wait()
            loads[frame // chunk * 2 + 1].wait()
        left = jnp.concatenate([rec_ref[frame], gan_ref[frame]], axis=0)
        out_ref[frame * block : (frame + 1) * block] = mat(left, both_ref[...], TN).astype(BF16)
        rows = pl.ds(frame * block, block)
        stores.append(pltpu.make_async_copy(out_ref.at[rows], out_hbm.at[rows], out_sems.at[frame]))
        stores[-1].start()
    for copy in stores:
        copy.wait()


def final_call(rec_taps, gan_taps, rec_sum, gan_sums, weight, pixels):
    frames, padded, block = rec_taps.shape
    channels = weight.shape[1]
    chunk = 4
    return pl.pallas_call(
        functools.partial(final_kernel, pixels=pixels, chunk=chunk),
        out_shape=(
            jax.ShapeDtypeStruct((frames * block, channels), BF16),
            jax.ShapeDtypeStruct((3, 3, 3, channels), F32),
            jax.ShapeDtypeStruct((1, 1), F32),
        ),
        in_specs=[HBM, HBM, VM, VM, VM],
        out_specs=(HBM, VM, VM),
        scratch_shapes=[
            pltpu.VMEM(rec_taps.shape, BF16),
            pltpu.VMEM(gan_taps.shape, BF16),
            pltpu.VMEM((2 * padded, channels), BF16),
            pltpu.VMEM((frames * block, channels), BF16),
            pltpu.SemaphoreType.DMA((2, frames // chunk)),
            pltpu.SemaphoreType.DMA((frames,)),
        ],
        compiler_params=WHOLE,
        cost_estimate=pl.CostEstimate(
            flops=4 * frames * block * channels * padded, bytes_accessed=4 * frames * block * channels, transcendentals=0
        ),
        name="feature_pull",
    )(rec_taps, gan_taps, rec_sum, gan_sums, weight)


def per_device(
    features, target, conv_weight, disc_first, disc_second, disc_third, disc_fourth, disc_head
):
    devices = lax.axis_size("row")
    clips = lax.axis_size("clip")
    _, frames, block_rows, cols, channels = features.shape
    group = frames // devices
    pixels = clips * devices * frames * block_rows * cols
    lanes = up_to((block_rows + 2) * cols, LANES)
    pitch = up_to(3 * group, 8)
    edge = lax.axis_index("row")
    feats = features.reshape(frames * block_rows * cols, channels)
    payload, own, weight = forward_call(feats, conv_weight, frames, devices, group, cols, lanes, pitch)
    trade = lambda values: lax.all_to_all(
        values.reshape(devices, pitch, lanes), "row", split_axis=0, concat_axis=0, tiled=True
    ).reshape(devices * pitch, lanes)
    arrived = trade(payload)
    wanted, upward, downward = edge_call(
        own, target[0].transpose(0, 2, 1, 3), frames, devices, group, block_rows, cols
    )
    below = lax.ppermute(upward, "row", [(i + 1, i) for i in range(devices - 1)])
    above = lax.ppermute(downward, "row", [(i, i + 1) for i in range(devices - 1)])
    ends = jnp.stack(
        [
            jnp.where(edge == 0, cols, 0),
            jnp.where(edge == devices - 1, (block_rows + 1) * cols, (block_rows + 2) * cols),
        ]
    ).astype(jnp.int32)
    rec_taps, rec_part = taps_call(
        rec_kernel, [pl.BlockSpec(memory_space=pltpu.SMEM), VM, VM, VM, VM], (ends, own, wanted, above, below), feats,
        jax.ShapeDtypeStruct((32, channels), F32), [], frames, devices, group, cols, block_rows, "rec_taps",
    )
    rec_sum = lax.psum(rec_part, ("clip", "row"))
    sent = disc_call(
        arrived, disc_first, disc_second, disc_third, disc_fourth, disc_head, devices, group, cols, block_rows
    )
    returned = trade(sent)
    gan_taps, gan_part = taps_call(
        gan_kernel, [VM], (returned,), feats, jax.ShapeDtypeStruct((clips * devices, 32, channels), BF16),
        [pltpu.VMEM((lanes // LANES, devices * pitch, LANES), F32)], frames, devices, group, cols, block_rows, "gan_taps",
    )
    gan_sums = lax.all_to_all(gan_part, ("clip", "row"), split_axis=0, concat_axis=0, tiled=True)
    image_back = returned.reshape(devices, pitch, lanes)[:, : 3 * group, cols : (block_rows + 1) * cols]
    image_back = image_back.reshape(devices, 3, group, block_rows, cols).transpose(0, 2, 3, 1, 4)
    image_back = image_back.reshape(1, frames, block_rows, 3, cols)
    feature_grad, weight_grad, adaptive = final_call(rec_taps, gan_taps, rec_sum, gan_sums, weight, pixels)
    return (feature_grad.reshape(features.shape), image_back, weight_grad, adaptive[0, 0])


def solution(mesh):
    rows = P("clip", None, "row", None, None)
    return jax.shard_map(
        per_device,
        mesh=mesh,
        in_specs=(rows, rows, P(), P(), P(), P(), P(), P()),
        out_specs=(rows, rows, P(), P()),
        check_vma=False,
    )
```

```python
import functools

import jax
import jax.numpy as jnp
import numpy as np
from jax import lax
from jax.experimental import pallas as pl
from jax.experimental.pallas import tpu as pltpu
from jax.sharding import PartitionSpec as P

loss_scale = 64.0
epsilon = 0.0001
F32 = jnp.float32
BF16 = jnp.bfloat16
LANES = 128
NN = (((1,), (0,)), ((), ()))
NT = (((1,), (1,)), ((), ()))
TN = (((0,), (0,)), ((), ()))
VM = pl.BlockSpec(memory_space=pltpu.VMEM)
HBM = pl.BlockSpec(memory_space=pl.ANY)
WHOLE = pltpu.CompilerParams(vmem_limit_bytes=60 * 2**20)
PART = pltpu.CompilerParams(vmem_limit_bytes=24 * 2**20)


def up_to(value, step):
    return -(-value // step) * step


def mat(left, right, dims=NN):
    return lax.dot_general(left, right, dims, preferred_element_type=F32)


def slot_of(frame, devices, group):
    return (frame % group) * devices + frame // group


def forward_kernel(
    feat_ref, weight_ref, pay_ref, own_ref, flat_ref, weight_scr, taps_ref, out_ref, *, frames, devices, group, cols, lanes
):
    pixels = feat_ref.shape[0] // frames
    pieces = pixels // LANES
    pitch = out_ref.shape[1] // devices
    taps = flat_ref.shape[0]
    weight_scr[...] = jnp.zeros_like(weight_scr)
    for a in range(3):
        for b in range(3):
            at = (a * 3 + b) * 3
            weight_scr[at : at + 3, :] = weight_ref[a, b].astype(F32)
    weight = weight_scr[...].astype(BF16)
    flat_ref[...] = weight
    out_ref[...] = jnp.zeros_like(out_ref)
    for frame in range(frames):
        product = mat(weight, feat_ref[frame * pixels : (frame + 1) * pixels, :], NT)
        slot = slot_of(frame, devices, group)
        for k in range(pieces):
            taps_ref[k, pl.ds(slot, taps, stride=frames), :] = product[:, k * LANES : (k + 1) * LANES]
    column = lax.broadcasted_iota(jnp.int32, (frames, pixels), 1) % cols

    def tap(a, b, o):
        rows = pl.ds(((a * 3 + b) * 3 + o) * frames, frames)
        return jnp.concatenate([taps_ref[k, rows, :] for k in range(pieces)], axis=1)

    for o in range(3):
        total = None
        for a in range(3):
            part = tap(a, 1, o)
            part = part + jnp.where(column == 0, 0.0, pltpu.roll(tap(a, 0, o), 1, 1))
            part = part + jnp.where(column == cols - 1, 0.0, pltpu.roll(tap(a, 2, o), pixels - 1, 1))
            part = jnp.concatenate([part, jnp.zeros((frames, lanes - pixels), F32)], axis=1)
            if a < 2:
                part = pltpu.roll(part, (2 - a) * cols, 1)
            total = part if total is None else total + part
        own_ref[o * frames : (o + 1) * frames, :] = total
        for part in range(group):
            rows = total[part * devices : (part + 1) * devices, :]
            for k in range(lanes // LANES):
                out_ref[k, pl.ds(o * group + part, devices, stride=pitch), :] = rows[:, k * LANES : (k + 1) * LANES]
    for k in range(lanes // LANES):
        pay_ref[:, k * LANES : (k + 1) * LANES] = out_ref[k].astype(BF16)


def forward_call(features, weight, frames, devices, group, cols, lanes, pitch):
    pixels = features.shape[0] // frames
    channels = features.shape[1]
    return pl.pallas_call(
        functools.partial(forward_kernel, frames=frames, devices=devices, group=group, cols=cols, lanes=lanes),
        out_shape=(
            jax.ShapeDtypeStruct((devices * pitch, lanes), BF16),
            jax.ShapeDtypeStruct((3 * frames, lanes), F32),
            jax.ShapeDtypeStruct((32, channels), BF16),
        ),
        in_specs=[VM, VM],
        out_specs=(VM,) * 3,
        scratch_shapes=[
            pltpu.VMEM((32, channels), F32),
            pltpu.VMEM((pixels // LANES, 32 * frames, LANES), F32),
            pltpu.VMEM((lanes // LANES, devices * pitch, LANES), F32),
        ],
        compiler_params=PART,
        cost_estimate=pl.CostEstimate(flops=2 * features.size * 27, bytes_accessed=2 * features.size, transcendentals=0),
        name="forward_taps",
    )(features, weight)


def edge_kernel(own_ref, target_ref, wanted_ref, up_ref, down_ref, scr, *, frames, devices, group, block_rows, cols):
    scr[:, 0:cols] = target_ref[...].reshape(scr.shape[0], cols).astype(F32)
    stride = group * 3 * block_rows
    for o in range(3):
        for part in range(group):
            at = o * frames + part * devices
            rows = [
                scr[pl.ds((part * 3 + o) * block_rows + y, devices, stride=stride), :][:, 0:cols]
                for y in range(block_rows)
            ]
            wanted_ref[at : at + devices, :] = jnp.concatenate(rows, axis=1)
    own = own_ref[...]
    wanted = wanted_ref[...]
    up_ref[...] = jnp.concatenate([own[:, 0 : 2 * cols], wanted[:, 0:cols]], axis=1).astype(BF16)
    down_ref[...] = jnp.concatenate(
        [own[:, block_rows * cols : (block_rows + 2) * cols], wanted[:, (block_rows - 1) * cols :]], axis=1
    ).astype(BF16)


def edge_call(own, target, frames, devices, group, block_rows, cols):
    return pl.pallas_call(
        functools.partial(
            edge_kernel, frames=frames, devices=devices, group=group, block_rows=block_rows, cols=cols
        ),
        out_shape=(
            jax.ShapeDtypeStruct((3 * frames, block_rows * cols), F32),
            jax.ShapeDtypeStruct((3 * frames, 3 * cols), BF16),
            jax.ShapeDtypeStruct((3 * frames, 3 * cols), BF16),
        ),
        in_specs=[VM, VM],
        out_specs=(VM,) * 3,
        scratch_shapes=[pltpu.VMEM((frames * 3 * block_rows, LANES), F32)],
        compiler_params=PART,
        cost_estimate=pl.CostEstimate(flops=10**9, bytes_accessed=10**7, transcendentals=0),
        name="edge_rows",
    )(own, target)


def shift_rows(values, step, period):
    size = values.shape[0]
    row = lax.broadcasted_iota(jnp.int32, values.shape, 0) % period
    rolled = pltpu.roll(values, step % size, 0)
    source = row - step
    return jnp.where((source >= 0) & (source < period), rolled, 0.0)


def gate_of(values):
    logistic = 1.0 / (1.0 + jnp.exp(-values))
    return (values * logistic).astype(BF16), logistic * (1.0 + values * (1.0 - logistic))


def disc_kernel(
    pay_ref, gather_ref, window_ref, band_ref, second_hbm, third_hbm, fourth_hbm, head_ref, unwindow_hbm, scatter_hbm, out_ref,
    zin, second, third, fourth, unwindow, scatter, rows_in, act_one, slope_one, cols_two, act_two, slope_two, act_three, cols_four,
    pull_four, pull_three, pull_two, zout, sems, *, devices, group, cols, block_rows, period,
):
    lanes = pay_ref.shape[1]
    pitch = pay_ref.shape[0] // devices
    span = block_rows + 2
    unit = group * period
    wide = 3 * cols
    d1 = (act_one.shape[1]) // (cols // 2 + 2)
    d2, d3, d4 = second.shape[1], third.shape[1], fourth.shape[1]
    x1, x2, x3 = cols // 2, cols // 4, cols // 8
    x4 = x3 - 1
    copies = [
        pltpu.make_async_copy(source, target, sems.at[i])
        for i, (source, target) in enumerate(
            (
                (second_hbm, second),
                (third_hbm, third),
                (fourth_hbm, fourth),
                (unwindow_hbm, unwindow),
                (scatter_hbm, scatter),
            )
        )
    ]
    for copy in copies:
        copy.start()
    for k in range(lanes // LANES):
        zin[k] = pay_ref[:, k * LANES : (k + 1) * LANES].astype(F32)
    for part in range(group):
        planes = []
        for o in range(3):
            pieces = [zin[k, pl.ds(o * group + part, devices, stride=pitch), :] for k in range(lanes // LANES)]
            planes.append(jnp.concatenate(pieces, axis=1))
        for i in range(span):
            row = jnp.concatenate([plane[:, i * cols : (i + 1) * cols] for plane in planes], axis=1)
            rows_in[pl.ds((i * group + part) * devices, devices), :] = row
    image = mat(gather_ref[...], rows_in[...].astype(BF16)).astype(BF16)
    wins = mat(image, window_ref[...])
    ext = [wins[r * unit : (r + 1) * unit] for r in range(8)]
    ext = [shift_rows(ext[7], 1, period)] + ext + [shift_rows(ext[0], -1, period)]
    width_one = act_one.shape[1]
    strip = 8 * d1
    band = band_ref[...]
    for k in range(-(-width_one // strip)):
        low, high = slice(2 * k * LANES, (2 * k + 1) * LANES), slice((2 * k + 1) * LANES, (2 * k + 2) * LANES)
        left = jnp.concatenate(
            [
                jnp.concatenate([ext[2 * p + h][:, low] + ext[2 * p + h + 1][:, high] for p in range(4)], axis=0)
                for h in (0, 2)
            ],
            axis=1,
        ).astype(BF16)
        start, end = k * strip, min((k + 1) * strip, width_one)
        act, slope = gate_of(mat(left, band[:, : end - start]))
        if k == 0 or end == width_one:
            lane = start + lax.broadcasted_iota(jnp.int32, slope.shape, 1)
            inside = (lane >= d1) & (lane < width_one - d1)
            slope = jnp.where(inside, slope, 0.0)
            act = jnp.where(inside, act.astype(F32), 0.0).astype(BF16)
        slope_one[:, start:end] = slope
        act_one[unit : 5 * unit, start:end] = act
        actual = act.astype(F32)
        act_one[0:unit, start:end] = shift_rows(actual[3 * unit :], 1, period).astype(BF16)
        act_one[5 * unit :, start:end] = shift_rows(actual[:unit], -1, period).astype(BF16)
    copies[0].wait()
    for x in range(x2):
        for a in range(4):
            for p in range(2):
                cols_two[(x * 2 + p) * unit : (x * 2 + p + 1) * unit, a * 4 * d1 : (a + 1) * 4 * d1] = act_one[
                    (2 * p + a) * unit : (2 * p + a + 1) * unit, 2 * x * d1 : (2 * x + 4) * d1
                ]
    pre = mat(cols_two[...], second[...])
    act, slope = gate_of(pre)
    slope_two[...] = slope
    act_two[:, 0:d2] = jnp.zeros((4 * unit, d2), BF16)
    act_two[:, (x2 + 1) * d2 :] = jnp.zeros((4 * unit, d2), BF16)
    for x in range(x2):
        block = act[x * 2 * unit : (x + 1) * 2 * unit]
        actual = block.astype(F32)
        at = slice((x + 1) * d2, (x + 2) * d2)
        act_two[unit : 3 * unit, at] = block
        act_two[0:unit, at] = shift_rows(actual[unit:], 1, period).astype(BF16)
        act_two[3 * unit :, at] = shift_rows(actual[:unit], -1, period).astype(BF16)
    copies[1].wait()
    left = jnp.concatenate(
        [
            jnp.concatenate([act_two[a * unit : (a + 1) * unit, 2 * x * d2 : (2 * x + 4) * d2] for a in range(4)], axis=1)
            for x in range(x3)
        ],
        axis=0,
    )
    act, slope_three = gate_of(mat(left, third[...]))
    act_three[:, 0:d3] = jnp.zeros((4 * unit, d3), BF16)
    act_three[:, (x3 + 1) * d3 :] = jnp.zeros((4 * unit, d3), BF16)
    for x in range(x3):
        block = act[x * unit : (x + 1) * unit]
        actual = block.astype(F32)
        at = slice((x + 1) * d3, (x + 2) * d3)
        act_three[unit : 2 * unit, at] = block
        for a in (0, 2, 3):
            act_three[a * unit : (a + 1) * unit, at] = shift_rows(actual, 1 - a, period).astype(BF16)
    for x in range(x4):
        for a in range(4):
            cols_four[x * unit : (x + 1) * unit, a * 4 * d3 : (a + 1) * 4 * d3] = act_three[
                a * unit : (a + 1) * unit, x * d3 : (x + 4) * d3
            ]
    copies[2].wait()
    pre = mat(cols_four[...], fourth[...])
    _, slope = gate_of(pre)
    row = lax.broadcasted_iota(jnp.int32, (unit, d4), 0) % period
    head = head_ref[...].astype(F32) * -loss_scale
    heads = []
    for x in range(x4):
        total = None
        for a in range(4):
            taps = [head[a * 4 + b : a * 4 + b + 1, :] for b in range(4) if 0 <= x - b + 1 < x4 - 1]
            tap = functools.reduce(lambda u, v: u + v, taps)
            inside = (row - a + 1 >= 0) & (row - a + 1 < period - 2) & (row < period - 1)
            term = jnp.where(inside, jnp.broadcast_to(tap, (unit, d4)), 0.0)
            total = term if total is None else total + term
        heads.append(total)
    cot = (jnp.concatenate(heads, axis=0) * slope).astype(BF16)
    pull_four[...] = mat(cot, fourth[...], NT)
    cots = []
    for x in range(x3):
        total = None
        for a in range(4):
            term = None
            for b in range(4):
                source = x - b + 1
                if 0 <= source < x4:
                    piece = pull_four[source * unit : (source + 1) * unit, (a * 4 + b) * d3 : (a * 4 + b + 1) * d3]
                    term = piece if term is None else term + piece
            if a != 1:
                term = shift_rows(term, a - 1, period)
            total = term if total is None else total + term
        cots.append((total * slope_three[x * unit : (x + 1) * unit]).astype(BF16))
    pull_three[...] = mat(jnp.concatenate(cots, axis=0), third[...], NT)
    cots = []
    for x in range(x2):
        terms = []
        for a in range(4):
            term = None
            for b in range(4):
                if (x - b + 1) % 2 == 0 and 0 <= (x - b + 1) // 2 < x3:
                    source = (x - b + 1) // 2
                    piece = pull_three[source * unit : (source + 1) * unit, (a * 4 + b) * d2 : (a * 4 + b + 1) * d2]
                    term = piece if term is None else term + piece
            terms.append(term)
        even = terms[1] + shift_rows(terms[3], 1, period)
        odd = terms[2] + shift_rows(terms[0], -1, period)
        both = jnp.concatenate([even, odd], axis=0)
        cots.append((both * slope_two[x * 2 * unit : (x + 1) * 2 * unit]).astype(BF16))
    pull_two[...] = mat(jnp.concatenate(cots, axis=0), second[...], NT)
    strips = []
    for k in range(x2 + 1):
        terms = {}
        for p in range(2):
            for a in range(4):
                term = None
                if k < x2:
                    term = pull_two[(2 * k + p) * unit : (2 * k + p + 1) * unit, a * 4 * d1 : (a * 4 + 2) * d1]
                if k > 0:
                    other = pull_two[(2 * k - 2 + p) * unit : (2 * k - 1 + p) * unit, (a * 4 + 2) * d1 : (a + 1) * 4 * d1]
                    term = other if term is None else term + other
                terms[p, a] = term
        both = jnp.concatenate(
            [
                terms[0, 1] + shift_rows(terms[1, 3], 1, period),
                terms[0, 2] + terms[1, 0],
                terms[0, 3] + terms[1, 1],
                terms[1, 2] + shift_rows(terms[0, 0], -1, period),
            ],
            axis=0,
        )
        strips.append((both * slope_one[:, 2 * k * d1 : (2 * k + 2) * d1]).astype(BF16))
    cot = jnp.concatenate(strips, axis=1)
    copies[3].wait()
    copies[4].wait()
    sums = []
    for k in range(-(-width_one // strip)):
        start, end = k * strip, min((k + 1) * strip, width_one)
        pulls = mat(cot[:, start:end], band[:, : end - start], NT)
        groups = []
        for m in range(5):
            terms = [
                pulls[p * unit : (p + 1) * unit, (m - p) * LANES : (m - p + 1) * LANES] for p in range(4) if 0 <= m - p < 2
            ]
            groups.append(functools.reduce(lambda u, v: u + v, terms))
        sums.append(jnp.concatenate(groups, axis=0))
    sums = jnp.concatenate(sums, axis=1)
    upper = sums.astype(BF16)
    lower = (sums - upper.astype(F32)).astype(BF16)
    both = mat(upper, unwindow[...]) + mat(lower, unwindow[...])
    half = both.shape[1] // 2
    odd = [both[m * unit : (m + 1) * unit, 0:wide] for m in range(5)]
    even = [both[m * unit : (m + 1) * unit, half : half + wide] for m in range(5)]
    phases = [even[r // 2] if r % 2 == 0 else odd[(r + 1) // 2] for r in range(8)]
    phases[0] = phases[0] + shift_rows(even[4], 1, period)
    phases[7] = phases[7] + shift_rows(odd[0], -1, period)
    image = jnp.concatenate(phases, axis=0).astype(BF16)
    rows = mat(scatter[...], image)
    zout[...] = jnp.zeros_like(zout)
    for part_at in range(group):
        picked = [rows[(i * group + part_at) * devices : (i * group + part_at + 1) * devices] for i in range(span)]
        for o in range(3):
            plane = [piece[:, o * cols : (o + 1) * cols] for piece in picked]
            plane.append(jnp.zeros((devices, lanes - span * cols), F32))
            plane = jnp.concatenate(plane, axis=1)
            for k in range(lanes // LANES):
                zout[k, pl.ds(o * group + part_at, devices, stride=pitch), :] = plane[:, k * LANES : (k + 1) * LANES]
    for k in range(lanes // LANES):
        out_ref[:, k * LANES : (k + 1) * LANES] = zout[k].astype(BF16)


def row_maps(devices, group, block_rows):
    height = devices * block_rows
    period = height // 8
    span = block_rows + 2
    gather = np.zeros((8 * group * period, span * group * devices), np.float32)
    for device in range(devices):
        for i in range(span):
            y = device * block_rows + i - 1
            if 0 <= y < height:
                for part in range(group):
                    gather[((y % 8) * group + part) * period + y // 8, (i * group + part) * devices + device] = 1.0
    return gather


def windows_of(cols, d1):
    wide = 3 * cols
    count = -(-(cols // 2 + 2) // 8)
    half = up_to(wide, LANES)
    window = np.zeros((wide, count * 2 * LANES), np.float32)
    unwindow = np.zeros((count * LANES, 2 * half), np.float32)
    for k in range(count):
        for c in range(3):
            for j in range(18):
                x = 16 * k - 3 + j
                if 0 <= x < cols:
                    for e in range(2):
                        at = e * LANES // 2 + c * 18 + j
                        window[c * cols + x, (2 * k + e) * LANES + at] = 1.0
                        unwindow[k * LANES + at, e * half + c * cols + x] = 1.0
    return window, unwindow


def band_of(first):
    d1 = first.shape[-1]
    tap = np.arange(18)[:, None] - 2 * (np.arange(8 * d1)[None, :] // d1)
    tiled = jnp.tile(first, (1, 1, 1, 8))
    band = jnp.zeros((4, 3, 18, 8 * d1), BF16)
    for b in range(4):
        band = jnp.where(jnp.asarray(tap == b), tiled[:, b, :, None, :], band)
    band = jnp.pad(band.reshape(4, 54, 8 * d1), ((0, 0), (0, LANES // 2 - 54), (0, 0)))
    return band.reshape(2 * LANES, 8 * d1)


def disc_call(payload, first, second, third, fourth, head, devices, group, cols, block_rows):
    period = devices * block_rows // 8
    unit = group * period
    d1, d2, d3, d4 = first.shape[-1], second.shape[-1], third.shape[-1], fourth.shape[-1]
    x2, x3 = cols // 4, cols // 8
    x4 = x3 - 1
    gather = row_maps(devices, group, block_rows)
    window, unwindow = windows_of(cols, d1)
    width_one = (cols // 2 + 2) * d1
    args = (
        payload,
        jnp.asarray(gather, BF16),
        jnp.asarray(window, BF16),
        band_of(first),
        second.reshape(16 * d1, d2),
        third.reshape(16 * d2, d3),
        fourth.reshape(16 * d3, d4),
        head.reshape(16, d4),
        jnp.asarray(unwindow, BF16),
        jnp.asarray(gather.T, BF16),
    )
    lanes = payload.shape[1]
    return pl.pallas_call(
        functools.partial(
            disc_kernel, devices=devices, group=group, cols=cols, block_rows=block_rows, period=period
        ),
        out_shape=jax.ShapeDtypeStruct(payload.shape, BF16),
        in_specs=[VM, VM, VM, VM, HBM, HBM, HBM, VM, HBM, HBM],
        out_specs=VM,
        scratch_shapes=[
            pltpu.VMEM((lanes // LANES, payload.shape[0], LANES), F32),
            pltpu.VMEM((16 * d1, d2), BF16),
            pltpu.VMEM((16 * d2, d3), BF16),
            pltpu.VMEM((16 * d3, d4), BF16),
            pltpu.VMEM(unwindow.shape, BF16),
            pltpu.VMEM(gather.T.shape, BF16),
            pltpu.VMEM((gather.shape[1], 3 * cols), F32),
            pltpu.VMEM((6 * unit, width_one), BF16),
            pltpu.VMEM((4 * unit, width_one), F32),
            pltpu.VMEM((x2 * 2 * unit, 16 * d1), BF16),
            pltpu.VMEM((4 * unit, (x2 + 2) * d2), BF16),
            pltpu.VMEM((x2 * 2 * unit, d2), F32),
            pltpu.VMEM((4 * unit, (x3 + 2) * d3), BF16),
            pltpu.VMEM((x4 * unit, 16 * d3), BF16),
            pltpu.VMEM((x4 * unit, 16 * d3), F32),
            pltpu.VMEM((x3 * unit, 16 * d2), F32),
            pltpu.VMEM((x2 * 2 * unit, 16 * d1), F32),
            pltpu.VMEM((lanes // LANES, payload.shape[0], LANES), F32),
            pltpu.SemaphoreType.DMA((5,)),
        ],
        compiler_params=WHOLE,
        cost_estimate=pl.CostEstimate(flops=4 * 10**9, bytes_accessed=8 * 10**6, transcendentals=10**6),
        name="disc_rows",
    )(*args)


def put_taps(plane, taps_ref, frames, cols, pieces, padded):
    lanes = plane.shape[1]
    column = lax.broadcasted_iota(jnp.int32, plane.shape, 1) % cols
    for b in range(3):
        moved = plane
        if b == 0:
            moved = jnp.where(column == cols - 1, 0.0, pltpu.roll(plane, lanes - 1, 1))
        if b == 2:
            moved = jnp.where(column == 0, 0.0, pltpu.roll(plane, 1, 1))
        for a in range(3):
            turned = moved if a == 2 else pltpu.roll(moved, lanes - (2 - a) * cols, 1)
            for k in range(pieces):
                taps_ref[k, pl.ds((a * 3 + b) * 3 * frames, 3 * frames), :] = turned[:, k * LANES : (k + 1) * LANES]
    for k in range(pieces):
        taps_ref[k, pl.ds(27 * frames, (padded - 27) * frames), :] = jnp.zeros(((padded - 27) * frames, LANES), F32)


def weigh(taps_ref, feat_ref, frames, devices, group, pieces, padded):
    pixels = pieces * LANES
    total = jnp.zeros((padded, feat_ref.shape[1]), F32)
    for frame in range(frames):
        rows = pl.ds(slot_of(frame, devices, group), padded, stride=frames)
        taps = jnp.concatenate([taps_ref[k, rows, :] for k in range(pieces)], axis=1).astype(BF16)
        total = total + mat(taps, feat_ref[frame * pixels : (frame + 1) * pixels, :])
    return total


def rec_kernel(
    ends_ref, own_ref, wanted_ref, above_ref, below_ref, feat_ref, part_ref, plane_ref, taps_ref,
    *, frames, devices, group, cols, block_rows,
):
    lanes = own_ref.shape[1]
    pieces = block_rows * cols // LANES
    none = lambda count: jnp.zeros((3 * frames, count), F32)
    rest = none(lanes - (block_rows + 2) * cols)
    above, below = above_ref[...].astype(F32), below_ref[...].astype(F32)
    added = jnp.concatenate(
        [above[:, : 2 * cols], none((block_rows - 2) * cols), below[:, : 2 * cols], rest], axis=1
    )
    asked = jnp.concatenate([above[:, 2 * cols :], wanted_ref[...], below[:, 2 * cols :], rest], axis=1)
    lane = lax.broadcasted_iota(jnp.int32, (3 * frames, lanes), 1)
    plane = loss_scale * (own_ref[...] + added - asked)
    plane = jnp.where((lane >= ends_ref[0]) & (lane < ends_ref[1]), plane, 0.0)
    plane_ref[...] = plane
    put_taps(plane, taps_ref, frames, cols, pieces, 32)
    part_ref[...] = weigh(taps_ref, feat_ref, frames, devices, group, pieces, 32).astype(BF16)


def unpack(plane_ref, zin, devices, group):
    lanes = plane_ref.shape[1]
    pitch = plane_ref.shape[0] // devices
    for k in range(lanes // LANES):
        zin[k] = plane_ref[:, k * LANES : (k + 1) * LANES].astype(F32)
    blocks = []
    for o in range(3):
        for part in range(group):
            row = pl.ds(o * group + part, devices, stride=pitch)
            blocks.append(jnp.concatenate([zin[k, row, :] for k in range(lanes // LANES)], axis=1))
    return jnp.concatenate(blocks, axis=0)


def gan_kernel(plane_ref, feat_ref, part_ref, taps_ref, zin, *, frames, devices, group, cols, block_rows):
    pieces = block_rows * cols // LANES
    put_taps(unpack(plane_ref, zin, devices, group), taps_ref, frames, cols, pieces, 32)
    total = weigh(taps_ref, feat_ref, frames, devices, group, pieces, 32).astype(BF16)
    for i in range(part_ref.shape[0]):
        part_ref[i] = total


def turn_kernel(
    rec_ref, plane_ref, out_ref, rec_taps, gan_taps, zin, *, frames, devices, group, cols, block_rows
):
    pieces = block_rows * cols // LANES
    pixels = pieces * LANES
    put_taps(rec_ref[...], rec_taps, frames, cols, pieces, 32)
    put_taps(unpack(plane_ref, zin, devices, group), gan_taps, frames, cols, pieces, 32)
    for pair in range(frames // 2):
        for k in range(pieces):
            parts = []
            for frame in (2 * pair, 2 * pair + 1):
                rows = pl.ds(slot_of(frame, devices, group), 32, stride=frames)
                parts += [rec_taps[k, rows, :], gan_taps[k, rows, :]]
            at = pair * pixels + k * LANES
            out_ref[at : at + LANES, :] = jnp.concatenate(parts, axis=0).T.astype(BF16)


def taps_call(kernel, specs, operands, out, scratch, frames, devices, group, cols, block_rows, flops, name):
    return pl.pallas_call(
        functools.partial(kernel, frames=frames, devices=devices, group=group, cols=cols, block_rows=block_rows),
        out_shape=out,
        in_specs=specs,
        out_specs=jax.tree.map(lambda _: VM, out),
        scratch_shapes=scratch,
        compiler_params=PART,
        cost_estimate=pl.CostEstimate(flops=flops, bytes_accessed=4 * 10**6, transcendentals=0),
        name=name,
    )(*operands)


def final_kernel(
    taps_ref, rec_sums, gan_sums, weight_ref, out_hbm, grad_ref, adapt_ref, both_ref, out_ref, sems, *, pixels, chunk
):
    total = []
    for ref in (rec_sums, gan_sums):
        value = ref[0].astype(F32)
        for i in range(1, ref.shape[0]):
            value = value + ref[i].astype(F32)
        total.append(value)
    rec, gan = total
    norm = lambda values: jnp.sqrt(jnp.sum(jnp.sum(values * values, axis=1, keepdims=True), axis=0, keepdims=True))
    adaptive = norm(rec) / (norm(gan) + epsilon)
    grad = (rec + adaptive * gan) / pixels
    for a in range(3):
        for b in range(3):
            at = (a * 3 + b) * 3
            grad_ref[a, b] = grad[at : at + 3, :]
    adapt_ref[...] = adaptive
    weight = weight_ref[...]
    padded, channels = weight.shape
    scaled = (adaptive * weight.astype(F32)).astype(BF16)
    both_ref[...] = jnp.zeros_like(both_ref)
    both_ref[0:padded, 0:channels] = weight
    both_ref[padded : 2 * padded, 0:channels] = scaled
    both_ref[2 * padded : 3 * padded, channels:] = weight
    both_ref[3 * padded :, channels:] = scaled
    pairs = taps_ref.shape[0] // chunk
    stores = []
    for pair in range(pairs):
        product = mat(taps_ref[pair * chunk : (pair + 1) * chunk], both_ref[...]).astype(BF16)
        rows = pl.ds(2 * pair * chunk, 2 * chunk)
        out_ref[2 * pair * chunk : (2 * pair + 1) * chunk] = product[:, :channels]
        out_ref[(2 * pair + 1) * chunk : (2 * pair + 2) * chunk] = product[:, channels:]
        stores.append(pltpu.make_async_copy(out_ref.at[rows], out_hbm.at[rows], sems.at[pair]))
        stores[-1].start()
    for copy in stores:
        copy.wait()


def final_call(taps, rec_sums, gan_sums, weight, pixels, chunk):
    padded, channels = weight.shape
    rows = 2 * taps.shape[0]
    return pl.pallas_call(
        functools.partial(final_kernel, pixels=pixels, chunk=chunk),
        out_shape=(
            jax.ShapeDtypeStruct((rows, channels), BF16),
            jax.ShapeDtypeStruct((3, 3, 3, channels), F32),
            jax.ShapeDtypeStruct((1, 1), F32),
        ),
        in_specs=[VM] * 4,
        out_specs=(HBM, VM, VM),
        scratch_shapes=[
            pltpu.VMEM((4 * padded, 2 * channels), BF16),
            pltpu.VMEM((rows, channels), BF16),
            pltpu.SemaphoreType.DMA((rows // (2 * chunk),)),
        ],
        compiler_params=PART,
        cost_estimate=pl.CostEstimate(flops=4 * rows * channels * padded, bytes_accessed=4 * rows * channels, transcendentals=0),
        name="feature_pull",
    )(taps, rec_sums, gan_sums, weight)


def per_device(
    features, target, conv_weight, disc_first, disc_second, disc_third, disc_fourth, disc_head
):
    devices = lax.axis_size("row")
    clips = lax.axis_size("clip")
    _, frames, block_rows, cols, channels = features.shape
    group = frames // devices
    pixels = clips * devices * frames * block_rows * cols
    lanes = up_to((block_rows + 2) * cols, LANES)
    pitch = up_to(3 * group, 8)
    edge = lax.axis_index("row")
    sizes = (frames, devices, group, cols, block_rows)
    feats = features.reshape(frames * block_rows * cols, channels)
    payload, own, weight = forward_call(feats, conv_weight, frames, devices, group, cols, lanes, pitch)
    trade = lambda values: lax.all_to_all(
        values.reshape(devices, pitch, lanes), "row", split_axis=0, concat_axis=0, tiled=True
    ).reshape(devices * pitch, lanes)
    arrived = trade(payload)
    wanted, upward, downward = edge_call(
        own, target[0].transpose(0, 2, 1, 3), frames, devices, group, block_rows, cols
    )
    arrived, upward, downward = lax.optimization_barrier((arrived, upward, downward))
    below = lax.ppermute(upward, "row", [(i + 1, i) for i in range(devices - 1)])
    above = lax.ppermute(downward, "row", [(i, i + 1) for i in range(devices - 1)])
    ends = jnp.stack(
        [
            jnp.where(edge == 0, cols, 0),
            jnp.where(edge == devices - 1, (block_rows + 1) * cols, (block_rows + 2) * cols),
        ]
    ).astype(jnp.int32)
    taps_scratch = pltpu.VMEM((block_rows * cols // LANES, 32 * frames, LANES), F32)
    plane_scratch = pltpu.VMEM((lanes // LANES, devices * pitch, LANES), F32)
    flops = 2 * features.size * 27
    rec_part, rec_plane = taps_call(
        rec_kernel, [pl.BlockSpec(memory_space=pltpu.SMEM)] + [VM] * 5, (ends, own, wanted, above, below, feats),
        (jax.ShapeDtypeStruct((32, channels), BF16), jax.ShapeDtypeStruct(own.shape, F32)),
        [taps_scratch], *sizes, flops, "rec_taps",
    )
    rec_sums = lax.all_gather(rec_part, ("clip", "row"))
    sent = disc_call(
        arrived, disc_first, disc_second, disc_third, disc_fourth, disc_head, devices, group, cols, block_rows
    )
    returned = trade(sent)
    returned, rec_plane = lax.optimization_barrier((returned, rec_plane))
    gan_part = taps_call(
        gan_kernel, [VM, VM], (returned, feats), jax.ShapeDtypeStruct((clips * devices, 32, channels), BF16),
        [taps_scratch, plane_scratch], *sizes, flops, "gan_taps",
    )
    gan_sums = lax.all_to_all(gan_part, ("clip", "row"), split_axis=0, concat_axis=0, tiled=True)
    taps = taps_call(
        turn_kernel, [VM, VM], (rec_plane, returned), jax.ShapeDtypeStruct((feats.shape[0] // 2, LANES), BF16),
        [taps_scratch, taps_scratch, plane_scratch], *sizes, flops, "turn_taps",
    )
    image_back = returned.reshape(devices, pitch, lanes)[:, : 3 * group, cols : (block_rows + 1) * cols]
    image_back = image_back.reshape(devices, 3, group, block_rows, cols).transpose(0, 2, 3, 1, 4)
    image_back = image_back.reshape(1, frames, block_rows, 3, cols)
    feature_grad, weight_grad, adaptive = final_call(taps, rec_sums, gan_sums, weight, pixels, block_rows * cols)
    return (feature_grad.reshape(features.shape), image_back, weight_grad, adaptive[0, 0])


def solution(mesh):
    rows = P("clip", None, "row", None, None)
    return jax.shard_map(
        per_device,
        mesh=mesh,
        in_specs=(rows, rows, P(), P(), P(), P(), P(), P()),
        out_specs=(rows, rows, P(), P()),
        check_vma=False,
    )
```

```python
import functools

import jax
import jax.numpy as jnp
import numpy as np
from jax import lax
from jax.experimental import pallas as pl
from jax.experimental.pallas import tpu as pltpu
from jax.sharding import PartitionSpec as P

loss_scale = 64.0
epsilon = 0.0001
F32 = jnp.float32
BF16 = jnp.bfloat16
LANES = 128
NN = (((1,), (0,)), ((), ()))
NT = (((1,), (1,)), ((), ()))
TN = (((0,), (0,)), ((), ()))
VM = pl.BlockSpec(memory_space=pltpu.VMEM)
HBM = pl.BlockSpec(memory_space=pl.ANY)
WHOLE = pltpu.CompilerParams(vmem_limit_bytes=60 * 2**20)
PART = pltpu.CompilerParams(vmem_limit_bytes=24 * 2**20)


def up_to(value, step):
    return -(-value // step) * step


def mat(left, right, dims=NN):
    return lax.dot_general(left, right, dims, preferred_element_type=F32)


def slot_of(frame, devices, group):
    return (frame % group) * devices + frame // group


def forward_kernel(
    feat_hbm, target_hbm, weight_hbm, pay_ref, own_ref, flat_ref, feat_ref, target_ref, weight_ref, weight_scr, target_scr,
    taps_ref, out_ref, sems, *, frames, devices, group, cols, lanes, chunks,
):
    pixels = feat_ref.shape[0] // frames
    pieces = pixels // LANES
    pitch = out_ref.shape[1] // devices
    taps = flat_ref.shape[0]
    block_rows = pixels // cols
    size = feat_ref.shape[0] // chunks
    copies = [
        pltpu.make_async_copy(weight_hbm, weight_ref, sems.at[chunks]),
        pltpu.make_async_copy(target_hbm, target_ref, sems.at[chunks + 1]),
    ] + [
        pltpu.make_async_copy(feat_hbm.at[pl.ds(i * size, size), :], feat_ref.at[pl.ds(i * size, size), :], sems.at[i])
        for i in range(chunks)
    ]
    for copy in copies:
        copy.start()
    weight_scr[...] = jnp.zeros_like(weight_scr)
    out_ref[...] = jnp.zeros_like(out_ref)
    copies[0].wait()
    copies[1].wait()
    for a in range(3):
        for b in range(3):
            at = (a * 3 + b) * 3
            weight_scr[at : at + 3, :] = weight_ref[a, b].astype(F32)
    weight = weight_scr[...].astype(BF16)
    flat_ref[...] = weight
    target_scr[:, 0:cols] = target_ref[...].reshape(target_scr.shape[0], cols).astype(F32)
    edges = []
    for y in (0, block_rows - 1):
        for o in range(3):
            for part in range(group):
                rows = pl.ds((part * 3 + o) * block_rows + y, devices, stride=group * 3 * block_rows)
                edges.append(target_scr[rows, :][:, 0:cols])
    edges.append(jnp.zeros((devices, lanes - len(edges) * cols), F32))
    edges = jnp.concatenate(edges, axis=1)
    for k in range(lanes // LANES):
        out_ref[k, pl.ds(3 * group, devices, stride=pitch), :] = edges[:, k * LANES : (k + 1) * LANES]
    for frame in range(frames):
        if frame % (frames // chunks) == 0:
            copies[2 + frame // (frames // chunks)].wait()
        product = mat(weight, feat_ref[frame * pixels : (frame + 1) * pixels, :], NT)
        slot = slot_of(frame, devices, group)
        for k in range(pieces):
            taps_ref[k, pl.ds(slot, taps, stride=frames), :] = product[:, k * LANES : (k + 1) * LANES]
    column = lax.broadcasted_iota(jnp.int32, (frames, pixels), 1) % cols

    def tap(a, b, o):
        rows = pl.ds(((a * 3 + b) * 3 + o) * frames, frames)
        return jnp.concatenate([taps_ref[k, rows, :] for k in range(pieces)], axis=1)

    for o in range(3):
        total = None
        for a in range(3):
            part = tap(a, 1, o)
            part = part + jnp.where(column == 0, 0.0, pltpu.roll(tap(a, 0, o), 1, 1))
            part = part + jnp.where(column == cols - 1, 0.0, pltpu.roll(tap(a, 2, o), pixels - 1, 1))
            part = jnp.concatenate([part, jnp.zeros((frames, lanes - pixels), F32)], axis=1)
            if a < 2:
                part = pltpu.roll(part, (2 - a) * cols, 1)
            total = part if total is None else total + part
        own_ref[o * frames : (o + 1) * frames, :] = total
        for part in range(group):
            rows = total[part * devices : (part + 1) * devices, :]
            for k in range(lanes // LANES):
                out_ref[k, pl.ds(o * group + part, devices, stride=pitch), :] = rows[:, k * LANES : (k + 1) * LANES]
    for k in range(lanes // LANES):
        pay_ref[:, k * LANES : (k + 1) * LANES] = out_ref[k].astype(BF16)


def forward_call(features, target, weight, frames, devices, group, cols, lanes, pitch):
    pixels = features.shape[0] // frames
    channels = features.shape[1]
    chunks = 4
    return pl.pallas_call(
        functools.partial(
            forward_kernel, frames=frames, devices=devices, group=group, cols=cols, lanes=lanes, chunks=chunks
        ),
        out_shape=(
            jax.ShapeDtypeStruct((devices * pitch, lanes), BF16),
            jax.ShapeDtypeStruct((3 * frames, lanes), F32),
            jax.ShapeDtypeStruct((32, channels), BF16),
        ),
        in_specs=[HBM, HBM, HBM],
        out_specs=(VM,) * 3,
        scratch_shapes=[
            pltpu.VMEM(features.shape, BF16),
            pltpu.VMEM(target.shape, BF16),
            pltpu.VMEM(weight.shape, BF16),
            pltpu.VMEM((32, channels), F32),
            pltpu.VMEM((3 * pixels // cols * frames, LANES), F32),
            pltpu.VMEM((pixels // LANES, 32 * frames, LANES), F32),
            pltpu.VMEM((lanes // LANES, devices * pitch, LANES), F32),
            pltpu.SemaphoreType.DMA((chunks + 2,)),
        ],
        compiler_params=WHOLE,
        cost_estimate=pl.CostEstimate(flops=2 * features.size * 27, bytes_accessed=2 * features.size, transcendentals=0),
        name="forward_taps",
    )(features, target, weight)


def inner_kernel(own_ref, target_ref, inner_ref, scr, *, frames, devices, group, block_rows, cols):
    scr[:, 0:cols] = target_ref[...].reshape(scr.shape[0], cols).astype(F32)
    stride = group * 3 * block_rows
    lanes = own_ref.shape[1]
    for o in range(3):
        for part in range(group):
            at = o * frames + part * devices
            rows = [jnp.zeros((devices, cols), F32)]
            rows += [
                scr[pl.ds((part * 3 + o) * block_rows + y, devices, stride=stride), :][:, 0:cols]
                for y in range(block_rows)
            ]
            rows.append(jnp.zeros((devices, lanes - (block_rows + 1) * cols), F32))
            wanted = jnp.concatenate(rows, axis=1)
            lane = lax.broadcasted_iota(jnp.int32, wanted.shape, 1)
            inside = (lane >= 2 * cols) & (lane < block_rows * cols)
            own = jnp.where(inside, own_ref[at : at + devices, :], 0.0)
            inner_ref[at : at + devices, :] = loss_scale * (own - wanted)


def inner_call(own, target, frames, devices, group, block_rows, cols):
    return pl.pallas_call(
        functools.partial(
            inner_kernel, frames=frames, devices=devices, group=group, block_rows=block_rows, cols=cols
        ),
        out_shape=jax.ShapeDtypeStruct(own.shape, F32),
        in_specs=[VM, VM],
        out_specs=VM,
        scratch_shapes=[pltpu.VMEM((frames * 3 * block_rows, LANES), F32)],
        compiler_params=PART,
        cost_estimate=pl.CostEstimate(flops=10**8, bytes_accessed=10**6, transcendentals=0),
        name="inner_rows",
    )(own, target)


def shift_rows(values, step, period):
    size = values.shape[0]
    row = lax.broadcasted_iota(jnp.int32, values.shape, 0) % period
    rolled = pltpu.roll(values, step % size, 0)
    source = row - step
    return jnp.where((source >= 0) & (source < period), rolled, 0.0)


def gate_of(values):
    logistic = 1.0 / (1.0 + jnp.exp(-values))
    return (values * logistic).astype(BF16), logistic * (1.0 + values * (1.0 - logistic))


def edge_planes(zin, zout, image, scatter, devices, group, cols, span, lanes, pitch):
    zout[...] = jnp.zeros_like(zout)
    step = group * devices
    first = mat(scatter[0 : 2 * step], image)
    last = mat(scatter[(span - 2) * step :], image)
    row = pl.ds(3 * group, devices, stride=pitch)
    target = jnp.concatenate([zin[k, row, :] for k in range(lanes // LANES)], axis=1)
    outer, inner = [], []
    for e, rows, out_at, in_at, move in ((0, first, 0, 1, 1), (1, last, 1, 0, -1)):
        for o in range(3):
            for part in range(group):
                pick = lambda i: rows[i * step + part * devices : i * step + (part + 1) * devices, o * cols : (o + 1) * cols]
                at = ((1 - e) * 3 * group + o * group + part) * cols
                wanted = shift_rows(target[:, at : at + cols], move, devices)
                outer.append(loss_scale * (pick(out_at) - wanted))
                inner.append(pick(in_at))
    for i, pieces in enumerate((outer, inner)):
        pieces.append(jnp.zeros((devices, lanes - 6 * group * cols), F32))
        plane = jnp.concatenate(pieces, axis=1)
        for k in range(lanes // LANES):
            zout[k, pl.ds(3 * group + i, devices, stride=pitch), :] = plane[:, k * LANES : (k + 1) * LANES]


def disc_kernel(
    pay_ref, gather_ref, window_ref, band_ref, second_hbm, third_hbm, fourth_hbm, head_ref, unwindow_hbm, scatter_hbm, out_ref,
    zin, second, third, fourth, unwindow, scatter, rows_in, act_one, slope_one, cols_two, act_two, slope_two, act_three, cols_four,
    pull_four, pull_three, pull_two, zout, sems, *, devices, group, cols, block_rows, period,
):
    lanes = pay_ref.shape[1]
    pitch = pay_ref.shape[0] // devices
    span = block_rows + 2
    unit = group * period
    wide = 3 * cols
    d1 = (act_one.shape[1]) // (cols // 2 + 2)
    d2, d3, d4 = second.shape[1], third.shape[1], fourth.shape[1]
    x1, x2, x3 = cols // 2, cols // 4, cols // 8
    x4 = x3 - 1
    copies = [
        pltpu.make_async_copy(source, target, sems.at[i])
        for i, (source, target) in enumerate(
            (
                (second_hbm, second),
                (third_hbm, third),
                (fourth_hbm, fourth),
                (unwindow_hbm, unwindow),
                (scatter_hbm, scatter),
            )
        )
    ]
    for i in (4, 0, 1, 2, 3):
        copies[i].start()
    for k in range(lanes // LANES):
        zin[k] = pay_ref[:, k * LANES : (k + 1) * LANES].astype(F32)
    for part in range(group):
        planes = []
        for o in range(3):
            pieces = [zin[k, pl.ds(o * group + part, devices, stride=pitch), :] for k in range(lanes // LANES)]
            planes.append(jnp.concatenate(pieces, axis=1))
        for i in range(span):
            row = jnp.concatenate([plane[:, i * cols : (i + 1) * cols] for plane in planes], axis=1)
            rows_in[pl.ds((i * group + part) * devices, devices), :] = row
    image = mat(gather_ref[...], rows_in[...].astype(BF16)).astype(BF16)
    wins = mat(image, window_ref[...])
    copies[4].wait()
    edge_planes(zin, zout, image, scatter, devices, group, cols, span, lanes, pitch)
    ext = [wins[r * unit : (r + 1) * unit] for r in range(8)]
    ext = [shift_rows(ext[7], 1, period)] + ext + [shift_rows(ext[0], -1, period)]
    width_one = act_one.shape[1]
    strip = 8 * d1
    band = band_ref[...]
    for k in range(-(-width_one // strip)):
        low, high = slice(2 * k * LANES, (2 * k + 1) * LANES), slice((2 * k + 1) * LANES, (2 * k + 2) * LANES)
        left = jnp.concatenate(
            [
                jnp.concatenate([ext[2 * p + h][:, low] + ext[2 * p + h + 1][:, high] for p in range(4)], axis=0)
                for h in (0, 2)
            ],
            axis=1,
        ).astype(BF16)
        start, end = k * strip, min((k + 1) * strip, width_one)
        act, slope = gate_of(mat(left, band[:, : end - start]))
        if k == 0 or end == width_one:
            lane = start + lax.broadcasted_iota(jnp.int32, slope.shape, 1)
            inside = (lane >= d1) & (lane < width_one - d1)
            slope = jnp.where(inside, slope, 0.0)
            act = jnp.where(inside, act.astype(F32), 0.0).astype(BF16)
        slope_one[:, start:end] = slope
        act_one[unit : 5 * unit, start:end] = act
        actual = act.astype(F32)
        act_one[0:unit, start:end] = shift_rows(actual[3 * unit :], 1, period).astype(BF16)
        act_one[5 * unit :, start:end] = shift_rows(actual[:unit], -1, period).astype(BF16)
    copies[0].wait()
    for x in range(x2):
        for a in range(4):
            for p in range(2):
                cols_two[(x * 2 + p) * unit : (x * 2 + p + 1) * unit, a * 4 * d1 : (a + 1) * 4 * d1] = act_one[
                    (2 * p + a) * unit : (2 * p + a + 1) * unit, 2 * x * d1 : (2 * x + 4) * d1
                ]
    pre = mat(cols_two[...], second[...])
    act, slope = gate_of(pre)
    slope_two[...] = slope
    act_two[:, 0:d2] = jnp.zeros((4 * unit, d2), BF16)
    act_two[:, (x2 + 1) * d2 :] = jnp.zeros((4 * unit, d2), BF16)
    for x in range(x2):
        block = act[x * 2 * unit : (x + 1) * 2 * unit]
        actual = block.astype(F32)
        at = slice((x + 1) * d2, (x + 2) * d2)
        act_two[unit : 3 * unit, at] = block
        act_two[0:unit, at] = shift_rows(actual[unit:], 1, period).astype(BF16)
        act_two[3 * unit :, at] = shift_rows(actual[:unit], -1, period).astype(BF16)
    copies[1].wait()
    left = jnp.concatenate(
        [
            jnp.concatenate([act_two[a * unit : (a + 1) * unit, 2 * x * d2 : (2 * x + 4) * d2] for a in range(4)], axis=1)
            for x in range(x3)
        ],
        axis=0,
    )
    act, slope_three = gate_of(mat(left, third[...]))
    act_three[:, 0:d3] = jnp.zeros((4 * unit, d3), BF16)
    act_three[:, (x3 + 1) * d3 :] = jnp.zeros((4 * unit, d3), BF16)
    for x in range(x3):
        block = act[x * unit : (x + 1) * unit]
        actual = block.astype(F32)
        at = slice((x + 1) * d3, (x + 2) * d3)
        act_three[unit : 2 * unit, at] = block
        for a in (0, 2, 3):
            act_three[a * unit : (a + 1) * unit, at] = shift_rows(actual, 1 - a, period).astype(BF16)
    for x in range(x4):
        for a in range(4):
            cols_four[x * unit : (x + 1) * unit, a * 4 * d3 : (a + 1) * 4 * d3] = act_three[
                a * unit : (a + 1) * unit, x * d3 : (x + 4) * d3
            ]
    copies[2].wait()
    pre = mat(cols_four[...], fourth[...])
    _, slope = gate_of(pre)
    row = lax.broadcasted_iota(jnp.int32, (unit, d4), 0) % period
    head = head_ref[...].astype(F32) * -loss_scale
    heads = []
    for x in range(x4):
        total = None
        for a in range(4):
            taps = [head[a * 4 + b : a * 4 + b + 1, :] for b in range(4) if 0 <= x - b + 1 < x4 - 1]
            tap = functools.reduce(lambda u, v: u + v, taps)
            inside = (row - a + 1 >= 0) & (row - a + 1 < period - 2) & (row < period - 1)
            term = jnp.where(inside, jnp.broadcast_to(tap, (unit, d4)), 0.0)
            total = term if total is None else total + term
        heads.append(total)
    cot = (jnp.concatenate(heads, axis=0) * slope).astype(BF16)
    pull_four[...] = mat(cot, fourth[...], NT)
    cots = []
    for x in range(x3):
        total = None
        for a in range(4):
            term = None
            for b in range(4):
                source = x - b + 1
                if 0 <= source < x4:
                    piece = pull_four[source * unit : (source + 1) * unit, (a * 4 + b) * d3 : (a * 4 + b + 1) * d3]
                    term = piece if term is None else term + piece
            if a != 1:
                term = shift_rows(term, a - 1, period)
            total = term if total is None else total + term
        cots.append((total * slope_three[x * unit : (x + 1) * unit]).astype(BF16))
    pull_three[...] = mat(jnp.concatenate(cots, axis=0), third[...], NT)
    cots = []
    for x in range(x2):
        terms = []
        for a in range(4):
            term = None
            for b in range(4):
                if (x - b + 1) % 2 == 0 and 0 <= (x - b + 1) // 2 < x3:
                    source = (x - b + 1) // 2
                    piece = pull_three[source * unit : (source + 1) * unit, (a * 4 + b) * d2 : (a * 4 + b + 1) * d2]
                    term = piece if term is None else term + piece
            terms.append(term)
        even = terms[1] + shift_rows(terms[3], 1, period)
        odd = terms[2] + shift_rows(terms[0], -1, period)
        both = jnp.concatenate([even, odd], axis=0)
        cots.append((both * slope_two[x * 2 * unit : (x + 1) * 2 * unit]).astype(BF16))
    pull_two[...] = mat(jnp.concatenate(cots, axis=0), second[...], NT)
    strips = []
    for k in range(x2 + 1):
        terms = {}
        for p in range(2):
            for a in range(4):
                term = None
                if k < x2:
                    term = pull_two[(2 * k + p) * unit : (2 * k + p + 1) * unit, a * 4 * d1 : (a * 4 + 2) * d1]
                if k > 0:
                    other = pull_two[(2 * k - 2 + p) * unit : (2 * k - 1 + p) * unit, (a * 4 + 2) * d1 : (a + 1) * 4 * d1]
                    term = other if term is None else term + other
                terms[p, a] = term
        both = jnp.concatenate(
            [
                terms[0, 1] + shift_rows(terms[1, 3], 1, period),
                terms[0, 2] + terms[1, 0],
                terms[0, 3] + terms[1, 1],
                terms[1, 2] + shift_rows(terms[0, 0], -1, period),
            ],
            axis=0,
        )
        strips.append((both * slope_one[:, 2 * k * d1 : (2 * k + 2) * d1]).astype(BF16))
    cot = jnp.concatenate(strips, axis=1)
    copies[3].wait()
    sums = []
    for k in range(-(-width_one // strip)):
        start, end = k * strip, min((k + 1) * strip, width_one)
        pulls = mat(cot[:, start:end], band[:, : end - start], NT)
        groups = []
        for m in range(5):
            terms = [
                pulls[p * unit : (p + 1) * unit, (m - p) * LANES : (m - p + 1) * LANES] for p in range(4) if 0 <= m - p < 2
            ]
            groups.append(functools.reduce(lambda u, v: u + v, terms))
        sums.append(jnp.concatenate(groups, axis=0))
    sums = jnp.concatenate(sums, axis=1)
    upper = sums.astype(BF16)
    lower = (sums - upper.astype(F32)).astype(BF16)
    both = mat(upper, unwindow[...]) + mat(lower, unwindow[...])
    half = both.shape[1] // 2
    odd = [both[m * unit : (m + 1) * unit, 0:wide] for m in range(5)]
    even = [both[m * unit : (m + 1) * unit, half : half + wide] for m in range(5)]
    phases = [even[r // 2] if r % 2 == 0 else odd[(r + 1) // 2] for r in range(8)]
    phases[0] = phases[0] + shift_rows(even[4], 1, period)
    phases[7] = phases[7] + shift_rows(odd[0], -1, period)
    image = jnp.concatenate(phases, axis=0).astype(BF16)
    rows = mat(scatter[...], image)
    for part_at in range(group):
        picked = [rows[(i * group + part_at) * devices : (i * group + part_at + 1) * devices] for i in range(span)]
        for o in range(3):
            plane = [piece[:, o * cols : (o + 1) * cols] for piece in picked]
            plane.append(jnp.zeros((devices, lanes - span * cols), F32))
            plane = jnp.concatenate(plane, axis=1)
            for k in range(lanes // LANES):
                zout[k, pl.ds(o * group + part_at, devices, stride=pitch), :] = plane[:, k * LANES : (k + 1) * LANES]
    for k in range(lanes // LANES):
        out_ref[:, k * LANES : (k + 1) * LANES] = zout[k].astype(BF16)


def row_maps(devices, group, block_rows):
    height = devices * block_rows
    period = height // 8
    span = block_rows + 2
    gather = np.zeros((8 * group * period, span * group * devices), np.float32)
    for device in range(devices):
        for i in range(span):
            y = device * block_rows + i - 1
            if 0 <= y < height:
                for part in range(group):
                    gather[((y % 8) * group + part) * period + y // 8, (i * group + part) * devices + device] = 1.0
    return gather


def windows_of(cols, d1):
    wide = 3 * cols
    count = -(-(cols // 2 + 2) // 8)
    half = up_to(wide, LANES)
    window = np.zeros((wide, count * 2 * LANES), np.float32)
    unwindow = np.zeros((count * LANES, 2 * half), np.float32)
    for k in range(count):
        for c in range(3):
            for j in range(18):
                x = 16 * k - 3 + j
                if 0 <= x < cols:
                    for e in range(2):
                        at = e * LANES // 2 + c * 18 + j
                        window[c * cols + x, (2 * k + e) * LANES + at] = 1.0
                        unwindow[k * LANES + at, e * half + c * cols + x] = 1.0
    return window, unwindow


def band_of(first):
    d1 = first.shape[-1]
    tap = np.arange(18)[:, None] - 2 * (np.arange(8 * d1)[None, :] // d1)
    tiled = jnp.tile(first, (1, 1, 1, 8))
    band = jnp.zeros((4, 3, 18, 8 * d1), BF16)
    for b in range(4):
        band = jnp.where(jnp.asarray(tap == b), tiled[:, b, :, None, :], band)
    band = jnp.pad(band.reshape(4, 54, 8 * d1), ((0, 0), (0, LANES // 2 - 54), (0, 0)))
    return band.reshape(2 * LANES, 8 * d1)


def disc_call(payload, first, second, third, fourth, head, devices, group, cols, block_rows):
    period = devices * block_rows // 8
    unit = group * period
    d1, d2, d3, d4 = first.shape[-1], second.shape[-1], third.shape[-1], fourth.shape[-1]
    x2, x3 = cols // 4, cols // 8
    x4 = x3 - 1
    gather = row_maps(devices, group, block_rows)
    window, unwindow = windows_of(cols, d1)
    width_one = (cols // 2 + 2) * d1
    args = (
        payload,
        jnp.asarray(gather, BF16),
        jnp.asarray(window, BF16),
        band_of(first),
        second.reshape(16 * d1, d2),
        third.reshape(16 * d2, d3),
        fourth.reshape(16 * d3, d4),
        head.reshape(16, d4),
        jnp.asarray(unwindow, BF16),
        jnp.asarray(gather.T, BF16),
    )
    lanes = payload.shape[1]
    return pl.pallas_call(
        functools.partial(
            disc_kernel, devices=devices, group=group, cols=cols, block_rows=block_rows, period=period
        ),
        out_shape=jax.ShapeDtypeStruct(payload.shape, BF16),
        in_specs=[VM, VM, VM, VM, HBM, HBM, HBM, VM, HBM, HBM],
        out_specs=VM,
        scratch_shapes=[
            pltpu.VMEM((lanes // LANES, payload.shape[0], LANES), F32),
            pltpu.VMEM((16 * d1, d2), BF16),
            pltpu.VMEM((16 * d2, d3), BF16),
            pltpu.VMEM((16 * d3, d4), BF16),
            pltpu.VMEM(unwindow.shape, BF16),
            pltpu.VMEM(gather.T.shape, BF16),
            pltpu.VMEM((gather.shape[1], 3 * cols), F32),
            pltpu.VMEM((6 * unit, width_one), BF16),
            pltpu.VMEM((4 * unit, width_one), F32),
            pltpu.VMEM((x2 * 2 * unit, 16 * d1), BF16),
            pltpu.VMEM((4 * unit, (x2 + 2) * d2), BF16),
            pltpu.VMEM((x2 * 2 * unit, d2), F32),
            pltpu.VMEM((4 * unit, (x3 + 2) * d3), BF16),
            pltpu.VMEM((x4 * unit, 16 * d3), BF16),
            pltpu.VMEM((x4 * unit, 16 * d3), F32),
            pltpu.VMEM((x3 * unit, 16 * d2), F32),
            pltpu.VMEM((x2 * 2 * unit, 16 * d1), F32),
            pltpu.VMEM((lanes // LANES, payload.shape[0], LANES), F32),
            pltpu.SemaphoreType.DMA((5,)),
        ],
        compiler_params=WHOLE,
        cost_estimate=pl.CostEstimate(flops=4 * 10**9, bytes_accessed=8 * 10**6, transcendentals=10**6),
        name="disc_rows",
    )(*args)


def put_taps(plane, taps_ref, frames, cols, pieces, padded):
    lanes = plane.shape[1]
    column = lax.broadcasted_iota(jnp.int32, plane.shape, 1) % cols
    for b in range(3):
        moved = plane
        if b == 0:
            moved = jnp.where(column == cols - 1, 0.0, pltpu.roll(plane, lanes - 1, 1))
        if b == 2:
            moved = jnp.where(column == 0, 0.0, pltpu.roll(plane, 1, 1))
        for a in range(3):
            turned = moved if a == 2 else pltpu.roll(moved, lanes - (2 - a) * cols, 1)
            for k in range(pieces):
                taps_ref[k, pl.ds((a * 3 + b) * 3 * frames, 3 * frames), :] = turned[:, k * LANES : (k + 1) * LANES]
    for k in range(pieces):
        taps_ref[k, pl.ds(27 * frames, (padded - 27) * frames), :] = jnp.zeros(((padded - 27) * frames, LANES), F32)


def unpack(plane_ref, zin, devices, group):
    lanes = plane_ref.shape[1]
    pitch = plane_ref.shape[0] // devices
    for k in range(lanes // LANES):
        zin[k] = plane_ref[:, k * LANES : (k + 1) * LANES].astype(F32)
    blocks = []
    for o in range(3):
        for part in range(group):
            row = pl.ds(o * group + part, devices, stride=pitch)
            blocks.append(jnp.concatenate([zin[k, row, :] for k in range(lanes // LANES)], axis=1))
    return jnp.concatenate(blocks, axis=0)


def rec_rows(inner_ref, zin, devices, group, cols, block_rows):
    lanes = inner_ref.shape[1]
    pitch = zin.shape[1] // devices
    edges = []
    for i in range(2):
        row = pl.ds(3 * group + i, devices, stride=pitch)
        edges.append(jnp.concatenate([zin[k, row, :] for k in range(lanes // LANES)], axis=1))
    blocks = []
    for i, e in ((0, 0), (1, 0), (1, 1), (0, 1)):
        pieces = [
            edges[i][:, (e * 3 * group + at) * cols : (e * 3 * group + at + 1) * cols] for at in range(3 * group)
        ]
        blocks.append(jnp.concatenate(pieces, axis=0))
    none = lambda count: jnp.zeros((blocks[0].shape[0], count), F32)
    above, first, last, below = blocks
    rest = lanes - (block_rows + 2) * cols
    return inner_ref[...], jnp.concatenate(
        [above, first * loss_scale, none((block_rows - 2) * cols), last * loss_scale, below, none(rest)], axis=1
    )


def both_kernel(
    inner_ref, plane_ref, feat_ref, part_ref, rec_ref, rec_taps, gan_taps, zin, *, frames, devices, group, cols, block_rows
):
    pieces = block_rows * cols // LANES
    put_taps(unpack(plane_ref, zin, devices, group), gan_taps, frames, cols, pieces, 32)
    inner, edges = rec_rows(inner_ref, zin, devices, group, cols, block_rows)
    rec = inner + edges
    rec_ref[...] = rec
    put_taps(rec, rec_taps, frames, cols, pieces, 32)
    pixels = pieces * LANES
    total = jnp.zeros(part_ref.shape, F32)
    for frame in range(frames):
        rows = pl.ds(slot_of(frame, devices, group), 32, stride=frames)
        taps = jnp.concatenate(
            [
                jnp.concatenate([taps_ref[k, rows, :] for k in range(pieces)], axis=1)
                for taps_ref in (rec_taps, gan_taps)
            ],
            axis=0,
        )
        total = total + mat(taps.astype(BF16), feat_ref[frame * pixels : (frame + 1) * pixels, :])
    part_ref[...] = total


def turn_kernel(
    rec_ref, plane_ref, out_ref, rec_taps, gan_taps, zin, *, frames, devices, group, cols, block_rows
):
    pieces = block_rows * cols // LANES
    pixels = pieces * LANES
    put_taps(rec_ref[...], rec_taps, frames, cols, pieces, 32)
    put_taps(unpack(plane_ref, zin, devices, group), gan_taps, frames, cols, pieces, 32)
    for pair in range(frames // 2):
        for k in range(pieces):
            parts = []
            for frame in (2 * pair, 2 * pair + 1):
                rows = pl.ds(slot_of(frame, devices, group), 32, stride=frames)
                parts += [rec_taps[k, rows, :], gan_taps[k, rows, :]]
            at = pair * pixels + k * LANES
            out_ref[at : at + LANES, :] = jnp.concatenate(parts, axis=0).T.astype(BF16)


def taps_call(kernel, specs, operands, out, scratch, frames, devices, group, cols, block_rows, flops, name):
    return pl.pallas_call(
        functools.partial(kernel, frames=frames, devices=devices, group=group, cols=cols, block_rows=block_rows),
        out_shape=out,
        in_specs=specs,
        out_specs=jax.tree.map(lambda _: VM, out),
        scratch_shapes=scratch,
        compiler_params=PART,
        cost_estimate=pl.CostEstimate(flops=flops, bytes_accessed=4 * 10**6, transcendentals=0),
        name=name,
    )(*operands)


def final_kernel(taps_ref, sums_ref, weight_ref, out_hbm, grad_ref, adapt_ref, both_ref, out_ref, sems, *, pixels, chunk):
    half = weight_ref.shape[0]
    rec, gan = sums_ref[0:half, :], sums_ref[half:, :]
    norm = lambda values: jnp.sqrt(jnp.sum(jnp.sum(values * values, axis=1, keepdims=True), axis=0, keepdims=True))
    adaptive = norm(rec) / (norm(gan) + epsilon)
    grad = (rec + adaptive * gan) / pixels
    for a in range(3):
        for b in range(3):
            at = (a * 3 + b) * 3
            grad_ref[a, b] = grad[at : at + 3, :]
    adapt_ref[...] = adaptive
    weight = weight_ref[...]
    padded, channels = weight.shape
    scaled = (adaptive * weight.astype(F32)).astype(BF16)
    both_ref[...] = jnp.zeros_like(both_ref)
    both_ref[0:padded, 0:channels] = weight
    both_ref[padded : 2 * padded, 0:channels] = scaled
    both_ref[2 * padded : 3 * padded, channels:] = weight
    both_ref[3 * padded :, channels:] = scaled
    pairs = taps_ref.shape[0] // chunk
    stores = []
    for pair in range(pairs):
        product = mat(taps_ref[pair * chunk : (pair + 1) * chunk], both_ref[...]).astype(BF16)
        rows = pl.ds(2 * pair * chunk, 2 * chunk)
        out_ref[2 * pair * chunk : (2 * pair + 1) * chunk] = product[:, :channels]
        out_ref[(2 * pair + 1) * chunk : (2 * pair + 2) * chunk] = product[:, channels:]
        stores.append(pltpu.make_async_copy(out_ref.at[rows], out_hbm.at[rows], sems.at[pair]))
        stores[-1].start()
    for copy in stores:
        copy.wait()


def final_call(taps, sums, weight, pixels, chunk):
    padded, channels = weight.shape
    rows = 2 * taps.shape[0]
    return pl.pallas_call(
        functools.partial(final_kernel, pixels=pixels, chunk=chunk),
        out_shape=(
            jax.ShapeDtypeStruct((rows, channels), BF16),
            jax.ShapeDtypeStruct((3, 3, 3, channels), F32),
            jax.ShapeDtypeStruct((1, 1), F32),
        ),
        in_specs=[VM] * 3,
        out_specs=(HBM, VM, VM),
        scratch_shapes=[
            pltpu.VMEM((4 * padded, 2 * channels), BF16),
            pltpu.VMEM((rows, channels), BF16),
            pltpu.SemaphoreType.DMA((rows // (2 * chunk),)),
        ],
        compiler_params=PART,
        cost_estimate=pl.CostEstimate(flops=4 * rows * channels * padded, bytes_accessed=4 * rows * channels, transcendentals=0),
        name="feature_pull",
    )(taps, sums, weight)


def per_device(
    features, target, conv_weight, disc_first, disc_second, disc_third, disc_fourth, disc_head
):
    devices = lax.axis_size("row")
    clips = lax.axis_size("clip")
    _, frames, block_rows, cols, channels = features.shape
    group = frames // devices
    pixels = clips * devices * frames * block_rows * cols
    lanes = up_to((block_rows + 2) * cols, LANES)
    pitch = up_to(3 * group + 2, 8)
    sizes = (frames, devices, group, cols, block_rows)
    feats = features.reshape(frames * block_rows * cols, channels)
    wanted = target[0].transpose(0, 2, 1, 3)
    payload, own, weight = forward_call(feats, wanted, conv_weight, frames, devices, group, cols, lanes, pitch)
    trade = lambda values: lax.all_to_all(
        values.reshape(devices, pitch, lanes), "row", split_axis=0, concat_axis=0, tiled=True
    ).reshape(devices * pitch, lanes)
    arrived = trade(payload)
    inner = inner_call(own, wanted, frames, devices, group, block_rows, cols)
    arrived, inner = lax.optimization_barrier((arrived, inner))
    sent = disc_call(
        arrived, disc_first, disc_second, disc_third, disc_fourth, disc_head, devices, group, cols, block_rows
    )
    returned = trade(sent)
    taps_scratch = pltpu.VMEM((block_rows * cols // LANES, 32 * frames, LANES), F32)
    plane_scratch = pltpu.VMEM((lanes // LANES, devices * pitch, LANES), F32)
    flops = 4 * features.size * 27
    part, rec_plane = taps_call(
        both_kernel, [VM, VM, VM], (inner, returned, feats),
        (jax.ShapeDtypeStruct((64, channels), F32), jax.ShapeDtypeStruct(own.shape, F32)),
        [taps_scratch, taps_scratch, plane_scratch], *sizes, flops, "both_taps",
    )
    everyone = clips * devices
    slices = up_to(part.size, everyone * LANES) // everyone // LANES
    part = jnp.pad(part, ((0, everyone * slices - part.shape[0]), (0, 0))).reshape(everyone, slices, LANES)
    share = lambda values: lax.all_to_all(values, ("clip", "row"), split_axis=0, concat_axis=0, tiled=True)
    mine = jnp.sum(share(part), axis=0)
    sums = share(jnp.broadcast_to(mine[None], part.shape)).reshape(everyone * slices, LANES)[:64]
    taps = taps_call(
        turn_kernel, [VM, VM], (rec_plane, returned), jax.ShapeDtypeStruct((feats.shape[0] // 2, LANES), BF16),
        [taps_scratch, taps_scratch, plane_scratch], *sizes, flops, "turn_taps",
    )
    image_back = returned.reshape(devices, pitch, lanes)[:, : 3 * group, cols : (block_rows + 1) * cols]
    image_back = image_back.reshape(devices, 3, group, block_rows, cols).transpose(0, 2, 3, 1, 4)
    image_back = image_back.reshape(1, frames, block_rows, 3, cols)
    feature_grad, weight_grad, adaptive = final_call(taps, sums, weight, pixels, block_rows * cols)
    return (feature_grad.reshape(features.shape), image_back, weight_grad, adaptive[0, 0])


def solution(mesh):
    rows = P("clip", None, "row", None, None)
    return jax.shard_map(
        per_device,
        mesh=mesh,
        in_specs=(rows, rows, P(), P(), P(), P(), P(), P()),
        out_specs=(rows, rows, P(), P()),
        check_vma=False,
    )
```

```python
import functools

import jax
import jax.numpy as jnp
import numpy as np
from jax import lax
from jax.experimental import pallas as pl
from jax.experimental.pallas import tpu as pltpu
from jax.sharding import PartitionSpec as P

loss_scale = 64.0
epsilon = 0.0001
F32 = jnp.float32
BF16 = jnp.bfloat16
LANES = 128
NN = (((1,), (0,)), ((), ()))
NT = (((1,), (1,)), ((), ()))
TN = (((0,), (0,)), ((), ()))
VM = pl.BlockSpec(memory_space=pltpu.VMEM)
HBM = pl.BlockSpec(memory_space=pl.ANY)
WHOLE = pltpu.CompilerParams(vmem_limit_bytes=60 * 2**20)
MOST = pltpu.CompilerParams(vmem_limit_bytes=119 * 2**19)
PART = pltpu.CompilerParams(vmem_limit_bytes=24 * 2**20)


def up_to(value, step):
    return -(-value // step) * step


def mat(left, right, dims=NN):
    return lax.dot_general(left, right, dims, preferred_element_type=F32)


def slot_of(frame, devices, group):
    return (frame % group) * devices + frame // group


def forward_kernel(
    feat_hbm, target_hbm, weight_hbm, pay_ref, own_ref, flat_ref, feat_ref, target_ref, weight_ref, weight_scr, target_scr,
    taps_ref, out_ref, sems, *, frames, devices, group, cols, lanes, chunks,
):
    pixels = feat_ref.shape[0] // frames
    pieces = pixels // LANES
    pitch = out_ref.shape[1] // devices
    taps = flat_ref.shape[0]
    block_rows = pixels // cols
    copies = [
        pltpu.make_async_copy(weight_hbm, weight_ref, sems.at[frames]),
        pltpu.make_async_copy(target_hbm, target_ref, sems.at[frames + 1]),
    ]
    for slot in range(frames):
        rows = pl.ds((slot % devices * group + slot // devices) * pixels, pixels)
        copies.append(pltpu.make_async_copy(feat_hbm.at[rows, :], feat_ref.at[rows, :], sems.at[slot]))
    for copy in copies:
        copy.start()
    weight_scr[...] = jnp.zeros_like(weight_scr)
    out_ref[...] = jnp.zeros_like(out_ref)
    copies[0].wait()
    copies[1].wait()
    for a in range(3):
        for b in range(3):
            at = (a * 3 + b) * 3
            weight_scr[at : at + 3, :] = weight_ref[a, b].astype(F32)
    weight = weight_scr[...].astype(BF16)
    flat_ref[...] = weight
    target_scr[:, 0:cols] = target_ref[...].reshape(target_scr.shape[0], cols).astype(F32)
    edges = []
    for y in (0, block_rows - 1):
        for o in range(3):
            for part in range(group):
                rows = pl.ds((part * 3 + o) * block_rows + y, devices, stride=group * 3 * block_rows)
                edges.append(target_scr[rows, :][:, 0:cols])
    edges.append(jnp.zeros((devices, lanes - len(edges) * cols), F32))
    edges = jnp.concatenate(edges, axis=1)
    for k in range(lanes // LANES):
        out_ref[k, pl.ds(3 * group, devices, stride=pitch), :] = edges[:, k * LANES : (k + 1) * LANES]
    column = lax.broadcasted_iota(jnp.int32, (devices, pixels), 1) % cols

    def finish(part):
        def tap(a, b, o):
            rows = pl.ds(((a * 3 + b) * 3 + o) * frames + part * devices, devices)
            return jnp.concatenate([taps_ref[k, rows, :] for k in range(pieces)], axis=1)

        for o in range(3):
            total = None
            for a in range(3):
                term = tap(a, 1, o)
                term = term + jnp.where(column == 0, 0.0, pltpu.roll(tap(a, 0, o), 1, 1))
                term = term + jnp.where(column == cols - 1, 0.0, pltpu.roll(tap(a, 2, o), pixels - 1, 1))
                term = jnp.concatenate([term, jnp.zeros((devices, lanes - pixels), F32)], axis=1)
                if a < 2:
                    term = pltpu.roll(term, (2 - a) * cols, 1)
                total = term if total is None else total + term
            at = o * frames + part * devices
            own_ref[at : at + devices, :] = total
            for k in range(lanes // LANES):
                rows = pl.ds(o * group + part, devices, stride=pitch)
                out_ref[k, rows, :] = total[:, k * LANES : (k + 1) * LANES]

    step = frames // chunks
    done = 0
    for chunk in range(chunks):
        for slot in range(chunk * step, (chunk + 1) * step):
            copies[2 + slot].wait()
        for slot in range(chunk * step, (chunk + 1) * step):
            frame = slot % devices * group + slot // devices
            product = mat(weight, feat_ref[frame * pixels : (frame + 1) * pixels, :], NT)
            for k in range(pieces):
                taps_ref[k, pl.ds(slot, taps, stride=frames), :] = product[:, k * LANES : (k + 1) * LANES]
        while (done + 1) * devices <= chunk * step or (chunk == chunks - 1 and done < group):
            finish(done)
            done += 1
    for k in range(lanes // LANES):
        pay_ref[:, k * LANES : (k + 1) * LANES] = out_ref[k].astype(BF16)


def forward_call(features, target, weight, frames, devices, group, cols, lanes, pitch):
    pixels = features.shape[0] // frames
    channels = features.shape[1]
    chunks = 4
    return pl.pallas_call(
        functools.partial(
            forward_kernel, frames=frames, devices=devices, group=group, cols=cols, lanes=lanes, chunks=chunks
        ),
        out_shape=(
            jax.ShapeDtypeStruct((devices * pitch, lanes), BF16),
            jax.ShapeDtypeStruct((3 * frames, lanes), F32),
            jax.ShapeDtypeStruct((32, channels), BF16),
        ),
        in_specs=[HBM, HBM, HBM],
        out_specs=(VM,) * 3,
        scratch_shapes=[
            pltpu.VMEM(features.shape, BF16),
            pltpu.VMEM(target.shape, BF16),
            pltpu.VMEM(weight.shape, BF16),
            pltpu.VMEM((32, channels), F32),
            pltpu.VMEM((3 * pixels // cols * frames, LANES), F32),
            pltpu.VMEM((pixels // LANES, 32 * frames, LANES), F32),
            pltpu.VMEM((lanes // LANES, devices * pitch, LANES), F32),
            pltpu.SemaphoreType.DMA((frames + 2,)),
        ],
        compiler_params=WHOLE,
        cost_estimate=pl.CostEstimate(flops=2 * features.size * 27, bytes_accessed=2 * features.size, transcendentals=0),
        name="forward_taps",
    )(features, target, weight)


def inner_kernel(own_ref, target_ref, inner_ref, scr, *, frames, devices, group, block_rows, cols):
    scr[:, 0:cols] = target_ref[...].reshape(scr.shape[0], cols).astype(F32)
    stride = group * 3 * block_rows
    lanes = own_ref.shape[1]
    for o in range(3):
        for part in range(group):
            at = o * frames + part * devices
            rows = [jnp.zeros((devices, cols), F32)]
            rows += [
                scr[pl.ds((part * 3 + o) * block_rows + y, devices, stride=stride), :][:, 0:cols]
                for y in range(block_rows)
            ]
            rows.append(jnp.zeros((devices, lanes - (block_rows + 1) * cols), F32))
            wanted = jnp.concatenate(rows, axis=1)
            lane = lax.broadcasted_iota(jnp.int32, wanted.shape, 1)
            inside = (lane >= 2 * cols) & (lane < block_rows * cols)
            own = jnp.where(inside, own_ref[at : at + devices, :], 0.0)
            inner_ref[at : at + devices, :] = loss_scale * (own - wanted)


def inner_call(own, target, frames, devices, group, block_rows, cols):
    return pl.pallas_call(
        functools.partial(
            inner_kernel, frames=frames, devices=devices, group=group, block_rows=block_rows, cols=cols
        ),
        out_shape=jax.ShapeDtypeStruct(own.shape, F32),
        in_specs=[VM, VM],
        out_specs=VM,
        scratch_shapes=[pltpu.VMEM((frames * 3 * block_rows, LANES), F32)],
        compiler_params=PART,
        cost_estimate=pl.CostEstimate(flops=10**8, bytes_accessed=10**6, transcendentals=0),
        name="inner_rows",
    )(own, target)


def shift_rows(values, step, period):
    size = values.shape[0]
    row = lax.broadcasted_iota(jnp.int32, values.shape, 0) % period
    rolled = pltpu.roll(values, step % size, 0)
    source = row - step
    return jnp.where((source >= 0) & (source < period), rolled, 0.0)


def gate_of(values):
    logistic = 1.0 / (1.0 + jnp.exp(-values))
    return (values * logistic).astype(BF16), logistic * (1.0 + values * (1.0 - logistic))


def edge_planes(zin, zout, image, scatter, devices, group, cols, span, lanes, pitch):
    zout[...] = jnp.zeros_like(zout)
    step = group * devices
    first = mat(scatter[0 : 2 * step], image)
    last = mat(scatter[(span - 2) * step :], image)
    row = pl.ds(3 * group, devices, stride=pitch)
    target = jnp.concatenate([zin[k, row, :] for k in range(lanes // LANES)], axis=1)
    outer, inner = [], []
    for e, rows, out_at, in_at, move in ((0, first, 0, 1, 1), (1, last, 1, 0, -1)):
        for o in range(3):
            for part in range(group):
                pick = lambda i: rows[i * step + part * devices : i * step + (part + 1) * devices, o * cols : (o + 1) * cols]
                at = ((1 - e) * 3 * group + o * group + part) * cols
                wanted = shift_rows(target[:, at : at + cols], move, devices)
                outer.append(loss_scale * (pick(out_at) - wanted))
                inner.append(pick(in_at))
    for i, pieces in enumerate((outer, inner)):
        pieces.append(jnp.zeros((devices, lanes - 6 * group * cols), F32))
        plane = jnp.concatenate(pieces, axis=1)
        for k in range(lanes // LANES):
            zout[k, pl.ds(3 * group + i, devices, stride=pitch), :] = plane[:, k * LANES : (k + 1) * LANES]


def disc_kernel(
    pay_ref, gather_ref, window_ref, band_ref, second_hbm, third_hbm, fourth_hbm, head_ref, unwindow_hbm, scatter_hbm, out_ref,
    zin, second, third, fourth, unwindow, scatter, rows_in, act_one, slope_one, cols_two, act_two, slope_two, act_three, cols_four,
    pull_four, pull_three, pull_two, zout, sems, *, devices, group, cols, block_rows, period,
):
    lanes = pay_ref.shape[1]
    pitch = pay_ref.shape[0] // devices
    span = block_rows + 2
    unit = group * period
    wide = 3 * cols
    d1 = (act_one.shape[1]) // (cols // 2 + 2)
    d2, d3, d4 = second.shape[1], third.shape[1], fourth.shape[1]
    x1, x2, x3 = cols // 2, cols // 4, cols // 8
    x4 = x3 - 1
    copies = [
        pltpu.make_async_copy(source, target, sems.at[i])
        for i, (source, target) in enumerate(
            (
                (second_hbm, second),
                (third_hbm, third),
                (fourth_hbm, fourth),
                (unwindow_hbm, unwindow),
                (scatter_hbm, scatter),
            )
        )
    ]
    for i in (4, 0, 1, 2, 3):
        copies[i].start()
    for k in range(lanes // LANES):
        zin[k] = pay_ref[:, k * LANES : (k + 1) * LANES].astype(F32)
    for part in range(group):
        planes = []
        for o in range(3):
            pieces = [zin[k, pl.ds(o * group + part, devices, stride=pitch), :] for k in range(lanes // LANES)]
            planes.append(jnp.concatenate(pieces, axis=1))
        for i in range(span):
            row = jnp.concatenate([plane[:, i * cols : (i + 1) * cols] for plane in planes], axis=1)
            rows_in[pl.ds((i * group + part) * devices, devices), :] = row
    image = mat(gather_ref[...], rows_in[...].astype(BF16)).astype(BF16)
    wins = mat(image, window_ref[...])
    copies[4].wait()
    edge_planes(zin, zout, image, scatter, devices, group, cols, span, lanes, pitch)
    ext = [wins[r * unit : (r + 1) * unit] for r in range(8)]
    ext = [shift_rows(ext[7], 1, period)] + ext + [shift_rows(ext[0], -1, period)]
    width_one = act_one.shape[1]
    strip = 8 * d1
    band = band_ref[...]
    for k in range(-(-width_one // strip)):
        low, high = slice(2 * k * LANES, (2 * k + 1) * LANES), slice((2 * k + 1) * LANES, (2 * k + 2) * LANES)
        left = jnp.concatenate(
            [
                jnp.concatenate([ext[2 * p + h][:, low] + ext[2 * p + h + 1][:, high] for p in range(4)], axis=0)
                for h in (0, 2)
            ],
            axis=1,
        ).astype(BF16)
        start, end = k * strip, min((k + 1) * strip, width_one)
        act, slope = gate_of(mat(left, band[:, : end - start]))
        if k == 0 or end == width_one:
            lane = start + lax.broadcasted_iota(jnp.int32, slope.shape, 1)
            inside = (lane >= d1) & (lane < width_one - d1)
            slope = jnp.where(inside, slope, 0.0)
            act = jnp.where(inside, act.astype(F32), 0.0).astype(BF16)
        slope_one[:, start:end] = slope
        act_one[unit : 5 * unit, start:end] = act
        actual = act.astype(F32)
        act_one[0:unit, start:end] = shift_rows(actual[3 * unit :], 1, period).astype(BF16)
        act_one[5 * unit :, start:end] = shift_rows(actual[:unit], -1, period).astype(BF16)
    copies[0].wait()
    for x in range(x2):
        for a in range(4):
            for p in range(2):
                cols_two[(x * 2 + p) * unit : (x * 2 + p + 1) * unit, a * 4 * d1 : (a + 1) * 4 * d1] = act_one[
                    (2 * p + a) * unit : (2 * p + a + 1) * unit, 2 * x * d1 : (2 * x + 4) * d1
                ]
    pre = mat(cols_two[...], second[...])
    act, slope = gate_of(pre)
    slope_two[...] = slope
    act_two[:, 0:d2] = jnp.zeros((4 * unit, d2), BF16)
    act_two[:, (x2 + 1) * d2 :] = jnp.zeros((4 * unit, d2), BF16)
    for x in range(x2):
        block = act[x * 2 * unit : (x + 1) * 2 * unit]
        actual = block.astype(F32)
        at = slice((x + 1) * d2, (x + 2) * d2)
        act_two[unit : 3 * unit, at] = block
        act_two[0:unit, at] = shift_rows(actual[unit:], 1, period).astype(BF16)
        act_two[3 * unit :, at] = shift_rows(actual[:unit], -1, period).astype(BF16)
    copies[1].wait()
    left = jnp.concatenate(
        [
            jnp.concatenate([act_two[a * unit : (a + 1) * unit, 2 * x * d2 : (2 * x + 4) * d2] for a in range(4)], axis=1)
            for x in range(x3)
        ],
        axis=0,
    )
    act, slope_three = gate_of(mat(left, third[...]))
    act_three[:, 0:d3] = jnp.zeros((4 * unit, d3), BF16)
    act_three[:, (x3 + 1) * d3 :] = jnp.zeros((4 * unit, d3), BF16)
    for x in range(x3):
        block = act[x * unit : (x + 1) * unit]
        actual = block.astype(F32)
        at = slice((x + 1) * d3, (x + 2) * d3)
        act_three[unit : 2 * unit, at] = block
        for a in (0, 2, 3):
            act_three[a * unit : (a + 1) * unit, at] = shift_rows(actual, 1 - a, period).astype(BF16)
    for x in range(x4):
        for a in range(4):
            cols_four[x * unit : (x + 1) * unit, a * 4 * d3 : (a + 1) * 4 * d3] = act_three[
                a * unit : (a + 1) * unit, x * d3 : (x + 4) * d3
            ]
    copies[2].wait()
    pre = mat(cols_four[...], fourth[...])
    _, slope = gate_of(pre)
    row = lax.broadcasted_iota(jnp.int32, (unit, d4), 0) % period
    head = head_ref[...].astype(F32) * -loss_scale
    heads = []
    for x in range(x4):
        total = None
        for a in range(4):
            taps = [head[a * 4 + b : a * 4 + b + 1, :] for b in range(4) if 0 <= x - b + 1 < x4 - 1]
            tap = functools.reduce(lambda u, v: u + v, taps)
            inside = (row - a + 1 >= 0) & (row - a + 1 < period - 2) & (row < period - 1)
            term = jnp.where(inside, jnp.broadcast_to(tap, (unit, d4)), 0.0)
            total = term if total is None else total + term
        heads.append(total)
    cot = (jnp.concatenate(heads, axis=0) * slope).astype(BF16)
    pull_four[...] = mat(cot, fourth[...], NT)
    cots = []
    for x in range(x3):
        total = None
        for a in range(4):
            term = None
            for b in range(4):
                source = x - b + 1
                if 0 <= source < x4:
                    piece = pull_four[source * unit : (source + 1) * unit, (a * 4 + b) * d3 : (a * 4 + b + 1) * d3]
                    term = piece if term is None else term + piece
            if a != 1:
                term = shift_rows(term, a - 1, period)
            total = term if total is None else total + term
        cots.append((total * slope_three[x * unit : (x + 1) * unit]).astype(BF16))
    pull_three[...] = mat(jnp.concatenate(cots, axis=0), third[...], NT)
    cots = []
    for x in range(x2):
        terms = []
        for a in range(4):
            term = None
            for b in range(4):
                if (x - b + 1) % 2 == 0 and 0 <= (x - b + 1) // 2 < x3:
                    source = (x - b + 1) // 2
                    piece = pull_three[source * unit : (source + 1) * unit, (a * 4 + b) * d2 : (a * 4 + b + 1) * d2]
                    term = piece if term is None else term + piece
            terms.append(term)
        even = terms[1] + shift_rows(terms[3], 1, period)
        odd = terms[2] + shift_rows(terms[0], -1, period)
        both = jnp.concatenate([even, odd], axis=0)
        cots.append((both * slope_two[x * 2 * unit : (x + 1) * 2 * unit]).astype(BF16))
    pull_two[...] = mat(jnp.concatenate(cots, axis=0), second[...], NT)
    strips = []
    for k in range(x2 + 1):
        terms = {}
        for p in range(2):
            for a in range(4):
                term = None
                if k < x2:
                    term = pull_two[(2 * k + p) * unit : (2 * k + p + 1) * unit, a * 4 * d1 : (a * 4 + 2) * d1]
                if k > 0:
                    other = pull_two[(2 * k - 2 + p) * unit : (2 * k - 1 + p) * unit, (a * 4 + 2) * d1 : (a + 1) * 4 * d1]
                    term = other if term is None else term + other
                terms[p, a] = term
        both = jnp.concatenate(
            [
                terms[0, 1] + shift_rows(terms[1, 3], 1, period),
                terms[0, 2] + terms[1, 0],
                terms[0, 3] + terms[1, 1],
                terms[1, 2] + shift_rows(terms[0, 0], -1, period),
            ],
            axis=0,
        )
        strips.append((both * slope_one[:, 2 * k * d1 : (2 * k + 2) * d1]).astype(BF16))
    cot = jnp.concatenate(strips, axis=1)
    copies[3].wait()
    sums = []
    for k in range(-(-width_one // strip)):
        start, end = k * strip, min((k + 1) * strip, width_one)
        pulls = mat(cot[:, start:end], band[:, : end - start], NT)
        groups = []
        for m in range(5):
            terms = [
                pulls[p * unit : (p + 1) * unit, (m - p) * LANES : (m - p + 1) * LANES] for p in range(4) if 0 <= m - p < 2
            ]
            groups.append(functools.reduce(lambda u, v: u + v, terms))
        sums.append(jnp.concatenate(groups, axis=0))
    sums = jnp.concatenate(sums, axis=1)
    upper = sums.astype(BF16)
    lower = (sums - upper.astype(F32)).astype(BF16)
    both = mat(upper, unwindow[...]) + mat(lower, unwindow[...])
    half = both.shape[1] // 2
    odd = [both[m * unit : (m + 1) * unit, 0:wide] for m in range(5)]
    even = [both[m * unit : (m + 1) * unit, half : half + wide] for m in range(5)]
    phases = [even[r // 2] if r % 2 == 0 else odd[(r + 1) // 2] for r in range(8)]
    phases[0] = phases[0] + shift_rows(even[4], 1, period)
    phases[7] = phases[7] + shift_rows(odd[0], -1, period)
    image = jnp.concatenate(phases, axis=0).astype(BF16)
    rows = mat(scatter[...], image)
    for part_at in range(group):
        picked = [rows[(i * group + part_at) * devices : (i * group + part_at + 1) * devices] for i in range(span)]
        for o in range(3):
            plane = [piece[:, o * cols : (o + 1) * cols] for piece in picked]
            plane.append(jnp.zeros((devices, lanes - span * cols), F32))
            plane = jnp.concatenate(plane, axis=1)
            for k in range(lanes // LANES):
                zout[k, pl.ds(o * group + part_at, devices, stride=pitch), :] = plane[:, k * LANES : (k + 1) * LANES]
    for k in range(lanes // LANES):
        out_ref[:, k * LANES : (k + 1) * LANES] = zout[k].astype(BF16)


def row_maps(devices, group, block_rows):
    height = devices * block_rows
    period = height // 8
    span = block_rows + 2
    gather = np.zeros((8 * group * period, span * group * devices), np.float32)
    for device in range(devices):
        for i in range(span):
            y = device * block_rows + i - 1
            if 0 <= y < height:
                for part in range(group):
                    gather[((y % 8) * group + part) * period + y // 8, (i * group + part) * devices + device] = 1.0
    return gather


def windows_of(cols, d1):
    wide = 3 * cols
    count = -(-(cols // 2 + 2) // 8)
    half = up_to(wide, LANES)
    window = np.zeros((wide, count * 2 * LANES), np.float32)
    unwindow = np.zeros((count * LANES, 2 * half), np.float32)
    for k in range(count):
        for c in range(3):
            for j in range(18):
                x = 16 * k - 3 + j
                if 0 <= x < cols:
                    for e in range(2):
                        at = e * LANES // 2 + c * 18 + j
                        window[c * cols + x, (2 * k + e) * LANES + at] = 1.0
                        unwindow[k * LANES + at, e * half + c * cols + x] = 1.0
    return window, unwindow


def band_of(first):
    d1 = first.shape[-1]
    tap = np.arange(18)[:, None] - 2 * (np.arange(8 * d1)[None, :] // d1)
    tiled = jnp.tile(first, (1, 1, 1, 8))
    band = jnp.zeros((4, 3, 18, 8 * d1), BF16)
    for b in range(4):
        band = jnp.where(jnp.asarray(tap == b), tiled[:, b, :, None, :], band)
    band = jnp.pad(band.reshape(4, 54, 8 * d1), ((0, 0), (0, LANES // 2 - 54), (0, 0)))
    return band.reshape(2 * LANES, 8 * d1)


def disc_call(payload, first, second, third, fourth, head, devices, group, cols, block_rows):
    period = devices * block_rows // 8
    unit = group * period
    d1, d2, d3, d4 = first.shape[-1], second.shape[-1], third.shape[-1], fourth.shape[-1]
    x2, x3 = cols // 4, cols // 8
    x4 = x3 - 1
    gather = row_maps(devices, group, block_rows)
    window, unwindow = windows_of(cols, d1)
    width_one = (cols // 2 + 2) * d1
    args = (
        payload,
        jnp.asarray(gather, BF16),
        jnp.asarray(window, BF16),
        band_of(first),
        second.reshape(16 * d1, d2),
        third.reshape(16 * d2, d3),
        fourth.reshape(16 * d3, d4),
        head.reshape(16, d4),
        jnp.asarray(unwindow, BF16),
        jnp.asarray(gather.T, BF16),
    )
    lanes = payload.shape[1]
    return pl.pallas_call(
        functools.partial(
            disc_kernel, devices=devices, group=group, cols=cols, block_rows=block_rows, period=period
        ),
        out_shape=jax.ShapeDtypeStruct(payload.shape, BF16),
        in_specs=[VM, VM, VM, VM, HBM, HBM, HBM, VM, HBM, HBM],
        out_specs=VM,
        scratch_shapes=[
            pltpu.VMEM((lanes // LANES, payload.shape[0], LANES), F32),
            pltpu.VMEM((16 * d1, d2), BF16),
            pltpu.VMEM((16 * d2, d3), BF16),
            pltpu.VMEM((16 * d3, d4), BF16),
            pltpu.VMEM(unwindow.shape, BF16),
            pltpu.VMEM(gather.T.shape, BF16),
            pltpu.VMEM((gather.shape[1], 3 * cols), F32),
            pltpu.VMEM((6 * unit, width_one), BF16),
            pltpu.VMEM((4 * unit, width_one), F32),
            pltpu.VMEM((x2 * 2 * unit, 16 * d1), BF16),
            pltpu.VMEM((4 * unit, (x2 + 2) * d2), BF16),
            pltpu.VMEM((x2 * 2 * unit, d2), F32),
            pltpu.VMEM((4 * unit, (x3 + 2) * d3), BF16),
            pltpu.VMEM((x4 * unit, 16 * d3), BF16),
            pltpu.VMEM((x4 * unit, 16 * d3), F32),
            pltpu.VMEM((x3 * unit, 16 * d2), F32),
            pltpu.VMEM((x2 * 2 * unit, 16 * d1), F32),
            pltpu.VMEM((lanes // LANES, payload.shape[0], LANES), F32),
            pltpu.SemaphoreType.DMA((5,)),
        ],
        compiler_params=MOST,
        cost_estimate=pl.CostEstimate(flops=4 * 10**9, bytes_accessed=8 * 10**6, transcendentals=10**6),
        name="disc_rows",
    )(*args)


def put_taps(plane, taps_ref, frames, cols, pieces, padded):
    lanes = plane.shape[1]
    column = lax.broadcasted_iota(jnp.int32, plane.shape, 1) % cols
    for b in range(3):
        moved = plane
        if b == 0:
            moved = jnp.where(column == cols - 1, 0.0, pltpu.roll(plane, lanes - 1, 1))
        if b == 2:
            moved = jnp.where(column == 0, 0.0, pltpu.roll(plane, 1, 1))
        for a in range(3):
            turned = moved if a == 2 else pltpu.roll(moved, lanes - (2 - a) * cols, 1)
            for k in range(pieces):
                taps_ref[k, pl.ds((a * 3 + b) * 3 * frames, 3 * frames), :] = turned[:, k * LANES : (k + 1) * LANES]
    for k in range(pieces):
        taps_ref[k, pl.ds(27 * frames, (padded - 27) * frames), :] = jnp.zeros(((padded - 27) * frames, LANES), F32)


def unpack(plane_ref, zin, devices, group):
    lanes = plane_ref.shape[1]
    pitch = plane_ref.shape[0] // devices
    for k in range(lanes // LANES):
        zin[k] = plane_ref[:, k * LANES : (k + 1) * LANES].astype(F32)
    blocks = []
    for o in range(3):
        for part in range(group):
            row = pl.ds(o * group + part, devices, stride=pitch)
            blocks.append(jnp.concatenate([zin[k, row, :] for k in range(lanes // LANES)], axis=1))
    return jnp.concatenate(blocks, axis=0)


def rec_rows(inner_ref, zin, devices, group, cols, block_rows):
    lanes = inner_ref.shape[1]
    pitch = zin.shape[1] // devices
    edges = []
    for i in range(2):
        row = pl.ds(3 * group + i, devices, stride=pitch)
        edges.append(jnp.concatenate([zin[k, row, :] for k in range(lanes // LANES)], axis=1))
    blocks = []
    for i, e in ((0, 0), (1, 0), (1, 1), (0, 1)):
        pieces = [
            edges[i][:, (e * 3 * group + at) * cols : (e * 3 * group + at + 1) * cols] for at in range(3 * group)
        ]
        blocks.append(jnp.concatenate(pieces, axis=0))
    none = lambda count: jnp.zeros((blocks[0].shape[0], count), F32)
    above, first, last, below = blocks
    rest = lanes - (block_rows + 2) * cols
    return inner_ref[...], jnp.concatenate(
        [above, first * loss_scale, none((block_rows - 2) * cols), last * loss_scale, below, none(rest)], axis=1
    )


def both_kernel(
    inner_ref, plane_ref, feat_ref, part_ref, rec_ref, rec_taps, gan_taps, zin, *, frames, devices, group, cols, block_rows
):
    pieces = block_rows * cols // LANES
    put_taps(unpack(plane_ref, zin, devices, group), gan_taps, frames, cols, pieces, 32)
    inner, edges = rec_rows(inner_ref, zin, devices, group, cols, block_rows)
    rec = inner + edges
    rec_ref[...] = rec
    put_taps(rec, rec_taps, frames, cols, pieces, 32)
    pixels = pieces * LANES
    total = jnp.zeros((64, feat_ref.shape[1]), F32)
    for frame in range(frames):
        rows = pl.ds(slot_of(frame, devices, group), 32, stride=frames)
        taps = jnp.concatenate(
            [
                jnp.concatenate([taps_ref[k, rows, :] for k in range(pieces)], axis=1)
                for taps_ref in (rec_taps, gan_taps)
            ],
            axis=0,
        )
        total = total + mat(taps.astype(BF16), feat_ref[frame * pixels : (frame + 1) * pixels, :])
    blank = jnp.zeros((part_ref.shape[1] - 54, total.shape[1]), F32)
    total = jnp.concatenate([total[0:27], total[32:59], blank], axis=0).astype(BF16)
    for i in range(part_ref.shape[0]):
        part_ref[i] = total


def turn_kernel(
    rec_ref, plane_ref, out_ref, rec_taps, gan_taps, zin, *, frames, devices, group, cols, block_rows
):
    pieces = block_rows * cols // LANES
    pixels = pieces * LANES
    put_taps(rec_ref[...], rec_taps, frames, cols, pieces, 32)
    put_taps(unpack(plane_ref, zin, devices, group), gan_taps, frames, cols, pieces, 32)
    for pair in range(frames // 2):
        for k in range(pieces):
            parts = []
            for frame in (2 * pair, 2 * pair + 1):
                rows = pl.ds(slot_of(frame, devices, group), 32, stride=frames)
                parts += [rec_taps[k, rows, :], gan_taps[k, rows, :]]
            at = pair * pixels + k * LANES
            out_ref[at : at + LANES, :] = jnp.concatenate(parts, axis=0).T.astype(BF16)


def taps_call(kernel, specs, operands, out, scratch, frames, devices, group, cols, block_rows, flops, name):
    return pl.pallas_call(
        functools.partial(kernel, frames=frames, devices=devices, group=group, cols=cols, block_rows=block_rows),
        out_shape=out,
        in_specs=specs,
        out_specs=jax.tree.map(lambda _: VM, out),
        scratch_shapes=scratch,
        compiler_params=PART,
        cost_estimate=pl.CostEstimate(flops=flops, bytes_accessed=4 * 10**6, transcendentals=0),
        name=name,
    )(*operands)


def final_kernel(taps_ref, sums_ref, weight_ref, out_hbm, grad_ref, adapt_ref, both_ref, out_ref, sems, *, pixels, chunk):
    total = sums_ref[0].astype(F32)
    for i in range(1, sums_ref.shape[0]):
        total = total + sums_ref[i].astype(F32)
    rec, gan = total[0:27], total[27:54]
    norm = lambda values: jnp.sqrt(jnp.sum(jnp.sum(values * values, axis=1, keepdims=True), axis=0, keepdims=True))
    adaptive = norm(rec) / (norm(gan) + epsilon)
    grad = (rec + adaptive * gan) / pixels
    for a in range(3):
        for b in range(3):
            at = (a * 3 + b) * 3
            grad_ref[a, b] = grad[at : at + 3, :]
    adapt_ref[...] = adaptive
    weight = weight_ref[...]
    padded, channels = weight.shape
    scaled = (adaptive * weight.astype(F32)).astype(BF16)
    both_ref[...] = jnp.zeros_like(both_ref)
    both_ref[0:padded, 0:channels] = weight
    both_ref[padded : 2 * padded, 0:channels] = scaled
    both_ref[2 * padded : 3 * padded, channels:] = weight
    both_ref[3 * padded :, channels:] = scaled
    pairs = taps_ref.shape[0] // chunk
    stores = []
    for pair in range(pairs):
        product = mat(taps_ref[pair * chunk : (pair + 1) * chunk], both_ref[...]).astype(BF16)
        rows = pl.ds(2 * pair * chunk, 2 * chunk)
        out_ref[2 * pair * chunk : (2 * pair + 1) * chunk] = product[:, :channels]
        out_ref[(2 * pair + 1) * chunk : (2 * pair + 2) * chunk] = product[:, channels:]
        stores.append(pltpu.make_async_copy(out_ref.at[rows], out_hbm.at[rows], sems.at[pair]))
        stores[-1].start()
    for copy in stores:
        copy.wait()


def final_call(taps, sums, weight, pixels, chunk):
    padded, channels = weight.shape
    rows = 2 * taps.shape[0]
    return pl.pallas_call(
        functools.partial(final_kernel, pixels=pixels, chunk=chunk),
        out_shape=(
            jax.ShapeDtypeStruct((rows, channels), BF16),
            jax.ShapeDtypeStruct((3, 3, 3, channels), F32),
            jax.ShapeDtypeStruct((1, 1), F32),
        ),
        in_specs=[VM] * 3,
        out_specs=(HBM, VM, VM),
        scratch_shapes=[
            pltpu.VMEM((4 * padded, 2 * channels), BF16),
            pltpu.VMEM((rows, channels), BF16),
            pltpu.SemaphoreType.DMA((rows // (2 * chunk),)),
        ],
        compiler_params=PART,
        cost_estimate=pl.CostEstimate(flops=4 * rows * channels * padded, bytes_accessed=4 * rows * channels, transcendentals=0),
        name="feature_pull",
    )(taps, sums, weight)


def per_device(
    features, target, conv_weight, disc_first, disc_second, disc_third, disc_fourth, disc_head
):
    devices = lax.axis_size("row")
    clips = lax.axis_size("clip")
    _, frames, block_rows, cols, channels = features.shape
    group = frames // devices
    pixels = clips * devices * frames * block_rows * cols
    lanes = up_to((block_rows + 2) * cols, LANES)
    pitch = up_to(3 * group + 2, 8)
    sizes = (frames, devices, group, cols, block_rows)
    feats = features.reshape(frames * block_rows * cols, channels)
    wanted = target[0].transpose(0, 2, 1, 3)
    payload, own, weight = forward_call(feats, wanted, conv_weight, frames, devices, group, cols, lanes, pitch)
    trade = lambda values: lax.all_to_all(
        values.reshape(devices, pitch, lanes), "row", split_axis=0, concat_axis=0, tiled=True
    ).reshape(devices * pitch, lanes)
    arrived = trade(payload)
    inner = inner_call(own, wanted, frames, devices, group, block_rows, cols)
    arrived, inner = lax.optimization_barrier((arrived, inner))
    sent = disc_call(
        arrived, disc_first, disc_second, disc_third, disc_fourth, disc_head, devices, group, cols, block_rows
    )
    returned = trade(sent)
    taps_scratch = pltpu.VMEM((block_rows * cols // LANES, 32 * frames, LANES), F32)
    plane_scratch = pltpu.VMEM((lanes // LANES, devices * pitch, LANES), F32)
    flops = 4 * features.size * 27
    part, rec_plane = taps_call(
        both_kernel, [VM, VM, VM], (inner, returned, feats),
        (jax.ShapeDtypeStruct((clips * devices, 56, channels), BF16), jax.ShapeDtypeStruct(own.shape, F32)),
        [taps_scratch, taps_scratch, plane_scratch], *sizes, flops, "both_taps",
    )
    sums = lax.all_to_all(part, ("clip", "row"), split_axis=0, concat_axis=0, tiled=True)
    taps = taps_call(
        turn_kernel, [VM, VM], (rec_plane, returned), jax.ShapeDtypeStruct((feats.shape[0] // 2, LANES), BF16),
        [taps_scratch, taps_scratch, plane_scratch], *sizes, flops, "turn_taps",
    )
    image_back = returned.reshape(devices, pitch, lanes)[:, : 3 * group, cols : (block_rows + 1) * cols]
    image_back = image_back.reshape(devices, 3, group, block_rows, cols).transpose(0, 2, 3, 1, 4)
    image_back = image_back.reshape(1, frames, block_rows, 3, cols)
    feature_grad, weight_grad, adaptive = final_call(taps, sums, weight, pixels, block_rows * cols)
    return (feature_grad.reshape(features.shape), image_back, weight_grad, adaptive[0, 0])


def solution(mesh):
    rows = P("clip", None, "row", None, None)
    return jax.shard_map(
        per_device,
        mesh=mesh,
        in_specs=(rows, rows, P(), P(), P(), P(), P(), P()),
        out_specs=(rows, rows, P(), P()),
        check_vma=False,
    )
```

```python
import functools

import jax
import jax.numpy as jnp
import numpy as np
from jax import lax
from jax.experimental import pallas as pl
from jax.experimental.pallas import tpu as pltpu
from jax.sharding import PartitionSpec as P

loss_scale = 64.0
epsilon = 0.0001
F32 = jnp.float32
BF16 = jnp.bfloat16
LANES = 128
NN = (((1,), (0,)), ((), ()))
NT = (((1,), (1,)), ((), ()))
TN = (((0,), (0,)), ((), ()))
VM = pl.BlockSpec(memory_space=pltpu.VMEM)
HBM = pl.BlockSpec(memory_space=pl.ANY)
WHOLE = pltpu.CompilerParams(vmem_limit_bytes=60 * 2**20)
MOST = pltpu.CompilerParams(vmem_limit_bytes=119 * 2**19)
PART = pltpu.CompilerParams(vmem_limit_bytes=24 * 2**20)


def up_to(value, step):
    return -(-value // step) * step


def mat(left, right, dims=NN):
    return lax.dot_general(left, right, dims, preferred_element_type=F32)


def slot_of(frame, devices, group):
    return (frame % group) * devices + frame // group


def forward_kernel(
    feat_hbm, target_hbm, weight_hbm, pay_ref, own_ref, flat_ref, feat_ref, target_ref, weight_ref, weight_scr, target_scr,
    taps_ref, out_ref, sems, *, frames, devices, group, cols, lanes, chunks,
):
    pixels = feat_ref.shape[0] // frames
    pieces = pixels // LANES
    pitch = out_ref.shape[1] // devices
    taps = flat_ref.shape[0]
    block_rows = pixels // cols
    copies = [
        pltpu.make_async_copy(weight_hbm, weight_ref, sems.at[frames]),
        pltpu.make_async_copy(target_hbm, target_ref, sems.at[frames + 1]),
    ]
    for slot in range(frames):
        rows = pl.ds((slot % devices * group + slot // devices) * pixels, pixels)
        copies.append(pltpu.make_async_copy(feat_hbm.at[rows, :], feat_ref.at[rows, :], sems.at[slot]))
    for i, copy in enumerate(copies):
        copy.start(priority=i % 2)
    weight_scr[...] = jnp.zeros_like(weight_scr)
    out_ref[...] = jnp.zeros_like(out_ref)
    copies[0].wait()
    copies[1].wait()
    for a in range(3):
        for b in range(3):
            at = (a * 3 + b) * 3
            weight_scr[at : at + 3, :] = weight_ref[a, b].astype(F32)
    weight = weight_scr[...].astype(BF16)
    flat_ref[...] = weight
    target_scr[:, 0:cols] = target_ref[...].reshape(target_scr.shape[0], cols).astype(F32)
    edges = []
    for y in (0, block_rows - 1):
        for o in range(3):
            for part in range(group):
                rows = pl.ds((part * 3 + o) * block_rows + y, devices, stride=group * 3 * block_rows)
                edges.append(target_scr[rows, :][:, 0:cols])
    edges.append(jnp.zeros((devices, lanes - len(edges) * cols), F32))
    edges = jnp.concatenate(edges, axis=1)
    for k in range(lanes // LANES):
        out_ref[k, pl.ds(3 * group, devices, stride=pitch), :] = edges[:, k * LANES : (k + 1) * LANES]
    column = lax.broadcasted_iota(jnp.int32, (devices, pixels), 1) % cols

    def finish(part):
        def tap(a, b, o):
            rows = pl.ds(((a * 3 + b) * 3 + o) * frames + part * devices, devices)
            return jnp.concatenate([taps_ref[k, rows, :] for k in range(pieces)], axis=1)

        for o in range(3):
            total = None
            for a in range(3):
                term = tap(a, 1, o)
                term = term + jnp.where(column == 0, 0.0, pltpu.roll(tap(a, 0, o), 1, 1))
                term = term + jnp.where(column == cols - 1, 0.0, pltpu.roll(tap(a, 2, o), pixels - 1, 1))
                term = jnp.concatenate([term, jnp.zeros((devices, lanes - pixels), F32)], axis=1)
                if a < 2:
                    term = pltpu.roll(term, (2 - a) * cols, 1)
                total = term if total is None else total + term
            at = o * frames + part * devices
            own_ref[at : at + devices, :] = total
            for k in range(lanes // LANES):
                rows = pl.ds(o * group + part, devices, stride=pitch)
                out_ref[k, rows, :] = total[:, k * LANES : (k + 1) * LANES]

    step = frames // chunks
    done = 0
    for chunk in range(chunks):
        for slot in range(chunk * step, (chunk + 1) * step):
            copies[2 + slot].wait()
        for slot in range(chunk * step, (chunk + 1) * step):
            frame = slot % devices * group + slot // devices
            product = mat(weight, feat_ref[frame * pixels : (frame + 1) * pixels, :], NT)
            for k in range(pieces):
                taps_ref[k, pl.ds(slot, taps, stride=frames), :] = product[:, k * LANES : (k + 1) * LANES]
        while (done + 1) * devices <= chunk * step or (chunk == chunks - 1 and done < group):
            finish(done)
            done += 1
    for k in range(lanes // LANES):
        pay_ref[:, k * LANES : (k + 1) * LANES] = out_ref[k].astype(BF16)


def forward_call(features, target, weight, frames, devices, group, cols, lanes, pitch):
    pixels = features.shape[0] // frames
    channels = features.shape[1]
    chunks = 4
    return pl.pallas_call(
        functools.partial(
            forward_kernel, frames=frames, devices=devices, group=group, cols=cols, lanes=lanes, chunks=chunks
        ),
        out_shape=(
            jax.ShapeDtypeStruct((devices * pitch, lanes), BF16),
            jax.ShapeDtypeStruct((3 * frames, lanes), F32),
            jax.ShapeDtypeStruct((32, channels), BF16),
        ),
        in_specs=[HBM, HBM, HBM],
        out_specs=(VM,) * 3,
        scratch_shapes=[
            pltpu.VMEM(features.shape, BF16),
            pltpu.VMEM(target.shape, BF16),
            pltpu.VMEM(weight.shape, BF16),
            pltpu.VMEM((32, channels), F32),
            pltpu.VMEM((3 * pixels // cols * frames, LANES), F32),
            pltpu.VMEM((pixels // LANES, 32 * frames, LANES), F32),
            pltpu.VMEM((lanes // LANES, devices * pitch, LANES), F32),
            pltpu.SemaphoreType.DMA((frames + 2,)),
        ],
        compiler_params=WHOLE,
        cost_estimate=pl.CostEstimate(flops=2 * features.size * 27, bytes_accessed=2 * features.size, transcendentals=0),
        name="forward_taps",
    )(features, target, weight)


def inner_kernel(own_ref, target_ref, inner_ref, scr, *, frames, devices, group, block_rows, cols):
    scr[:, 0:cols] = target_ref[...].reshape(scr.shape[0], cols).astype(F32)
    stride = group * 3 * block_rows
    lanes = own_ref.shape[1]
    for o in range(3):
        for part in range(group):
            at = o * frames + part * devices
            rows = [jnp.zeros((devices, cols), F32)]
            rows += [
                scr[pl.ds((part * 3 + o) * block_rows + y, devices, stride=stride), :][:, 0:cols]
                for y in range(block_rows)
            ]
            rows.append(jnp.zeros((devices, lanes - (block_rows + 1) * cols), F32))
            wanted = jnp.concatenate(rows, axis=1)
            lane = lax.broadcasted_iota(jnp.int32, wanted.shape, 1)
            inside = (lane >= 2 * cols) & (lane < block_rows * cols)
            own = jnp.where(inside, own_ref[at : at + devices, :], 0.0)
            inner_ref[at : at + devices, :] = loss_scale * (own - wanted)


def inner_call(own, target, frames, devices, group, block_rows, cols):
    return pl.pallas_call(
        functools.partial(
            inner_kernel, frames=frames, devices=devices, group=group, block_rows=block_rows, cols=cols
        ),
        out_shape=jax.ShapeDtypeStruct(own.shape, F32),
        in_specs=[VM, VM],
        out_specs=VM,
        scratch_shapes=[pltpu.VMEM((frames * 3 * block_rows, LANES), F32)],
        compiler_params=PART,
        cost_estimate=pl.CostEstimate(flops=10**8, bytes_accessed=10**6, transcendentals=0),
        name="inner_rows",
    )(own, target)


def shift_rows(values, step, period):
    size = values.shape[0]
    row = lax.broadcasted_iota(jnp.int32, values.shape, 0) % period
    rolled = pltpu.roll(values, step % size, 0)
    source = row - step
    return jnp.where((source >= 0) & (source < period), rolled, 0.0)


def gate_of(values):
    logistic = 1.0 / (1.0 + jnp.exp(-values))
    return (values * logistic).astype(BF16), logistic * (1.0 + values * (1.0 - logistic))


def edge_planes(zin, zout, first, last, devices, group, cols, lanes, pitch):
    row = pl.ds(3 * group, devices, stride=pitch)
    target = jnp.concatenate([zin[k, row, :] for k in range(lanes // LANES)], axis=1)
    outer, inner = [], []
    for e, rows, other, move in ((0, first, last, 1), (1, last, first, -1)):
        for o in range(3):
            for part in range(group):
                at = ((1 - e) * 3 * group + o * group + part) * cols
                near = other[part][:, o * cols : (o + 1) * cols] - target[:, at : at + cols]
                outer.append(shift_rows(loss_scale * near, move, devices))
                inner.append(rows[part][:, o * cols : (o + 1) * cols])
    for i, pieces in enumerate((outer, inner)):
        pieces.append(jnp.zeros((devices, lanes - 6 * group * cols), F32))
        plane = jnp.concatenate(pieces, axis=1)
        for k in range(lanes // LANES):
            zout[k, pl.ds(3 * group + i, devices, stride=pitch), :] = plane[:, k * LANES : (k + 1) * LANES]


def disc_kernel(
    pay_ref, head_ref, window_hbm, band_hbm, second_hbm, third_hbm, fourth_hbm, unwindow_hbm, out_ref,
    zin, window, band_ref, second, third, fourth, unwindow, rows_in, act_one, slope_one, cols_two, act_two, slope_two, act_three, cols_four,
    pull_four, pull_three, pull_two, zout, sems, *, devices, group, cols, block_rows, period,
):
    lanes = pay_ref.shape[1]
    pitch = pay_ref.shape[0] // devices
    span = block_rows + 2
    unit = group * period
    wide = 3 * cols
    d1 = (act_one.shape[1]) // (cols // 2 + 2)
    d2, d3, d4 = second.shape[1], third.shape[1], fourth.shape[1]
    x1, x2, x3 = cols // 2, cols // 4, cols // 8
    x4 = x3 - 1
    pairs = (
        (window_hbm, window),
        (band_hbm, band_ref),
        (second_hbm, second),
        (third_hbm, third),
        (fourth_hbm, fourth),
        (unwindow_hbm, unwindow),
    )
    copies = [pltpu.make_async_copy(source, target, sems.at[i]) for i, (source, target) in enumerate(pairs)]
    for i, copy in enumerate(copies):
        copy.start(priority=i % 2)
    cells = block_rows // 8
    spot = lambda y, part: pl.ds((y % 8 * group + part) * period + y // 8, devices, stride=cells)
    for k in range(lanes // LANES):
        zin[k] = pay_ref[:, k * LANES : (k + 1) * LANES].astype(F32)
    zout[...] = jnp.zeros_like(zout)
    firsts, lasts = [], []
    for part in range(group):
        planes = []
        for o in range(3):
            pieces = [zin[k, pl.ds(o * group + part, devices, stride=pitch), :] for k in range(lanes // LANES)]
            planes.append(jnp.concatenate(pieces, axis=1))
        lines = [
            jnp.concatenate(
                [plane[:, i * cols : (i + 1) * cols] for plane in planes]
                + [jnp.zeros((devices, 2 * LANES - wide), F32)],
                axis=1,
            )
            for i in range(span)
        ]
        lines[1] = lines[1] + shift_rows(lines[span - 1], 1, devices)
        lines[block_rows] = lines[block_rows] + shift_rows(lines[0], -1, devices)
        for y in range(block_rows):
            for k in range(2):
                rows_in[k, spot(y, part), :] = lines[y + 1][:, k * LANES : (k + 1) * LANES]
        firsts.append(lines[1])
        lasts.append(lines[block_rows])
    image = jnp.concatenate([rows_in[0], rows_in[1]], axis=1)[:, :wide].astype(BF16)
    copies[0].wait()
    copies[1].wait()
    wins = mat(image, window[...])
    ext = [wins[r * unit : (r + 1) * unit] for r in range(8)]
    ext = [shift_rows(ext[7], 1, period)] + ext + [shift_rows(ext[0], -1, period)]
    width_one = act_one.shape[1]
    strip = 8 * d1
    band = band_ref[...]
    for k in range(-(-width_one // strip)):
        low, high = slice(2 * k * LANES, (2 * k + 1) * LANES), slice((2 * k + 1) * LANES, (2 * k + 2) * LANES)
        left = jnp.concatenate(
            [
                jnp.concatenate([ext[2 * p + h][:, low] + ext[2 * p + h + 1][:, high] for p in range(4)], axis=0)
                for h in (0, 2)
            ],
            axis=1,
        ).astype(BF16)
        start, end = k * strip, min((k + 1) * strip, width_one)
        act, slope = gate_of(mat(left, band[:, : end - start]))
        if k == 0 or end == width_one:
            lane = start + lax.broadcasted_iota(jnp.int32, slope.shape, 1)
            inside = (lane >= d1) & (lane < width_one - d1)
            slope = jnp.where(inside, slope, 0.0)
            act = jnp.where(inside, act.astype(F32), 0.0).astype(BF16)
        slope_one[:, start:end] = slope
        act_one[unit : 5 * unit, start:end] = act
        actual = act.astype(F32)
        act_one[0:unit, start:end] = shift_rows(actual[3 * unit :], 1, period).astype(BF16)
        act_one[5 * unit :, start:end] = shift_rows(actual[:unit], -1, period).astype(BF16)
    copies[2].wait()
    for x in range(x2):
        for a in range(4):
            for p in range(2):
                cols_two[(x * 2 + p) * unit : (x * 2 + p + 1) * unit, a * 4 * d1 : (a + 1) * 4 * d1] = act_one[
                    (2 * p + a) * unit : (2 * p + a + 1) * unit, 2 * x * d1 : (2 * x + 4) * d1
                ]
    pre = mat(cols_two[...], second[...])
    act, slope = gate_of(pre)
    slope_two[...] = slope
    act_two[:, 0:d2] = jnp.zeros((4 * unit, d2), BF16)
    act_two[:, (x2 + 1) * d2 :] = jnp.zeros((4 * unit, d2), BF16)
    for x in range(x2):
        block = act[x * 2 * unit : (x + 1) * 2 * unit]
        actual = block.astype(F32)
        at = slice((x + 1) * d2, (x + 2) * d2)
        act_two[unit : 3 * unit, at] = block
        act_two[0:unit, at] = shift_rows(actual[unit:], 1, period).astype(BF16)
        act_two[3 * unit :, at] = shift_rows(actual[:unit], -1, period).astype(BF16)
    copies[3].wait()
    left = jnp.concatenate(
        [
            jnp.concatenate([act_two[a * unit : (a + 1) * unit, 2 * x * d2 : (2 * x + 4) * d2] for a in range(4)], axis=1)
            for x in range(x3)
        ],
        axis=0,
    )
    act, slope_three = gate_of(mat(left, third[...]))
    act_three[:, 0:d3] = jnp.zeros((4 * unit, d3), BF16)
    act_three[:, (x3 + 1) * d3 :] = jnp.zeros((4 * unit, d3), BF16)
    for x in range(x3):
        block = act[x * unit : (x + 1) * unit]
        actual = block.astype(F32)
        at = slice((x + 1) * d3, (x + 2) * d3)
        act_three[unit : 2 * unit, at] = block
        for a in (0, 2, 3):
            act_three[a * unit : (a + 1) * unit, at] = shift_rows(actual, 1 - a, period).astype(BF16)
    for x in range(x4):
        for a in range(4):
            cols_four[x * unit : (x + 1) * unit, a * 4 * d3 : (a + 1) * 4 * d3] = act_three[
                a * unit : (a + 1) * unit, x * d3 : (x + 4) * d3
            ]
    copies[4].wait()
    pre = mat(cols_four[...], fourth[...])
    edge_planes(zin, zout, firsts, lasts, devices, group, cols, lanes, pitch)
    _, slope = gate_of(pre)
    row = lax.broadcasted_iota(jnp.int32, (unit, d4), 0) % period
    head = head_ref[...].astype(F32) * -loss_scale
    heads = []
    for x in range(x4):
        total = None
        for a in range(4):
            taps = [head[a * 4 + b : a * 4 + b + 1, :] for b in range(4) if 0 <= x - b + 1 < x4 - 1]
            tap = functools.reduce(lambda u, v: u + v, taps)
            inside = (row - a + 1 >= 0) & (row - a + 1 < period - 2) & (row < period - 1)
            term = jnp.where(inside, jnp.broadcast_to(tap, (unit, d4)), 0.0)
            total = term if total is None else total + term
        heads.append(total)
    cot = (jnp.concatenate(heads, axis=0) * slope).astype(BF16)
    pull_four[...] = mat(cot, fourth[...], NT)
    cots = []
    for x in range(x3):
        total = None
        for a in range(4):
            term = None
            for b in range(4):
                source = x - b + 1
                if 0 <= source < x4:
                    piece = pull_four[source * unit : (source + 1) * unit, (a * 4 + b) * d3 : (a * 4 + b + 1) * d3]
                    term = piece if term is None else term + piece
            if a != 1:
                term = shift_rows(term, a - 1, period)
            total = term if total is None else total + term
        cots.append((total * slope_three[x * unit : (x + 1) * unit]).astype(BF16))
    pull_three[...] = mat(jnp.concatenate(cots, axis=0), third[...], NT)
    cots = []
    for x in range(x2):
        terms = []
        for a in range(4):
            term = None
            for b in range(4):
                if (x - b + 1) % 2 == 0 and 0 <= (x - b + 1) // 2 < x3:
                    source = (x - b + 1) // 2
                    piece = pull_three[source * unit : (source + 1) * unit, (a * 4 + b) * d2 : (a * 4 + b + 1) * d2]
                    term = piece if term is None else term + piece
            terms.append(term)
        even = terms[1] + shift_rows(terms[3], 1, period)
        odd = terms[2] + shift_rows(terms[0], -1, period)
        both = jnp.concatenate([even, odd], axis=0)
        cots.append((both * slope_two[x * 2 * unit : (x + 1) * 2 * unit]).astype(BF16))
    pull_two[...] = mat(jnp.concatenate(cots, axis=0), second[...], NT)
    strips = []
    for k in range(x2 + 1):
        terms = {}
        for p in range(2):
            for a in range(4):
                term = None
                if k < x2:
                    term = pull_two[(2 * k + p) * unit : (2 * k + p + 1) * unit, a * 4 * d1 : (a * 4 + 2) * d1]
                if k > 0:
                    other = pull_two[(2 * k - 2 + p) * unit : (2 * k - 1 + p) * unit, (a * 4 + 2) * d1 : (a + 1) * 4 * d1]
                    term = other if term is None else term + other
                terms[p, a] = term
        both = jnp.concatenate(
            [
                terms[0, 1] + shift_rows(terms[1, 3], 1, period),
                terms[0, 2] + terms[1, 0],
                terms[0, 3] + terms[1, 1],
                terms[1, 2] + shift_rows(terms[0, 0], -1, period),
            ],
            axis=0,
        )
        strips.append((both * slope_one[:, 2 * k * d1 : (2 * k + 2) * d1]).astype(BF16))
    cot = jnp.concatenate(strips, axis=1)
    copies[5].wait()
    sums = []
    for k in range(-(-width_one // strip)):
        start, end = k * strip, min((k + 1) * strip, width_one)
        pulls = mat(cot[:, start:end], band[:, : end - start], NT)
        groups = []
        for m in range(5):
            terms = [
                pulls[p * unit : (p + 1) * unit, (m - p) * LANES : (m - p + 1) * LANES] for p in range(4) if 0 <= m - p < 2
            ]
            groups.append(functools.reduce(lambda u, v: u + v, terms))
        sums.append(jnp.concatenate(groups, axis=0))
    sums = jnp.concatenate(sums, axis=1)
    upper = sums.astype(BF16)
    lower = (sums - upper.astype(F32)).astype(BF16)
    both = mat(upper, unwindow[...]) + mat(lower, unwindow[...])
    half = both.shape[1] // 2
    odd = [both[m * unit : (m + 1) * unit, 0:wide] for m in range(5)]
    even = [both[m * unit : (m + 1) * unit, half : half + wide] for m in range(5)]
    phases = [even[r // 2] if r % 2 == 0 else odd[(r + 1) // 2] for r in range(8)]
    phases[0] = phases[0] + shift_rows(even[4], 1, period)
    phases[7] = phases[7] + shift_rows(odd[0], -1, period)
    image = jnp.concatenate(phases, axis=0)
    image = jnp.concatenate([image, jnp.zeros((image.shape[0], 2 * LANES - wide), F32)], axis=1)
    for k in range(2):
        rows_in[k] = image[:, k * LANES : (k + 1) * LANES]
    for part in range(group):
        lines = [
            jnp.concatenate([rows_in[k, spot(y, part), :] for k in range(2)], axis=1)[:, :wide]
            for y in range(block_rows)
        ]
        lines = [shift_rows(lines[-1], 1, devices)] + lines + [shift_rows(lines[0], -1, devices)]
        for o in range(3):
            plane = [line[:, o * cols : (o + 1) * cols] for line in lines]
            plane.append(jnp.zeros((devices, lanes - span * cols), F32))
            plane = jnp.concatenate(plane, axis=1)
            for k in range(lanes // LANES):
                zout[k, pl.ds(o * group + part, devices, stride=pitch), :] = plane[:, k * LANES : (k + 1) * LANES]
    for k in range(lanes // LANES):
        out_ref[:, k * LANES : (k + 1) * LANES] = zout[k].astype(BF16)


def windows_of(cols, d1):
    wide = 3 * cols
    count = -(-(cols // 2 + 2) // 8)
    half = up_to(wide, LANES)
    window = np.zeros((wide, count * 2 * LANES), np.float32)
    unwindow = np.zeros((count * LANES, 2 * half), np.float32)
    for k in range(count):
        for c in range(3):
            for j in range(18):
                x = 16 * k - 3 + j
                if 0 <= x < cols:
                    for e in range(2):
                        at = e * LANES // 2 + c * 18 + j
                        window[c * cols + x, (2 * k + e) * LANES + at] = 1.0
                        unwindow[k * LANES + at, e * half + c * cols + x] = 1.0
    return window, unwindow


def band_of(first):
    d1 = first.shape[-1]
    tap = np.arange(18)[:, None] - 2 * (np.arange(8 * d1)[None, :] // d1)
    tiled = jnp.tile(first, (1, 1, 1, 8))
    band = jnp.zeros((4, 3, 18, 8 * d1), BF16)
    for b in range(4):
        band = jnp.where(jnp.asarray(tap == b), tiled[:, b, :, None, :], band)
    band = jnp.pad(band.reshape(4, 54, 8 * d1), ((0, 0), (0, LANES // 2 - 54), (0, 0)))
    return band.reshape(2 * LANES, 8 * d1)


def disc_call(payload, first, second, third, fourth, head, devices, group, cols, block_rows):
    period = devices * block_rows // 8
    unit = group * period
    d1, d2, d3, d4 = first.shape[-1], second.shape[-1], third.shape[-1], fourth.shape[-1]
    x2, x3 = cols // 4, cols // 8
    x4 = x3 - 1
    window, unwindow = windows_of(cols, d1)
    width_one = (cols // 2 + 2) * d1
    args = (
        payload,
        head.reshape(16, d4),
        jnp.asarray(window, BF16),
        band_of(first),
        second.reshape(16 * d1, d2),
        third.reshape(16 * d2, d3),
        fourth.reshape(16 * d3, d4),
        jnp.asarray(unwindow, BF16),
    )
    lanes = payload.shape[1]
    return pl.pallas_call(
        functools.partial(
            disc_kernel, devices=devices, group=group, cols=cols, block_rows=block_rows, period=period
        ),
        out_shape=jax.ShapeDtypeStruct(payload.shape, BF16),
        in_specs=[VM, VM] + [HBM] * 6,
        out_specs=VM,
        scratch_shapes=[
            pltpu.VMEM((lanes // LANES, payload.shape[0], LANES), F32),
            pltpu.VMEM(window.shape, BF16),
            pltpu.VMEM((2 * LANES, 8 * d1), BF16),
            pltpu.VMEM((16 * d1, d2), BF16),
            pltpu.VMEM((16 * d2, d3), BF16),
            pltpu.VMEM((16 * d3, d4), BF16),
            pltpu.VMEM(unwindow.shape, BF16),
            pltpu.VMEM((2, 8 * unit, LANES), F32),
            pltpu.VMEM((6 * unit, width_one), BF16),
            pltpu.VMEM((4 * unit, width_one), F32),
            pltpu.VMEM((x2 * 2 * unit, 16 * d1), BF16),
            pltpu.VMEM((4 * unit, (x2 + 2) * d2), BF16),
            pltpu.VMEM((x2 * 2 * unit, d2), F32),
            pltpu.VMEM((4 * unit, (x3 + 2) * d3), BF16),
            pltpu.VMEM((x4 * unit, 16 * d3), BF16),
            pltpu.VMEM((x4 * unit, 16 * d3), F32),
            pltpu.VMEM((x3 * unit, 16 * d2), F32),
            pltpu.VMEM((x2 * 2 * unit, 16 * d1), F32),
            pltpu.VMEM((lanes // LANES, payload.shape[0], LANES), F32),
            pltpu.SemaphoreType.DMA((6,)),
        ],
        compiler_params=MOST,
        cost_estimate=pl.CostEstimate(flops=4 * 10**9, bytes_accessed=8 * 10**6, transcendentals=10**6),
        name="disc_rows",
    )(*args)


def put_taps(plane, taps_ref, frames, cols, pieces, padded):
    lanes = plane.shape[1]
    column = lax.broadcasted_iota(jnp.int32, plane.shape, 1) % cols
    for b in range(3):
        moved = plane
        if b == 0:
            moved = jnp.where(column == cols - 1, 0.0, pltpu.roll(plane, lanes - 1, 1))
        if b == 2:
            moved = jnp.where(column == 0, 0.0, pltpu.roll(plane, 1, 1))
        for a in range(3):
            turned = moved if a == 2 else pltpu.roll(moved, lanes - (2 - a) * cols, 1)
            for k in range(pieces):
                taps_ref[k, pl.ds((a * 3 + b) * 3 * frames, 3 * frames), :] = turned[:, k * LANES : (k + 1) * LANES]
    for k in range(pieces):
        taps_ref[k, pl.ds(27 * frames, (padded - 27) * frames), :] = jnp.zeros(((padded - 27) * frames, LANES), F32)


def unpack(plane_ref, zin, devices, group):
    lanes = plane_ref.shape[1]
    pitch = plane_ref.shape[0] // devices
    for k in range(lanes // LANES):
        zin[k] = plane_ref[:, k * LANES : (k + 1) * LANES].astype(F32)
    blocks = []
    for o in range(3):
        for part in range(group):
            row = pl.ds(o * group + part, devices, stride=pitch)
            blocks.append(jnp.concatenate([zin[k, row, :] for k in range(lanes // LANES)], axis=1))
    return jnp.concatenate(blocks, axis=0)


def rec_rows(inner_ref, zin, devices, group, cols, block_rows):
    lanes = inner_ref.shape[1]
    pitch = zin.shape[1] // devices
    edges = []
    for i in range(2):
        row = pl.ds(3 * group + i, devices, stride=pitch)
        edges.append(jnp.concatenate([zin[k, row, :] for k in range(lanes // LANES)], axis=1))
    blocks = []
    for i, e in ((0, 0), (1, 0), (1, 1), (0, 1)):
        pieces = [
            edges[i][:, (e * 3 * group + at) * cols : (e * 3 * group + at + 1) * cols] for at in range(3 * group)
        ]
        blocks.append(jnp.concatenate(pieces, axis=0))
    none = lambda count: jnp.zeros((blocks[0].shape[0], count), F32)
    above, first, last, below = blocks
    rest = lanes - (block_rows + 2) * cols
    return inner_ref[...], jnp.concatenate(
        [above, first * loss_scale, none((block_rows - 2) * cols), last * loss_scale, below, none(rest)], axis=1
    )


def both_kernel(
    inner_ref, plane_ref, feat_ref, part_ref, rec_ref, rec_taps, gan_taps, zin, *, frames, devices, group, cols, block_rows
):
    pieces = block_rows * cols // LANES
    put_taps(unpack(plane_ref, zin, devices, group), gan_taps, frames, cols, pieces, 32)
    inner, edges = rec_rows(inner_ref, zin, devices, group, cols, block_rows)
    rec = inner + edges
    rec_ref[...] = rec
    put_taps(rec, rec_taps, frames, cols, pieces, 32)
    pixels = pieces * LANES
    total = jnp.zeros((64, feat_ref.shape[1]), F32)
    for frame in range(frames):
        rows = pl.ds(slot_of(frame, devices, group), 32, stride=frames)
        taps = jnp.concatenate(
            [
                jnp.concatenate([taps_ref[k, rows, :] for k in range(pieces)], axis=1)
                for taps_ref in (rec_taps, gan_taps)
            ],
            axis=0,
        )
        total = total + mat(taps.astype(BF16), feat_ref[frame * pixels : (frame + 1) * pixels, :])
    blank = jnp.zeros((part_ref.shape[1] - 54, total.shape[1]), F32)
    total = jnp.concatenate([total[0:27], total[32:59], blank], axis=0).astype(BF16)
    for i in range(part_ref.shape[0]):
        part_ref[i] = total


def turn_kernel(
    rec_ref, plane_ref, out_ref, rec_taps, gan_taps, zin, *, frames, devices, group, cols, block_rows
):
    pieces = block_rows * cols // LANES
    pixels = pieces * LANES
    put_taps(rec_ref[...], rec_taps, frames, cols, pieces, 32)
    put_taps(unpack(plane_ref, zin, devices, group), gan_taps, frames, cols, pieces, 32)
    for pair in range(frames // 2):
        for k in range(pieces):
            parts = []
            for frame in (2 * pair, 2 * pair + 1):
                rows = pl.ds(slot_of(frame, devices, group), 32, stride=frames)
                parts += [rec_taps[k, rows, :], gan_taps[k, rows, :]]
            at = pair * pixels + k * LANES
            out_ref[at : at + LANES, :] = jnp.concatenate(parts, axis=0).T.astype(BF16)


def taps_call(kernel, specs, operands, out, scratch, frames, devices, group, cols, block_rows, flops, name):
    return pl.pallas_call(
        functools.partial(kernel, frames=frames, devices=devices, group=group, cols=cols, block_rows=block_rows),
        out_shape=out,
        in_specs=specs,
        out_specs=jax.tree.map(lambda _: VM, out),
        scratch_shapes=scratch,
        compiler_params=PART,
        cost_estimate=pl.CostEstimate(flops=flops, bytes_accessed=4 * 10**6, transcendentals=0),
        name=name,
    )(*operands)


def final_kernel(taps_ref, sums_ref, weight_ref, out_hbm, grad_ref, adapt_ref, both_ref, out_ref, sems, *, pixels, chunk):
    total = sums_ref[0].astype(F32)
    for i in range(1, sums_ref.shape[0]):
        total = total + sums_ref[i].astype(F32)
    rec, gan = total[0:27], total[27:54]
    norm = lambda values: jnp.sqrt(jnp.sum(jnp.sum(values * values, axis=1, keepdims=True), axis=0, keepdims=True))
    adaptive = norm(rec) / (norm(gan) + epsilon)
    grad = (rec + adaptive * gan) / pixels
    for a in range(3):
        for b in range(3):
            at = (a * 3 + b) * 3
            grad_ref[a, b] = grad[at : at + 3, :]
    adapt_ref[...] = adaptive
    weight = weight_ref[...]
    padded, channels = weight.shape
    scaled = (adaptive * weight.astype(F32)).astype(BF16)
    both_ref[...] = jnp.zeros_like(both_ref)
    both_ref[0:padded, 0:channels] = weight
    both_ref[padded : 2 * padded, 0:channels] = scaled
    both_ref[2 * padded : 3 * padded, channels:] = weight
    both_ref[3 * padded :, channels:] = scaled
    pairs = taps_ref.shape[0] // chunk
    stores = []
    for pair in range(pairs):
        product = mat(taps_ref[pair * chunk : (pair + 1) * chunk], both_ref[...]).astype(BF16)
        rows = pl.ds(2 * pair * chunk, 2 * chunk)
        out_ref[2 * pair * chunk : (2 * pair + 1) * chunk] = product[:, :channels]
        out_ref[(2 * pair + 1) * chunk : (2 * pair + 2) * chunk] = product[:, channels:]
        stores.append(pltpu.make_async_copy(out_ref.at[rows], out_hbm.at[rows], sems.at[pair]))
        stores[-1].start(priority=pair % 2)
    for copy in stores:
        copy.wait()


def final_call(taps, sums, weight, pixels, chunk):
    padded, channels = weight.shape
    rows = 2 * taps.shape[0]
    return pl.pallas_call(
        functools.partial(final_kernel, pixels=pixels, chunk=chunk),
        out_shape=(
            jax.ShapeDtypeStruct((rows, channels), BF16),
            jax.ShapeDtypeStruct((3, 3, 3, channels), F32),
            jax.ShapeDtypeStruct((1, 1), F32),
        ),
        in_specs=[VM] * 3,
        out_specs=(HBM, VM, VM),
        scratch_shapes=[
            pltpu.VMEM((4 * padded, 2 * channels), BF16),
            pltpu.VMEM((rows, channels), BF16),
            pltpu.SemaphoreType.DMA((rows // (2 * chunk),)),
        ],
        compiler_params=PART,
        cost_estimate=pl.CostEstimate(flops=4 * rows * channels * padded, bytes_accessed=4 * rows * channels, transcendentals=0),
        name="feature_pull",
    )(taps, sums, weight)


def per_device(
    features, target, conv_weight, disc_first, disc_second, disc_third, disc_fourth, disc_head
):
    row = ("far", "near")
    devices = lax.axis_size(row)
    clips = lax.axis_size("clip")
    _, frames, block_rows, cols, channels = features.shape
    group = frames // devices
    pixels = clips * devices * frames * block_rows * cols
    lanes = up_to((block_rows + 2) * cols, LANES)
    pitch = up_to(3 * group + 2, 8)
    sizes = (frames, devices, group, cols, block_rows)
    feats = features.reshape(frames * block_rows * cols, channels)
    wanted = target[0].transpose(0, 2, 1, 3)
    payload, own, weight = forward_call(feats, wanted, conv_weight, frames, devices, group, cols, lanes, pitch)
    trade = lambda values: lax.all_to_all(
        values.reshape(devices, pitch, lanes), row, split_axis=0, concat_axis=0, tiled=True
    ).reshape(devices * pitch, lanes)
    arrived = trade(payload)
    inner = inner_call(own, wanted, frames, devices, group, block_rows, cols)
    arrived, inner = lax.optimization_barrier((arrived, inner))
    sent = disc_call(
        arrived, disc_first, disc_second, disc_third, disc_fourth, disc_head, devices, group, cols, block_rows
    )
    returned = trade(sent)
    taps_scratch = pltpu.VMEM((block_rows * cols // LANES, 32 * frames, LANES), F32)
    plane_scratch = pltpu.VMEM((lanes // LANES, devices * pitch, LANES), F32)
    flops = 4 * features.size * 27
    part, rec_plane = taps_call(
        both_kernel, [VM, VM, VM], (inner, returned, feats),
        (jax.ShapeDtypeStruct((clips * lax.axis_size("near"), 56, channels), BF16), jax.ShapeDtypeStruct(own.shape, F32)),
        [taps_scratch, taps_scratch, plane_scratch], *sizes, flops, "both_taps",
    )
    share = lambda values, axes: lax.all_to_all(values, axes, split_axis=0, concat_axis=0, tiled=True)
    sums = share(sum_call(share(part, ("clip", "near")), lax.axis_size("far")), "far")
    taps = taps_call(
        turn_kernel, [VM, VM], (rec_plane, returned), jax.ShapeDtypeStruct((feats.shape[0] // 2, LANES), BF16),
        [taps_scratch, taps_scratch, plane_scratch], *sizes, flops, "turn_taps",
    )
    image_back = returned.reshape(devices, pitch, lanes)[:, : 3 * group, cols : (block_rows + 1) * cols]
    image_back = image_back.reshape(devices, 3, group, block_rows, cols).transpose(0, 2, 3, 1, 4)
    image_back = image_back.reshape(1, frames, block_rows, 3, cols)
    feature_grad, weight_grad, adaptive = final_call(taps, sums, weight, pixels, block_rows * cols)
    return (feature_grad.reshape(features.shape), image_back, weight_grad, adaptive[0, 0])


def sum_kernel(parts_ref, out_ref):
    total = parts_ref[0].astype(F32)
    for i in range(1, parts_ref.shape[0]):
        total = total + parts_ref[i].astype(F32)
    total = total.astype(BF16)
    for i in range(out_ref.shape[0]):
        out_ref[i] = total


def sum_call(parts, copies):
    return pl.pallas_call(
        sum_kernel,
        out_shape=jax.ShapeDtypeStruct((copies,) + parts.shape[1:], BF16),
        in_specs=[VM],
        out_specs=VM,
        compiler_params=PART,
        name="sum_parts",
    )(parts)


def solution(mesh):
    clips, devices = mesh.shape["clip"], mesh.shape["row"]
    near = 2 if devices % 2 == 0 else 1
    split = jax.sharding.Mesh(mesh.devices.reshape(clips, devices // near, near), ("clip", "far", "near"))
    rows = P("clip", None, ("far", "near"), None, None)
    return jax.shard_map(
        per_device,
        mesh=split,
        in_specs=(rows, rows, P(), P(), P(), P(), P(), P()),
        out_specs=(rows, rows, P(), P()),
        check_vma=False,
    )
```

```python
import functools

import jax
import jax.numpy as jnp
import numpy as np
from jax import lax
from jax.experimental import pallas as pl
from jax.experimental.pallas import tpu as pltpu
from jax.sharding import PartitionSpec as P

loss_scale = 64.0
epsilon = 0.0001
F32 = jnp.float32
BF16 = jnp.bfloat16
LANES = 128
NN = (((1,), (0,)), ((), ()))
NT = (((1,), (1,)), ((), ()))
TN = (((0,), (0,)), ((), ()))
VM = pl.BlockSpec(memory_space=pltpu.VMEM)
HBM = pl.BlockSpec(memory_space=pl.ANY)
WHOLE = pltpu.CompilerParams(vmem_limit_bytes=60 * 2**20)
MOST = pltpu.CompilerParams(vmem_limit_bytes=119 * 2**19)
PART = pltpu.CompilerParams(vmem_limit_bytes=24 * 2**20)


def up_to(value, step):
    return -(-value // step) * step


def mat(left, right, dims=NN):
    return lax.dot_general(left, right, dims, preferred_element_type=F32)


def slot_of(frame, devices, group):
    return (frame % group) * devices + frame // group


def forward_kernel(
    feat_hbm, target_hbm, weight_hbm, pay_ref, feat_ref, target_ref, weight_ref, weight_scr, target_scr,
    taps_ref, out_ref, sems, *, frames, devices, group, cols, lanes, chunks,
):
    pixels = feat_ref.shape[0] // frames
    pieces = pixels // LANES
    pitch = out_ref.shape[1] // devices
    taps = weight_scr.shape[0]
    block_rows = pixels // cols
    copies = [
        pltpu.make_async_copy(weight_hbm, weight_ref, sems.at[frames]),
        pltpu.make_async_copy(target_hbm, target_ref, sems.at[frames + 1]),
    ]
    for slot in range(frames):
        rows = pl.ds((slot % devices * group + slot // devices) * pixels, pixels)
        copies.append(pltpu.make_async_copy(feat_hbm.at[rows, :], feat_ref.at[rows, :], sems.at[slot]))
    for copy in copies:
        copy.start()
    weight_scr[...] = jnp.zeros_like(weight_scr)
    out_ref[...] = jnp.zeros_like(out_ref)
    copies[0].wait()
    copies[1].wait()
    for a in range(3):
        for b in range(3):
            at = (a * 3 + b) * 3
            weight_scr[at : at + 3, :] = weight_ref[a, b].astype(F32)
    weight = weight_scr[...].astype(BF16)
    target_scr[:, 0:cols] = target_ref[...].reshape(target_scr.shape[0], cols).astype(F32)
    edges = []
    for y in (0, block_rows - 1):
        for o in range(3):
            for part in range(group):
                rows = pl.ds((part * 3 + o) * block_rows + y, devices, stride=group * 3 * block_rows)
                edges.append(target_scr[rows, :][:, 0:cols])
    edges.append(jnp.zeros((devices, lanes - len(edges) * cols), F32))
    edges = jnp.concatenate(edges, axis=1)
    for k in range(lanes // LANES):
        out_ref[k, pl.ds(3 * group, devices, stride=pitch), :] = edges[:, k * LANES : (k + 1) * LANES]
    column = lax.broadcasted_iota(jnp.int32, (devices, pixels), 1) % cols

    def finish(part):
        def tap(a, b, o):
            rows = pl.ds(((a * 3 + b) * 3 + o) * frames + part * devices, devices)
            return jnp.concatenate([taps_ref[k, rows, :] for k in range(pieces)], axis=1)

        for o in range(3):
            total = None
            for a in range(3):
                term = tap(a, 1, o)
                term = term + jnp.where(column == 0, 0.0, pltpu.roll(tap(a, 0, o), 1, 1))
                term = term + jnp.where(column == cols - 1, 0.0, pltpu.roll(tap(a, 2, o), pixels - 1, 1))
                term = jnp.concatenate([term, jnp.zeros((devices, lanes - pixels), F32)], axis=1)
                if a < 2:
                    term = pltpu.roll(term, (2 - a) * cols, 1)
                total = term if total is None else total + term
            for k in range(lanes // LANES):
                rows = pl.ds(o * group + part, devices, stride=pitch)
                out_ref[k, rows, :] = total[:, k * LANES : (k + 1) * LANES]

    step = frames // chunks
    done = 0
    for chunk in range(chunks):
        for slot in range(chunk * step, (chunk + 1) * step):
            copies[2 + slot].wait()
        for slot in range(chunk * step, (chunk + 1) * step):
            frame = slot % devices * group + slot // devices
            product = mat(weight, feat_ref[frame * pixels : (frame + 1) * pixels, :], NT)
            for k in range(pieces):
                taps_ref[k, pl.ds(slot, taps, stride=frames), :] = product[:, k * LANES : (k + 1) * LANES]
        while (done + 1) * devices <= chunk * step or (chunk == chunks - 1 and done < group):
            finish(done)
            done += 1
    for k in range(lanes // LANES):
        pay_ref[:, k * LANES : (k + 1) * LANES] = out_ref[k].astype(BF16)


def forward_call(features, target, weight, frames, devices, group, cols, lanes, pitch):
    pixels = features.shape[0] // frames
    channels = features.shape[1]
    chunks = 2
    return pl.pallas_call(
        functools.partial(
            forward_kernel, frames=frames, devices=devices, group=group, cols=cols, lanes=lanes, chunks=chunks
        ),
        out_shape=jax.ShapeDtypeStruct((devices * pitch, lanes), BF16),
        in_specs=[HBM, HBM, HBM],
        out_specs=VM,
        scratch_shapes=[
            pltpu.VMEM(features.shape, BF16),
            pltpu.VMEM(target.shape, BF16),
            pltpu.VMEM(weight.shape, BF16),
            pltpu.VMEM((32, channels), F32),
            pltpu.VMEM((3 * pixels // cols * frames, LANES), F32),
            pltpu.VMEM((pixels // LANES, 32 * frames, LANES), F32),
            pltpu.VMEM((lanes // LANES, devices * pitch, LANES), F32),
            pltpu.SemaphoreType.DMA((frames + 2,)),
        ],
        compiler_params=WHOLE,
        cost_estimate=pl.CostEstimate(flops=2 * features.size * 27, bytes_accessed=2 * features.size, transcendentals=0),
        name="forward_taps",
    )(features, target, weight)


def inner_kernel(pay_ref, target_ref, inner_ref, scr, zin, *, frames, devices, group, block_rows, cols):
    scr[:, 0:cols] = target_ref[...].reshape(scr.shape[0], cols).astype(F32)
    stride = group * 3 * block_rows
    lanes = pay_ref.shape[1]
    pitch = pay_ref.shape[0] // devices
    for k in range(lanes // LANES):
        zin[k] = pay_ref[:, k * LANES : (k + 1) * LANES].astype(F32)
    for o in range(3):
        for part in range(group):
            at = o * frames + part * devices
            rows = [jnp.zeros((devices, cols), F32)]
            rows += [
                scr[pl.ds((part * 3 + o) * block_rows + y, devices, stride=stride), :][:, 0:cols]
                for y in range(block_rows)
            ]
            rows.append(jnp.zeros((devices, lanes - (block_rows + 1) * cols), F32))
            wanted = jnp.concatenate(rows, axis=1)
            lane = lax.broadcasted_iota(jnp.int32, wanted.shape, 1)
            inside = (lane >= 2 * cols) & (lane < block_rows * cols)
            row = pl.ds(o * group + part, devices, stride=pitch)
            own = jnp.concatenate([zin[k, row, :] for k in range(lanes // LANES)], axis=1)
            inner_ref[at : at + devices, :] = loss_scale * (jnp.where(inside, own, 0.0) - wanted)


def inner_call(payload, target, frames, devices, group, block_rows, cols):
    lanes = payload.shape[1]
    return pl.pallas_call(
        functools.partial(
            inner_kernel, frames=frames, devices=devices, group=group, block_rows=block_rows, cols=cols
        ),
        out_shape=jax.ShapeDtypeStruct((3 * frames, lanes), F32),
        in_specs=[VM, VM],
        out_specs=VM,
        scratch_shapes=[
            pltpu.VMEM((frames * 3 * block_rows, LANES), F32),
            pltpu.VMEM((lanes // LANES, payload.shape[0], LANES), F32),
        ],
        compiler_params=PART,
        cost_estimate=pl.CostEstimate(flops=10**8, bytes_accessed=10**6, transcendentals=0),
        name="inner_rows",
    )(payload, target)


def shift_rows(values, step, period):
    size = values.shape[0]
    row = lax.broadcasted_iota(jnp.int32, values.shape, 0) % period
    rolled = pltpu.roll(values, step % size, 0)
    source = row - step
    return jnp.where((source >= 0) & (source < period), rolled, 0.0)


def gate_of(values):
    logistic = 0.5 + 0.5 * jnp.tanh(0.5 * values)
    return (values * logistic).astype(BF16), logistic * (1.0 + values * (1.0 - logistic))


def edge_planes(zin, zout, first, last, devices, group, cols, lanes, pitch):
    row = pl.ds(3 * group, devices, stride=pitch)
    target = jnp.concatenate([zin[k, row, :] for k in range(lanes // LANES)], axis=1)
    outer, inner = [], []
    for e, rows, other, move in ((0, first, last, 1), (1, last, first, -1)):
        for o in range(3):
            for part in range(group):
                at = ((1 - e) * 3 * group + o * group + part) * cols
                near = other[part][:, o * cols : (o + 1) * cols] - target[:, at : at + cols]
                outer.append(shift_rows(loss_scale * near, move, devices))
                inner.append(rows[part][:, o * cols : (o + 1) * cols])
    for i, pieces in enumerate((outer, inner)):
        pieces.append(jnp.zeros((devices, lanes - 6 * group * cols), F32))
        plane = jnp.concatenate(pieces, axis=1)
        for k in range(lanes // LANES):
            zout[k, pl.ds(3 * group + i, devices, stride=pitch), :] = plane[:, k * LANES : (k + 1) * LANES]


def disc_kernel(
    pay_ref, head_ref, window_hbm, band_hbm, second_hbm, third_hbm, fourth_hbm, unwindow_hbm, out_ref,
    zin, window, band_ref, second, third, fourth, unwindow, rows_in, act_one, slope_one, cols_two, act_two, slope_two, act_three, cols_four,
    pull_four, pull_three, pull_two, zout, sems, *, devices, group, cols, block_rows, period,
):
    lanes = pay_ref.shape[1]
    pitch = pay_ref.shape[0] // devices
    span = block_rows + 2
    unit = group * period
    wide = 3 * cols
    d1 = (act_one.shape[1]) // (cols // 2 + 2)
    d2, d3, d4 = second.shape[1], third.shape[1], fourth.shape[1]
    x1, x2, x3 = cols // 2, cols // 4, cols // 8
    x4 = x3 - 1
    pairs = (
        (window_hbm, window),
        (band_hbm, band_ref),
        (second_hbm, second),
        (third_hbm, third),
        (fourth_hbm, fourth),
        (unwindow_hbm, unwindow),
    )
    copies = [pltpu.make_async_copy(source, target, sems.at[i]) for i, (source, target) in enumerate(pairs)]
    for copy in copies:
        copy.start()
    cells = block_rows // 8
    spot = lambda y, part: pl.ds((y % 8 * group + part) * period + y // 8, devices, stride=cells)
    for k in range(lanes // LANES):
        zin[k] = pay_ref[:, k * LANES : (k + 1) * LANES].astype(F32)
    zout[...] = jnp.zeros_like(zout)
    firsts, lasts = [], []
    for part in range(group):
        planes = []
        for o in range(3):
            pieces = [zin[k, pl.ds(o * group + part, devices, stride=pitch), :] for k in range(lanes // LANES)]
            planes.append(jnp.concatenate(pieces, axis=1))
        lines = [
            jnp.concatenate(
                [plane[:, i * cols : (i + 1) * cols] for plane in planes]
                + [jnp.zeros((devices, 2 * LANES - wide), F32)],
                axis=1,
            )
            for i in range(span)
        ]
        lines[1] = lines[1] + shift_rows(lines[span - 1], 1, devices)
        lines[block_rows] = lines[block_rows] + shift_rows(lines[0], -1, devices)
        for y in range(block_rows):
            for k in range(2):
                rows_in[k, spot(y, part), :] = lines[y + 1][:, k * LANES : (k + 1) * LANES]
        firsts.append(lines[1])
        lasts.append(lines[block_rows])
    image = jnp.concatenate([rows_in[0], rows_in[1]], axis=1)[:, :wide].astype(BF16)
    copies[0].wait()
    copies[1].wait()
    wins = mat(image, window[...])
    ext = [wins[r * unit : (r + 1) * unit] for r in range(8)]
    ext = [shift_rows(ext[7], 1, period)] + ext + [shift_rows(ext[0], -1, period)]
    width_one = act_one.shape[1]
    strip = 8 * d1
    band = band_ref[...]
    for k in range(-(-width_one // strip)):
        low, high = slice(2 * k * LANES, (2 * k + 1) * LANES), slice((2 * k + 1) * LANES, (2 * k + 2) * LANES)
        left = jnp.concatenate(
            [
                jnp.concatenate([ext[2 * p + h][:, low] + ext[2 * p + h + 1][:, high] for p in range(4)], axis=0)
                for h in (0, 2)
            ],
            axis=1,
        ).astype(BF16)
        start, end = k * strip, min((k + 1) * strip, width_one)
        act, slope = gate_of(mat(left, band[:, : end - start]))
        if k == 0 or end == width_one:
            lane = start + lax.broadcasted_iota(jnp.int32, slope.shape, 1)
            inside = (lane >= d1) & (lane < width_one - d1)
            slope = jnp.where(inside, slope, 0.0)
            act = jnp.where(inside, act.astype(F32), 0.0).astype(BF16)
        slope_one[:, start:end] = slope
        act_one[unit : 5 * unit, start:end] = act
        actual = act.astype(F32)
        act_one[0:unit, start:end] = shift_rows(actual[3 * unit :], 1, period).astype(BF16)
        act_one[5 * unit :, start:end] = shift_rows(actual[:unit], -1, period).astype(BF16)
    copies[2].wait()
    for x in range(x2):
        for a in range(4):
            for p in range(2):
                cols_two[(x * 2 + p) * unit : (x * 2 + p + 1) * unit, a * 4 * d1 : (a + 1) * 4 * d1] = act_one[
                    (2 * p + a) * unit : (2 * p + a + 1) * unit, 2 * x * d1 : (2 * x + 4) * d1
                ]
    pre = mat(cols_two[...], second[...])
    act, slope = gate_of(pre)
    slope_two[...] = slope
    act_two[:, 0:d2] = jnp.zeros((4 * unit, d2), BF16)
    act_two[:, (x2 + 1) * d2 :] = jnp.zeros((4 * unit, d2), BF16)
    for x in range(x2):
        block = act[x * 2 * unit : (x + 1) * 2 * unit]
        actual = block.astype(F32)
        at = slice((x + 1) * d2, (x + 2) * d2)
        act_two[unit : 3 * unit, at] = block
        act_two[0:unit, at] = shift_rows(actual[unit:], 1, period).astype(BF16)
        act_two[3 * unit :, at] = shift_rows(actual[:unit], -1, period).astype(BF16)
    copies[3].wait()
    left = jnp.concatenate(
        [
            jnp.concatenate([act_two[a * unit : (a + 1) * unit, 2 * x * d2 : (2 * x + 4) * d2] for a in range(4)], axis=1)
            for x in range(x3)
        ],
        axis=0,
    )
    act, slope_three = gate_of(mat(left, third[...]))
    act_three[:, 0:d3] = jnp.zeros((4 * unit, d3), BF16)
    act_three[:, (x3 + 1) * d3 :] = jnp.zeros((4 * unit, d3), BF16)
    for x in range(x3):
        block = act[x * unit : (x + 1) * unit]
        actual = block.astype(F32)
        at = slice((x + 1) * d3, (x + 2) * d3)
        act_three[unit : 2 * unit, at] = block
        for a in (0, 2, 3):
            act_three[a * unit : (a + 1) * unit, at] = shift_rows(actual, 1 - a, period).astype(BF16)
    for x in range(x4):
        for a in range(4):
            cols_four[x * unit : (x + 1) * unit, a * 4 * d3 : (a + 1) * 4 * d3] = act_three[
                a * unit : (a + 1) * unit, x * d3 : (x + 4) * d3
            ]
    copies[4].wait()
    pre = mat(cols_four[...], fourth[...])
    edge_planes(zin, zout, firsts, lasts, devices, group, cols, lanes, pitch)
    _, slope = gate_of(pre)
    row = lax.broadcasted_iota(jnp.int32, (unit, d4), 0) % period
    head = head_ref[...].astype(F32) * -loss_scale
    heads = []
    for x in range(x4):
        total = None
        for a in range(4):
            taps = [head[a * 4 + b : a * 4 + b + 1, :] for b in range(4) if 0 <= x - b + 1 < x4 - 1]
            tap = functools.reduce(lambda u, v: u + v, taps)
            inside = (row - a + 1 >= 0) & (row - a + 1 < period - 2) & (row < period - 1)
            term = jnp.where(inside, jnp.broadcast_to(tap, (unit, d4)), 0.0)
            total = term if total is None else total + term
        heads.append(total)
    cot = (jnp.concatenate(heads, axis=0) * slope).astype(BF16)
    pull_four[...] = mat(cot, fourth[...], NT)
    cots = []
    for x in range(x3):
        total = None
        for a in range(4):
            term = None
            for b in range(4):
                source = x - b + 1
                if 0 <= source < x4:
                    piece = pull_four[source * unit : (source + 1) * unit, (a * 4 + b) * d3 : (a * 4 + b + 1) * d3]
                    term = piece if term is None else term + piece
            if a != 1:
                term = shift_rows(term, a - 1, period)
            total = term if total is None else total + term
        cots.append((total * slope_three[x * unit : (x + 1) * unit]).astype(BF16))
    pull_three[...] = mat(jnp.concatenate(cots, axis=0), third[...], NT)
    cots = []
    for x in range(x2):
        terms = []
        for a in range(4):
            term = None
            for b in range(4):
                if (x - b + 1) % 2 == 0 and 0 <= (x - b + 1) // 2 < x3:
                    source = (x - b + 1) // 2
                    piece = pull_three[source * unit : (source + 1) * unit, (a * 4 + b) * d2 : (a * 4 + b + 1) * d2]
                    term = piece if term is None else term + piece
            terms.append(term)
        even = terms[1] + shift_rows(terms[3], 1, period)
        odd = terms[2] + shift_rows(terms[0], -1, period)
        both = jnp.concatenate([even, odd], axis=0)
        cots.append((both * slope_two[x * 2 * unit : (x + 1) * 2 * unit]).astype(BF16))
    pull_two[...] = mat(jnp.concatenate(cots, axis=0), second[...], NT)
    strips = []
    for k in range(x2 + 1):
        terms = {}
        for p in range(2):
            for a in range(4):
                term = None
                if k < x2:
                    term = pull_two[(2 * k + p) * unit : (2 * k + p + 1) * unit, a * 4 * d1 : (a * 4 + 2) * d1]
                if k > 0:
                    other = pull_two[(2 * k - 2 + p) * unit : (2 * k - 1 + p) * unit, (a * 4 + 2) * d1 : (a + 1) * 4 * d1]
                    term = other if term is None else term + other
                terms[p, a] = term
        both = jnp.concatenate(
            [
                terms[0, 1] + shift_rows(terms[1, 3], 1, period),
                terms[0, 2] + terms[1, 0],
                terms[0, 3] + terms[1, 1],
                terms[1, 2] + shift_rows(terms[0, 0], -1, period),
            ],
            axis=0,
        )
        strips.append((both * slope_one[:, 2 * k * d1 : (2 * k + 2) * d1]).astype(BF16))
    cot = jnp.concatenate(strips, axis=1)
    copies[5].wait()
    sums = []
    for k in range(-(-width_one // strip)):
        start, end = k * strip, min((k + 1) * strip, width_one)
        pulls = mat(cot[:, start:end], band[:, : end - start], NT)
        groups = []
        for m in range(5):
            terms = [
                pulls[p * unit : (p + 1) * unit, (m - p) * LANES : (m - p + 1) * LANES] for p in range(4) if 0 <= m - p < 2
            ]
            groups.append(functools.reduce(lambda u, v: u + v, terms))
        sums.append(jnp.concatenate(groups, axis=0))
    sums = jnp.concatenate(sums, axis=1)
    upper = sums.astype(BF16)
    lower = (sums - upper.astype(F32)).astype(BF16)
    both = mat(upper, unwindow[...]) + mat(lower, unwindow[...])
    half = both.shape[1] // 2
    odd = [both[m * unit : (m + 1) * unit, 0:wide] for m in range(5)]
    even = [both[m * unit : (m + 1) * unit, half : half + wide] for m in range(5)]
    phases = [even[r // 2] if r % 2 == 0 else odd[(r + 1) // 2] for r in range(8)]
    phases[0] = phases[0] + shift_rows(even[4], 1, period)
    phases[7] = phases[7] + shift_rows(odd[0], -1, period)
    image = jnp.concatenate(phases, axis=0)
    image = jnp.concatenate([image, jnp.zeros((image.shape[0], 2 * LANES - wide), F32)], axis=1)
    for k in range(2):
        rows_in[k] = image[:, k * LANES : (k + 1) * LANES]
    for part in range(group):
        lines = [
            jnp.concatenate([rows_in[k, spot(y, part), :] for k in range(2)], axis=1)[:, :wide]
            for y in range(block_rows)
        ]
        lines = [shift_rows(lines[-1], 1, devices)] + lines + [shift_rows(lines[0], -1, devices)]
        for o in range(3):
            plane = [line[:, o * cols : (o + 1) * cols] for line in lines]
            plane.append(jnp.zeros((devices, lanes - span * cols), F32))
            plane = jnp.concatenate(plane, axis=1)
            for k in range(lanes // LANES):
                zout[k, pl.ds(o * group + part, devices, stride=pitch), :] = plane[:, k * LANES : (k + 1) * LANES]
    for k in range(lanes // LANES):
        out_ref[:, k * LANES : (k + 1) * LANES] = zout[k].astype(BF16)


def windows_of(cols, d1):
    wide = 3 * cols
    count = -(-(cols // 2 + 2) // 8)
    half = up_to(wide, LANES)
    window = np.zeros((wide, count * 2 * LANES), np.float32)
    unwindow = np.zeros((count * LANES, 2 * half), np.float32)
    for k in range(count):
        for c in range(3):
            for j in range(18):
                x = 16 * k - 3 + j
                if 0 <= x < cols:
                    for e in range(2):
                        at = e * LANES // 2 + c * 18 + j
                        window[c * cols + x, (2 * k + e) * LANES + at] = 1.0
                        unwindow[k * LANES + at, e * half + c * cols + x] = 1.0
    return window, unwindow


def band_of(first):
    d1 = first.shape[-1]
    tap = np.arange(18)[:, None] - 2 * (np.arange(8 * d1)[None, :] // d1)
    tiled = jnp.tile(first, (1, 1, 1, 8))
    band = jnp.zeros((4, 3, 18, 8 * d1), BF16)
    for b in range(4):
        band = jnp.where(jnp.asarray(tap == b), tiled[:, b, :, None, :], band)
    band = jnp.pad(band.reshape(4, 54, 8 * d1), ((0, 0), (0, LANES // 2 - 54), (0, 0)))
    return band.reshape(2 * LANES, 8 * d1)


def disc_call(payload, first, second, third, fourth, head, devices, group, cols, block_rows):
    period = devices * block_rows // 8
    unit = group * period
    d1, d2, d3, d4 = first.shape[-1], second.shape[-1], third.shape[-1], fourth.shape[-1]
    x2, x3 = cols // 4, cols // 8
    x4 = x3 - 1
    window, unwindow = windows_of(cols, d1)
    width_one = (cols // 2 + 2) * d1
    args = (
        payload,
        head.reshape(16, d4),
        jnp.asarray(window, BF16),
        band_of(first),
        second.reshape(16 * d1, d2),
        third.reshape(16 * d2, d3),
        fourth.reshape(16 * d3, d4),
        jnp.asarray(unwindow, BF16),
    )
    lanes = payload.shape[1]
    return pl.pallas_call(
        functools.partial(
            disc_kernel, devices=devices, group=group, cols=cols, block_rows=block_rows, period=period
        ),
        out_shape=jax.ShapeDtypeStruct(payload.shape, BF16),
        in_specs=[VM, VM] + [HBM] * 6,
        out_specs=VM,
        scratch_shapes=[
            pltpu.VMEM((lanes // LANES, payload.shape[0], LANES), F32),
            pltpu.VMEM(window.shape, BF16),
            pltpu.VMEM((2 * LANES, 8 * d1), BF16),
            pltpu.VMEM((16 * d1, d2), BF16),
            pltpu.VMEM((16 * d2, d3), BF16),
            pltpu.VMEM((16 * d3, d4), BF16),
            pltpu.VMEM(unwindow.shape, BF16),
            pltpu.VMEM((2, 8 * unit, LANES), F32),
            pltpu.VMEM((6 * unit, width_one), BF16),
            pltpu.VMEM((4 * unit, width_one), F32),
            pltpu.VMEM((x2 * 2 * unit, 16 * d1), BF16),
            pltpu.VMEM((4 * unit, (x2 + 2) * d2), BF16),
            pltpu.VMEM((x2 * 2 * unit, d2), F32),
            pltpu.VMEM((4 * unit, (x3 + 2) * d3), BF16),
            pltpu.VMEM((x4 * unit, 16 * d3), BF16),
            pltpu.VMEM((x4 * unit, 16 * d3), F32),
            pltpu.VMEM((x3 * unit, 16 * d2), F32),
            pltpu.VMEM((x2 * 2 * unit, 16 * d1), F32),
            pltpu.VMEM((lanes // LANES, payload.shape[0], LANES), F32),
            pltpu.SemaphoreType.DMA((6,)),
        ],
        compiler_params=MOST,
        cost_estimate=pl.CostEstimate(flops=4 * 10**9, bytes_accessed=8 * 10**6, transcendentals=10**6),
        name="disc_rows",
    )(*args)


def put_taps(plane, taps_ref, frames, cols, pieces, padded):
    lanes = plane.shape[1]
    column = lax.broadcasted_iota(jnp.int32, plane.shape, 1) % cols
    for b in range(3):
        moved = plane
        if b == 0:
            moved = jnp.where(column == cols - 1, 0.0, pltpu.roll(plane, lanes - 1, 1))
        if b == 2:
            moved = jnp.where(column == 0, 0.0, pltpu.roll(plane, 1, 1))
        for a in range(3):
            turned = moved if a == 2 else pltpu.roll(moved, lanes - (2 - a) * cols, 1)
            for k in range(pieces):
                taps_ref[k, pl.ds((a * 3 + b) * 3 * frames, 3 * frames), :] = turned[:, k * LANES : (k + 1) * LANES]
    for k in range(pieces):
        taps_ref[k, pl.ds(27 * frames, (padded - 27) * frames), :] = jnp.zeros(((padded - 27) * frames, LANES), F32)


def unpack(plane_ref, zin, devices, group):
    lanes = plane_ref.shape[1]
    pitch = plane_ref.shape[0] // devices
    for k in range(lanes // LANES):
        zin[k] = plane_ref[:, k * LANES : (k + 1) * LANES].astype(F32)
    blocks = []
    for o in range(3):
        for part in range(group):
            row = pl.ds(o * group + part, devices, stride=pitch)
            blocks.append(jnp.concatenate([zin[k, row, :] for k in range(lanes // LANES)], axis=1))
    return jnp.concatenate(blocks, axis=0)


def rec_rows(inner_ref, zin, devices, group, cols, block_rows):
    lanes = inner_ref.shape[1]
    pitch = zin.shape[1] // devices
    edges = []
    for i in range(2):
        row = pl.ds(3 * group + i, devices, stride=pitch)
        edges.append(jnp.concatenate([zin[k, row, :] for k in range(lanes // LANES)], axis=1))
    blocks = []
    for i, e in ((0, 0), (1, 0), (1, 1), (0, 1)):
        pieces = [
            edges[i][:, (e * 3 * group + at) * cols : (e * 3 * group + at + 1) * cols] for at in range(3 * group)
        ]
        blocks.append(jnp.concatenate(pieces, axis=0))
    none = lambda count: jnp.zeros((blocks[0].shape[0], count), F32)
    above, first, last, below = blocks
    rest = lanes - (block_rows + 2) * cols
    return inner_ref[...], jnp.concatenate(
        [above, first * loss_scale, none((block_rows - 2) * cols), last * loss_scale, below, none(rest)], axis=1
    )


def both_kernel(
    inner_ref, plane_ref, feat_ref, part_ref, rec_ref, rec_taps, gan_taps, zin, *, frames, devices, group, cols, block_rows
):
    pieces = block_rows * cols // LANES
    put_taps(unpack(plane_ref, zin, devices, group), gan_taps, frames, cols, pieces, 32)
    inner, edges = rec_rows(inner_ref, zin, devices, group, cols, block_rows)
    rec = inner + edges
    rec_ref[...] = rec
    put_taps(rec, rec_taps, frames, cols, pieces, 32)
    pixels = pieces * LANES
    total = jnp.zeros((64, feat_ref.shape[1]), F32)
    for frame in range(frames):
        rows = pl.ds(slot_of(frame, devices, group), 32, stride=frames)
        taps = jnp.concatenate(
            [
                jnp.concatenate([taps_ref[k, rows, :] for k in range(pieces)], axis=1)
                for taps_ref in (rec_taps, gan_taps)
            ],
            axis=0,
        )
        total = total + mat(taps.astype(BF16), feat_ref[frame * pixels : (frame + 1) * pixels, :])
    blank = jnp.zeros((part_ref.shape[1] - 54, total.shape[1]), F32)
    total = jnp.concatenate([total[0:27], total[32:59], blank], axis=0).astype(BF16)
    for i in range(part_ref.shape[0]):
        part_ref[i] = total


def turn_kernel(
    rec_ref, plane_ref, out_ref, rec_taps, gan_taps, zin, *, frames, devices, group, cols, block_rows
):
    pieces = block_rows * cols // LANES
    pixels = pieces * LANES
    put_taps(rec_ref[...], rec_taps, frames, cols, pieces, 32)
    put_taps(unpack(plane_ref, zin, devices, group), gan_taps, frames, cols, pieces, 32)
    for pair in range(frames // 2):
        for k in range(pieces):
            parts = []
            for frame in (2 * pair, 2 * pair + 1):
                rows = pl.ds(slot_of(frame, devices, group), 32, stride=frames)
                parts += [rec_taps[k, rows, :], gan_taps[k, rows, :]]
            at = pair * pixels + k * LANES
            out_ref[at : at + LANES, :] = jnp.concatenate(parts, axis=0).T.astype(BF16)


def taps_call(kernel, specs, operands, out, scratch, frames, devices, group, cols, block_rows, flops, name):
    return pl.pallas_call(
        functools.partial(kernel, frames=frames, devices=devices, group=group, cols=cols, block_rows=block_rows),
        out_shape=out,
        in_specs=specs,
        out_specs=jax.tree.map(lambda _: VM, out),
        scratch_shapes=scratch,
        compiler_params=PART,
        cost_estimate=pl.CostEstimate(flops=flops, bytes_accessed=4 * 10**6, transcendentals=0),
        name=name,
    )(*operands)


def final_kernel(
    taps_ref, sums_ref, weight_ref, out_hbm, grad_ref, adapt_ref, weight_scr, both_ref, out_ref, sems, *, pixels, chunk
):
    weight_scr[...] = jnp.zeros_like(weight_scr)
    for a in range(3):
        for b in range(3):
            at = (a * 3 + b) * 3
            weight_scr[at : at + 3, :] = weight_ref[a, b].astype(F32)
    total = sums_ref[0].astype(F32)
    for i in range(1, sums_ref.shape[0]):
        total = total + sums_ref[i].astype(F32)
    rec, gan = total[0:27], total[27:54]
    norm = lambda values: jnp.sqrt(jnp.sum(jnp.sum(values * values, axis=1, keepdims=True), axis=0, keepdims=True))
    adaptive = norm(rec) / (norm(gan) + epsilon)
    grad = (rec + adaptive * gan) / pixels
    for a in range(3):
        for b in range(3):
            at = (a * 3 + b) * 3
            grad_ref[a, b] = grad[at : at + 3, :]
    adapt_ref[...] = adaptive
    weight = weight_scr[...].astype(BF16)
    padded, channels = weight.shape
    scaled = (adaptive * weight.astype(F32)).astype(BF16)
    both_ref[...] = jnp.zeros_like(both_ref)
    both_ref[0:padded, 0:channels] = weight
    both_ref[padded : 2 * padded, 0:channels] = scaled
    both_ref[2 * padded : 3 * padded, channels:] = weight
    both_ref[3 * padded :, channels:] = scaled
    pairs = taps_ref.shape[0] // chunk
    stores = []
    for pair in range(pairs):
        product = mat(taps_ref[pair * chunk : (pair + 1) * chunk], both_ref[...]).astype(BF16)
        rows = pl.ds(2 * pair * chunk, 2 * chunk)
        out_ref[2 * pair * chunk : (2 * pair + 1) * chunk] = product[:, :channels]
        out_ref[(2 * pair + 1) * chunk : (2 * pair + 2) * chunk] = product[:, channels:]
        stores.append(pltpu.make_async_copy(out_ref.at[rows], out_hbm.at[rows], sems.at[pair]))
        stores[-1].start()
    for copy in stores:
        copy.wait()


def final_call(taps, sums, weight, pixels, chunk):
    padded, channels = 32, weight.shape[-1]
    rows = 2 * taps.shape[0]
    return pl.pallas_call(
        functools.partial(final_kernel, pixels=pixels, chunk=chunk),
        out_shape=(
            jax.ShapeDtypeStruct((rows, channels), BF16),
            jax.ShapeDtypeStruct((3, 3, 3, channels), F32),
            jax.ShapeDtypeStruct((1, 1), F32),
        ),
        in_specs=[VM] * 3,
        out_specs=(HBM, VM, VM),
        scratch_shapes=[
            pltpu.VMEM((padded, channels), F32),
            pltpu.VMEM((4 * padded, 2 * channels), BF16),
            pltpu.VMEM((rows, channels), BF16),
            pltpu.SemaphoreType.DMA((rows // (2 * chunk),)),
        ],
        compiler_params=PART,
        cost_estimate=pl.CostEstimate(flops=4 * rows * channels * padded, bytes_accessed=4 * rows * channels, transcendentals=0),
        name="feature_pull",
    )(taps, sums, weight)


def per_device(
    features, target, conv_weight, disc_first, disc_second, disc_third, disc_fourth, disc_head
):
    row = ("far", "near")
    devices = lax.axis_size(row)
    clips = lax.axis_size("clip")
    _, frames, block_rows, cols, channels = features.shape
    group = frames // devices
    pixels = clips * devices * frames * block_rows * cols
    lanes = up_to((block_rows + 2) * cols, LANES)
    pitch = up_to(3 * group + 2, 8)
    sizes = (frames, devices, group, cols, block_rows)
    feats = features.reshape(frames * block_rows * cols, channels)
    wanted = target[0].transpose(0, 2, 1, 3)
    payload = forward_call(feats, wanted, conv_weight, frames, devices, group, cols, lanes, pitch)
    trade = lambda values: lax.all_to_all(
        values.reshape(devices, pitch, lanes), row, split_axis=0, concat_axis=0, tiled=True
    ).reshape(devices * pitch, lanes)
    arrived = trade(payload)
    inner = inner_call(payload, wanted, frames, devices, group, block_rows, cols)
    arrived, inner = lax.optimization_barrier((arrived, inner))
    sent = disc_call(
        arrived, disc_first, disc_second, disc_third, disc_fourth, disc_head, devices, group, cols, block_rows
    )
    returned = trade(sent)
    taps_scratch = pltpu.VMEM((block_rows * cols // LANES, 32 * frames, LANES), F32)
    plane_scratch = pltpu.VMEM((lanes // LANES, devices * pitch, LANES), F32)
    flops = 4 * features.size * 27
    part, rec_plane = taps_call(
        both_kernel, [VM, VM, VM], (inner, returned, feats),
        (jax.ShapeDtypeStruct((clips * lax.axis_size("near"), 56, channels), BF16), jax.ShapeDtypeStruct(inner.shape, F32)),
        [taps_scratch, taps_scratch, plane_scratch], *sizes, flops, "both_taps",
    )
    share = lambda values, axes: lax.all_to_all(values, axes, split_axis=0, concat_axis=0, tiled=True)
    sums = share(sum_call(share(part, ("clip", "near")), lax.axis_size("far")), "far")
    taps = taps_call(
        turn_kernel, [VM, VM], (rec_plane, returned), jax.ShapeDtypeStruct((feats.shape[0] // 2, LANES), BF16),
        [taps_scratch, taps_scratch, plane_scratch], *sizes, flops, "turn_taps",
    )
    image_back = returned.reshape(devices, pitch, lanes)[:, : 3 * group, cols : (block_rows + 1) * cols]
    image_back = image_back.reshape(devices, 3, group, block_rows, cols).transpose(0, 2, 3, 1, 4)
    image_back = image_back.reshape(1, frames, block_rows, 3, cols)
    feature_grad, weight_grad, adaptive = final_call(taps, sums, conv_weight, pixels, block_rows * cols)
    return (feature_grad.reshape(features.shape), image_back, weight_grad, adaptive[0, 0])


def sum_kernel(parts_ref, out_ref):
    total = parts_ref[0].astype(F32)
    for i in range(1, parts_ref.shape[0]):
        total = total + parts_ref[i].astype(F32)
    total = total.astype(BF16)
    for i in range(out_ref.shape[0]):
        out_ref[i] = total


def sum_call(parts, copies):
    return pl.pallas_call(
        sum_kernel,
        out_shape=jax.ShapeDtypeStruct((copies,) + parts.shape[1:], BF16),
        in_specs=[VM],
        out_specs=VM,
        compiler_params=PART,
        name="sum_parts",
    )(parts)


def solution(mesh):
    clips, devices = mesh.shape["clip"], mesh.shape["row"]
    near = 2 if devices % 2 == 0 else 1
    split = jax.sharding.Mesh(mesh.devices.reshape(clips, devices // near, near), ("clip", "far", "near"))
    rows = P("clip", None, ("far", "near"), None, None)
    return jax.shard_map(
        per_device,
        mesh=split,
        in_specs=(rows, rows, P(), P(), P(), P(), P(), P()),
        out_specs=(rows, rows, P(), P()),
        check_vma=False,
    )
```

```python
import functools

import jax
import jax.numpy as jnp
import numpy as np
from jax import lax
from jax.experimental import pallas as pl
from jax.experimental.pallas import tpu as pltpu
from jax.sharding import PartitionSpec as P

loss_scale = 64.0
epsilon = 0.0001
F32 = jnp.float32
BF16 = jnp.bfloat16
LANES = 128
NN = (((1,), (0,)), ((), ()))
NT = (((1,), (1,)), ((), ()))
TN = (((0,), (0,)), ((), ()))
VM = pl.BlockSpec(memory_space=pltpu.VMEM)
HBM = pl.BlockSpec(memory_space=pl.ANY)
WHOLE = pltpu.CompilerParams(vmem_limit_bytes=60 * 2**20)
MOST = pltpu.CompilerParams(vmem_limit_bytes=115 * 2**19)
PART = pltpu.CompilerParams(vmem_limit_bytes=24 * 2**20)


def up_to(value, step):
    return -(-value // step) * step


def mat(left, right, dims=NN):
    return lax.dot_general(left, right, dims, preferred_element_type=F32)


def slot_of(frame, devices, group):
    return (frame % group) * devices + frame // group


def forward_kernel(
    feat_hbm, target_hbm, weight_hbm, pay_ref, feat_ref, target_ref, weight_ref, weight_scr, target_scr,
    taps_ref, out_ref, sems, *, frames, devices, group, cols, lanes, chunks,
):
    pixels = feat_ref.shape[0] // frames
    pieces = pixels // LANES
    pitch = out_ref.shape[1] // devices
    taps = weight_scr.shape[0]
    block_rows = pixels // cols
    copies = [
        pltpu.make_async_copy(weight_hbm, weight_ref, sems.at[frames]),
        pltpu.make_async_copy(target_hbm, target_ref, sems.at[frames + 1]),
    ]
    for slot in range(frames):
        rows = pl.ds((slot % devices * group + slot // devices) * pixels, pixels)
        copies.append(pltpu.make_async_copy(feat_hbm.at[rows, :], feat_ref.at[rows, :], sems.at[slot]))
    for copy in copies:
        copy.start()
    weight_scr[...] = jnp.zeros_like(weight_scr)
    out_ref[...] = jnp.zeros_like(out_ref)
    copies[0].wait()
    for a in range(3):
        for b in range(3):
            at = (a * 3 + b) * 3
            weight_scr[at : at + 3, :] = weight_ref[a, b].astype(F32)
    weight = weight_scr[...].astype(BF16)
    column = lax.broadcasted_iota(jnp.int32, (devices, pixels), 1) % cols

    def finish(part):
        def tap(a, b, o):
            rows = pl.ds(((a * 3 + b) * 3 + o) * frames + part * devices, devices)
            return jnp.concatenate([taps_ref[k, rows, :] for k in range(pieces)], axis=1)

        for o in range(3):
            total = None
            for a in range(3):
                term = tap(a, 1, o)
                term = term + jnp.where(column == 0, 0.0, pltpu.roll(tap(a, 0, o), 1, 1))
                term = term + jnp.where(column == cols - 1, 0.0, pltpu.roll(tap(a, 2, o), pixels - 1, 1))
                term = jnp.concatenate([term, jnp.zeros((devices, lanes - pixels), F32)], axis=1)
                if a < 2:
                    term = pltpu.roll(term, (2 - a) * cols, 1)
                total = term if total is None else total + term
            for k in range(lanes // LANES):
                rows = pl.ds(o * group + part, devices, stride=pitch)
                out_ref[k, rows, :] = total[:, k * LANES : (k + 1) * LANES]

    def edge_rows():
        target_scr[:, 0:cols] = target_ref[...].reshape(target_scr.shape[0], cols).astype(F32)
        edges = []
        for y in (0, block_rows - 1):
            for o in range(3):
                for part in range(group):
                    rows = pl.ds((part * 3 + o) * block_rows + y, devices, stride=group * 3 * block_rows)
                    edges.append(target_scr[rows, :][:, 0:cols])
        edges.append(jnp.zeros((devices, lanes - len(edges) * cols), F32))
        edges = jnp.concatenate(edges, axis=1)
        for k in range(lanes // LANES):
            out_ref[k, pl.ds(3 * group, devices, stride=pitch), :] = edges[:, k * LANES : (k + 1) * LANES]

    step = frames // chunks
    done = 0
    for chunk in range(chunks):
        for slot in range(chunk * step, (chunk + 1) * step):
            copies[2 + slot].wait()
        for slot in range(chunk * step, (chunk + 1) * step):
            frame = slot % devices * group + slot // devices
            product = mat(weight, feat_ref[frame * pixels : (frame + 1) * pixels, :], NT)
            for k in range(pieces):
                taps_ref[k, pl.ds(slot, taps, stride=frames), :] = product[:, k * LANES : (k + 1) * LANES]
        if chunk == 0:
            copies[1].wait()
            edge_rows()
        while (done + 1) * devices <= chunk * step or (chunk == chunks - 1 and done < group):
            finish(done)
            done += 1
    for k in range(lanes // LANES):
        pay_ref[:, k * LANES : (k + 1) * LANES] = out_ref[k].astype(BF16)


def forward_call(features, target, weight, frames, devices, group, cols, lanes, pitch):
    pixels = features.shape[0] // frames
    channels = features.shape[1]
    chunks = 2
    return pl.pallas_call(
        functools.partial(
            forward_kernel, frames=frames, devices=devices, group=group, cols=cols, lanes=lanes, chunks=chunks
        ),
        out_shape=jax.ShapeDtypeStruct((devices * pitch, lanes), BF16),
        in_specs=[HBM, HBM, HBM],
        out_specs=VM,
        scratch_shapes=[
            pltpu.VMEM(features.shape, BF16),
            pltpu.VMEM(target.shape, BF16),
            pltpu.VMEM(weight.shape, BF16),
            pltpu.VMEM((32, channels), F32),
            pltpu.VMEM((3 * pixels // cols * frames, LANES), F32),
            pltpu.VMEM((pixels // LANES, 32 * frames, LANES), F32),
            pltpu.VMEM((lanes // LANES, devices * pitch, LANES), F32),
            pltpu.SemaphoreType.DMA((frames + 2,)),
        ],
        compiler_params=WHOLE,
        cost_estimate=pl.CostEstimate(flops=2 * features.size * 27, bytes_accessed=2 * features.size, transcendentals=0),
        name="forward_taps",
    )(features, target, weight)


def inner_kernel(pay_ref, target_ref, inner_ref, scr, zin, *, frames, devices, group, block_rows, cols):
    scr[:, 0:cols] = target_ref[...].reshape(scr.shape[0], cols).astype(F32)
    stride = group * 3 * block_rows
    lanes = pay_ref.shape[1]
    pitch = pay_ref.shape[0] // devices
    for k in range(lanes // LANES):
        zin[k] = pay_ref[:, k * LANES : (k + 1) * LANES].astype(F32)
    for o in range(3):
        for part in range(group):
            at = o * frames + part * devices
            rows = [jnp.zeros((devices, cols), F32)]
            rows += [
                scr[pl.ds((part * 3 + o) * block_rows + y, devices, stride=stride), :][:, 0:cols]
                for y in range(block_rows)
            ]
            rows.append(jnp.zeros((devices, lanes - (block_rows + 1) * cols), F32))
            wanted = jnp.concatenate(rows, axis=1)
            lane = lax.broadcasted_iota(jnp.int32, wanted.shape, 1)
            inside = (lane >= 2 * cols) & (lane < block_rows * cols)
            row = pl.ds(o * group + part, devices, stride=pitch)
            own = jnp.concatenate([zin[k, row, :] for k in range(lanes // LANES)], axis=1)
            inner_ref[at : at + devices, :] = loss_scale * (jnp.where(inside, own, 0.0) - wanted)


def inner_call(payload, target, frames, devices, group, block_rows, cols):
    lanes = payload.shape[1]
    return pl.pallas_call(
        functools.partial(
            inner_kernel, frames=frames, devices=devices, group=group, block_rows=block_rows, cols=cols
        ),
        out_shape=jax.ShapeDtypeStruct((3 * frames, lanes), F32),
        in_specs=[VM, VM],
        out_specs=VM,
        scratch_shapes=[
            pltpu.VMEM((frames * 3 * block_rows, LANES), F32),
            pltpu.VMEM((lanes // LANES, payload.shape[0], LANES), F32),
        ],
        compiler_params=PART,
        cost_estimate=pl.CostEstimate(flops=10**8, bytes_accessed=10**6, transcendentals=0),
        name="inner_rows",
    )(payload, target)


def shift_rows(values, step, period):
    size = values.shape[0]
    row = lax.broadcasted_iota(jnp.int32, values.shape, 0) % period
    rolled = pltpu.roll(values, step % size, 0)
    source = row - step
    return jnp.where((source >= 0) & (source < period), rolled, 0.0)


def gate_of(values):
    logistic = 0.5 + 0.5 * jnp.tanh(0.5 * values)
    return (values * logistic).astype(BF16), logistic * (1.0 + values * (1.0 - logistic))


def edge_planes(zin, zout, first, last, devices, group, cols, lanes, pitch):
    row = pl.ds(3 * group, devices, stride=pitch)
    target = jnp.concatenate([zin[k, row, :] for k in range(lanes // LANES)], axis=1)
    outer, inner = [], []
    for e, rows, other, move in ((0, first, last, 1), (1, last, first, -1)):
        for o in range(3):
            for part in range(group):
                at = ((1 - e) * 3 * group + o * group + part) * cols
                near = other[part][:, o * cols : (o + 1) * cols] - target[:, at : at + cols]
                outer.append(shift_rows(loss_scale * near, move, devices))
                inner.append(rows[part][:, o * cols : (o + 1) * cols])
    for i, pieces in enumerate((outer, inner)):
        pieces.append(jnp.zeros((devices, lanes - 6 * group * cols), F32))
        plane = jnp.concatenate(pieces, axis=1)
        for k in range(lanes // LANES):
            zout[k, pl.ds(3 * group + i, devices, stride=pitch), :] = plane[:, k * LANES : (k + 1) * LANES]


def disc_kernel(
    pay_ref, head_ref, window, band_ref, second, third, unwindow, fourth_hbm, out_ref,
    zin, fourth, rows_in, act_one, slope_one, cols_two, act_two, slope_two, act_three, cols_four,
    pull_four, pull_three, pull_two, zout, sems, *, devices, group, cols, block_rows, period,
):
    lanes = pay_ref.shape[1]
    pitch = pay_ref.shape[0] // devices
    span = block_rows + 2
    unit = group * period
    wide = 3 * cols
    d1 = (act_one.shape[1]) // (cols // 2 + 2)
    d2, d3, d4 = second.shape[1], third.shape[1], fourth.shape[1]
    x1, x2, x3 = cols // 2, cols // 4, cols // 8
    x4 = x3 - 1
    quarter = fourth.shape[0] // 4
    copies = [
        pltpu.make_async_copy(
            fourth_hbm.at[pl.ds(a * quarter, quarter), :], fourth.at[pl.ds(a * quarter, quarter), :], sems.at[a]
        )
        for a in range(4)
    ]
    for copy in copies:
        copy.start()
    cells = block_rows // 8
    spot = lambda y, part: pl.ds((y % 8 * group + part) * period + y // 8, devices, stride=cells)
    for k in range(lanes // LANES):
        zin[k] = pay_ref[:, k * LANES : (k + 1) * LANES].astype(F32)
    zout[...] = jnp.zeros_like(zout)
    firsts, lasts = [], []
    for part in range(group):
        planes = []
        for o in range(3):
            pieces = [zin[k, pl.ds(o * group + part, devices, stride=pitch), :] for k in range(lanes // LANES)]
            planes.append(jnp.concatenate(pieces, axis=1))
        lines = [
            jnp.concatenate(
                [plane[:, i * cols : (i + 1) * cols] for plane in planes]
                + [jnp.zeros((devices, 2 * LANES - wide), F32)],
                axis=1,
            )
            for i in range(span)
        ]
        lines[1] = lines[1] + shift_rows(lines[span - 1], 1, devices)
        lines[block_rows] = lines[block_rows] + shift_rows(lines[0], -1, devices)
        for y in range(block_rows):
            for k in range(2):
                rows_in[k, spot(y, part), :] = lines[y + 1][:, k * LANES : (k + 1) * LANES]
        firsts.append(lines[1])
        lasts.append(lines[block_rows])
    image = jnp.concatenate([rows_in[0], rows_in[1]], axis=1)[:, :wide].astype(BF16)
    wins = mat(image, window[...])
    ext = [wins[r * unit : (r + 1) * unit] for r in range(8)]
    ext = [shift_rows(ext[7], 1, period)] + ext + [shift_rows(ext[0], -1, period)]
    width_one = act_one.shape[1]
    strip = 8 * d1
    band = band_ref[...]
    for k in range(-(-width_one // strip)):
        low, high = slice(2 * k * LANES, (2 * k + 1) * LANES), slice((2 * k + 1) * LANES, (2 * k + 2) * LANES)
        left = jnp.concatenate(
            [
                jnp.concatenate([ext[2 * p + h][:, low] + ext[2 * p + h + 1][:, high] for p in range(4)], axis=0)
                for h in (0, 2)
            ],
            axis=1,
        ).astype(BF16)
        start, end = k * strip, min((k + 1) * strip, width_one)
        act, slope = gate_of(mat(left, band[:, : end - start]))
        if k == 0 or end == width_one:
            lane = start + lax.broadcasted_iota(jnp.int32, slope.shape, 1)
            inside = (lane >= d1) & (lane < width_one - d1)
            slope = jnp.where(inside, slope, 0.0)
            act = jnp.where(inside, act.astype(F32), 0.0).astype(BF16)
        slope_one[:, start:end] = slope
        act_one[unit : 5 * unit, start:end] = act
        actual = act.astype(F32)
        act_one[0:unit, start:end] = shift_rows(actual[3 * unit :], 1, period).astype(BF16)
        act_one[5 * unit :, start:end] = shift_rows(actual[:unit], -1, period).astype(BF16)
    for x in range(x2):
        for a in range(4):
            for p in range(2):
                cols_two[(x * 2 + p) * unit : (x * 2 + p + 1) * unit, a * 4 * d1 : (a + 1) * 4 * d1] = act_one[
                    (2 * p + a) * unit : (2 * p + a + 1) * unit, 2 * x * d1 : (2 * x + 4) * d1
                ]
    pre = mat(cols_two[...], second[...])
    act, slope = gate_of(pre)
    slope_two[...] = slope
    act_two[:, 0:d2] = jnp.zeros((4 * unit, d2), BF16)
    act_two[:, (x2 + 1) * d2 :] = jnp.zeros((4 * unit, d2), BF16)
    for x in range(x2):
        block = act[x * 2 * unit : (x + 1) * 2 * unit]
        actual = block.astype(F32)
        at = slice((x + 1) * d2, (x + 2) * d2)
        act_two[unit : 3 * unit, at] = block
        act_two[0:unit, at] = shift_rows(actual[unit:], 1, period).astype(BF16)
        act_two[3 * unit :, at] = shift_rows(actual[:unit], -1, period).astype(BF16)
    left = jnp.concatenate(
        [
            jnp.concatenate([act_two[a * unit : (a + 1) * unit, 2 * x * d2 : (2 * x + 4) * d2] for a in range(4)], axis=1)
            for x in range(x3)
        ],
        axis=0,
    )
    act, slope_three = gate_of(mat(left, third[...]))
    act_three[:, 0:d3] = jnp.zeros((4 * unit, d3), BF16)
    act_three[:, (x3 + 1) * d3 :] = jnp.zeros((4 * unit, d3), BF16)
    for x in range(x3):
        block = act[x * unit : (x + 1) * unit]
        actual = block.astype(F32)
        at = slice((x + 1) * d3, (x + 2) * d3)
        act_three[unit : 2 * unit, at] = block
        for a in (0, 2, 3):
            act_three[a * unit : (a + 1) * unit, at] = shift_rows(actual, 1 - a, period).astype(BF16)
    for x in range(x4):
        for a in range(4):
            cols_four[x * unit : (x + 1) * unit, a * 4 * d3 : (a + 1) * 4 * d3] = act_three[
                a * unit : (a + 1) * unit, x * d3 : (x + 4) * d3
            ]
    edge_planes(zin, zout, firsts, lasts, devices, group, cols, lanes, pitch)
    pre = None
    for a in range(4):
        copies[a].wait()
        term = mat(cols_four[:, a * quarter : (a + 1) * quarter], fourth[a * quarter : (a + 1) * quarter, :])
        pre = term if pre is None else pre + term
    _, slope = gate_of(pre)
    row = lax.broadcasted_iota(jnp.int32, (unit, d4), 0) % period
    head = head_ref[...].astype(F32) * -loss_scale
    heads = []
    for x in range(x4):
        total = None
        for a in range(4):
            taps = [head[a * 4 + b : a * 4 + b + 1, :] for b in range(4) if 0 <= x - b + 1 < x4 - 1]
            tap = functools.reduce(lambda u, v: u + v, taps)
            inside = (row - a + 1 >= 0) & (row - a + 1 < period - 2) & (row < period - 1)
            term = jnp.where(inside, jnp.broadcast_to(tap, (unit, d4)), 0.0)
            total = term if total is None else total + term
        heads.append(total)
    cot = (jnp.concatenate(heads, axis=0) * slope).astype(BF16)
    pull_four[...] = mat(cot, fourth[...], NT)
    cots = []
    for x in range(x3):
        total = None
        for a in range(4):
            term = None
            for b in range(4):
                source = x - b + 1
                if 0 <= source < x4:
                    piece = pull_four[source * unit : (source + 1) * unit, (a * 4 + b) * d3 : (a * 4 + b + 1) * d3]
                    term = piece if term is None else term + piece
            if a != 1:
                term = shift_rows(term, a - 1, period)
            total = term if total is None else total + term
        cots.append((total * slope_three[x * unit : (x + 1) * unit]).astype(BF16))
    pull_three[...] = mat(jnp.concatenate(cots, axis=0), third[...], NT)
    cots = []
    for x in range(x2):
        terms = []
        for a in range(4):
            term = None
            for b in range(4):
                if (x - b + 1) % 2 == 0 and 0 <= (x - b + 1) // 2 < x3:
                    source = (x - b + 1) // 2
                    piece = pull_three[source * unit : (source + 1) * unit, (a * 4 + b) * d2 : (a * 4 + b + 1) * d2]
                    term = piece if term is None else term + piece
            terms.append(term)
        even = terms[1] + shift_rows(terms[3], 1, period)
        odd = terms[2] + shift_rows(terms[0], -1, period)
        both = jnp.concatenate([even, odd], axis=0)
        cots.append((both * slope_two[x * 2 * unit : (x + 1) * 2 * unit]).astype(BF16))
    pull_two[...] = mat(jnp.concatenate(cots, axis=0), second[...], NT)
    strips = []
    for k in range(x2 + 1):
        terms = {}
        for p in range(2):
            for a in range(4):
                term = None
                if k < x2:
                    term = pull_two[(2 * k + p) * unit : (2 * k + p + 1) * unit, a * 4 * d1 : (a * 4 + 2) * d1]
                if k > 0:
                    other = pull_two[(2 * k - 2 + p) * unit : (2 * k - 1 + p) * unit, (a * 4 + 2) * d1 : (a + 1) * 4 * d1]
                    term = other if term is None else term + other
                terms[p, a] = term
        both = jnp.concatenate(
            [
                terms[0, 1] + shift_rows(terms[1, 3], 1, period),
                terms[0, 2] + terms[1, 0],
                terms[0, 3] + terms[1, 1],
                terms[1, 2] + shift_rows(terms[0, 0], -1, period),
            ],
            axis=0,
        )
        strips.append((both * slope_one[:, 2 * k * d1 : (2 * k + 2) * d1]).astype(BF16))
    cot = jnp.concatenate(strips, axis=1)
    sums = []
    for k in range(-(-width_one // strip)):
        start, end = k * strip, min((k + 1) * strip, width_one)
        pulls = mat(cot[:, start:end], band[:, : end - start], NT)
        groups = []
        for m in range(5):
            terms = [
                pulls[p * unit : (p + 1) * unit, (m - p) * LANES : (m - p + 1) * LANES] for p in range(4) if 0 <= m - p < 2
            ]
            groups.append(functools.reduce(lambda u, v: u + v, terms))
        sums.append(jnp.concatenate(groups, axis=0))
    sums = jnp.concatenate(sums, axis=1)
    upper = sums.astype(BF16)
    lower = (sums - upper.astype(F32)).astype(BF16)
    low = lax.broadcasted_iota(jnp.int32, upper.shape, 1) % LANES < LANES // 2
    blank = jnp.zeros_like(upper)
    split = [jnp.where(low, upper, blank), jnp.where(low, lower, blank), jnp.where(low, blank, upper), jnp.where(low, blank, lower)]
    both = mat(jnp.concatenate(split, axis=0), unwindow[...])
    size = 5 * unit
    odd = both[:size] + both[size : 2 * size]
    even = both[2 * size : 3 * size] + both[3 * size :]
    odd = [odd[m * unit : (m + 1) * unit, :] for m in range(5)]
    even = [even[m * unit : (m + 1) * unit, :] for m in range(5)]
    phases = [even[r // 2] if r % 2 == 0 else odd[(r + 1) // 2] for r in range(8)]
    phases[0] = phases[0] + shift_rows(even[4], 1, period)
    phases[7] = phases[7] + shift_rows(odd[0], -1, period)
    image = jnp.concatenate(phases, axis=0)
    image = jnp.concatenate([image, jnp.zeros((image.shape[0], 2 * LANES - wide), F32)], axis=1)
    for k in range(2):
        rows_in[k] = image[:, k * LANES : (k + 1) * LANES]
    for part in range(group):
        lines = [
            jnp.concatenate([rows_in[k, spot(y, part), :] for k in range(2)], axis=1)[:, :wide]
            for y in range(block_rows)
        ]
        lines = [shift_rows(lines[-1], 1, devices)] + lines + [shift_rows(lines[0], -1, devices)]
        for o in range(3):
            plane = [line[:, o * cols : (o + 1) * cols] for line in lines]
            plane.append(jnp.zeros((devices, lanes - span * cols), F32))
            plane = jnp.concatenate(plane, axis=1)
            for k in range(lanes // LANES):
                zout[k, pl.ds(o * group + part, devices, stride=pitch), :] = plane[:, k * LANES : (k + 1) * LANES]
    for k in range(lanes // LANES):
        out_ref[:, k * LANES : (k + 1) * LANES] = zout[k].astype(BF16)


def windows_of(cols, d1):
    wide = 3 * cols
    count = -(-(cols // 2 + 2) // 8)
    window = np.zeros((wide, count * 2 * LANES), np.float32)
    unwindow = np.zeros((count * LANES, wide), np.float32)
    for k in range(count):
        for c in range(3):
            for j in range(18):
                x = 16 * k - 3 + j
                if 0 <= x < cols:
                    for e in range(2):
                        at = e * LANES // 2 + c * 18 + j
                        window[c * cols + x, (2 * k + e) * LANES + at] = 1.0
                        unwindow[k * LANES + at, c * cols + x] = 1.0
    return window, unwindow


def stage_kernel(
    first_ref, window_hbm, unwindow_hbm, second_hbm, third_hbm, window, unwindow, second, third, band, scr, sems
):
    pairs = ((window_hbm, window), (second_hbm, second), (third_hbm, third), (unwindow_hbm, unwindow))
    copies = [pltpu.make_async_copy(source, target, sems.at[i]) for i, (source, target) in enumerate(pairs)]
    for copy in copies:
        copy.start()
    d1 = first_ref.shape[-1]
    scr[...] = jnp.zeros_like(scr)
    row = lax.broadcasted_iota(jnp.int32, (18, 8 * d1), 0)
    tap = row - 2 * (lax.broadcasted_iota(jnp.int32, (18, 8 * d1), 1) // d1)
    for a in range(4):
        lines = [first_ref[a, b].astype(F32) for b in range(4)]
        for c in range(3):
            block = jnp.zeros((18, 8 * d1), F32)
            for b in range(4):
                line = jnp.concatenate([lines[b][c : c + 1, :]] * 8, axis=1)
                block = jnp.where(tap == b, jnp.broadcast_to(line, block.shape), block)
            at = a * LANES // 2 + c * 18
            scr[at : at + 18, :] = block
    band[...] = scr[...].astype(BF16)
    for copy in copies:
        copy.wait()


def stage_call(first, second, third, cols):
    d1, d2, d3 = first.shape[-1], second.shape[-1], third.shape[-1]
    window, unwindow = windows_of(cols, d1)
    operands = (
        first,
        jnp.asarray(window, BF16),
        jnp.asarray(unwindow, BF16),
        second.reshape(16 * d1, d2),
        third.reshape(16 * d2, d3),
    )
    shapes = [value.shape for value in operands[1:]] + [(2 * LANES, 8 * d1)]
    return pl.pallas_call(
        stage_kernel,
        out_shape=tuple(jax.ShapeDtypeStruct(shape, BF16) for shape in shapes),
        in_specs=[VM] + [HBM] * 4,
        out_specs=(VM,) * 5,
        scratch_shapes=[pltpu.VMEM((2 * LANES, 8 * d1), F32), pltpu.SemaphoreType.DMA((4,))],
        compiler_params=PART,
        cost_estimate=pl.CostEstimate(flops=10**8, bytes_accessed=4 * 10**6, transcendentals=0),
        name="stage_weights",
    )(*operands)


def disc_call(payload, staged, fourth, head, devices, group, cols, block_rows):
    period = devices * block_rows // 8
    unit = group * period
    window, unwindow, second, third, band = staged
    d1, d2, d3, d4 = band.shape[1] // 8, second.shape[1], third.shape[1], fourth.shape[-1]
    x2, x3 = cols // 4, cols // 8
    x4 = x3 - 1
    width_one = (cols // 2 + 2) * d1
    args = (
        payload,
        head.reshape(16, d4),
        window,
        band,
        second,
        third,
        unwindow,
        fourth.reshape(16 * d3, d4),
    )
    lanes = payload.shape[1]
    return pl.pallas_call(
        functools.partial(
            disc_kernel, devices=devices, group=group, cols=cols, block_rows=block_rows, period=period
        ),
        out_shape=jax.ShapeDtypeStruct(payload.shape, BF16),
        in_specs=[VM] * 7 + [HBM],
        out_specs=VM,
        scratch_shapes=[
            pltpu.VMEM((lanes // LANES, payload.shape[0], LANES), F32),
            pltpu.VMEM((16 * d3, d4), BF16),
            pltpu.VMEM((2, 8 * unit, LANES), F32),
            pltpu.VMEM((6 * unit, width_one), BF16),
            pltpu.VMEM((4 * unit, width_one), F32),
            pltpu.VMEM((x2 * 2 * unit, 16 * d1), BF16),
            pltpu.VMEM((4 * unit, (x2 + 2) * d2), BF16),
            pltpu.VMEM((x2 * 2 * unit, d2), F32),
            pltpu.VMEM((4 * unit, (x3 + 2) * d3), BF16),
            pltpu.VMEM((x4 * unit, 16 * d3), BF16),
            pltpu.VMEM((x4 * unit, 16 * d3), F32),
            pltpu.VMEM((x3 * unit, 16 * d2), F32),
            pltpu.VMEM((x2 * 2 * unit, 16 * d1), F32),
            pltpu.VMEM((lanes // LANES, payload.shape[0], LANES), F32),
            pltpu.SemaphoreType.DMA((4,)),
        ],
        compiler_params=MOST,
        cost_estimate=pl.CostEstimate(flops=4 * 10**9, bytes_accessed=8 * 10**6, transcendentals=10**6),
        name="disc_rows",
    )(*args)


def put_taps(plane, taps_ref, frames, cols, pieces, padded):
    lanes = plane.shape[1]
    column = lax.broadcasted_iota(jnp.int32, plane.shape, 1) % cols
    for b in range(3):
        moved = plane
        if b == 0:
            moved = jnp.where(column == cols - 1, 0.0, pltpu.roll(plane, lanes - 1, 1))
        if b == 2:
            moved = jnp.where(column == 0, 0.0, pltpu.roll(plane, 1, 1))
        for a in range(3):
            turned = moved if a == 2 else pltpu.roll(moved, lanes - (2 - a) * cols, 1)
            for k in range(pieces):
                taps_ref[k, pl.ds((a * 3 + b) * 3 * frames, 3 * frames), :] = turned[:, k * LANES : (k + 1) * LANES]
    for k in range(pieces):
        taps_ref[k, pl.ds(27 * frames, (padded - 27) * frames), :] = jnp.zeros(((padded - 27) * frames, LANES), F32)


def unpack(plane_ref, zin, devices, group):
    lanes = plane_ref.shape[1]
    pitch = plane_ref.shape[0] // devices
    for k in range(lanes // LANES):
        zin[k] = plane_ref[:, k * LANES : (k + 1) * LANES].astype(F32)
    blocks = []
    for o in range(3):
        for part in range(group):
            row = pl.ds(o * group + part, devices, stride=pitch)
            blocks.append(jnp.concatenate([zin[k, row, :] for k in range(lanes // LANES)], axis=1))
    return jnp.concatenate(blocks, axis=0)


def rec_rows(inner_ref, zin, devices, group, cols, block_rows):
    lanes = inner_ref.shape[1]
    pitch = zin.shape[1] // devices
    edges = []
    for i in range(2):
        row = pl.ds(3 * group + i, devices, stride=pitch)
        edges.append(jnp.concatenate([zin[k, row, :] for k in range(lanes // LANES)], axis=1))
    blocks = []
    for i, e in ((0, 0), (1, 0), (1, 1), (0, 1)):
        pieces = [
            edges[i][:, (e * 3 * group + at) * cols : (e * 3 * group + at + 1) * cols] for at in range(3 * group)
        ]
        blocks.append(jnp.concatenate(pieces, axis=0))
    none = lambda count: jnp.zeros((blocks[0].shape[0], count), F32)
    above, first, last, below = blocks
    rest = lanes - (block_rows + 2) * cols
    return inner_ref[...], jnp.concatenate(
        [above, first * loss_scale, none((block_rows - 2) * cols), last * loss_scale, below, none(rest)], axis=1
    )


def both_kernel(
    inner_ref, plane_ref, feat_ref, part_ref, rec_taps, gan_taps, zin, *, frames, devices, group, cols, block_rows
):
    pieces = block_rows * cols // LANES
    put_taps(unpack(plane_ref, zin, devices, group), gan_taps, frames, cols, pieces, 32)
    inner, edges = rec_rows(inner_ref, zin, devices, group, cols, block_rows)
    put_taps(inner + edges, rec_taps, frames, cols, pieces, 32)
    pixels = pieces * LANES
    total = jnp.zeros((64, feat_ref.shape[1]), F32)
    for frame in range(frames):
        rows = pl.ds(slot_of(frame, devices, group), 32, stride=frames)
        taps = jnp.concatenate(
            [
                jnp.concatenate([taps_ref[k, rows, :] for k in range(pieces)], axis=1)
                for taps_ref in (rec_taps, gan_taps)
            ],
            axis=0,
        )
        total = total + mat(taps.astype(BF16), feat_ref[frame * pixels : (frame + 1) * pixels, :])
    blank = jnp.zeros((part_ref.shape[1] - 54, total.shape[1]), F32)
    total = jnp.concatenate([total[0:27], total[32:59], blank], axis=0).astype(BF16)
    for i in range(part_ref.shape[0]):
        part_ref[i] = total


def turn_kernel(
    inner_ref, plane_ref, out_ref, rec_taps, gan_taps, zin, *, frames, devices, group, cols, block_rows
):
    pieces = block_rows * cols // LANES
    pixels = pieces * LANES
    put_taps(unpack(plane_ref, zin, devices, group), gan_taps, frames, cols, pieces, 32)
    inner, edges = rec_rows(inner_ref, zin, devices, group, cols, block_rows)
    put_taps(inner + edges, rec_taps, frames, cols, pieces, 32)
    for pair in range(frames // 2):
        for k in range(pieces):
            parts = []
            for frame in (2 * pair, 2 * pair + 1):
                rows = pl.ds(slot_of(frame, devices, group), 32, stride=frames)
                parts += [rec_taps[k, rows, :], gan_taps[k, rows, :]]
            at = pair * pixels + k * LANES
            out_ref[at : at + LANES, :] = jnp.concatenate(parts, axis=0).T.astype(BF16)


def taps_call(kernel, specs, operands, out, scratch, frames, devices, group, cols, block_rows, flops, name):
    return pl.pallas_call(
        functools.partial(kernel, frames=frames, devices=devices, group=group, cols=cols, block_rows=block_rows),
        out_shape=out,
        in_specs=specs,
        out_specs=jax.tree.map(lambda _: VM, out),
        scratch_shapes=scratch,
        compiler_params=PART,
        cost_estimate=pl.CostEstimate(flops=flops, bytes_accessed=4 * 10**6, transcendentals=0),
        name=name,
    )(*operands)


def final_kernel(
    taps_ref, sums_ref, weight_ref, out_hbm, grad_ref, adapt_ref, weight_scr, both_ref, out_ref, sems, *, pixels, chunk
):
    weight_scr[...] = jnp.zeros_like(weight_scr)
    for a in range(3):
        for b in range(3):
            at = (a * 3 + b) * 3
            weight_scr[at : at + 3, :] = weight_ref[a, b].astype(F32)
    total = sums_ref[0].astype(F32)
    for i in range(1, sums_ref.shape[0]):
        total = total + sums_ref[i].astype(F32)
    rec, gan = total[0:27], total[27:54]
    norm = lambda values: jnp.sqrt(jnp.sum(jnp.sum(values * values, axis=1, keepdims=True), axis=0, keepdims=True))
    adaptive = norm(rec) / (norm(gan) + epsilon)
    grad = (rec + adaptive * gan) / pixels
    for a in range(3):
        for b in range(3):
            at = (a * 3 + b) * 3
            grad_ref[a, b] = grad[at : at + 3, :]
    adapt_ref[...] = adaptive
    weight = weight_scr[...].astype(BF16)
    padded, channels = weight.shape
    scaled = (adaptive * weight.astype(F32)).astype(BF16)
    both_ref[...] = jnp.zeros_like(both_ref)
    both_ref[0:padded, 0:channels] = weight
    both_ref[padded : 2 * padded, 0:channels] = scaled
    both_ref[2 * padded : 3 * padded, channels:] = weight
    both_ref[3 * padded :, channels:] = scaled
    pairs = taps_ref.shape[0] // chunk
    stores = []
    for pair in range(pairs):
        product = mat(taps_ref[pair * chunk : (pair + 1) * chunk], both_ref[...]).astype(BF16)
        rows = pl.ds(2 * pair * chunk, 2 * chunk)
        out_ref[2 * pair * chunk : (2 * pair + 1) * chunk] = product[:, :channels]
        out_ref[(2 * pair + 1) * chunk : (2 * pair + 2) * chunk] = product[:, channels:]
        stores.append(pltpu.make_async_copy(out_ref.at[rows], out_hbm.at[rows], sems.at[pair]))
        stores[-1].start()
    for copy in stores:
        copy.wait()


def final_call(taps, sums, weight, pixels, chunk):
    padded, channels = 32, weight.shape[-1]
    rows = 2 * taps.shape[0]
    return pl.pallas_call(
        functools.partial(final_kernel, pixels=pixels, chunk=chunk),
        out_shape=(
            jax.ShapeDtypeStruct((rows, channels), BF16),
            jax.ShapeDtypeStruct((3, 3, 3, channels), F32),
            jax.ShapeDtypeStruct((1, 1), F32),
        ),
        in_specs=[VM] * 3,
        out_specs=(HBM, VM, VM),
        scratch_shapes=[
            pltpu.VMEM((padded, channels), F32),
            pltpu.VMEM((4 * padded, 2 * channels), BF16),
            pltpu.VMEM((rows, channels), BF16),
            pltpu.SemaphoreType.DMA((rows // (2 * chunk),)),
        ],
        compiler_params=PART,
        cost_estimate=pl.CostEstimate(flops=4 * rows * channels * padded, bytes_accessed=4 * rows * channels, transcendentals=0),
        name="feature_pull",
    )(taps, sums, weight)


def per_device(
    features, target, conv_weight, disc_first, disc_second, disc_third, disc_fourth, disc_head
):
    row = ("far", "near")
    devices = lax.axis_size(row)
    clips = lax.axis_size("clip")
    _, frames, block_rows, cols, channels = features.shape
    group = frames // devices
    pixels = clips * devices * frames * block_rows * cols
    lanes = up_to((block_rows + 2) * cols, LANES)
    pitch = up_to(3 * group + 2, 8)
    sizes = (frames, devices, group, cols, block_rows)
    feats = features.reshape(frames * block_rows * cols, channels)
    wanted = target[0].transpose(0, 2, 1, 3)
    payload = forward_call(feats, wanted, conv_weight, frames, devices, group, cols, lanes, pitch)
    trade = lambda values: lax.all_to_all(
        values.reshape(devices, pitch, lanes), row, split_axis=0, concat_axis=0, tiled=True
    ).reshape(devices * pitch, lanes)
    arrived = trade(payload)
    inner = inner_call(payload, wanted, frames, devices, group, block_rows, cols)
    _, disc_first = lax.optimization_barrier((payload, disc_first))
    staged = stage_call(disc_first, disc_second, disc_third, cols)
    arrived, inner = lax.optimization_barrier((arrived, inner))
    sent = disc_call(arrived, staged, disc_fourth, disc_head, devices, group, cols, block_rows)
    returned = trade(sent)
    taps_scratch = pltpu.VMEM((block_rows * cols // LANES, 32 * frames, LANES), F32)
    plane_scratch = pltpu.VMEM((lanes // LANES, devices * pitch, LANES), F32)
    flops = 4 * features.size * 27
    part = taps_call(
        both_kernel, [VM, VM, VM], (inner, returned, feats),
        jax.ShapeDtypeStruct((clips * lax.axis_size("near"), 56, channels), BF16),
        [taps_scratch, taps_scratch, plane_scratch], *sizes, flops, "both_taps",
    )
    share = lambda values, axes: lax.all_to_all(values, axes, split_axis=0, concat_axis=0, tiled=True)
    sums = share(sum_call(share(part, ("clip", "near")), lax.axis_size("far")), "far")
    taps = taps_call(
        turn_kernel, [VM, VM], (inner, returned), jax.ShapeDtypeStruct((feats.shape[0] // 2, LANES), BF16),
        [taps_scratch, taps_scratch, plane_scratch], *sizes, flops, "turn_taps",
    )
    image_back = returned.reshape(devices, pitch, lanes)[:, : 3 * group, cols : (block_rows + 1) * cols]
    image_back = image_back.reshape(devices, 3, group, block_rows, cols).transpose(0, 2, 3, 1, 4)
    image_back = image_back.reshape(1, frames, block_rows, 3, cols)
    feature_grad, weight_grad, adaptive = final_call(taps, sums, conv_weight, pixels, block_rows * cols)
    return (feature_grad.reshape(features.shape), image_back, weight_grad, adaptive[0, 0])


def sum_kernel(parts_ref, out_ref):
    total = parts_ref[0].astype(F32)
    for i in range(1, parts_ref.shape[0]):
        total = total + parts_ref[i].astype(F32)
    total = total.astype(BF16)
    for i in range(out_ref.shape[0]):
        out_ref[i] = total


def sum_call(parts, copies):
    return pl.pallas_call(
        sum_kernel,
        out_shape=jax.ShapeDtypeStruct((copies,) + parts.shape[1:], BF16),
        in_specs=[VM],
        out_specs=VM,
        compiler_params=PART,
        name="sum_parts",
    )(parts)


def solution(mesh):
    clips, devices = mesh.shape["clip"], mesh.shape["row"]
    near = 2 if devices % 2 == 0 else 1
    split = jax.sharding.Mesh(mesh.devices.reshape(clips, devices // near, near), ("clip", "far", "near"))
    rows = P("clip", None, ("far", "near"), None, None)
    return jax.shard_map(
        per_device,
        mesh=split,
        in_specs=(rows, rows, P(), P(), P(), P(), P(), P()),
        out_specs=(rows, rows, P(), P()),
        check_vma=False,
    )
```

```python
import functools

import jax
import jax.numpy as jnp
import numpy as np
from jax import lax
from jax.experimental import pallas as pl
from jax.experimental.pallas import tpu as pltpu
from jax.sharding import PartitionSpec as P

loss_scale = 64.0
epsilon = 0.0001
F32 = jnp.float32
BF16 = jnp.bfloat16
LANES = 128
NN = (((1,), (0,)), ((), ()))
NT = (((1,), (1,)), ((), ()))
TN = (((0,), (0,)), ((), ()))
VM = pl.BlockSpec(memory_space=pltpu.VMEM)
HBM = pl.BlockSpec(memory_space=pl.ANY)
WHOLE = pltpu.CompilerParams(vmem_limit_bytes=60 * 2**20)
MOST = pltpu.CompilerParams(vmem_limit_bytes=48 * 2**20)
PART = pltpu.CompilerParams(vmem_limit_bytes=24 * 2**20)


def up_to(value, step):
    return -(-value // step) * step


def mat(left, right, dims=NN):
    return lax.dot_general(left, right, dims, preferred_element_type=F32)


def slot_of(frame, devices, group):
    return (frame % group) * devices + frame // group


def forward_kernel(
    feat_hbm, target_hbm, weight_hbm, pay_ref, feat_ref, target_ref, weight_ref, weight_scr, target_scr,
    taps_ref, out_ref, sems, *, frames, devices, group, cols, lanes, chunks,
):
    pixels = feat_ref.shape[0] // frames
    pieces = pixels // LANES
    pitch = out_ref.shape[1] // devices
    taps = weight_scr.shape[0]
    block_rows = pixels // cols
    copies = [
        pltpu.make_async_copy(weight_hbm, weight_ref, sems.at[frames]),
        pltpu.make_async_copy(target_hbm, target_ref, sems.at[frames + 1]),
    ]
    for slot in range(frames):
        rows = pl.ds((slot % devices * group + slot // devices) * pixels, pixels)
        copies.append(pltpu.make_async_copy(feat_hbm.at[rows, :], feat_ref.at[rows, :], sems.at[slot]))
    for copy in copies:
        copy.start()
    weight_scr[...] = jnp.zeros_like(weight_scr)
    out_ref[...] = jnp.zeros_like(out_ref)
    copies[0].wait()
    for a in range(3):
        for b in range(3):
            at = (a * 3 + b) * 3
            weight_scr[at : at + 3, :] = weight_ref[a, b].astype(F32)
    weight = weight_scr[...].astype(BF16)
    column = lax.broadcasted_iota(jnp.int32, (devices, pixels), 1) % cols

    def finish(part):
        def tap(a, b, o):
            rows = pl.ds(((a * 3 + b) * 3 + o) * frames + part * devices, devices)
            return jnp.concatenate([taps_ref[k, rows, :] for k in range(pieces)], axis=1)

        for o in range(3):
            total = None
            for a in range(3):
                term = tap(a, 1, o)
                term = term + jnp.where(column == 0, 0.0, pltpu.roll(tap(a, 0, o), 1, 1))
                term = term + jnp.where(column == cols - 1, 0.0, pltpu.roll(tap(a, 2, o), pixels - 1, 1))
                term = jnp.concatenate([term, jnp.zeros((devices, lanes - pixels), F32)], axis=1)
                if a < 2:
                    term = pltpu.roll(term, (2 - a) * cols, 1)
                total = term if total is None else total + term
            for k in range(lanes // LANES):
                rows = pl.ds(o * group + part, devices, stride=pitch)
                out_ref[k, rows, :] = total[:, k * LANES : (k + 1) * LANES]

    def edge_rows():
        target_scr[:, 0:cols] = target_ref[...].reshape(target_scr.shape[0], cols).astype(F32)
        edges = []
        for y in (0, block_rows - 1):
            for o in range(3):
                for part in range(group):
                    rows = pl.ds((part * 3 + o) * block_rows + y, devices, stride=group * 3 * block_rows)
                    edges.append(target_scr[rows, :][:, 0:cols])
        edges.append(jnp.zeros((devices, lanes - len(edges) * cols), F32))
        edges = jnp.concatenate(edges, axis=1)
        for k in range(lanes // LANES):
            out_ref[k, pl.ds(3 * group, devices, stride=pitch), :] = edges[:, k * LANES : (k + 1) * LANES]

    copies[1].wait()
    edge_rows()
    step = frames // chunks
    done = 0
    for chunk in range(chunks):
        for slot in range(chunk * step, (chunk + 1) * step):
            copies[2 + slot].wait()
        for slot in range(chunk * step, (chunk + 1) * step):
            frame = slot % devices * group + slot // devices
            product = mat(weight, feat_ref[frame * pixels : (frame + 1) * pixels, :], NT)
            for k in range(pieces):
                taps_ref[k, pl.ds(slot, taps, stride=frames), :] = product[:, k * LANES : (k + 1) * LANES]
        while (done + 1) * devices <= chunk * step or (chunk == chunks - 1 and done < group):
            finish(done)
            done += 1
    for k in range(lanes // LANES):
        pay_ref[:, k * LANES : (k + 1) * LANES] = out_ref[k].astype(BF16)


def forward_call(features, target, weight, frames, devices, group, cols, lanes, pitch):
    pixels = features.shape[0] // frames
    channels = features.shape[1]
    chunks = 2
    return pl.pallas_call(
        functools.partial(
            forward_kernel, frames=frames, devices=devices, group=group, cols=cols, lanes=lanes, chunks=chunks
        ),
        out_shape=jax.ShapeDtypeStruct((devices * pitch, lanes), BF16),
        in_specs=[HBM, HBM, HBM],
        out_specs=VM,
        scratch_shapes=[
            pltpu.VMEM(features.shape, BF16),
            pltpu.VMEM(target.shape, BF16),
            pltpu.VMEM(weight.shape, BF16),
            pltpu.VMEM((32, channels), F32),
            pltpu.VMEM((3 * pixels // cols * frames, LANES), F32),
            pltpu.VMEM((pixels // LANES, 32 * frames, LANES), F32),
            pltpu.VMEM((lanes // LANES, devices * pitch, LANES), F32),
            pltpu.SemaphoreType.DMA((frames + 2,)),
        ],
        compiler_params=WHOLE,
        cost_estimate=pl.CostEstimate(flops=2 * features.size * 27, bytes_accessed=2 * features.size, transcendentals=0),
        name="forward_taps",
    )(features, target, weight)


def inner_kernel(pay_ref, target_ref, inner_ref, scr, zin, *, frames, devices, group, block_rows, cols):
    scr[:, 0:cols] = target_ref[...].reshape(scr.shape[0], cols).astype(F32)
    stride = group * 3 * block_rows
    lanes = pay_ref.shape[1]
    pitch = pay_ref.shape[0] // devices
    for k in range(lanes // LANES):
        zin[k] = pay_ref[:, k * LANES : (k + 1) * LANES].astype(F32)
    for o in range(3):
        for part in range(group):
            at = o * frames + part * devices
            rows = [jnp.zeros((devices, cols), F32)]
            rows += [
                scr[pl.ds((part * 3 + o) * block_rows + y, devices, stride=stride), :][:, 0:cols]
                for y in range(block_rows)
            ]
            rows.append(jnp.zeros((devices, lanes - (block_rows + 1) * cols), F32))
            wanted = jnp.concatenate(rows, axis=1)
            lane = lax.broadcasted_iota(jnp.int32, wanted.shape, 1)
            inside = (lane >= 2 * cols) & (lane < block_rows * cols)
            row = pl.ds(o * group + part, devices, stride=pitch)
            own = jnp.concatenate([zin[k, row, :] for k in range(lanes // LANES)], axis=1)
            inner_ref[at : at + devices, :] = loss_scale * (jnp.where(inside, own, 0.0) - wanted)


def inner_call(payload, target, frames, devices, group, block_rows, cols):
    lanes = payload.shape[1]
    return pl.pallas_call(
        functools.partial(
            inner_kernel, frames=frames, devices=devices, group=group, block_rows=block_rows, cols=cols
        ),
        out_shape=jax.ShapeDtypeStruct((3 * frames, lanes), F32),
        in_specs=[VM, VM],
        out_specs=VM,
        scratch_shapes=[
            pltpu.VMEM((frames * 3 * block_rows, LANES), F32),
            pltpu.VMEM((lanes // LANES, payload.shape[0], LANES), F32),
        ],
        compiler_params=PART,
        cost_estimate=pl.CostEstimate(flops=10**8, bytes_accessed=10**6, transcendentals=0),
        name="inner_rows",
    )(payload, target)


def shift_rows(values, step, period):
    size = values.shape[0]
    row = lax.broadcasted_iota(jnp.int32, values.shape, 0) % period
    rolled = pltpu.roll(values, step % size, 0)
    source = row - step
    return jnp.where((source >= 0) & (source < period), rolled, 0.0)


def gate_of(values):
    logistic = 0.5 + 0.5 * jnp.tanh(0.5 * values)
    return (values * logistic).astype(BF16), logistic * (1.0 + values * (1.0 - logistic))


def edge_planes(zin, zout, first, last, devices, group, cols, lanes, pitch):
    row = pl.ds(3 * group, devices, stride=pitch)
    target = jnp.concatenate([zin[k, row, :] for k in range(lanes // LANES)], axis=1)
    outer, inner = [], []
    for e, rows, other, move in ((0, first, last, 1), (1, last, first, -1)):
        for o in range(3):
            for part in range(group):
                at = ((1 - e) * 3 * group + o * group + part) * cols
                near = other[part][:, o * cols : (o + 1) * cols] - target[:, at : at + cols]
                outer.append(shift_rows(loss_scale * near, move, devices))
                inner.append(rows[part][:, o * cols : (o + 1) * cols])
    for i, pieces in enumerate((outer, inner)):
        pieces.append(jnp.zeros((devices, lanes - 6 * group * cols), F32))
        plane = jnp.concatenate(pieces, axis=1)
        for k in range(lanes // LANES):
            zout[k, pl.ds(3 * group + i, devices, stride=pitch), :] = plane[:, k * LANES : (k + 1) * LANES]


def disc_kernel(
    pay_ref, head_ref, window, band_ref, second, third, unwindow, fourth_hbm, out_ref,
    zin, fourth, rows_in, act_one, slope_one, cols_two, act_two, slope_two, act_three, cols_four,
    pull_four, pull_three, pull_two, zout, sems, *, devices, group, cols, block_rows, period,
):
    lanes = pay_ref.shape[1]
    pitch = pay_ref.shape[0] // devices
    span = block_rows + 2
    unit = group * period
    wide = 3 * cols
    d1 = (act_one.shape[1]) // (cols // 2 + 2)
    d2, d3, d4 = second.shape[1], third.shape[1], fourth.shape[1]
    x1, x2, x3 = cols // 2, cols // 4, cols // 8
    x4 = x3 - 1
    quarter = fourth.shape[0] // 4
    copies = [
        pltpu.make_async_copy(
            fourth_hbm.at[pl.ds(a * quarter, quarter), :], fourth.at[pl.ds(a * quarter, quarter), :], sems.at[a]
        )
        for a in range(4)
    ]
    for copy in copies:
        copy.start()
    cells = block_rows // 8
    spot = lambda y, part: pl.ds((y % 8 * group + part) * period + y // 8, devices, stride=cells)
    for k in range(lanes // LANES):
        zin[k] = pay_ref[:, k * LANES : (k + 1) * LANES].astype(F32)
    zout[...] = jnp.zeros_like(zout)
    firsts, lasts = [], []
    for part in range(group):
        planes = []
        for o in range(3):
            pieces = [zin[k, pl.ds(o * group + part, devices, stride=pitch), :] for k in range(lanes // LANES)]
            planes.append(jnp.concatenate(pieces, axis=1))
        lines = [
            jnp.concatenate(
                [plane[:, i * cols : (i + 1) * cols] for plane in planes]
                + [jnp.zeros((devices, 2 * LANES - wide), F32)],
                axis=1,
            )
            for i in range(span)
        ]
        lines[1] = lines[1] + shift_rows(lines[span - 1], 1, devices)
        lines[block_rows] = lines[block_rows] + shift_rows(lines[0], -1, devices)
        for y in range(block_rows):
            for k in range(2):
                rows_in[k, spot(y, part), :] = lines[y + 1][:, k * LANES : (k + 1) * LANES]
        firsts.append(lines[1])
        lasts.append(lines[block_rows])
    image = jnp.concatenate([rows_in[0], rows_in[1]], axis=1)[:, :wide].astype(BF16)
    wins = mat(image, window[...])
    ext = [wins[r * unit : (r + 1) * unit] for r in range(8)]
    ext = [shift_rows(ext[7], 1, period)] + ext + [shift_rows(ext[0], -1, period)]
    width_one = act_one.shape[1]
    strip = 8 * d1
    band = band_ref[...]
    for k in range(-(-width_one // strip)):
        low, high = slice(2 * k * LANES, (2 * k + 1) * LANES), slice((2 * k + 1) * LANES, (2 * k + 2) * LANES)
        left = jnp.concatenate(
            [
                jnp.concatenate([ext[2 * p + h][:, low] + ext[2 * p + h + 1][:, high] for p in range(4)], axis=0)
                for h in (0, 2)
            ],
            axis=1,
        ).astype(BF16)
        start, end = k * strip, min((k + 1) * strip, width_one)
        act, slope = gate_of(mat(left, band[:, : end - start]))
        if k == 0 or end == width_one:
            lane = start + lax.broadcasted_iota(jnp.int32, slope.shape, 1)
            inside = (lane >= d1) & (lane < width_one - d1)
            slope = jnp.where(inside, slope, 0.0)
            act = jnp.where(inside, act.astype(F32), 0.0).astype(BF16)
        slope_one[:, start:end] = slope
        act_one[unit : 5 * unit, start:end] = act
        actual = act.astype(F32)
        act_one[0:unit, start:end] = shift_rows(actual[3 * unit :], 1, period).astype(BF16)
        act_one[5 * unit :, start:end] = shift_rows(actual[:unit], -1, period).astype(BF16)
    for x in range(x2):
        for a in range(4):
            for p in range(2):
                cols_two[(x * 2 + p) * unit : (x * 2 + p + 1) * unit, a * 4 * d1 : (a + 1) * 4 * d1] = act_one[
                    (2 * p + a) * unit : (2 * p + a + 1) * unit, 2 * x * d1 : (2 * x + 4) * d1
                ]
    pre = mat(cols_two[...], second[...])
    act, slope = gate_of(pre)
    slope_two[...] = slope
    act_two[:, 0:d2] = jnp.zeros((4 * unit, d2), BF16)
    act_two[:, (x2 + 1) * d2 :] = jnp.zeros((4 * unit, d2), BF16)
    for x in range(x2):
        block = act[x * 2 * unit : (x + 1) * 2 * unit]
        actual = block.astype(F32)
        at = slice((x + 1) * d2, (x + 2) * d2)
        act_two[unit : 3 * unit, at] = block
        act_two[0:unit, at] = shift_rows(actual[unit:], 1, period).astype(BF16)
        act_two[3 * unit :, at] = shift_rows(actual[:unit], -1, period).astype(BF16)
    left = jnp.concatenate(
        [
            jnp.concatenate([act_two[a * unit : (a + 1) * unit, 2 * x * d2 : (2 * x + 4) * d2] for a in range(4)], axis=1)
            for x in range(x3)
        ],
        axis=0,
    )
    act, slope_three = gate_of(mat(left, third[...]))
    act_three[:, 0:d3] = jnp.zeros((4 * unit, d3), BF16)
    act_three[:, (x3 + 1) * d3 :] = jnp.zeros((4 * unit, d3), BF16)
    for x in range(x3):
        block = act[x * unit : (x + 1) * unit]
        actual = block.astype(F32)
        at = slice((x + 1) * d3, (x + 2) * d3)
        act_three[unit : 2 * unit, at] = block
        for a in (0, 2, 3):
            act_three[a * unit : (a + 1) * unit, at] = shift_rows(actual, 1 - a, period).astype(BF16)
    for x in range(x4):
        for a in range(4):
            cols_four[x * unit : (x + 1) * unit, a * 4 * d3 : (a + 1) * 4 * d3] = act_three[
                a * unit : (a + 1) * unit, x * d3 : (x + 4) * d3
            ]
    edge_planes(zin, zout, firsts, lasts, devices, group, cols, lanes, pitch)
    pre = None
    for a in range(4):
        copies[a].wait()
        term = mat(cols_four[:, a * quarter : (a + 1) * quarter], fourth[a * quarter : (a + 1) * quarter, :])
        pre = term if pre is None else pre + term
    _, slope = gate_of(pre)
    row = lax.broadcasted_iota(jnp.int32, (unit, d4), 0) % period
    head = head_ref[...].astype(F32) * -loss_scale
    heads = []
    for x in range(x4):
        total = None
        for a in range(4):
            taps = [head[a * 4 + b : a * 4 + b + 1, :] for b in range(4) if 0 <= x - b + 1 < x4 - 1]
            tap = functools.reduce(lambda u, v: u + v, taps)
            inside = (row - a + 1 >= 0) & (row - a + 1 < period - 2) & (row < period - 1)
            term = jnp.where(inside, jnp.broadcast_to(tap, (unit, d4)), 0.0)
            total = term if total is None else total + term
        heads.append(total)
    cot = (jnp.concatenate(heads, axis=0) * slope).astype(BF16)
    pull_four[...] = mat(cot, fourth[...], NT)
    cots = []
    for x in range(x3):
        total = None
        for a in range(4):
            term = None
            for b in range(4):
                source = x - b + 1
                if 0 <= source < x4:
                    piece = pull_four[source * unit : (source + 1) * unit, (a * 4 + b) * d3 : (a * 4 + b + 1) * d3]
                    term = piece if term is None else term + piece
            if a != 1:
                term = shift_rows(term, a - 1, period)
            total = term if total is None else total + term
        cots.append((total * slope_three[x * unit : (x + 1) * unit]).astype(BF16))
    pull_three[...] = mat(jnp.concatenate(cots, axis=0), third[...], NT)
    cots = []
    for x in range(x2):
        terms = []
        for a in range(4):
            term = None
            for b in range(4):
                if (x - b + 1) % 2 == 0 and 0 <= (x - b + 1) // 2 < x3:
                    source = (x - b + 1) // 2
                    piece = pull_three[source * unit : (source + 1) * unit, (a * 4 + b) * d2 : (a * 4 + b + 1) * d2]
                    term = piece if term is None else term + piece
            terms.append(term)
        even = terms[1] + shift_rows(terms[3], 1, period)
        odd = terms[2] + shift_rows(terms[0], -1, period)
        both = jnp.concatenate([even, odd], axis=0)
        cots.append((both * slope_two[x * 2 * unit : (x + 1) * 2 * unit]).astype(BF16))
    pull_two[...] = mat(jnp.concatenate(cots, axis=0), second[...], NT)
    strips = []
    for k in range(x2 + 1):
        terms = {}
        for p in range(2):
            for a in range(4):
                term = None
                if k < x2:
                    term = pull_two[(2 * k + p) * unit : (2 * k + p + 1) * unit, a * 4 * d1 : (a * 4 + 2) * d1]
                if k > 0:
                    other = pull_two[(2 * k - 2 + p) * unit : (2 * k - 1 + p) * unit, (a * 4 + 2) * d1 : (a + 1) * 4 * d1]
                    term = other if term is None else term + other
                terms[p, a] = term
        both = jnp.concatenate(
            [
                terms[0, 1] + shift_rows(terms[1, 3], 1, period),
                terms[0, 2] + terms[1, 0],
                terms[0, 3] + terms[1, 1],
                terms[1, 2] + shift_rows(terms[0, 0], -1, period),
            ],
            axis=0,
        )
        strips.append((both * slope_one[:, 2 * k * d1 : (2 * k + 2) * d1]).astype(BF16))
    cot = jnp.concatenate(strips, axis=1)
    sums = []
    for k in range(-(-width_one // strip)):
        start, end = k * strip, min((k + 1) * strip, width_one)
        pulls = mat(cot[:, start:end], band[:, : end - start], NT)
        groups = []
        for m in range(5):
            terms = [
                pulls[p * unit : (p + 1) * unit, (m - p) * LANES : (m - p + 1) * LANES] for p in range(4) if 0 <= m - p < 2
            ]
            groups.append(functools.reduce(lambda u, v: u + v, terms))
        sums.append(jnp.concatenate(groups, axis=0))
    sums = jnp.concatenate(sums, axis=1)
    upper = sums.astype(BF16)
    lower = (sums - upper.astype(F32)).astype(BF16)
    low = lax.broadcasted_iota(jnp.int32, upper.shape, 1) % LANES < LANES // 2
    blank = jnp.zeros_like(upper)
    split = [jnp.where(low, upper, blank), jnp.where(low, lower, blank), jnp.where(low, blank, upper), jnp.where(low, blank, lower)]
    both = mat(jnp.concatenate(split, axis=0), unwindow[...])
    size = 5 * unit
    odd = both[:size] + both[size : 2 * size]
    even = both[2 * size : 3 * size] + both[3 * size :]
    odd = [odd[m * unit : (m + 1) * unit, :] for m in range(5)]
    even = [even[m * unit : (m + 1) * unit, :] for m in range(5)]
    phases = [even[r // 2] if r % 2 == 0 else odd[(r + 1) // 2] for r in range(8)]
    phases[0] = phases[0] + shift_rows(even[4], 1, period)
    phases[7] = phases[7] + shift_rows(odd[0], -1, period)
    image = jnp.concatenate(phases, axis=0)
    image = jnp.concatenate([image, jnp.zeros((image.shape[0], 2 * LANES - wide), F32)], axis=1)
    for k in range(2):
        rows_in[k] = image[:, k * LANES : (k + 1) * LANES]
    for part in range(group):
        lines = [
            jnp.concatenate([rows_in[k, spot(y, part), :] for k in range(2)], axis=1)[:, :wide]
            for y in range(block_rows)
        ]
        lines = [shift_rows(lines[-1], 1, devices)] + lines + [shift_rows(lines[0], -1, devices)]
        for o in range(3):
            plane = [line[:, o * cols : (o + 1) * cols] for line in lines]
            plane.append(jnp.zeros((devices, lanes - span * cols), F32))
            plane = jnp.concatenate(plane, axis=1)
            for k in range(lanes // LANES):
                zout[k, pl.ds(o * group + part, devices, stride=pitch), :] = plane[:, k * LANES : (k + 1) * LANES]
    for k in range(lanes // LANES):
        out_ref[:, k * LANES : (k + 1) * LANES] = zout[k].astype(BF16)


def windows_of(cols, d1):
    wide = 3 * cols
    count = -(-(cols // 2 + 2) // 8)
    window = np.zeros((wide, count * 2 * LANES), np.float32)
    unwindow = np.zeros((count * LANES, wide), np.float32)
    for k in range(count):
        for c in range(3):
            for j in range(18):
                x = 16 * k - 3 + j
                if 0 <= x < cols:
                    for e in range(2):
                        at = e * LANES // 2 + c * 18 + j
                        window[c * cols + x, (2 * k + e) * LANES + at] = 1.0
                        unwindow[k * LANES + at, c * cols + x] = 1.0
    return window, unwindow


def stage_kernel(
    first_ref, window_hbm, unwindow_hbm, second_hbm, third_hbm, window, unwindow, second, third, band, scr, sems
):
    pairs = ((window_hbm, window), (second_hbm, second), (third_hbm, third), (unwindow_hbm, unwindow))
    copies = [pltpu.make_async_copy(source, target, sems.at[i]) for i, (source, target) in enumerate(pairs)]
    for copy in copies:
        copy.start()
    d1 = first_ref.shape[-1]
    scr[...] = jnp.zeros_like(scr)
    row = lax.broadcasted_iota(jnp.int32, (18, 8 * d1), 0)
    tap = row - 2 * (lax.broadcasted_iota(jnp.int32, (18, 8 * d1), 1) // d1)
    for a in range(4):
        lines = [first_ref[a, b].astype(F32) for b in range(4)]
        for c in range(3):
            block = jnp.zeros((18, 8 * d1), F32)
            for b in range(4):
                line = jnp.concatenate([lines[b][c : c + 1, :]] * 8, axis=1)
                block = jnp.where(tap == b, jnp.broadcast_to(line, block.shape), block)
            at = a * LANES // 2 + c * 18
            scr[at : at + 18, :] = block
    band[...] = scr[...].astype(BF16)
    for copy in copies:
        copy.wait()


def stage_call(first, second, third, cols):
    d1, d2, d3 = first.shape[-1], second.shape[-1], third.shape[-1]
    window, unwindow = windows_of(cols, d1)
    operands = (
        first,
        jnp.asarray(window, BF16),
        jnp.asarray(unwindow, BF16),
        second.reshape(16 * d1, d2),
        third.reshape(16 * d2, d3),
    )
    shapes = [value.shape for value in operands[1:]] + [(2 * LANES, 8 * d1)]
    return pl.pallas_call(
        stage_kernel,
        out_shape=tuple(jax.ShapeDtypeStruct(shape, BF16) for shape in shapes),
        in_specs=[VM] + [HBM] * 4,
        out_specs=(VM,) * 5,
        scratch_shapes=[pltpu.VMEM((2 * LANES, 8 * d1), F32), pltpu.SemaphoreType.DMA((4,))],
        compiler_params=PART,
        cost_estimate=pl.CostEstimate(flops=10**8, bytes_accessed=4 * 10**6, transcendentals=0),
        name="stage_weights",
    )(*operands)


def disc_call(payload, staged, fourth, head, devices, group, cols, block_rows):
    period = devices * block_rows // 8
    unit = group * period
    window, unwindow, second, third, band = staged
    d1, d2, d3, d4 = band.shape[1] // 8, second.shape[1], third.shape[1], fourth.shape[-1]
    x2, x3 = cols // 4, cols // 8
    x4 = x3 - 1
    width_one = (cols // 2 + 2) * d1
    args = (
        payload,
        head.reshape(16, d4),
        window,
        band,
        second,
        third,
        unwindow,
        fourth.reshape(16 * d3, d4),
    )
    lanes = payload.shape[1]
    return pl.pallas_call(
        functools.partial(
            disc_kernel, devices=devices, group=group, cols=cols, block_rows=block_rows, period=period
        ),
        out_shape=jax.ShapeDtypeStruct(payload.shape, BF16),
        in_specs=[VM] * 7 + [HBM],
        out_specs=VM,
        scratch_shapes=[
            pltpu.VMEM((lanes // LANES, payload.shape[0], LANES), F32),
            pltpu.VMEM((16 * d3, d4), BF16),
            pltpu.VMEM((2, 8 * unit, LANES), F32),
            pltpu.VMEM((6 * unit, width_one), BF16),
            pltpu.VMEM((4 * unit, width_one), F32),
            pltpu.VMEM((x2 * 2 * unit, 16 * d1), BF16),
            pltpu.VMEM((4 * unit, (x2 + 2) * d2), BF16),
            pltpu.VMEM((x2 * 2 * unit, d2), F32),
            pltpu.VMEM((4 * unit, (x3 + 2) * d3), BF16),
            pltpu.VMEM((x4 * unit, 16 * d3), BF16),
            pltpu.VMEM((x4 * unit, 16 * d3), F32),
            pltpu.VMEM((x3 * unit, 16 * d2), F32),
            pltpu.VMEM((x2 * 2 * unit, 16 * d1), F32),
            pltpu.VMEM((lanes // LANES, payload.shape[0], LANES), F32),
            pltpu.SemaphoreType.DMA((4,)),
        ],
        compiler_params=MOST,
        cost_estimate=pl.CostEstimate(flops=4 * 10**9, bytes_accessed=8 * 10**6, transcendentals=10**6),
        name="disc_rows",
    )(*args)


def put_taps(plane, taps_ref, frames, cols, pieces, padded):
    lanes = plane.shape[1]
    column = lax.broadcasted_iota(jnp.int32, plane.shape, 1) % cols
    for b in range(3):
        moved = plane
        if b == 0:
            moved = jnp.where(column == cols - 1, 0.0, pltpu.roll(plane, lanes - 1, 1))
        if b == 2:
            moved = jnp.where(column == 0, 0.0, pltpu.roll(plane, 1, 1))
        for a in range(3):
            turned = moved if a == 2 else pltpu.roll(moved, lanes - (2 - a) * cols, 1)
            for k in range(pieces):
                taps_ref[k, pl.ds((a * 3 + b) * 3 * frames, 3 * frames), :] = turned[:, k * LANES : (k + 1) * LANES]
    for k in range(pieces):
        taps_ref[k, pl.ds(27 * frames, (padded - 27) * frames), :] = jnp.zeros(((padded - 27) * frames, LANES), F32)


def unpack(plane_ref, zin, devices, group):
    lanes = plane_ref.shape[1]
    pitch = plane_ref.shape[0] // devices
    for k in range(lanes // LANES):
        zin[k] = plane_ref[:, k * LANES : (k + 1) * LANES].astype(F32)
    blocks = []
    for o in range(3):
        for part in range(group):
            row = pl.ds(o * group + part, devices, stride=pitch)
            blocks.append(jnp.concatenate([zin[k, row, :] for k in range(lanes // LANES)], axis=1))
    return jnp.concatenate(blocks, axis=0)


def rec_rows(inner_ref, zin, devices, group, cols, block_rows):
    lanes = inner_ref.shape[1]
    pitch = zin.shape[1] // devices
    edges = []
    for i in range(2):
        row = pl.ds(3 * group + i, devices, stride=pitch)
        edges.append(jnp.concatenate([zin[k, row, :] for k in range(lanes // LANES)], axis=1))
    blocks = []
    for i, e in ((0, 0), (1, 0), (1, 1), (0, 1)):
        pieces = [
            edges[i][:, (e * 3 * group + at) * cols : (e * 3 * group + at + 1) * cols] for at in range(3 * group)
        ]
        blocks.append(jnp.concatenate(pieces, axis=0))
    none = lambda count: jnp.zeros((blocks[0].shape[0], count), F32)
    above, first, last, below = blocks
    rest = lanes - (block_rows + 2) * cols
    return inner_ref[...], jnp.concatenate(
        [above, first * loss_scale, none((block_rows - 2) * cols), last * loss_scale, below, none(rest)], axis=1
    )


def both_kernel(
    inner_ref, plane_ref, feat_ref, part_ref, rec_taps, gan_taps, zin, *, frames, devices, group, cols, block_rows
):
    pieces = block_rows * cols // LANES
    put_taps(unpack(plane_ref, zin, devices, group), gan_taps, frames, cols, pieces, 32)
    inner, edges = rec_rows(inner_ref, zin, devices, group, cols, block_rows)
    put_taps(inner + edges, rec_taps, frames, cols, pieces, 32)
    pixels = pieces * LANES
    total = jnp.zeros((64, feat_ref.shape[1]), F32)
    for frame in range(frames):
        rows = pl.ds(slot_of(frame, devices, group), 32, stride=frames)
        taps = jnp.concatenate(
            [
                jnp.concatenate([taps_ref[k, rows, :] for k in range(pieces)], axis=1)
                for taps_ref in (rec_taps, gan_taps)
            ],
            axis=0,
        )
        total = total + mat(taps.astype(BF16), feat_ref[frame * pixels : (frame + 1) * pixels, :])
    blank = jnp.zeros((part_ref.shape[1] - 54, total.shape[1]), F32)
    total = jnp.concatenate([total[0:27], total[32:59], blank], axis=0).astype(BF16)
    for i in range(part_ref.shape[0]):
        part_ref[i] = total


def turn_kernel(
    inner_ref, plane_ref, out_ref, rec_taps, gan_taps, zin, *, frames, devices, group, cols, block_rows
):
    pieces = block_rows * cols // LANES
    pixels = pieces * LANES
    put_taps(unpack(plane_ref, zin, devices, group), gan_taps, frames, cols, pieces, 32)
    inner, edges = rec_rows(inner_ref, zin, devices, group, cols, block_rows)
    put_taps(inner + edges, rec_taps, frames, cols, pieces, 32)
    for pair in range(frames // 2):
        for k in range(pieces):
            parts = []
            for frame in (2 * pair, 2 * pair + 1):
                rows = pl.ds(slot_of(frame, devices, group), 32, stride=frames)
                parts += [rec_taps[k, rows, :], gan_taps[k, rows, :]]
            at = pair * pixels + k * LANES
            out_ref[at : at + LANES, :] = jnp.concatenate(parts, axis=0).T.astype(BF16)


def taps_call(kernel, specs, operands, out, scratch, frames, devices, group, cols, block_rows, flops, name):
    return pl.pallas_call(
        functools.partial(kernel, frames=frames, devices=devices, group=group, cols=cols, block_rows=block_rows),
        out_shape=out,
        in_specs=specs,
        out_specs=jax.tree.map(lambda _: VM, out),
        scratch_shapes=scratch,
        compiler_params=PART,
        cost_estimate=pl.CostEstimate(flops=flops, bytes_accessed=4 * 10**6, transcendentals=0),
        name=name,
    )(*operands)


def final_kernel(
    taps_ref, sums_ref, weight_ref, out_hbm, grad_ref, adapt_ref, weight_scr, both_ref, out_ref, sems, *, pixels, chunk
):
    weight_scr[...] = jnp.zeros_like(weight_scr)
    for a in range(3):
        for b in range(3):
            at = (a * 3 + b) * 3
            weight_scr[at : at + 3, :] = weight_ref[a, b].astype(F32)
    total = sums_ref[0].astype(F32)
    for i in range(1, sums_ref.shape[0]):
        total = total + sums_ref[i].astype(F32)
    rec, gan = total[0:27], total[27:54]
    norm = lambda values: jnp.sqrt(jnp.sum(jnp.sum(values * values, axis=1, keepdims=True), axis=0, keepdims=True))
    adaptive = norm(rec) / (norm(gan) + epsilon)
    grad = (rec + adaptive * gan) / pixels
    for a in range(3):
        for b in range(3):
            at = (a * 3 + b) * 3
            grad_ref[a, b] = grad[at : at + 3, :]
    adapt_ref[...] = adaptive
    weight = weight_scr[...].astype(BF16)
    padded, channels = weight.shape
    scaled = (adaptive * weight.astype(F32)).astype(BF16)
    both_ref[...] = jnp.zeros_like(both_ref)
    both_ref[0:padded, 0:channels] = weight
    both_ref[padded : 2 * padded, 0:channels] = scaled
    both_ref[2 * padded : 3 * padded, channels:] = weight
    both_ref[3 * padded :, channels:] = scaled
    pairs = taps_ref.shape[0] // chunk
    stores = []
    for pair in range(pairs):
        product = mat(taps_ref[pair * chunk : (pair + 1) * chunk], both_ref[...]).astype(BF16)
        rows = pl.ds(2 * pair * chunk, 2 * chunk)
        out_ref[2 * pair * chunk : (2 * pair + 1) * chunk] = product[:, :channels]
        out_ref[(2 * pair + 1) * chunk : (2 * pair + 2) * chunk] = product[:, channels:]
        stores.append(pltpu.make_async_copy(out_ref.at[rows], out_hbm.at[rows], sems.at[pair]))
        stores[-1].start()
    for copy in stores:
        copy.wait()


def final_call(taps, sums, weight, pixels, chunk):
    padded, channels = 32, weight.shape[-1]
    rows = 2 * taps.shape[0]
    return pl.pallas_call(
        functools.partial(final_kernel, pixels=pixels, chunk=chunk),
        out_shape=(
            jax.ShapeDtypeStruct((rows, channels), BF16),
            jax.ShapeDtypeStruct((3, 3, 3, channels), F32),
            jax.ShapeDtypeStruct((1, 1), F32),
        ),
        in_specs=[VM] * 3,
        out_specs=(HBM, VM, VM),
        scratch_shapes=[
            pltpu.VMEM((padded, channels), F32),
            pltpu.VMEM((4 * padded, 2 * channels), BF16),
            pltpu.VMEM((rows, channels), BF16),
            pltpu.SemaphoreType.DMA((rows // (2 * chunk),)),
        ],
        compiler_params=PART,
        cost_estimate=pl.CostEstimate(flops=4 * rows * channels * padded, bytes_accessed=4 * rows * channels, transcendentals=0),
        name="feature_pull",
    )(taps, sums, weight)


def per_device(
    features, target, conv_weight, disc_first, disc_second, disc_third, disc_fourth, disc_head
):
    row = ("far", "near")
    devices = lax.axis_size(row)
    clips = lax.axis_size("clip")
    _, frames, block_rows, cols, channels = features.shape
    group = frames // devices
    pixels = clips * devices * frames * block_rows * cols
    lanes = up_to((block_rows + 2) * cols, LANES)
    pitch = up_to(3 * group + 2, 8)
    sizes = (frames, devices, group, cols, block_rows)
    feats = features.reshape(frames * block_rows * cols, channels)
    wanted = target[0].transpose(0, 2, 1, 3)
    payload = forward_call(feats, wanted, conv_weight, frames, devices, group, cols, lanes, pitch)
    trade = lambda values: lax.all_to_all(
        values.reshape(devices, pitch, lanes), row, split_axis=0, concat_axis=0, tiled=True
    ).reshape(devices * pitch, lanes)
    arrived = trade(payload)
    inner = inner_call(payload, wanted, frames, devices, group, block_rows, cols)
    _, disc_first = lax.optimization_barrier((payload, disc_first))
    staged = stage_call(disc_first, disc_second, disc_third, cols)
    arrived, inner = lax.optimization_barrier((arrived, inner))
    sent = disc_call(arrived, staged, disc_fourth, disc_head, devices, group, cols, block_rows)
    returned = trade(sent)
    taps_scratch = pltpu.VMEM((block_rows * cols // LANES, 32 * frames, LANES), F32)
    plane_scratch = pltpu.VMEM((lanes // LANES, devices * pitch, LANES), F32)
    flops = 4 * features.size * 27
    part = taps_call(
        both_kernel, [VM, VM, VM], (inner, returned, feats),
        jax.ShapeDtypeStruct((clips * lax.axis_size("near"), 56, channels), BF16),
        [taps_scratch, taps_scratch, plane_scratch], *sizes, flops, "both_taps",
    )
    share = lambda values, axes: lax.all_to_all(values, axes, split_axis=0, concat_axis=0, tiled=True)
    sums = share(sum_call(share(part, ("clip", "near")), lax.axis_size("far")), "far")
    taps = taps_call(
        turn_kernel, [VM, VM], (inner, returned), jax.ShapeDtypeStruct((feats.shape[0] // 2, LANES), BF16),
        [taps_scratch, taps_scratch, plane_scratch], *sizes, flops, "turn_taps",
    )
    image_back = returned.reshape(devices, pitch, lanes)[:, : 3 * group, cols : (block_rows + 1) * cols]
    image_back = image_back.reshape(devices, 3, group, block_rows, cols).transpose(0, 2, 3, 1, 4)
    image_back = image_back.reshape(1, frames, block_rows, 3, cols)
    feature_grad, weight_grad, adaptive = final_call(taps, sums, conv_weight, pixels, block_rows * cols)
    return (feature_grad.reshape(features.shape), image_back, weight_grad, adaptive[0, 0])


def sum_kernel(parts_ref, out_ref):
    total = parts_ref[0].astype(F32)
    for i in range(1, parts_ref.shape[0]):
        total = total + parts_ref[i].astype(F32)
    total = total.astype(BF16)
    for i in range(out_ref.shape[0]):
        out_ref[i] = total


def sum_call(parts, copies):
    return pl.pallas_call(
        sum_kernel,
        out_shape=jax.ShapeDtypeStruct((copies,) + parts.shape[1:], BF16),
        in_specs=[VM],
        out_specs=VM,
        compiler_params=PART,
        name="sum_parts",
    )(parts)


def solution(mesh):
    clips, devices = mesh.shape["clip"], mesh.shape["row"]
    near = 2 if devices % 2 == 0 else 1
    split = jax.sharding.Mesh(mesh.devices.reshape(clips, devices // near, near), ("clip", "far", "near"))
    rows = P("clip", None, ("far", "near"), None, None)
    return jax.shard_map(
        per_device,
        mesh=split,
        in_specs=(rows, rows, P(), P(), P(), P(), P(), P()),
        out_specs=(rows, rows, P(), P()),
        check_vma=False,
    )
```

```python
import functools

import jax
import jax.numpy as jnp
import numpy as np
from jax import lax
from jax.experimental import pallas as pl
from jax.experimental.pallas import tpu as pltpu
from jax.sharding import PartitionSpec as P

loss_scale = 64.0
epsilon = 0.0001
F32 = jnp.float32
BF16 = jnp.bfloat16
LANES = 128
NN = (((1,), (0,)), ((), ()))
NT = (((1,), (1,)), ((), ()))
TN = (((0,), (0,)), ((), ()))
VM = pl.BlockSpec(memory_space=pltpu.VMEM)
HBM = pl.BlockSpec(memory_space=pl.ANY)
WHOLE = pltpu.CompilerParams(vmem_limit_bytes=60 * 2**20)
MOST = pltpu.CompilerParams(vmem_limit_bytes=48 * 2**20)
PART = pltpu.CompilerParams(vmem_limit_bytes=24 * 2**20)


def up_to(value, step):
    return -(-value // step) * step


def mat(left, right, dims=NN):
    return lax.dot_general(left, right, dims, preferred_element_type=F32)


def slot_of(frame, devices, group):
    return (frame % group) * devices + frame // group


def forward_kernel(
    feat_hbm, target_hbm, weight_hbm, pay_ref, feat_ref, target_ref, weight_ref, weight_scr, target_scr,
    taps_ref, out_ref, sems, *, frames, devices, group, cols, lanes, chunks,
):
    pixels = feat_ref.shape[0] // frames
    pieces = pixels // LANES
    pitch = out_ref.shape[1] // devices
    taps = weight_scr.shape[0]
    block_rows = pixels // cols
    copies = [
        pltpu.make_async_copy(weight_hbm, weight_ref, sems.at[frames]),
        pltpu.make_async_copy(target_hbm, target_ref, sems.at[frames + 1]),
    ]
    for slot in range(frames):
        rows = pl.ds((slot % devices * group + slot // devices) * pixels, pixels)
        copies.append(pltpu.make_async_copy(feat_hbm.at[rows, :], feat_ref.at[rows, :], sems.at[slot]))
    for copy in copies:
        copy.start()
    weight_scr[...] = jnp.zeros_like(weight_scr)
    out_ref[...] = jnp.zeros_like(out_ref)
    copies[0].wait()
    for a in range(3):
        for b in range(3):
            at = (a * 3 + b) * 3
            weight_scr[at : at + 3, :] = weight_ref[a, b].astype(F32)
    weight = weight_scr[...].astype(BF16)
    column = lax.broadcasted_iota(jnp.int32, (devices, pixels), 1) % cols

    def finish(part):
        def tap(a, b, o):
            rows = pl.ds(((a * 3 + b) * 3 + o) * frames + part * devices, devices)
            return jnp.concatenate([taps_ref[k, rows, :] for k in range(pieces)], axis=1)

        for o in range(3):
            total = None
            for a in range(3):
                term = tap(a, 1, o)
                term = term + jnp.where(column == 0, 0.0, pltpu.roll(tap(a, 0, o), 1, 1))
                term = term + jnp.where(column == cols - 1, 0.0, pltpu.roll(tap(a, 2, o), pixels - 1, 1))
                term = jnp.concatenate([term, jnp.zeros((devices, lanes - pixels), F32)], axis=1)
                if a < 2:
                    term = pltpu.roll(term, (2 - a) * cols, 1)
                total = term if total is None else total + term
            for k in range(lanes // LANES):
                rows = pl.ds(o * group + part, devices, stride=pitch)
                out_ref[k, rows, :] = total[:, k * LANES : (k + 1) * LANES]

    def edge_rows():
        target_scr[:, 0:cols] = target_ref[...].reshape(target_scr.shape[0], cols).astype(F32)
        edges = []
        for y in (0, block_rows - 1):
            for o in range(3):
                for part in range(group):
                    rows = pl.ds((part * 3 + o) * block_rows + y, devices, stride=group * 3 * block_rows)
                    edges.append(target_scr[rows, :][:, 0:cols])
        edges.append(jnp.zeros((devices, lanes - len(edges) * cols), F32))
        edges = jnp.concatenate(edges, axis=1)
        for k in range(lanes // LANES):
            out_ref[k, pl.ds(3 * group, devices, stride=pitch), :] = edges[:, k * LANES : (k + 1) * LANES]

    copies[1].wait()
    edge_rows()
    step = frames // chunks
    done = 0
    for chunk in range(chunks):
        for slot in range(chunk * step, (chunk + 1) * step):
            copies[2 + slot].wait()
        for slot in range(chunk * step, (chunk + 1) * step):
            frame = slot % devices * group + slot // devices
            product = mat(weight, feat_ref[frame * pixels : (frame + 1) * pixels, :], NT)
            for k in range(pieces):
                taps_ref[k, pl.ds(slot, taps, stride=frames), :] = product[:, k * LANES : (k + 1) * LANES]
        while (done + 1) * devices <= chunk * step or (chunk == chunks - 1 and done < group):
            finish(done)
            done += 1
    for k in range(lanes // LANES):
        pay_ref[:, k * LANES : (k + 1) * LANES] = out_ref[k].astype(BF16)


def forward_call(features, target, weight, frames, devices, group, cols, lanes, pitch):
    pixels = features.shape[0] // frames
    channels = features.shape[1]
    chunks = 2
    return pl.pallas_call(
        functools.partial(
            forward_kernel, frames=frames, devices=devices, group=group, cols=cols, lanes=lanes, chunks=chunks
        ),
        out_shape=jax.ShapeDtypeStruct((devices * pitch, lanes), BF16),
        in_specs=[HBM, HBM, HBM],
        out_specs=VM,
        scratch_shapes=[
            pltpu.VMEM(features.shape, BF16),
            pltpu.VMEM(target.shape, BF16),
            pltpu.VMEM(weight.shape, BF16),
            pltpu.VMEM((32, channels), F32),
            pltpu.VMEM((3 * pixels // cols * frames, LANES), F32),
            pltpu.VMEM((pixels // LANES, 32 * frames, LANES), F32),
            pltpu.VMEM((lanes // LANES, devices * pitch, LANES), F32),
            pltpu.SemaphoreType.DMA((frames + 2,)),
        ],
        compiler_params=WHOLE,
        cost_estimate=pl.CostEstimate(flops=2 * features.size * 27, bytes_accessed=2 * features.size, transcendentals=0),
        name="forward_taps",
    )(features, target, weight)


def inner_kernel(pay_ref, target_ref, inner_ref, scr, zin, *, frames, devices, group, block_rows, cols):
    scr[:, 0:cols] = target_ref[...].reshape(scr.shape[0], cols).astype(F32)
    stride = group * 3 * block_rows
    lanes = pay_ref.shape[1]
    pitch = pay_ref.shape[0] // devices
    for k in range(lanes // LANES):
        zin[k] = pay_ref[:, k * LANES : (k + 1) * LANES].astype(F32)
    for o in range(3):
        for part in range(group):
            at = o * frames + part * devices
            rows = [jnp.zeros((devices, cols), F32)]
            rows += [
                scr[pl.ds((part * 3 + o) * block_rows + y, devices, stride=stride), :][:, 0:cols]
                for y in range(block_rows)
            ]
            rows.append(jnp.zeros((devices, lanes - (block_rows + 1) * cols), F32))
            wanted = jnp.concatenate(rows, axis=1)
            lane = lax.broadcasted_iota(jnp.int32, wanted.shape, 1)
            inside = (lane >= 2 * cols) & (lane < block_rows * cols)
            row = pl.ds(o * group + part, devices, stride=pitch)
            own = jnp.concatenate([zin[k, row, :] for k in range(lanes // LANES)], axis=1)
            inner_ref[at : at + devices, :] = loss_scale * (jnp.where(inside, own, 0.0) - wanted)


def inner_call(payload, target, frames, devices, group, block_rows, cols):
    lanes = payload.shape[1]
    return pl.pallas_call(
        functools.partial(
            inner_kernel, frames=frames, devices=devices, group=group, block_rows=block_rows, cols=cols
        ),
        out_shape=jax.ShapeDtypeStruct((3 * frames, lanes), F32),
        in_specs=[VM, VM],
        out_specs=VM,
        scratch_shapes=[
            pltpu.VMEM((frames * 3 * block_rows, LANES), F32),
            pltpu.VMEM((lanes // LANES, payload.shape[0], LANES), F32),
        ],
        compiler_params=PART,
        cost_estimate=pl.CostEstimate(flops=10**8, bytes_accessed=10**6, transcendentals=0),
        name="inner_rows",
    )(payload, target)


def shift_rows(values, step, period):
    size = values.shape[0]
    row = lax.broadcasted_iota(jnp.int32, values.shape, 0) % period
    rolled = pltpu.roll(values, step % size, 0)
    source = row - step
    return jnp.where((source >= 0) & (source < period), rolled, 0.0)


def gate_of(values):
    logistic = 0.5 + 0.5 * jnp.tanh(0.5 * values)
    return (values * logistic).astype(BF16), logistic * (1.0 + values * (1.0 - logistic))


def edge_planes(zin, zout, first, last, devices, group, cols, lanes, pitch):
    row = pl.ds(3 * group, devices, stride=pitch)
    target = jnp.concatenate([zin[k, row, :] for k in range(lanes // LANES)], axis=1)
    outer, inner = [], []
    for e, rows, other, move in ((0, first, last, 1), (1, last, first, -1)):
        for o in range(3):
            for part in range(group):
                at = ((1 - e) * 3 * group + o * group + part) * cols
                near = other[part][:, o * cols : (o + 1) * cols] - target[:, at : at + cols]
                outer.append(shift_rows(loss_scale * near, move, devices))
                inner.append(rows[part][:, o * cols : (o + 1) * cols])
    for i, pieces in enumerate((outer, inner)):
        pieces.append(jnp.zeros((devices, lanes - 6 * group * cols), F32))
        plane = jnp.concatenate(pieces, axis=1)
        for k in range(lanes // LANES):
            zout[k, pl.ds(3 * group + i, devices, stride=pitch), :] = plane[:, k * LANES : (k + 1) * LANES]


def disc_kernel(
    pay_ref, head_ref, window, band_ref, second, unwindow, third_hbm, fourth_hbm, out_ref,
    zin, third, fourth, rows_in, act_one, slope_one, cols_two, act_two, slope_two, act_three, cols_four,
    pull_four, pull_three, pull_two, zout, sems, *, devices, group, cols, block_rows, period,
):
    lanes = pay_ref.shape[1]
    pitch = pay_ref.shape[0] // devices
    span = block_rows + 2
    unit = group * period
    wide = 3 * cols
    d1 = (act_one.shape[1]) // (cols // 2 + 2)
    d2, d3, d4 = second.shape[1], third.shape[1], fourth.shape[1]
    x1, x2, x3 = cols // 2, cols // 4, cols // 8
    x4 = x3 - 1
    quarter = fourth.shape[0] // 4
    copies = [
        pltpu.make_async_copy(
            fourth_hbm.at[pl.ds(a * quarter, quarter), :], fourth.at[pl.ds(a * quarter, quarter), :], sems.at[a]
        )
        for a in range(4)
    ]
    copies.append(pltpu.make_async_copy(third_hbm, third, sems.at[4]))
    for i in (4, 0, 1, 2, 3):
        copies[i].start()
    cells = block_rows // 8
    spot = lambda y, part: pl.ds((y % 8 * group + part) * period + y // 8, devices, stride=cells)
    for k in range(lanes // LANES):
        zin[k] = pay_ref[:, k * LANES : (k + 1) * LANES].astype(F32)
    zout[...] = jnp.zeros_like(zout)
    firsts, lasts = [], []
    for part in range(group):
        planes = []
        for o in range(3):
            pieces = [zin[k, pl.ds(o * group + part, devices, stride=pitch), :] for k in range(lanes // LANES)]
            planes.append(jnp.concatenate(pieces, axis=1))
        lines = [
            jnp.concatenate(
                [plane[:, i * cols : (i + 1) * cols] for plane in planes]
                + [jnp.zeros((devices, 2 * LANES - wide), F32)],
                axis=1,
            )
            for i in range(span)
        ]
        lines[1] = lines[1] + shift_rows(lines[span - 1], 1, devices)
        lines[block_rows] = lines[block_rows] + shift_rows(lines[0], -1, devices)
        for y in range(block_rows):
            for k in range(2):
                rows_in[k, spot(y, part), :] = lines[y + 1][:, k * LANES : (k + 1) * LANES]
        firsts.append(lines[1])
        lasts.append(lines[block_rows])
    image = jnp.concatenate([rows_in[0], rows_in[1]], axis=1)[:, :wide].astype(BF16)
    wins = mat(image, window[...])
    ext = [wins[r * unit : (r + 1) * unit] for r in range(8)]
    ext = [shift_rows(ext[7], 1, period)] + ext + [shift_rows(ext[0], -1, period)]
    width_one = act_one.shape[1]
    strip = 8 * d1
    band = band_ref[...]
    for k in range(-(-width_one // strip)):
        low, high = slice(2 * k * LANES, (2 * k + 1) * LANES), slice((2 * k + 1) * LANES, (2 * k + 2) * LANES)
        left = jnp.concatenate(
            [
                jnp.concatenate([ext[2 * p + h][:, low] + ext[2 * p + h + 1][:, high] for p in range(4)], axis=0)
                for h in (0, 2)
            ],
            axis=1,
        ).astype(BF16)
        start, end = k * strip, min((k + 1) * strip, width_one)
        act, slope = gate_of(mat(left, band[:, : end - start]))
        if k == 0 or end == width_one:
            lane = start + lax.broadcasted_iota(jnp.int32, slope.shape, 1)
            inside = (lane >= d1) & (lane < width_one - d1)
            slope = jnp.where(inside, slope, 0.0)
            act = jnp.where(inside, act.astype(F32), 0.0).astype(BF16)
        slope_one[:, start:end] = slope
        act_one[unit : 5 * unit, start:end] = act
        actual = act.astype(F32)
        act_one[0:unit, start:end] = shift_rows(actual[3 * unit :], 1, period).astype(BF16)
        act_one[5 * unit :, start:end] = shift_rows(actual[:unit], -1, period).astype(BF16)
    for x in range(x2):
        for a in range(4):
            for p in range(2):
                cols_two[(x * 2 + p) * unit : (x * 2 + p + 1) * unit, a * 4 * d1 : (a + 1) * 4 * d1] = act_one[
                    (2 * p + a) * unit : (2 * p + a + 1) * unit, 2 * x * d1 : (2 * x + 4) * d1
                ]
    pre = mat(cols_two[...], second[...])
    act, slope = gate_of(pre)
    slope_two[...] = slope
    act_two[:, 0:d2] = jnp.zeros((4 * unit, d2), BF16)
    act_two[:, (x2 + 1) * d2 :] = jnp.zeros((4 * unit, d2), BF16)
    for x in range(x2):
        block = act[x * 2 * unit : (x + 1) * 2 * unit]
        actual = block.astype(F32)
        at = slice((x + 1) * d2, (x + 2) * d2)
        act_two[unit : 3 * unit, at] = block
        act_two[0:unit, at] = shift_rows(actual[unit:], 1, period).astype(BF16)
        act_two[3 * unit :, at] = shift_rows(actual[:unit], -1, period).astype(BF16)
    left = jnp.concatenate(
        [
            jnp.concatenate([act_two[a * unit : (a + 1) * unit, 2 * x * d2 : (2 * x + 4) * d2] for a in range(4)], axis=1)
            for x in range(x3)
        ],
        axis=0,
    )
    copies[4].wait()
    act, slope_three = gate_of(mat(left, third[...]))
    act_three[:, 0:d3] = jnp.zeros((4 * unit, d3), BF16)
    act_three[:, (x3 + 1) * d3 :] = jnp.zeros((4 * unit, d3), BF16)
    for x in range(x3):
        block = act[x * unit : (x + 1) * unit]
        actual = block.astype(F32)
        at = slice((x + 1) * d3, (x + 2) * d3)
        act_three[unit : 2 * unit, at] = block
        for a in (0, 2, 3):
            act_three[a * unit : (a + 1) * unit, at] = shift_rows(actual, 1 - a, period).astype(BF16)
    for x in range(x4):
        for a in range(4):
            cols_four[x * unit : (x + 1) * unit, a * 4 * d3 : (a + 1) * 4 * d3] = act_three[
                a * unit : (a + 1) * unit, x * d3 : (x + 4) * d3
            ]
    edge_planes(zin, zout, firsts, lasts, devices, group, cols, lanes, pitch)
    pre = None
    for a in range(4):
        copies[a].wait()
        term = mat(cols_four[:, a * quarter : (a + 1) * quarter], fourth[a * quarter : (a + 1) * quarter, :])
        pre = term if pre is None else pre + term
    _, slope = gate_of(pre)
    row = lax.broadcasted_iota(jnp.int32, (unit, d4), 0) % period
    head = head_ref[...].astype(F32) * -loss_scale
    heads = []
    for x in range(x4):
        total = None
        for a in range(4):
            taps = [head[a * 4 + b : a * 4 + b + 1, :] for b in range(4) if 0 <= x - b + 1 < x4 - 1]
            tap = functools.reduce(lambda u, v: u + v, taps)
            inside = (row - a + 1 >= 0) & (row - a + 1 < period - 2) & (row < period - 1)
            term = jnp.where(inside, jnp.broadcast_to(tap, (unit, d4)), 0.0)
            total = term if total is None else total + term
        heads.append(total)
    cot = (jnp.concatenate(heads, axis=0) * slope).astype(BF16)
    pull_four[...] = mat(cot, fourth[...], NT)
    cots = []
    for x in range(x3):
        total = None
        for a in range(4):
            term = None
            for b in range(4):
                source = x - b + 1
                if 0 <= source < x4:
                    piece = pull_four[source * unit : (source + 1) * unit, (a * 4 + b) * d3 : (a * 4 + b + 1) * d3]
                    term = piece if term is None else term + piece
            if a != 1:
                term = shift_rows(term, a - 1, period)
            total = term if total is None else total + term
        cots.append((total * slope_three[x * unit : (x + 1) * unit]).astype(BF16))
    pull_three[...] = mat(jnp.concatenate(cots, axis=0), third[...], NT)
    cots = []
    for x in range(x2):
        terms = []
        for a in range(4):
            term = None
            for b in range(4):
                if (x - b + 1) % 2 == 0 and 0 <= (x - b + 1) // 2 < x3:
                    source = (x - b + 1) // 2
                    piece = pull_three[source * unit : (source + 1) * unit, (a * 4 + b) * d2 : (a * 4 + b + 1) * d2]
                    term = piece if term is None else term + piece
            terms.append(term)
        even = terms[1] + shift_rows(terms[3], 1, period)
        odd = terms[2] + shift_rows(terms[0], -1, period)
        both = jnp.concatenate([even, odd], axis=0)
        cots.append((both * slope_two[x * 2 * unit : (x + 1) * 2 * unit]).astype(BF16))
    pull_two[...] = mat(jnp.concatenate(cots, axis=0), second[...], NT)
    strips = []
    for k in range(x2 + 1):
        terms = {}
        for p in range(2):
            for a in range(4):
                term = None
                if k < x2:
                    term = pull_two[(2 * k + p) * unit : (2 * k + p + 1) * unit, a * 4 * d1 : (a * 4 + 2) * d1]
                if k > 0:
                    other = pull_two[(2 * k - 2 + p) * unit : (2 * k - 1 + p) * unit, (a * 4 + 2) * d1 : (a + 1) * 4 * d1]
                    term = other if term is None else term + other
                terms[p, a] = term
        both = jnp.concatenate(
            [
                terms[0, 1] + shift_rows(terms[1, 3], 1, period),
                terms[0, 2] + terms[1, 0],
                terms[0, 3] + terms[1, 1],
                terms[1, 2] + shift_rows(terms[0, 0], -1, period),
            ],
            axis=0,
        )
        strips.append((both * slope_one[:, 2 * k * d1 : (2 * k + 2) * d1]).astype(BF16))
    cot = jnp.concatenate(strips, axis=1)
    sums = []
    for k in range(-(-width_one // strip)):
        start, end = k * strip, min((k + 1) * strip, width_one)
        pulls = mat(cot[:, start:end], band[:, : end - start], NT)
        groups = []
        for m in range(5):
            terms = [
                pulls[p * unit : (p + 1) * unit, (m - p) * LANES : (m - p + 1) * LANES] for p in range(4) if 0 <= m - p < 2
            ]
            groups.append(functools.reduce(lambda u, v: u + v, terms))
        sums.append(jnp.concatenate(groups, axis=0))
    sums = jnp.concatenate(sums, axis=1)
    upper = sums.astype(BF16)
    lower = (sums - upper.astype(F32)).astype(BF16)
    low = lax.broadcasted_iota(jnp.int32, upper.shape, 1) % LANES < LANES // 2
    blank = jnp.zeros_like(upper)
    split = [jnp.where(low, upper, blank), jnp.where(low, lower, blank), jnp.where(low, blank, upper), jnp.where(low, blank, lower)]
    both = mat(jnp.concatenate(split, axis=0), unwindow[...])
    size = 5 * unit
    odd = both[:size] + both[size : 2 * size]
    even = both[2 * size : 3 * size] + both[3 * size :]
    odd = [odd[m * unit : (m + 1) * unit, :] for m in range(5)]
    even = [even[m * unit : (m + 1) * unit, :] for m in range(5)]
    phases = [even[r // 2] if r % 2 == 0 else odd[(r + 1) // 2] for r in range(8)]
    phases[0] = phases[0] + shift_rows(even[4], 1, period)
    phases[7] = phases[7] + shift_rows(odd[0], -1, period)
    image = jnp.concatenate(phases, axis=0)
    image = jnp.concatenate([image, jnp.zeros((image.shape[0], 2 * LANES - wide), F32)], axis=1)
    for k in range(2):
        rows_in[k] = image[:, k * LANES : (k + 1) * LANES]
    for part in range(group):
        lines = [
            jnp.concatenate([rows_in[k, spot(y, part), :] for k in range(2)], axis=1)[:, :wide]
            for y in range(block_rows)
        ]
        lines = [shift_rows(lines[-1], 1, devices)] + lines + [shift_rows(lines[0], -1, devices)]
        for o in range(3):
            plane = [line[:, o * cols : (o + 1) * cols] for line in lines]
            plane.append(jnp.zeros((devices, lanes - span * cols), F32))
            plane = jnp.concatenate(plane, axis=1)
            for k in range(lanes // LANES):
                zout[k, pl.ds(o * group + part, devices, stride=pitch), :] = plane[:, k * LANES : (k + 1) * LANES]
    for k in range(lanes // LANES):
        out_ref[:, k * LANES : (k + 1) * LANES] = zout[k].astype(BF16)


def window_of(at, cols):
    k, rest = at // LANES, at % LANES
    inner = rest % (LANES // 2)
    colour = jnp.where(inner >= 18, 1, 0) + jnp.where(inner >= 36, 1, 0)
    x = 16 * k - 3 + inner - 18 * colour
    inside = (inner < 54) & (x >= 0) & (x < cols)
    return jnp.where(inside, colour * cols + x, -1), rest // (LANES // 2)


def stage_kernel(first_ref, second_hbm, window, unwindow, second, band, scr, sem, *, cols):
    copy = pltpu.make_async_copy(second_hbm, second, sem.at[0])
    copy.start()
    row = lax.broadcasted_iota(jnp.int32, window.shape, 0)
    lane = lax.broadcasted_iota(jnp.int32, window.shape, 1)
    place, half = window_of(lane // (2 * LANES) * LANES + lane % LANES, cols)
    window[...] = jnp.where((place == row) & (half == lane // LANES % 2), 1.0, 0.0).astype(BF16)
    place, _ = window_of(lax.broadcasted_iota(jnp.int32, unwindow.shape, 0), cols)
    column = lax.broadcasted_iota(jnp.int32, unwindow.shape, 1)
    unwindow[...] = jnp.where(place == column, 1.0, 0.0).astype(BF16)
    d1 = first_ref.shape[-1]
    scr[...] = jnp.zeros_like(scr)
    row = lax.broadcasted_iota(jnp.int32, (18, 8 * d1), 0)
    tap = row - 2 * (lax.broadcasted_iota(jnp.int32, (18, 8 * d1), 1) // d1)
    for a in range(4):
        lines = [first_ref[a, b].astype(F32) for b in range(4)]
        for c in range(3):
            block = jnp.zeros((18, 8 * d1), F32)
            for b in range(4):
                line = jnp.concatenate([lines[b][c : c + 1, :]] * 8, axis=1)
                block = jnp.where(tap == b, jnp.broadcast_to(line, block.shape), block)
            at = a * LANES // 2 + c * 18
            scr[at : at + 18, :] = block
    band[...] = scr[...].astype(BF16)
    copy.wait()


def stage_call(first, second, cols):
    d1, d2 = first.shape[-1], second.shape[-1]
    count = -(-(cols // 2 + 2) // 8)
    shapes = [(3 * cols, count * 2 * LANES), (count * LANES, 3 * cols), (16 * d1, d2), (2 * LANES, 8 * d1)]
    return pl.pallas_call(
        functools.partial(stage_kernel, cols=cols),
        out_shape=tuple(jax.ShapeDtypeStruct(shape, BF16) for shape in shapes),
        in_specs=[VM, HBM],
        out_specs=(VM,) * 4,
        scratch_shapes=[pltpu.VMEM((2 * LANES, 8 * d1), F32), pltpu.SemaphoreType.DMA((1,))],
        compiler_params=PART,
        cost_estimate=pl.CostEstimate(flops=10**8, bytes_accessed=4 * 10**6, transcendentals=0),
        name="stage_weights",
    )(first, second.reshape(16 * d1, d2))


def disc_call(payload, staged, third, fourth, head, devices, group, cols, block_rows):
    period = devices * block_rows // 8
    unit = group * period
    window, unwindow, second, band = staged
    d1, d2, d3, d4 = band.shape[1] // 8, second.shape[1], third.shape[-1], fourth.shape[-1]
    x2, x3 = cols // 4, cols // 8
    x4 = x3 - 1
    width_one = (cols // 2 + 2) * d1
    args = (
        payload,
        head.reshape(16, d4),
        window,
        band,
        second,
        unwindow,
        third.reshape(16 * d2, d3),
        fourth.reshape(16 * d3, d4),
    )
    lanes = payload.shape[1]
    return pl.pallas_call(
        functools.partial(
            disc_kernel, devices=devices, group=group, cols=cols, block_rows=block_rows, period=period
        ),
        out_shape=jax.ShapeDtypeStruct(payload.shape, BF16),
        in_specs=[VM] * 6 + [HBM] * 2,
        out_specs=VM,
        scratch_shapes=[
            pltpu.VMEM((lanes // LANES, payload.shape[0], LANES), F32),
            pltpu.VMEM((16 * d2, d3), BF16),
            pltpu.VMEM((16 * d3, d4), BF16),
            pltpu.VMEM((2, 8 * unit, LANES), F32),
            pltpu.VMEM((6 * unit, width_one), BF16),
            pltpu.VMEM((4 * unit, width_one), F32),
            pltpu.VMEM((x2 * 2 * unit, 16 * d1), BF16),
            pltpu.VMEM((4 * unit, (x2 + 2) * d2), BF16),
            pltpu.VMEM((x2 * 2 * unit, d2), F32),
            pltpu.VMEM((4 * unit, (x3 + 2) * d3), BF16),
            pltpu.VMEM((x4 * unit, 16 * d3), BF16),
            pltpu.VMEM((x4 * unit, 16 * d3), F32),
            pltpu.VMEM((x3 * unit, 16 * d2), F32),
            pltpu.VMEM((x2 * 2 * unit, 16 * d1), F32),
            pltpu.VMEM((lanes // LANES, payload.shape[0], LANES), F32),
            pltpu.SemaphoreType.DMA((5,)),
        ],
        compiler_params=MOST,
        cost_estimate=pl.CostEstimate(flops=4 * 10**9, bytes_accessed=8 * 10**6, transcendentals=10**6),
        name="disc_rows",
    )(*args)


def put_taps(plane, taps_ref, frames, cols, pieces, padded):
    lanes = plane.shape[1]
    column = lax.broadcasted_iota(jnp.int32, plane.shape, 1) % cols
    for b in range(3):
        moved = plane
        if b == 0:
            moved = jnp.where(column == cols - 1, 0.0, pltpu.roll(plane, lanes - 1, 1))
        if b == 2:
            moved = jnp.where(column == 0, 0.0, pltpu.roll(plane, 1, 1))
        for a in range(3):
            turned = moved if a == 2 else pltpu.roll(moved, lanes - (2 - a) * cols, 1)
            for k in range(pieces):
                taps_ref[k, pl.ds((a * 3 + b) * 3 * frames, 3 * frames), :] = turned[:, k * LANES : (k + 1) * LANES]
    for k in range(pieces):
        taps_ref[k, pl.ds(27 * frames, (padded - 27) * frames), :] = jnp.zeros(((padded - 27) * frames, LANES), F32)


def unpack(plane_ref, zin, devices, group):
    lanes = plane_ref.shape[1]
    pitch = plane_ref.shape[0] // devices
    for k in range(lanes // LANES):
        zin[k] = plane_ref[:, k * LANES : (k + 1) * LANES].astype(F32)
    blocks = []
    for o in range(3):
        for part in range(group):
            row = pl.ds(o * group + part, devices, stride=pitch)
            blocks.append(jnp.concatenate([zin[k, row, :] for k in range(lanes // LANES)], axis=1))
    return jnp.concatenate(blocks, axis=0)


def rec_rows(inner_ref, zin, devices, group, cols, block_rows):
    lanes = inner_ref.shape[1]
    pitch = zin.shape[1] // devices
    edges = []
    for i in range(2):
        row = pl.ds(3 * group + i, devices, stride=pitch)
        edges.append(jnp.concatenate([zin[k, row, :] for k in range(lanes // LANES)], axis=1))
    blocks = []
    for i, e in ((0, 0), (1, 0), (1, 1), (0, 1)):
        pieces = [
            edges[i][:, (e * 3 * group + at) * cols : (e * 3 * group + at + 1) * cols] for at in range(3 * group)
        ]
        blocks.append(jnp.concatenate(pieces, axis=0))
    none = lambda count: jnp.zeros((blocks[0].shape[0], count), F32)
    above, first, last, below = blocks
    rest = lanes - (block_rows + 2) * cols
    return inner_ref[...], jnp.concatenate(
        [above, first * loss_scale, none((block_rows - 2) * cols), last * loss_scale, below, none(rest)], axis=1
    )


def both_kernel(
    inner_ref, plane_ref, feat_ref, part_ref, rec_taps, gan_taps, zin, *, frames, devices, group, cols, block_rows
):
    pieces = block_rows * cols // LANES
    put_taps(unpack(plane_ref, zin, devices, group), gan_taps, frames, cols, pieces, 32)
    inner, edges = rec_rows(inner_ref, zin, devices, group, cols, block_rows)
    put_taps(inner + edges, rec_taps, frames, cols, pieces, 32)
    pixels = pieces * LANES
    total = jnp.zeros((64, feat_ref.shape[1]), F32)
    for frame in range(frames):
        rows = pl.ds(slot_of(frame, devices, group), 32, stride=frames)
        taps = jnp.concatenate(
            [
                jnp.concatenate([taps_ref[k, rows, :] for k in range(pieces)], axis=1)
                for taps_ref in (rec_taps, gan_taps)
            ],
            axis=0,
        )
        total = total + mat(taps.astype(BF16), feat_ref[frame * pixels : (frame + 1) * pixels, :])
    blank = jnp.zeros((part_ref.shape[1] - 54, total.shape[1]), F32)
    total = jnp.concatenate([total[0:27], total[32:59], blank], axis=0).astype(BF16)
    for i in range(part_ref.shape[0]):
        part_ref[i] = total


def turn_kernel(
    inner_ref, plane_ref, out_ref, rec_taps, gan_taps, zin, *, frames, devices, group, cols, block_rows
):
    pieces = block_rows * cols // LANES
    pixels = pieces * LANES
    put_taps(unpack(plane_ref, zin, devices, group), gan_taps, frames, cols, pieces, 32)
    inner, edges = rec_rows(inner_ref, zin, devices, group, cols, block_rows)
    put_taps(inner + edges, rec_taps, frames, cols, pieces, 32)
    for pair in range(frames // 2):
        for k in range(pieces):
            parts = []
            for frame in (2 * pair, 2 * pair + 1):
                rows = pl.ds(slot_of(frame, devices, group), 32, stride=frames)
                parts += [rec_taps[k, rows, :], gan_taps[k, rows, :]]
            at = pair * pixels + k * LANES
            out_ref[at : at + LANES, :] = jnp.concatenate(parts, axis=0).T.astype(BF16)


def taps_call(kernel, specs, operands, out, scratch, frames, devices, group, cols, block_rows, flops, name):
    return pl.pallas_call(
        functools.partial(kernel, frames=frames, devices=devices, group=group, cols=cols, block_rows=block_rows),
        out_shape=out,
        in_specs=specs,
        out_specs=jax.tree.map(lambda _: VM, out),
        scratch_shapes=scratch,
        compiler_params=PART,
        cost_estimate=pl.CostEstimate(flops=flops, bytes_accessed=4 * 10**6, transcendentals=0),
        name=name,
    )(*operands)


def final_kernel(
    taps_ref, sums_ref, weight_ref, out_hbm, grad_ref, adapt_ref, weight_scr, both_ref, out_ref, sems, *, pixels, chunk
):
    weight_scr[...] = jnp.zeros_like(weight_scr)
    for a in range(3):
        for b in range(3):
            at = (a * 3 + b) * 3
            weight_scr[at : at + 3, :] = weight_ref[a, b].astype(F32)
    total = sums_ref[0].astype(F32)
    for i in range(1, sums_ref.shape[0]):
        total = total + sums_ref[i].astype(F32)
    rec, gan = total[0:27], total[27:54]
    norm = lambda values: jnp.sqrt(jnp.sum(jnp.sum(values * values, axis=1, keepdims=True), axis=0, keepdims=True))
    adaptive = norm(rec) / (norm(gan) + epsilon)
    grad = (rec + adaptive * gan) / pixels
    for a in range(3):
        for b in range(3):
            at = (a * 3 + b) * 3
            grad_ref[a, b] = grad[at : at + 3, :]
    adapt_ref[...] = adaptive
    weight = weight_scr[...].astype(BF16)
    padded, channels = weight.shape
    scaled = (adaptive * weight.astype(F32)).astype(BF16)
    both_ref[...] = jnp.zeros_like(both_ref)
    both_ref[0:padded, 0:channels] = weight
    both_ref[padded : 2 * padded, 0:channels] = scaled
    both_ref[2 * padded : 3 * padded, channels:] = weight
    both_ref[3 * padded :, channels:] = scaled
    pairs = taps_ref.shape[0] // chunk
    stores = []
    for pair in range(pairs):
        product = mat(taps_ref[pair * chunk : (pair + 1) * chunk], both_ref[...]).astype(BF16)
        rows = pl.ds(2 * pair * chunk, 2 * chunk)
        out_ref[2 * pair * chunk : (2 * pair + 1) * chunk] = product[:, :channels]
        out_ref[(2 * pair + 1) * chunk : (2 * pair + 2) * chunk] = product[:, channels:]
        stores.append(pltpu.make_async_copy(out_ref.at[rows], out_hbm.at[rows], sems.at[pair]))
        stores[-1].start()
    for copy in stores:
        copy.wait()


def final_call(taps, sums, weight, pixels, chunk):
    padded, channels = 32, weight.shape[-1]
    rows = 2 * taps.shape[0]
    return pl.pallas_call(
        functools.partial(final_kernel, pixels=pixels, chunk=chunk),
        out_shape=(
            jax.ShapeDtypeStruct((rows, channels), BF16),
            jax.ShapeDtypeStruct((3, 3, 3, channels), F32),
            jax.ShapeDtypeStruct((1, 1), F32),
        ),
        in_specs=[VM] * 3,
        out_specs=(HBM, VM, VM),
        scratch_shapes=[
            pltpu.VMEM((padded, channels), F32),
            pltpu.VMEM((4 * padded, 2 * channels), BF16),
            pltpu.VMEM((rows, channels), BF16),
            pltpu.SemaphoreType.DMA((rows // (2 * chunk),)),
        ],
        compiler_params=PART,
        cost_estimate=pl.CostEstimate(flops=4 * rows * channels * padded, bytes_accessed=4 * rows * channels, transcendentals=0),
        name="feature_pull",
    )(taps, sums, weight)


def per_device(
    features, target, conv_weight, disc_first, disc_second, disc_third, disc_fourth, disc_head
):
    row = ("far", "near")
    devices = lax.axis_size(row)
    clips = lax.axis_size("clip")
    _, frames, block_rows, cols, channels = features.shape
    group = frames // devices
    pixels = clips * devices * frames * block_rows * cols
    lanes = up_to((block_rows + 2) * cols, LANES)
    pitch = up_to(3 * group + 2, 8)
    sizes = (frames, devices, group, cols, block_rows)
    feats = features.reshape(frames * block_rows * cols, channels)
    wanted = target[0].transpose(0, 2, 1, 3)
    payload = forward_call(feats, wanted, conv_weight, frames, devices, group, cols, lanes, pitch)
    trade = lambda values: lax.all_to_all(
        values.reshape(devices, pitch, lanes), row, split_axis=0, concat_axis=0, tiled=True
    ).reshape(devices * pitch, lanes)
    arrived = trade(payload)
    inner = inner_call(payload, wanted, frames, devices, group, block_rows, cols)
    _, disc_first = lax.optimization_barrier((payload, disc_first))
    staged = stage_call(disc_first, disc_second, cols)
    arrived, inner = lax.optimization_barrier((arrived, inner))
    sent = disc_call(arrived, staged, disc_third, disc_fourth, disc_head, devices, group, cols, block_rows)
    returned = trade(sent)
    taps_scratch = pltpu.VMEM((block_rows * cols // LANES, 32 * frames, LANES), F32)
    plane_scratch = pltpu.VMEM((lanes // LANES, devices * pitch, LANES), F32)
    flops = 4 * features.size * 27
    part = taps_call(
        both_kernel, [VM, VM, VM], (inner, returned, feats),
        jax.ShapeDtypeStruct((clips * lax.axis_size("near"), 56, channels), BF16),
        [taps_scratch, taps_scratch, plane_scratch], *sizes, flops, "both_taps",
    )
    share = lambda values, axes: lax.all_to_all(values, axes, split_axis=0, concat_axis=0, tiled=True)
    sums = share(sum_call(share(part, ("clip", "near")), lax.axis_size("far")), "far")
    taps = taps_call(
        turn_kernel, [VM, VM], (inner, returned), jax.ShapeDtypeStruct((feats.shape[0] // 2, LANES), BF16),
        [taps_scratch, taps_scratch, plane_scratch], *sizes, flops, "turn_taps",
    )
    image_back = returned.reshape(devices, pitch, lanes)[:, : 3 * group, cols : (block_rows + 1) * cols]
    image_back = image_back.reshape(devices, 3, group, block_rows, cols).transpose(0, 2, 3, 1, 4)
    image_back = image_back.reshape(1, frames, block_rows, 3, cols)
    feature_grad, weight_grad, adaptive = final_call(taps, sums, conv_weight, pixels, block_rows * cols)
    return (feature_grad.reshape(features.shape), image_back, weight_grad, adaptive[0, 0])


def sum_kernel(parts_ref, out_ref):
    total = parts_ref[0].astype(F32)
    for i in range(1, parts_ref.shape[0]):
        total = total + parts_ref[i].astype(F32)
    total = total.astype(BF16)
    for i in range(out_ref.shape[0]):
        out_ref[i] = total


def sum_call(parts, copies):
    return pl.pallas_call(
        sum_kernel,
        out_shape=jax.ShapeDtypeStruct((copies,) + parts.shape[1:], BF16),
        in_specs=[VM],
        out_specs=VM,
        compiler_params=PART,
        name="sum_parts",
    )(parts)


def solution(mesh):
    clips, devices = mesh.shape["clip"], mesh.shape["row"]
    near = 2 if devices % 2 == 0 else 1
    split = jax.sharding.Mesh(mesh.devices.reshape(clips, devices // near, near), ("clip", "far", "near"))
    rows = P("clip", None, ("far", "near"), None, None)
    return jax.shard_map(
        per_device,
        mesh=split,
        in_specs=(rows, rows, P(), P(), P(), P(), P(), P()),
        out_specs=(rows, rows, P(), P()),
        check_vma=False,
    )
```

```python
import functools

import jax
import jax.numpy as jnp
import numpy as np
from jax import lax
from jax.experimental import pallas as pl
from jax.experimental.pallas import tpu as pltpu
from jax.sharding import PartitionSpec as P

loss_scale = 64.0
epsilon = 0.0001
F32 = jnp.float32
BF16 = jnp.bfloat16
LANES = 128
NN = (((1,), (0,)), ((), ()))
NT = (((1,), (1,)), ((), ()))
TN = (((0,), (0,)), ((), ()))
VM = pl.BlockSpec(memory_space=pltpu.VMEM)
HBM = pl.BlockSpec(memory_space=pl.ANY)
WHOLE = pltpu.CompilerParams(vmem_limit_bytes=60 * 2**20)
MOST = pltpu.CompilerParams(vmem_limit_bytes=48 * 2**20)
PART = pltpu.CompilerParams(vmem_limit_bytes=24 * 2**20)


def up_to(value, step):
    return -(-value // step) * step


def mat(left, right, dims=NN):
    return lax.dot_general(left, right, dims, preferred_element_type=F32)


def slot_of(frame, devices, group):
    return (frame % group) * devices + frame // group


def forward_kernel(
    feat_hbm, target_hbm, weight_hbm, pay_ref, feat_ref, target_ref, weight_ref, weight_scr, target_scr,
    out_ref, sems, *taps_refs, frames, devices, group, cols, lanes, chunks,
):
    pixels = feat_ref.shape[0] // frames
    pieces = pixels // LANES
    pitch = out_ref.shape[1] // devices
    taps = weight_scr.shape[0]
    block_rows = pixels // cols
    copies = [
        pltpu.make_async_copy(weight_hbm, weight_ref, sems.at[frames]),
        pltpu.make_async_copy(target_hbm, target_ref, sems.at[frames + 1]),
    ]
    for slot in range(frames):
        rows = pl.ds((slot % devices * group + slot // devices) * pixels, pixels)
        copies.append(pltpu.make_async_copy(feat_hbm.at[rows, :], feat_ref.at[rows, :], sems.at[slot]))
    for copy in copies:
        copy.start()
    weight_scr[...] = jnp.zeros_like(weight_scr)
    out_ref[...] = jnp.zeros_like(out_ref)
    copies[0].wait()
    for a in range(3):
        for b in range(3):
            at = (a * 3 + b) * 3
            weight_scr[at : at + 3, :] = weight_ref[a, b].astype(F32)
    weight = weight_scr[...].astype(BF16)
    column = lax.broadcasted_iota(jnp.int32, (devices, pixels), 1) % cols

    def finish(part):
        def tap(a, b, o):
            rows = pl.ds(((a * 3 + b) * 3 + o) * devices, devices)
            return jnp.concatenate([taps_refs[part][k, rows, :] for k in range(pieces)], axis=1)

        for o in range(3):
            total = None
            for a in range(3):
                term = tap(a, 1, o)
                term = term + jnp.where(column == 0, 0.0, pltpu.roll(tap(a, 0, o), 1, 1))
                term = term + jnp.where(column == cols - 1, 0.0, pltpu.roll(tap(a, 2, o), pixels - 1, 1))
                term = jnp.concatenate([term, jnp.zeros((devices, lanes - pixels), F32)], axis=1)
                if a < 2:
                    term = pltpu.roll(term, (2 - a) * cols, 1)
                total = term if total is None else total + term
            for k in range(lanes // LANES):
                rows = pl.ds(o * group + part, devices, stride=pitch)
                out_ref[k, rows, :] = total[:, k * LANES : (k + 1) * LANES]

    def edge_rows():
        target_scr[:, 0:cols] = target_ref[...].reshape(target_scr.shape[0], cols).astype(F32)
        edges = []
        for y in (0, block_rows - 1):
            for o in range(3):
                for part in range(group):
                    rows = pl.ds((part * 3 + o) * block_rows + y, devices, stride=group * 3 * block_rows)
                    edges.append(target_scr[rows, :][:, 0:cols])
        edges.append(jnp.zeros((devices, lanes - len(edges) * cols), F32))
        edges = jnp.concatenate(edges, axis=1)
        for k in range(lanes // LANES):
            out_ref[k, pl.ds(3 * group, devices, stride=pitch), :] = edges[:, k * LANES : (k + 1) * LANES]

    copies[1].wait()
    edge_rows()
    step = frames // chunks
    done = 0
    for chunk in range(chunks):
        for slot in range(chunk * step, (chunk + 1) * step):
            copies[2 + slot].wait()
        for slot in range(chunk * step, (chunk + 1) * step):
            frame = slot % devices * group + slot // devices
            product = mat(weight, feat_ref[frame * pixels : (frame + 1) * pixels, :], NT)
            for k in range(pieces):
                rows = pl.ds(slot % devices, taps, stride=devices)
                taps_refs[slot // devices][k, rows, :] = product[:, k * LANES : (k + 1) * LANES]
        while (done + 1) * devices <= chunk * step or (chunk == chunks - 1 and done < group):
            finish(done)
            done += 1
    for k in range(lanes // LANES):
        pay_ref[:, k * LANES : (k + 1) * LANES] = out_ref[k].astype(BF16)


def forward_call(features, target, weight, frames, devices, group, cols, lanes, pitch):
    pixels = features.shape[0] // frames
    channels = features.shape[1]
    chunks = 2
    return pl.pallas_call(
        functools.partial(
            forward_kernel, frames=frames, devices=devices, group=group, cols=cols, lanes=lanes, chunks=chunks
        ),
        out_shape=jax.ShapeDtypeStruct((devices * pitch, lanes), BF16),
        in_specs=[HBM, HBM, HBM],
        out_specs=VM,
        scratch_shapes=[
            pltpu.VMEM(features.shape, BF16),
            pltpu.VMEM(target.shape, BF16),
            pltpu.VMEM(weight.shape, BF16),
            pltpu.VMEM((32, channels), F32),
            pltpu.VMEM((3 * pixels // cols * frames, LANES), F32),
            pltpu.VMEM((lanes // LANES, devices * pitch, LANES), F32),
            pltpu.SemaphoreType.DMA((frames + 2,)),
        ]
        + [pltpu.VMEM((pixels // LANES, 32 * devices, LANES), F32)] * group,
        compiler_params=WHOLE,
        cost_estimate=pl.CostEstimate(flops=2 * features.size * 27, bytes_accessed=2 * features.size, transcendentals=0),
        name="forward_taps",
    )(features, target, weight)


def inner_kernel(pay_ref, target_ref, inner_ref, scr, zin, *, frames, devices, group, block_rows, cols):
    scr[:, 0:cols] = target_ref[...].reshape(scr.shape[0], cols).astype(F32)
    stride = group * 3 * block_rows
    lanes = pay_ref.shape[1]
    pitch = pay_ref.shape[0] // devices
    for k in range(lanes // LANES):
        zin[k] = pay_ref[:, k * LANES : (k + 1) * LANES].astype(F32)
    for o in range(3):
        for part in range(group):
            at = o * frames + part * devices
            rows = [jnp.zeros((devices, cols), F32)]
            rows += [
                scr[pl.ds((part * 3 + o) * block_rows + y, devices, stride=stride), :][:, 0:cols]
                for y in range(block_rows)
            ]
            rows.append(jnp.zeros((devices, lanes - (block_rows + 1) * cols), F32))
            wanted = jnp.concatenate(rows, axis=1)
            lane = lax.broadcasted_iota(jnp.int32, wanted.shape, 1)
            inside = (lane >= 2 * cols) & (lane < block_rows * cols)
            row = pl.ds(o * group + part, devices, stride=pitch)
            own = jnp.concatenate([zin[k, row, :] for k in range(lanes // LANES)], axis=1)
            inner_ref[at : at + devices, :] = loss_scale * (jnp.where(inside, own, 0.0) - wanted)


def inner_call(payload, target, frames, devices, group, block_rows, cols):
    lanes = payload.shape[1]
    return pl.pallas_call(
        functools.partial(
            inner_kernel, frames=frames, devices=devices, group=group, block_rows=block_rows, cols=cols
        ),
        out_shape=jax.ShapeDtypeStruct((3 * frames, lanes), F32),
        in_specs=[VM, VM],
        out_specs=VM,
        scratch_shapes=[
            pltpu.VMEM((frames * 3 * block_rows, LANES), F32),
            pltpu.VMEM((lanes // LANES, payload.shape[0], LANES), F32),
        ],
        compiler_params=PART,
        cost_estimate=pl.CostEstimate(flops=10**8, bytes_accessed=10**6, transcendentals=0),
        name="inner_rows",
    )(payload, target)


def shift_rows(values, step, period):
    size = values.shape[0]
    row = lax.broadcasted_iota(jnp.int32, values.shape, 0) % period
    rolled = pltpu.roll(values, step % size, 0)
    source = row - step
    return jnp.where((source >= 0) & (source < period), rolled, 0.0)


def gate_of(values):
    logistic = 0.5 + 0.5 * jnp.tanh(0.5 * values)
    return (values * logistic).astype(BF16), logistic * (1.0 + values * (1.0 - logistic))


def edge_planes(zin, zout, first, last, devices, group, cols, lanes, pitch):
    row = pl.ds(3 * group, devices, stride=pitch)
    target = jnp.concatenate([zin[k, row, :] for k in range(lanes // LANES)], axis=1)
    outer, inner = [], []
    for e, rows, other, move in ((0, first, last, 1), (1, last, first, -1)):
        for o in range(3):
            for part in range(group):
                at = ((1 - e) * 3 * group + o * group + part) * cols
                near = other[part][:, o * cols : (o + 1) * cols] - target[:, at : at + cols]
                outer.append(shift_rows(loss_scale * near, move, devices))
                inner.append(rows[part][:, o * cols : (o + 1) * cols])
    for i, pieces in enumerate((outer, inner)):
        pieces.append(jnp.zeros((devices, lanes - 6 * group * cols), F32))
        plane = jnp.concatenate(pieces, axis=1)
        for k in range(lanes // LANES):
            zout[k, pl.ds(3 * group + i, devices, stride=pitch), :] = plane[:, k * LANES : (k + 1) * LANES]


def disc_kernel(
    pay_ref, head_ref, window, band_ref, second, unwindow, third_hbm, fourth_hbm, out_ref,
    zin, third, fourth, rows_in, act_one, slope_one, cols_two, act_two, slope_two, act_three, cols_four,
    pull_four, pull_three, pull_two, zout, sems, *, devices, group, cols, block_rows, period,
):
    lanes = pay_ref.shape[1]
    pitch = pay_ref.shape[0] // devices
    span = block_rows + 2
    unit = group * period
    wide = 3 * cols
    d1 = (act_one.shape[1]) // (cols // 2 + 2)
    d2, d3, d4 = second.shape[1], third.shape[1], fourth.shape[1]
    x1, x2, x3 = cols // 2, cols // 4, cols // 8
    x4 = x3 - 1
    quarter = fourth.shape[0] // 4
    copies = [
        pltpu.make_async_copy(
            fourth_hbm.at[pl.ds(a * quarter, quarter), :], fourth.at[pl.ds(a * quarter, quarter), :], sems.at[a]
        )
        for a in range(4)
    ]
    copies.append(pltpu.make_async_copy(third_hbm, third, sems.at[4]))
    for i in (4, 0, 1, 2, 3):
        copies[i].start()
    cells = block_rows // 8
    spot = lambda y, part: pl.ds((y % 8 * group + part) * period + y // 8, devices, stride=cells)
    for k in range(lanes // LANES):
        zin[k] = pay_ref[:, k * LANES : (k + 1) * LANES].astype(F32)
    zout[...] = jnp.zeros_like(zout)
    firsts, lasts = [], []
    for part in range(group):
        planes = []
        for o in range(3):
            pieces = [zin[k, pl.ds(o * group + part, devices, stride=pitch), :] for k in range(lanes // LANES)]
            planes.append(jnp.concatenate(pieces, axis=1))
        lines = [
            jnp.concatenate(
                [plane[:, i * cols : (i + 1) * cols] for plane in planes]
                + [jnp.zeros((devices, 2 * LANES - wide), F32)],
                axis=1,
            )
            for i in range(span)
        ]
        lines[1] = lines[1] + shift_rows(lines[span - 1], 1, devices)
        lines[block_rows] = lines[block_rows] + shift_rows(lines[0], -1, devices)
        for y in range(block_rows):
            for k in range(2):
                rows_in[k, spot(y, part), :] = lines[y + 1][:, k * LANES : (k + 1) * LANES]
        firsts.append(lines[1])
        lasts.append(lines[block_rows])
    image = jnp.concatenate([rows_in[0], rows_in[1]], axis=1)[:, :wide].astype(BF16)
    wins = mat(image, window[...])
    ext = [wins[r * unit : (r + 1) * unit] for r in range(8)]
    ext = [shift_rows(ext[7], 1, period)] + ext + [shift_rows(ext[0], -1, period)]
    width_one = act_one.shape[1]
    strip = 8 * d1
    band = band_ref[...]
    for k in range(-(-width_one // strip)):
        low, high = slice(2 * k * LANES, (2 * k + 1) * LANES), slice((2 * k + 1) * LANES, (2 * k + 2) * LANES)
        left = jnp.concatenate(
            [
                jnp.concatenate([ext[2 * p + h][:, low] + ext[2 * p + h + 1][:, high] for p in range(4)], axis=0)
                for h in (0, 2)
            ],
            axis=1,
        ).astype(BF16)
        start, end = k * strip, min((k + 1) * strip, width_one)
        act, slope = gate_of(mat(left, band[:, : end - start]))
        if k == 0 or end == width_one:
            lane = start + lax.broadcasted_iota(jnp.int32, slope.shape, 1)
            inside = (lane >= d1) & (lane < width_one - d1)
            slope = jnp.where(inside, slope, 0.0)
            act = jnp.where(inside, act.astype(F32), 0.0).astype(BF16)
        slope_one[:, start:end] = slope
        act_one[unit : 5 * unit, start:end] = act
        actual = act.astype(F32)
        act_one[0:unit, start:end] = shift_rows(actual[3 * unit :], 1, period).astype(BF16)
        act_one[5 * unit :, start:end] = shift_rows(actual[:unit], -1, period).astype(BF16)
    for x in range(x2):
        for a in range(4):
            for p in range(2):
                cols_two[(x * 2 + p) * unit : (x * 2 + p + 1) * unit, a * 4 * d1 : (a + 1) * 4 * d1] = act_one[
                    (2 * p + a) * unit : (2 * p + a + 1) * unit, 2 * x * d1 : (2 * x + 4) * d1
                ]
    pre = mat(cols_two[...], second[...])
    act, slope = gate_of(pre)
    slope_two[...] = slope
    act_two[:, 0:d2] = jnp.zeros((4 * unit, d2), BF16)
    act_two[:, (x2 + 1) * d2 :] = jnp.zeros((4 * unit, d2), BF16)
    for x in range(x2):
        block = act[x * 2 * unit : (x + 1) * 2 * unit]
        actual = block.astype(F32)
        at = slice((x + 1) * d2, (x + 2) * d2)
        act_two[unit : 3 * unit, at] = block
        act_two[0:unit, at] = shift_rows(actual[unit:], 1, period).astype(BF16)
        act_two[3 * unit :, at] = shift_rows(actual[:unit], -1, period).astype(BF16)
    left = jnp.concatenate(
        [
            jnp.concatenate([act_two[a * unit : (a + 1) * unit, 2 * x * d2 : (2 * x + 4) * d2] for a in range(4)], axis=1)
            for x in range(x3)
        ],
        axis=0,
    )
    copies[4].wait()
    act, slope_three = gate_of(mat(left, third[...]))
    act_three[:, 0:d3] = jnp.zeros((4 * unit, d3), BF16)
    act_three[:, (x3 + 1) * d3 :] = jnp.zeros((4 * unit, d3), BF16)
    for x in range(x3):
        block = act[x * unit : (x + 1) * unit]
        actual = block.astype(F32)
        at = slice((x + 1) * d3, (x + 2) * d3)
        act_three[unit : 2 * unit, at] = block
        for a in (0, 2, 3):
            act_three[a * unit : (a + 1) * unit, at] = shift_rows(actual, 1 - a, period).astype(BF16)
    for x in range(x4):
        for a in range(4):
            cols_four[x * unit : (x + 1) * unit, a * 4 * d3 : (a + 1) * 4 * d3] = act_three[
                a * unit : (a + 1) * unit, x * d3 : (x + 4) * d3
            ]
    edge_planes(zin, zout, firsts, lasts, devices, group, cols, lanes, pitch)
    row = lax.broadcasted_iota(jnp.int32, (unit, d4), 0) % period
    head = head_ref[...].astype(F32) * -loss_scale
    heads = []
    for x in range(x4):
        total = None
        for a in range(4):
            taps = [head[a * 4 + b : a * 4 + b + 1, :] for b in range(4) if 0 <= x - b + 1 < x4 - 1]
            tap = functools.reduce(lambda u, v: u + v, taps)
            inside = (row - a + 1 >= 0) & (row - a + 1 < period - 2) & (row < period - 1)
            term = jnp.where(inside, jnp.broadcast_to(tap, (unit, d4)), 0.0)
            total = term if total is None else total + term
        heads.append(total)
    pre = None
    for a in range(4):
        copies[a].wait()
        term = mat(cols_four[:, a * quarter : (a + 1) * quarter], fourth[a * quarter : (a + 1) * quarter, :])
        pre = term if pre is None else pre + term
    _, slope = gate_of(pre)
    cot = (jnp.concatenate(heads, axis=0) * slope).astype(BF16)
    pull_four[...] = mat(cot, fourth[...], NT)
    cots = []
    for x in range(x3):
        total = None
        for a in range(4):
            term = None
            for b in range(4):
                source = x - b + 1
                if 0 <= source < x4:
                    piece = pull_four[source * unit : (source + 1) * unit, (a * 4 + b) * d3 : (a * 4 + b + 1) * d3]
                    term = piece if term is None else term + piece
            if a != 1:
                term = shift_rows(term, a - 1, period)
            total = term if total is None else total + term
        cots.append((total * slope_three[x * unit : (x + 1) * unit]).astype(BF16))
    pull_three[...] = mat(jnp.concatenate(cots, axis=0), third[...], NT)
    cots = []
    for x in range(x2):
        terms = []
        for a in range(4):
            term = None
            for b in range(4):
                if (x - b + 1) % 2 == 0 and 0 <= (x - b + 1) // 2 < x3:
                    source = (x - b + 1) // 2
                    piece = pull_three[source * unit : (source + 1) * unit, (a * 4 + b) * d2 : (a * 4 + b + 1) * d2]
                    term = piece if term is None else term + piece
            terms.append(term)
        even = terms[1] + shift_rows(terms[3], 1, period)
        odd = terms[2] + shift_rows(terms[0], -1, period)
        both = jnp.concatenate([even, odd], axis=0)
        cots.append((both * slope_two[x * 2 * unit : (x + 1) * 2 * unit]).astype(BF16))
    pull_two[...] = mat(jnp.concatenate(cots, axis=0), second[...], NT)
    strips = []
    for k in range(x2 + 1):
        terms = {}
        for p in range(2):
            for a in range(4):
                term = None
                if k < x2:
                    term = pull_two[(2 * k + p) * unit : (2 * k + p + 1) * unit, a * 4 * d1 : (a * 4 + 2) * d1]
                if k > 0:
                    other = pull_two[(2 * k - 2 + p) * unit : (2 * k - 1 + p) * unit, (a * 4 + 2) * d1 : (a + 1) * 4 * d1]
                    term = other if term is None else term + other
                terms[p, a] = term
        both = jnp.concatenate(
            [
                terms[0, 1] + shift_rows(terms[1, 3], 1, period),
                terms[0, 2] + terms[1, 0],
                terms[0, 3] + terms[1, 1],
                terms[1, 2] + shift_rows(terms[0, 0], -1, period),
            ],
            axis=0,
        )
        strips.append((both * slope_one[:, 2 * k * d1 : (2 * k + 2) * d1]).astype(BF16))
    cot = jnp.concatenate(strips, axis=1)
    sums = []
    for k in range(-(-width_one // strip)):
        start, end = k * strip, min((k + 1) * strip, width_one)
        pulls = mat(cot[:, start:end], band[:, : end - start], NT)
        groups = []
        for m in range(5):
            terms = [
                pulls[p * unit : (p + 1) * unit, (m - p) * LANES : (m - p + 1) * LANES] for p in range(4) if 0 <= m - p < 2
            ]
            groups.append(functools.reduce(lambda u, v: u + v, terms))
        sums.append(jnp.concatenate(groups, axis=0))
    sums = jnp.concatenate(sums, axis=1)
    upper = sums.astype(BF16)
    lower = (sums - upper.astype(F32)).astype(BF16)
    low = lax.broadcasted_iota(jnp.int32, upper.shape, 1) % LANES < LANES // 2
    blank = jnp.zeros_like(upper)
    split = [jnp.where(low, upper, blank), jnp.where(low, lower, blank), jnp.where(low, blank, upper), jnp.where(low, blank, lower)]
    both = mat(jnp.concatenate(split, axis=0), unwindow[...])
    size = 5 * unit
    odd = both[:size] + both[size : 2 * size]
    even = both[2 * size : 3 * size] + both[3 * size :]
    odd = [odd[m * unit : (m + 1) * unit, :] for m in range(5)]
    even = [even[m * unit : (m + 1) * unit, :] for m in range(5)]
    phases = [even[r // 2] if r % 2 == 0 else odd[(r + 1) // 2] for r in range(8)]
    phases[0] = phases[0] + shift_rows(even[4], 1, period)
    phases[7] = phases[7] + shift_rows(odd[0], -1, period)
    image = jnp.concatenate(phases, axis=0)
    image = jnp.concatenate([image, jnp.zeros((image.shape[0], 2 * LANES - wide), F32)], axis=1)
    for k in range(2):
        rows_in[k] = image[:, k * LANES : (k + 1) * LANES]
    for part in range(group):
        lines = [
            jnp.concatenate([rows_in[k, spot(y, part), :] for k in range(2)], axis=1)[:, :wide]
            for y in range(block_rows)
        ]
        lines = [shift_rows(lines[-1], 1, devices)] + lines + [shift_rows(lines[0], -1, devices)]
        for o in range(3):
            plane = [line[:, o * cols : (o + 1) * cols] for line in lines]
            plane.append(jnp.zeros((devices, lanes - span * cols), F32))
            plane = jnp.concatenate(plane, axis=1)
            for k in range(lanes // LANES):
                zout[k, pl.ds(o * group + part, devices, stride=pitch), :] = plane[:, k * LANES : (k + 1) * LANES]
    for k in range(lanes // LANES):
        out_ref[:, k * LANES : (k + 1) * LANES] = zout[k].astype(BF16)


def window_of(at, cols):
    k, rest = at // LANES, at % LANES
    inner = rest % (LANES // 2)
    colour = jnp.where(inner >= 18, 1, 0) + jnp.where(inner >= 36, 1, 0)
    x = 16 * k - 3 + inner - 18 * colour
    inside = (inner < 54) & (x >= 0) & (x < cols)
    return jnp.where(inside, colour * cols + x, -1), rest // (LANES // 2)


def stage_kernel(first_ref, second_hbm, window, unwindow, second, band, scr, sem, *, cols):
    copy = pltpu.make_async_copy(second_hbm, second, sem.at[0])
    copy.start()
    row = lax.broadcasted_iota(jnp.int32, window.shape, 0)
    lane = lax.broadcasted_iota(jnp.int32, window.shape, 1)
    place, half = window_of(lane // (2 * LANES) * LANES + lane % LANES, cols)
    window[...] = jnp.where((place == row) & (half == lane // LANES % 2), 1.0, 0.0).astype(BF16)
    place, _ = window_of(lax.broadcasted_iota(jnp.int32, unwindow.shape, 0), cols)
    column = lax.broadcasted_iota(jnp.int32, unwindow.shape, 1)
    unwindow[...] = jnp.where(place == column, 1.0, 0.0).astype(BF16)
    d1 = first_ref.shape[-1]
    scr[...] = jnp.zeros_like(scr)
    row = lax.broadcasted_iota(jnp.int32, (18, 8 * d1), 0)
    tap = row - 2 * (lax.broadcasted_iota(jnp.int32, (18, 8 * d1), 1) // d1)
    for a in range(4):
        lines = [first_ref[a, b].astype(F32) for b in range(4)]
        for c in range(3):
            block = jnp.zeros((18, 8 * d1), F32)
            for b in range(4):
                line = jnp.concatenate([lines[b][c : c + 1, :]] * 8, axis=1)
                block = jnp.where(tap == b, jnp.broadcast_to(line, block.shape), block)
            at = a * LANES // 2 + c * 18
            scr[at : at + 18, :] = block
    band[...] = scr[...].astype(BF16)
    copy.wait()


def stage_call(first, second, cols):
    d1, d2 = first.shape[-1], second.shape[-1]
    count = -(-(cols // 2 + 2) // 8)
    shapes = [(3 * cols, count * 2 * LANES), (count * LANES, 3 * cols), (16 * d1, d2), (2 * LANES, 8 * d1)]
    return pl.pallas_call(
        functools.partial(stage_kernel, cols=cols),
        out_shape=tuple(jax.ShapeDtypeStruct(shape, BF16) for shape in shapes),
        in_specs=[VM, HBM],
        out_specs=(VM,) * 4,
        scratch_shapes=[pltpu.VMEM((2 * LANES, 8 * d1), F32), pltpu.SemaphoreType.DMA((1,))],
        compiler_params=PART,
        cost_estimate=pl.CostEstimate(flops=10**8, bytes_accessed=4 * 10**6, transcendentals=0),
        name="stage_weights",
    )(first, second.reshape(16 * d1, d2))


def disc_call(payload, staged, third, fourth, head, devices, group, cols, block_rows):
    period = devices * block_rows // 8
    unit = group * period
    window, unwindow, second, band = staged
    d1, d2, d3, d4 = band.shape[1] // 8, second.shape[1], third.shape[-1], fourth.shape[-1]
    x2, x3 = cols // 4, cols // 8
    x4 = x3 - 1
    width_one = (cols // 2 + 2) * d1
    args = (
        payload,
        head.reshape(16, d4),
        window,
        band,
        second,
        unwindow,
        third.reshape(16 * d2, d3),
        fourth.reshape(16 * d3, d4),
    )
    lanes = payload.shape[1]
    return pl.pallas_call(
        functools.partial(
            disc_kernel, devices=devices, group=group, cols=cols, block_rows=block_rows, period=period
        ),
        out_shape=jax.ShapeDtypeStruct(payload.shape, BF16),
        in_specs=[VM] * 6 + [HBM] * 2,
        out_specs=VM,
        scratch_shapes=[
            pltpu.VMEM((lanes // LANES, payload.shape[0], LANES), F32),
            pltpu.VMEM((16 * d2, d3), BF16),
            pltpu.VMEM((16 * d3, d4), BF16),
            pltpu.VMEM((2, 8 * unit, LANES), F32),
            pltpu.VMEM((6 * unit, width_one), BF16),
            pltpu.VMEM((4 * unit, width_one), F32),
            pltpu.VMEM((x2 * 2 * unit, 16 * d1), BF16),
            pltpu.VMEM((4 * unit, (x2 + 2) * d2), BF16),
            pltpu.VMEM((x2 * 2 * unit, d2), F32),
            pltpu.VMEM((4 * unit, (x3 + 2) * d3), BF16),
            pltpu.VMEM((x4 * unit, 16 * d3), BF16),
            pltpu.VMEM((x4 * unit, 16 * d3), F32),
            pltpu.VMEM((x3 * unit, 16 * d2), F32),
            pltpu.VMEM((x2 * 2 * unit, 16 * d1), F32),
            pltpu.VMEM((lanes // LANES, payload.shape[0], LANES), F32),
            pltpu.SemaphoreType.DMA((5,)),
        ],
        compiler_params=MOST,
        cost_estimate=pl.CostEstimate(flops=4 * 10**9, bytes_accessed=8 * 10**6, transcendentals=10**6),
        name="disc_rows",
    )(*args)


def put_taps(plane, taps_ref, frames, cols, pieces, padded):
    lanes = plane.shape[1]
    column = lax.broadcasted_iota(jnp.int32, plane.shape, 1) % cols
    for b in range(3):
        moved = plane
        if b == 0:
            moved = jnp.where(column == cols - 1, 0.0, pltpu.roll(plane, lanes - 1, 1))
        if b == 2:
            moved = jnp.where(column == 0, 0.0, pltpu.roll(plane, 1, 1))
        for a in range(3):
            turned = moved if a == 2 else pltpu.roll(moved, lanes - (2 - a) * cols, 1)
            for k in range(pieces):
                taps_ref[k, pl.ds((a * 3 + b) * 3 * frames, 3 * frames), :] = turned[:, k * LANES : (k + 1) * LANES]
    for k in range(pieces):
        taps_ref[k, pl.ds(27 * frames, (padded - 27) * frames), :] = jnp.zeros(((padded - 27) * frames, LANES), F32)


def unpack(plane_ref, zin, devices, group):
    lanes = plane_ref.shape[1]
    pitch = plane_ref.shape[0] // devices
    for k in range(lanes // LANES):
        zin[k] = plane_ref[:, k * LANES : (k + 1) * LANES].astype(F32)
    blocks = []
    for o in range(3):
        for part in range(group):
            row = pl.ds(o * group + part, devices, stride=pitch)
            blocks.append(jnp.concatenate([zin[k, row, :] for k in range(lanes // LANES)], axis=1))
    return jnp.concatenate(blocks, axis=0)


def rec_rows(inner_ref, zin, devices, group, cols, block_rows):
    lanes = inner_ref.shape[1]
    pitch = zin.shape[1] // devices
    edges = []
    for i in range(2):
        row = pl.ds(3 * group + i, devices, stride=pitch)
        edges.append(jnp.concatenate([zin[k, row, :] for k in range(lanes // LANES)], axis=1))
    blocks = []
    for i, e in ((0, 0), (1, 0), (1, 1), (0, 1)):
        pieces = [
            edges[i][:, (e * 3 * group + at) * cols : (e * 3 * group + at + 1) * cols] for at in range(3 * group)
        ]
        blocks.append(jnp.concatenate(pieces, axis=0))
    none = lambda count: jnp.zeros((blocks[0].shape[0], count), F32)
    above, first, last, below = blocks
    rest = lanes - (block_rows + 2) * cols
    return inner_ref[...], jnp.concatenate(
        [above, first * loss_scale, none((block_rows - 2) * cols), last * loss_scale, below, none(rest)], axis=1
    )


def both_kernel(
    inner_ref, plane_ref, feat_ref, part_ref, rec_taps, gan_taps, zin, *, frames, devices, group, cols, block_rows
):
    pieces = block_rows * cols // LANES
    put_taps(unpack(plane_ref, zin, devices, group), gan_taps, frames, cols, pieces, 32)
    inner, edges = rec_rows(inner_ref, zin, devices, group, cols, block_rows)
    put_taps(inner + edges, rec_taps, frames, cols, pieces, 32)
    pixels = pieces * LANES
    total = jnp.zeros((64, feat_ref.shape[1]), F32)
    for frame in range(frames):
        rows = pl.ds(slot_of(frame, devices, group), 32, stride=frames)
        taps = jnp.concatenate(
            [
                jnp.concatenate([taps_ref[k, rows, :] for k in range(pieces)], axis=1)
                for taps_ref in (rec_taps, gan_taps)
            ],
            axis=0,
        )
        total = total + mat(taps.astype(BF16), feat_ref[frame * pixels : (frame + 1) * pixels, :])
    blank = jnp.zeros((part_ref.shape[1] - 54, total.shape[1]), F32)
    total = jnp.concatenate([total[0:27], total[32:59], blank], axis=0).astype(BF16)
    for i in range(part_ref.shape[0]):
        part_ref[i] = total


def turn_kernel(
    inner_ref, plane_ref, out_ref, rec_taps, gan_taps, zin, *, frames, devices, group, cols, block_rows
):
    pieces = block_rows * cols // LANES
    pixels = pieces * LANES
    put_taps(unpack(plane_ref, zin, devices, group), gan_taps, frames, cols, pieces, 32)
    inner, edges = rec_rows(inner_ref, zin, devices, group, cols, block_rows)
    put_taps(inner + edges, rec_taps, frames, cols, pieces, 32)
    for pair in range(frames // 2):
        for k in range(pieces):
            parts = []
            for frame in (2 * pair, 2 * pair + 1):
                rows = pl.ds(slot_of(frame, devices, group), 32, stride=frames)
                parts += [rec_taps[k, rows, :], gan_taps[k, rows, :]]
            at = pair * pixels + k * LANES
            out_ref[at : at + LANES, :] = jnp.concatenate(parts, axis=0).T.astype(BF16)


def taps_call(kernel, specs, operands, out, scratch, frames, devices, group, cols, block_rows, flops, name):
    return pl.pallas_call(
        functools.partial(kernel, frames=frames, devices=devices, group=group, cols=cols, block_rows=block_rows),
        out_shape=out,
        in_specs=specs,
        out_specs=jax.tree.map(lambda _: VM, out),
        scratch_shapes=scratch,
        compiler_params=PART,
        cost_estimate=pl.CostEstimate(flops=flops, bytes_accessed=4 * 10**6, transcendentals=0),
        name=name,
    )(*operands)


def final_kernel(
    taps_ref, sums_ref, weight_ref, out_hbm, grad_ref, adapt_ref, weight_scr, both_ref, out_ref, sems, *, pixels, chunk
):
    weight_scr[...] = jnp.zeros_like(weight_scr)
    for a in range(3):
        for b in range(3):
            at = (a * 3 + b) * 3
            weight_scr[at : at + 3, :] = weight_ref[a, b].astype(F32)
    total = sums_ref[0].astype(F32)
    for i in range(1, sums_ref.shape[0]):
        total = total + sums_ref[i].astype(F32)
    rec, gan = total[0:27], total[27:54]
    norm = lambda values: jnp.sqrt(jnp.sum(jnp.sum(values * values, axis=1, keepdims=True), axis=0, keepdims=True))
    adaptive = norm(rec) / (norm(gan) + epsilon)
    grad = (rec + adaptive * gan) / pixels
    for a in range(3):
        for b in range(3):
            at = (a * 3 + b) * 3
            grad_ref[a, b] = grad[at : at + 3, :]
    adapt_ref[...] = adaptive
    weight = weight_scr[...].astype(BF16)
    padded, channels = weight.shape
    scaled = (adaptive * weight.astype(F32)).astype(BF16)
    both_ref[...] = jnp.zeros_like(both_ref)
    both_ref[0:padded, 0:channels] = weight
    both_ref[padded : 2 * padded, 0:channels] = scaled
    both_ref[2 * padded : 3 * padded, channels:] = weight
    both_ref[3 * padded :, channels:] = scaled
    pairs = taps_ref.shape[0] // chunk
    stores = []
    for pair in range(pairs):
        product = mat(taps_ref[pair * chunk : (pair + 1) * chunk], both_ref[...]).astype(BF16)
        rows = pl.ds(2 * pair * chunk, 2 * chunk)
        out_ref[2 * pair * chunk : (2 * pair + 1) * chunk] = product[:, :channels]
        out_ref[(2 * pair + 1) * chunk : (2 * pair + 2) * chunk] = product[:, channels:]
        stores.append(pltpu.make_async_copy(out_ref.at[rows], out_hbm.at[rows], sems.at[pair]))
        stores[-1].start()
    for copy in stores:
        copy.wait()


def final_call(taps, sums, weight, pixels, chunk):
    padded, channels = 32, weight.shape[-1]
    rows = 2 * taps.shape[0]
    return pl.pallas_call(
        functools.partial(final_kernel, pixels=pixels, chunk=chunk),
        out_shape=(
            jax.ShapeDtypeStruct((rows, channels), BF16),
            jax.ShapeDtypeStruct((3, 3, 3, channels), F32),
            jax.ShapeDtypeStruct((1, 1), F32),
        ),
        in_specs=[VM] * 3,
        out_specs=(HBM, VM, VM),
        scratch_shapes=[
            pltpu.VMEM((padded, channels), F32),
            pltpu.VMEM((4 * padded, 2 * channels), BF16),
            pltpu.VMEM((rows, channels), BF16),
            pltpu.SemaphoreType.DMA((rows // (2 * chunk),)),
        ],
        compiler_params=PART,
        cost_estimate=pl.CostEstimate(flops=4 * rows * channels * padded, bytes_accessed=4 * rows * channels, transcendentals=0),
        name="feature_pull",
    )(taps, sums, weight)


def per_device(
    features, target, conv_weight, disc_first, disc_second, disc_third, disc_fourth, disc_head
):
    row = ("far", "near")
    devices = lax.axis_size(row)
    clips = lax.axis_size("clip")
    _, frames, block_rows, cols, channels = features.shape
    group = frames // devices
    pixels = clips * devices * frames * block_rows * cols
    lanes = up_to((block_rows + 2) * cols, LANES)
    pitch = up_to(3 * group + 2, 8)
    sizes = (frames, devices, group, cols, block_rows)
    feats = features.reshape(frames * block_rows * cols, channels)
    wanted = target[0].transpose(0, 2, 1, 3)
    payload = forward_call(feats, wanted, conv_weight, frames, devices, group, cols, lanes, pitch)
    trade = lambda values: lax.all_to_all(
        values.reshape(devices, pitch, lanes), row, split_axis=0, concat_axis=0, tiled=True
    ).reshape(devices * pitch, lanes)
    arrived = trade(payload)
    inner = inner_call(payload, wanted, frames, devices, group, block_rows, cols)
    _, disc_first = lax.optimization_barrier((payload, disc_first))
    staged = stage_call(disc_first, disc_second, cols)
    arrived, inner = lax.optimization_barrier((arrived, inner))
    sent = disc_call(arrived, staged, disc_third, disc_fourth, disc_head, devices, group, cols, block_rows)
    returned = trade(sent)
    taps_scratch = pltpu.VMEM((block_rows * cols // LANES, 32 * frames, LANES), F32)
    plane_scratch = pltpu.VMEM((lanes // LANES, devices * pitch, LANES), F32)
    flops = 4 * features.size * 27
    part = taps_call(
        both_kernel, [VM, VM, VM], (inner, returned, feats),
        jax.ShapeDtypeStruct((clips * lax.axis_size("near"), 56, channels), BF16),
        [taps_scratch, taps_scratch, plane_scratch], *sizes, flops, "both_taps",
    )
    share = lambda values, axes: lax.all_to_all(values, axes, split_axis=0, concat_axis=0, tiled=True)
    sums = share(sum_call(share(part, ("clip", "near")), lax.axis_size("far")), "far")
    taps = taps_call(
        turn_kernel, [VM, VM], (inner, returned), jax.ShapeDtypeStruct((feats.shape[0] // 2, LANES), BF16),
        [taps_scratch, taps_scratch, plane_scratch], *sizes, flops, "turn_taps",
    )
    image_back = returned.reshape(devices, pitch, lanes)[:, : 3 * group, cols : (block_rows + 1) * cols]
    image_back = image_back.reshape(devices, 3, group, block_rows, cols).transpose(0, 2, 3, 1, 4)
    image_back = image_back.reshape(1, frames, block_rows, 3, cols)
    feature_grad, weight_grad, adaptive = final_call(taps, sums, conv_weight, pixels, block_rows * cols)
    return (feature_grad.reshape(features.shape), image_back, weight_grad, adaptive[0, 0])


def sum_kernel(parts_ref, out_ref):
    total = parts_ref[0].astype(F32)
    for i in range(1, parts_ref.shape[0]):
        total = total + parts_ref[i].astype(F32)
    total = total.astype(BF16)
    for i in range(out_ref.shape[0]):
        out_ref[i] = total


def sum_call(parts, copies):
    return pl.pallas_call(
        sum_kernel,
        out_shape=jax.ShapeDtypeStruct((copies,) + parts.shape[1:], BF16),
        in_specs=[VM],
        out_specs=VM,
        compiler_params=PART,
        name="sum_parts",
    )(parts)


def solution(mesh):
    clips, devices = mesh.shape["clip"], mesh.shape["row"]
    near = 2 if devices % 2 == 0 else 1
    split = jax.sharding.Mesh(mesh.devices.reshape(clips, devices // near, near), ("clip", "far", "near"))
    rows = P("clip", None, ("far", "near"), None, None)
    return jax.shard_map(
        per_device,
        mesh=split,
        in_specs=(rows, rows, P(), P(), P(), P(), P(), P()),
        out_specs=(rows, rows, P(), P()),
        check_vma=False,
    )
```

```python
import functools

import jax
import jax.numpy as jnp
import numpy as np
from jax import lax
from jax.experimental import pallas as pl
from jax.experimental.pallas import tpu as pltpu
from jax.sharding import PartitionSpec as P

loss_scale = 64.0
epsilon = 0.0001
F32 = jnp.float32
BF16 = jnp.bfloat16
LANES = 128
NN = (((1,), (0,)), ((), ()))
NT = (((1,), (1,)), ((), ()))
TN = (((0,), (0,)), ((), ()))
VM = pl.BlockSpec(memory_space=pltpu.VMEM)
HBM = pl.BlockSpec(memory_space=pl.ANY)
WHOLE = pltpu.CompilerParams(vmem_limit_bytes=60 * 2**20)
MOST = pltpu.CompilerParams(vmem_limit_bytes=48 * 2**20)
PART = pltpu.CompilerParams(vmem_limit_bytes=24 * 2**20)


def up_to(value, step):
    return -(-value // step) * step


def mat(left, right, dims=NN):
    return lax.dot_general(left, right, dims, preferred_element_type=F32)


def slot_of(frame, devices, group):
    return (frame % group) * devices + frame // group


def forward_kernel(
    feat_hbm, target_hbm, weight_hbm, pay_ref, feat_ref, target_ref, weight_ref, weight_scr, target_scr,
    out_ref, sems, *taps_refs, frames, devices, group, cols, lanes, chunks,
):
    pixels = feat_ref.shape[0] // frames
    pieces = pixels // LANES
    pitch = out_ref.shape[1] // devices
    taps = weight_scr.shape[0]
    block_rows = pixels // cols
    copies = [
        pltpu.make_async_copy(weight_hbm, weight_ref, sems.at[frames]),
        pltpu.make_async_copy(target_hbm, target_ref, sems.at[frames + 1]),
    ]
    for slot in range(frames):
        rows = pl.ds((slot % devices * group + slot // devices) * pixels, pixels)
        copies.append(pltpu.make_async_copy(feat_hbm.at[rows, :], feat_ref.at[rows, :], sems.at[slot]))
    for copy in copies[:1] + copies[2:] + copies[1:2]:
        copy.start()
    weight_scr[...] = jnp.zeros_like(weight_scr)
    out_ref[...] = jnp.zeros_like(out_ref)
    copies[0].wait()
    for a in range(3):
        for b in range(3):
            at = (a * 3 + b) * 3
            weight_scr[at : at + 3, :] = weight_ref[a, b].astype(F32)
    weight = weight_scr[...].astype(BF16)
    column = lax.broadcasted_iota(jnp.int32, (devices, pixels), 1) % cols

    def finish(part):
        def tap(a, b, o):
            rows = pl.ds(((a * 3 + b) * 3 + o) * devices, devices)
            return jnp.concatenate([taps_refs[part][k, rows, :] for k in range(pieces)], axis=1)

        for o in range(3):
            total = None
            for a in range(3):
                term = tap(a, 1, o)
                term = term + jnp.where(column == 0, 0.0, pltpu.roll(tap(a, 0, o), 1, 1))
                term = term + jnp.where(column == cols - 1, 0.0, pltpu.roll(tap(a, 2, o), pixels - 1, 1))
                term = jnp.concatenate([term, jnp.zeros((devices, lanes - pixels), F32)], axis=1)
                if a < 2:
                    term = pltpu.roll(term, (2 - a) * cols, 1)
                total = term if total is None else total + term
            for k in range(lanes // LANES):
                rows = pl.ds(o * group + part, devices, stride=pitch)
                out_ref[k, rows, :] = total[:, k * LANES : (k + 1) * LANES]

    def edge_rows():
        target_scr[:, 0:cols] = target_ref[...].reshape(target_scr.shape[0], cols).astype(F32)
        edges = []
        for y in (0, block_rows - 1):
            for o in range(3):
                for part in range(group):
                    rows = pl.ds((part * 3 + o) * block_rows + y, devices, stride=group * 3 * block_rows)
                    edges.append(target_scr[rows, :][:, 0:cols])
        edges.append(jnp.zeros((devices, lanes - len(edges) * cols), F32))
        edges = jnp.concatenate(edges, axis=1)
        for k in range(lanes // LANES):
            out_ref[k, pl.ds(3 * group, devices, stride=pitch), :] = edges[:, k * LANES : (k + 1) * LANES]

    step = frames // chunks
    done = 0
    for chunk in range(chunks):
        for slot in range(chunk * step, (chunk + 1) * step):
            copies[2 + slot].wait()
        if chunk == chunks - 1:
            copies[1].wait()
        for slot in range(chunk * step, (chunk + 1) * step):
            frame = slot % devices * group + slot // devices
            product = mat(weight, feat_ref[frame * pixels : (frame + 1) * pixels, :], NT)
            for k in range(pieces):
                rows = pl.ds(slot % devices, taps, stride=devices)
                taps_refs[slot // devices][k, rows, :] = product[:, k * LANES : (k + 1) * LANES]
        if chunk == chunks - 1:
            edge_rows()
        while (done + 1) * devices <= chunk * step or (chunk == chunks - 1 and done < group):
            finish(done)
            done += 1
    for k in range(lanes // LANES):
        pay_ref[:, k * LANES : (k + 1) * LANES] = out_ref[k].astype(BF16)


def forward_call(features, target, weight, frames, devices, group, cols, lanes, pitch):
    pixels = features.shape[0] // frames
    channels = features.shape[1]
    chunks = 2
    return pl.pallas_call(
        functools.partial(
            forward_kernel, frames=frames, devices=devices, group=group, cols=cols, lanes=lanes, chunks=chunks
        ),
        out_shape=jax.ShapeDtypeStruct((devices * pitch, lanes), BF16),
        in_specs=[HBM, HBM, HBM],
        out_specs=VM,
        scratch_shapes=[
            pltpu.VMEM(features.shape, BF16),
            pltpu.VMEM(target.shape, BF16),
            pltpu.VMEM(weight.shape, BF16),
            pltpu.VMEM((32, channels), F32),
            pltpu.VMEM((3 * pixels // cols * frames, LANES), F32),
            pltpu.VMEM((lanes // LANES, devices * pitch, LANES), F32),
            pltpu.SemaphoreType.DMA((frames + 2,)),
        ]
        + [pltpu.VMEM((pixels // LANES, 32 * devices, LANES), F32)] * group,
        compiler_params=WHOLE,
        cost_estimate=pl.CostEstimate(flops=2 * features.size * 27, bytes_accessed=2 * features.size, transcendentals=0),
        name="forward_taps",
    )(features, target, weight)


def inner_kernel(pay_ref, target_ref, inner_ref, scr, zin, *, frames, devices, group, block_rows, cols):
    scr[:, 0:cols] = target_ref[...].reshape(scr.shape[0], cols).astype(F32)
    stride = group * 3 * block_rows
    lanes = pay_ref.shape[1]
    pitch = pay_ref.shape[0] // devices
    for k in range(lanes // LANES):
        zin[k] = pay_ref[:, k * LANES : (k + 1) * LANES].astype(F32)
    for o in range(3):
        for part in range(group):
            at = o * frames + part * devices
            rows = [jnp.zeros((devices, cols), F32)]
            rows += [
                scr[pl.ds((part * 3 + o) * block_rows + y, devices, stride=stride), :][:, 0:cols]
                for y in range(block_rows)
            ]
            rows.append(jnp.zeros((devices, lanes - (block_rows + 1) * cols), F32))
            wanted = jnp.concatenate(rows, axis=1)
            lane = lax.broadcasted_iota(jnp.int32, wanted.shape, 1)
            inside = (lane >= 2 * cols) & (lane < block_rows * cols)
            row = pl.ds(o * group + part, devices, stride=pitch)
            own = jnp.concatenate([zin[k, row, :] for k in range(lanes // LANES)], axis=1)
            inner_ref[at : at + devices, :] = loss_scale * (jnp.where(inside, own, 0.0) - wanted)


def inner_call(payload, target, frames, devices, group, block_rows, cols):
    lanes = payload.shape[1]
    return pl.pallas_call(
        functools.partial(
            inner_kernel, frames=frames, devices=devices, group=group, block_rows=block_rows, cols=cols
        ),
        out_shape=jax.ShapeDtypeStruct((3 * frames, lanes), F32),
        in_specs=[VM, VM],
        out_specs=VM,
        scratch_shapes=[
            pltpu.VMEM((frames * 3 * block_rows, LANES), F32),
            pltpu.VMEM((lanes // LANES, payload.shape[0], LANES), F32),
        ],
        compiler_params=PART,
        cost_estimate=pl.CostEstimate(flops=10**8, bytes_accessed=10**6, transcendentals=0),
        name="inner_rows",
    )(payload, target)


def shift_rows(values, step, period):
    size = values.shape[0]
    row = lax.broadcasted_iota(jnp.int32, values.shape, 0) % period
    rolled = pltpu.roll(values, step % size, 0)
    source = row - step
    return jnp.where((source >= 0) & (source < period), rolled, 0.0)


def gate_of(values):
    logistic = 0.5 + 0.5 * jnp.tanh(0.5 * values)
    return (values * logistic).astype(BF16), logistic * (1.0 + values * (1.0 - logistic))


def edge_planes(zin, zout, first, last, devices, group, cols, lanes, pitch):
    row = pl.ds(3 * group, devices, stride=pitch)
    target = jnp.concatenate([zin[k, row, :] for k in range(lanes // LANES)], axis=1)
    outer, inner = [], []
    for e, rows, other, move in ((0, first, last, 1), (1, last, first, -1)):
        for o in range(3):
            for part in range(group):
                at = ((1 - e) * 3 * group + o * group + part) * cols
                near = other[part][:, o * cols : (o + 1) * cols] - target[:, at : at + cols]
                outer.append(shift_rows(loss_scale * near, move, devices))
                inner.append(rows[part][:, o * cols : (o + 1) * cols])
    for i, pieces in enumerate((outer, inner)):
        pieces.append(jnp.zeros((devices, lanes - 6 * group * cols), F32))
        plane = jnp.concatenate(pieces, axis=1)
        for k in range(lanes // LANES):
            zout[k, pl.ds(3 * group + i, devices, stride=pitch), :] = plane[:, k * LANES : (k + 1) * LANES]


def disc_kernel(
    pay_ref, head_ref, window, band_ref, second, unwindow, third_hbm, fourth_hbm, out_ref,
    zin, third, fourth, rows_in, act_one, slope_one, cols_two, act_two, slope_two, act_three, cols_four,
    pull_four, pull_three, pull_two, zout, sems, *, devices, group, cols, block_rows, period,
):
    lanes = pay_ref.shape[1]
    pitch = pay_ref.shape[0] // devices
    span = block_rows + 2
    unit = group * period
    wide = 3 * cols
    d1 = (act_one.shape[1]) // (cols // 2 + 2)
    d2, d3, d4 = second.shape[1], third.shape[1], fourth.shape[1]
    x1, x2, x3 = cols // 2, cols // 4, cols // 8
    x4 = x3 - 1
    quarter = fourth.shape[0] // 4
    copies = [
        pltpu.make_async_copy(
            fourth_hbm.at[pl.ds(a * quarter, quarter), :], fourth.at[pl.ds(a * quarter, quarter), :], sems.at[a]
        )
        for a in range(4)
    ]
    copies.append(pltpu.make_async_copy(third_hbm, third, sems.at[4]))
    for i in (4, 0, 1, 2, 3):
        copies[i].start()
    cells = block_rows // 8
    spot = lambda y, part: pl.ds((y % 8 * group + part) * period + y // 8, devices, stride=cells)
    for k in range(lanes // LANES):
        zin[k] = pay_ref[:, k * LANES : (k + 1) * LANES].astype(F32)
    zout[...] = jnp.zeros_like(zout)
    firsts, lasts = [], []
    for part in range(group):
        planes = []
        for o in range(3):
            pieces = [zin[k, pl.ds(o * group + part, devices, stride=pitch), :] for k in range(lanes // LANES)]
            planes.append(jnp.concatenate(pieces, axis=1))
        lines = [
            jnp.concatenate(
                [plane[:, i * cols : (i + 1) * cols] for plane in planes]
                + [jnp.zeros((devices, 2 * LANES - wide), F32)],
                axis=1,
            )
            for i in range(span)
        ]
        lines[1] = lines[1] + shift_rows(lines[span - 1], 1, devices)
        lines[block_rows] = lines[block_rows] + shift_rows(lines[0], -1, devices)
        for y in range(block_rows):
            for k in range(2):
                rows_in[k, spot(y, part), :] = lines[y + 1][:, k * LANES : (k + 1) * LANES]
        firsts.append(lines[1])
        lasts.append(lines[block_rows])
    image = jnp.concatenate([rows_in[0], rows_in[1]], axis=1)[:, :wide].astype(BF16)
    wins = mat(image, window[...])
    ext = [wins[r * unit : (r + 1) * unit] for r in range(8)]
    ext = [shift_rows(ext[7], 1, period)] + ext + [shift_rows(ext[0], -1, period)]
    width_one = act_one.shape[1]
    strip = 8 * d1
    band = band_ref[...]
    for k in range(-(-width_one // strip)):
        low, high = slice(2 * k * LANES, (2 * k + 1) * LANES), slice((2 * k + 1) * LANES, (2 * k + 2) * LANES)
        left = jnp.concatenate(
            [
                jnp.concatenate([ext[2 * p + h][:, low] + ext[2 * p + h + 1][:, high] for p in range(4)], axis=0)
                for h in (0, 2)
            ],
            axis=1,
        ).astype(BF16)
        start, end = k * strip, min((k + 1) * strip, width_one)
        act, slope = gate_of(mat(left, band[:, : end - start]))
        if k == 0 or end == width_one:
            lane = start + lax.broadcasted_iota(jnp.int32, slope.shape, 1)
            inside = (lane >= d1) & (lane < width_one - d1)
            slope = jnp.where(inside, slope, 0.0)
            act = jnp.where(inside, act.astype(F32), 0.0).astype(BF16)
        slope_one[:, start:end] = slope
        act_one[unit : 5 * unit, start:end] = act
        actual = act.astype(F32)
        act_one[0:unit, start:end] = shift_rows(actual[3 * unit :], 1, period).astype(BF16)
        act_one[5 * unit :, start:end] = shift_rows(actual[:unit], -1, period).astype(BF16)
    for x in range(x2):
        for a in range(4):
            for p in range(2):
                cols_two[(x * 2 + p) * unit : (x * 2 + p + 1) * unit, a * 4 * d1 : (a + 1) * 4 * d1] = act_one[
                    (2 * p + a) * unit : (2 * p + a + 1) * unit, 2 * x * d1 : (2 * x + 4) * d1
                ]
    pre = mat(cols_two[...], second[...])
    act, slope = gate_of(pre)
    slope_two[...] = slope
    act_two[:, 0:d2] = jnp.zeros((4 * unit, d2), BF16)
    act_two[:, (x2 + 1) * d2 :] = jnp.zeros((4 * unit, d2), BF16)
    for x in range(x2):
        block = act[x * 2 * unit : (x + 1) * 2 * unit]
        actual = block.astype(F32)
        at = slice((x + 1) * d2, (x + 2) * d2)
        act_two[unit : 3 * unit, at] = block
        act_two[0:unit, at] = shift_rows(actual[unit:], 1, period).astype(BF16)
        act_two[3 * unit :, at] = shift_rows(actual[:unit], -1, period).astype(BF16)
    left = jnp.concatenate(
        [
            jnp.concatenate([act_two[a * unit : (a + 1) * unit, 2 * x * d2 : (2 * x + 4) * d2] for a in range(4)], axis=1)
            for x in range(x3)
        ],
        axis=0,
    )
    copies[4].wait()
    act, slope_three = gate_of(mat(left, third[...]))
    act_three[:, 0:d3] = jnp.zeros((4 * unit, d3), BF16)
    act_three[:, (x3 + 1) * d3 :] = jnp.zeros((4 * unit, d3), BF16)
    for x in range(x3):
        block = act[x * unit : (x + 1) * unit]
        actual = block.astype(F32)
        at = slice((x + 1) * d3, (x + 2) * d3)
        act_three[unit : 2 * unit, at] = block
        for a in (0, 2, 3):
            act_three[a * unit : (a + 1) * unit, at] = shift_rows(actual, 1 - a, period).astype(BF16)
    for x in range(x4):
        for a in range(4):
            cols_four[x * unit : (x + 1) * unit, a * 4 * d3 : (a + 1) * 4 * d3] = act_three[
                a * unit : (a + 1) * unit, x * d3 : (x + 4) * d3
            ]
    edge_planes(zin, zout, firsts, lasts, devices, group, cols, lanes, pitch)
    row = lax.broadcasted_iota(jnp.int32, (unit, d4), 0) % period
    head = head_ref[...].astype(F32) * -loss_scale
    heads = []
    for x in range(x4):
        total = None
        for a in range(4):
            taps = [head[a * 4 + b : a * 4 + b + 1, :] for b in range(4) if 0 <= x - b + 1 < x4 - 1]
            tap = functools.reduce(lambda u, v: u + v, taps)
            inside = (row - a + 1 >= 0) & (row - a + 1 < period - 2) & (row < period - 1)
            term = jnp.where(inside, jnp.broadcast_to(tap, (unit, d4)), 0.0)
            total = term if total is None else total + term
        heads.append(total)
    pre = None
    for a in range(4):
        copies[a].wait()
        term = mat(cols_four[:, a * quarter : (a + 1) * quarter], fourth[a * quarter : (a + 1) * quarter, :])
        pre = term if pre is None else pre + term
    _, slope = gate_of(pre)
    cot = (jnp.concatenate(heads, axis=0) * slope).astype(BF16)
    pull_four[...] = mat(cot, fourth[...], NT)
    cots = []
    for x in range(x3):
        total = None
        for a in range(4):
            term = None
            for b in range(4):
                source = x - b + 1
                if 0 <= source < x4:
                    piece = pull_four[source * unit : (source + 1) * unit, (a * 4 + b) * d3 : (a * 4 + b + 1) * d3]
                    term = piece if term is None else term + piece
            if a != 1:
                term = shift_rows(term, a - 1, period)
            total = term if total is None else total + term
        cots.append((total * slope_three[x * unit : (x + 1) * unit]).astype(BF16))
    pull_three[...] = mat(jnp.concatenate(cots, axis=0), third[...], NT)
    cots = []
    for x in range(x2):
        terms = []
        for a in range(4):
            term = None
            for b in range(4):
                if (x - b + 1) % 2 == 0 and 0 <= (x - b + 1) // 2 < x3:
                    source = (x - b + 1) // 2
                    piece = pull_three[source * unit : (source + 1) * unit, (a * 4 + b) * d2 : (a * 4 + b + 1) * d2]
                    term = piece if term is None else term + piece
            terms.append(term)
        even = terms[1] + shift_rows(terms[3], 1, period)
        odd = terms[2] + shift_rows(terms[0], -1, period)
        both = jnp.concatenate([even, odd], axis=0)
        cots.append((both * slope_two[x * 2 * unit : (x + 1) * 2 * unit]).astype(BF16))
    pull_two[...] = mat(jnp.concatenate(cots, axis=0), second[...], NT)
    strips = []
    for k in range(x2 + 1):
        terms = {}
        for p in range(2):
            for a in range(4):
                term = None
                if k < x2:
                    term = pull_two[(2 * k + p) * unit : (2 * k + p + 1) * unit, a * 4 * d1 : (a * 4 + 2) * d1]
                if k > 0:
                    other = pull_two[(2 * k - 2 + p) * unit : (2 * k - 1 + p) * unit, (a * 4 + 2) * d1 : (a + 1) * 4 * d1]
                    term = other if term is None else term + other
                terms[p, a] = term
        both = jnp.concatenate(
            [
                terms[0, 1] + shift_rows(terms[1, 3], 1, period),
                terms[0, 2] + terms[1, 0],
                terms[0, 3] + terms[1, 1],
                terms[1, 2] + shift_rows(terms[0, 0], -1, period),
            ],
            axis=0,
        )
        strips.append((both * slope_one[:, 2 * k * d1 : (2 * k + 2) * d1]).astype(BF16))
    cot = jnp.concatenate(strips, axis=1)
    sums = []
    for k in range(-(-width_one // strip)):
        start, end = k * strip, min((k + 1) * strip, width_one)
        pulls = mat(cot[:, start:end], band[:, : end - start], NT)
        groups = []
        for m in range(5):
            terms = [
                pulls[p * unit : (p + 1) * unit, (m - p) * LANES : (m - p + 1) * LANES] for p in range(4) if 0 <= m - p < 2
            ]
            groups.append(functools.reduce(lambda u, v: u + v, terms))
        sums.append(jnp.concatenate(groups, axis=0))
    sums = jnp.concatenate(sums, axis=1)
    upper = sums.astype(BF16)
    lower = (sums - upper.astype(F32)).astype(BF16)
    low = lax.broadcasted_iota(jnp.int32, upper.shape, 1) % LANES < LANES // 2
    blank = jnp.zeros_like(upper)
    split = [jnp.where(low, upper, blank), jnp.where(low, lower, blank), jnp.where(low, blank, upper), jnp.where(low, blank, lower)]
    both = mat(jnp.concatenate(split, axis=0), unwindow[...])
    size = 5 * unit
    odd = both[:size] + both[size : 2 * size]
    even = both[2 * size : 3 * size] + both[3 * size :]
    odd = [odd[m * unit : (m + 1) * unit, :] for m in range(5)]
    even = [even[m * unit : (m + 1) * unit, :] for m in range(5)]
    phases = [even[r // 2] if r % 2 == 0 else odd[(r + 1) // 2] for r in range(8)]
    phases[0] = phases[0] + shift_rows(even[4], 1, period)
    phases[7] = phases[7] + shift_rows(odd[0], -1, period)
    image = jnp.concatenate(phases, axis=0)
    image = jnp.concatenate([image, jnp.zeros((image.shape[0], 2 * LANES - wide), F32)], axis=1)
    for k in range(2):
        rows_in[k] = image[:, k * LANES : (k + 1) * LANES]
    for part in range(group):
        lines = [
            jnp.concatenate([rows_in[k, spot(y, part), :] for k in range(2)], axis=1)[:, :wide]
            for y in range(block_rows)
        ]
        lines = [shift_rows(lines[-1], 1, devices)] + lines + [shift_rows(lines[0], -1, devices)]
        for o in range(3):
            plane = [line[:, o * cols : (o + 1) * cols] for line in lines]
            plane.append(jnp.zeros((devices, lanes - span * cols), F32))
            plane = jnp.concatenate(plane, axis=1)
            for k in range(lanes // LANES):
                zout[k, pl.ds(o * group + part, devices, stride=pitch), :] = plane[:, k * LANES : (k + 1) * LANES]
    for k in range(lanes // LANES):
        out_ref[:, k * LANES : (k + 1) * LANES] = zout[k].astype(BF16)


def window_of(at, cols):
    k, rest = at // LANES, at % LANES
    inner = rest % (LANES // 2)
    colour = jnp.where(inner >= 18, 1, 0) + jnp.where(inner >= 36, 1, 0)
    x = 16 * k - 3 + inner - 18 * colour
    inside = (inner < 54) & (x >= 0) & (x < cols)
    return jnp.where(inside, colour * cols + x, -1), rest // (LANES // 2)


def stage_kernel(first_ref, second_hbm, window, unwindow, second, band, scr, sem, *, cols):
    copy = pltpu.make_async_copy(second_hbm, second, sem.at[0])
    copy.start()
    row = lax.broadcasted_iota(jnp.int32, window.shape, 0)
    lane = lax.broadcasted_iota(jnp.int32, window.shape, 1)
    place, half = window_of(lane // (2 * LANES) * LANES + lane % LANES, cols)
    window[...] = jnp.where((place == row) & (half == lane // LANES % 2), 1.0, 0.0).astype(BF16)
    place, _ = window_of(lax.broadcasted_iota(jnp.int32, unwindow.shape, 0), cols)
    column = lax.broadcasted_iota(jnp.int32, unwindow.shape, 1)
    unwindow[...] = jnp.where(place == column, 1.0, 0.0).astype(BF16)
    d1 = first_ref.shape[-1]
    scr[...] = jnp.zeros_like(scr)
    row = lax.broadcasted_iota(jnp.int32, (18, 8 * d1), 0)
    tap = row - 2 * (lax.broadcasted_iota(jnp.int32, (18, 8 * d1), 1) // d1)
    for a in range(4):
        lines = [first_ref[a, b].astype(F32) for b in range(4)]
        for c in range(3):
            block = jnp.zeros((18, 8 * d1), F32)
            for b in range(4):
                line = jnp.concatenate([lines[b][c : c + 1, :]] * 8, axis=1)
                block = jnp.where(tap == b, jnp.broadcast_to(line, block.shape), block)
            at = a * LANES // 2 + c * 18
            scr[at : at + 18, :] = block
    band[...] = scr[...].astype(BF16)
    copy.wait()


def stage_call(first, second, cols):
    d1, d2 = first.shape[-1], second.shape[-1]
    count = -(-(cols // 2 + 2) // 8)
    shapes = [(3 * cols, count * 2 * LANES), (count * LANES, 3 * cols), (16 * d1, d2), (2 * LANES, 8 * d1)]
    return pl.pallas_call(
        functools.partial(stage_kernel, cols=cols),
        out_shape=tuple(jax.ShapeDtypeStruct(shape, BF16) for shape in shapes),
        in_specs=[VM, HBM],
        out_specs=(VM,) * 4,
        scratch_shapes=[pltpu.VMEM((2 * LANES, 8 * d1), F32), pltpu.SemaphoreType.DMA((1,))],
        compiler_params=PART,
        cost_estimate=pl.CostEstimate(flops=10**8, bytes_accessed=4 * 10**6, transcendentals=0),
        name="stage_weights",
    )(first, second.reshape(16 * d1, d2))


def disc_call(payload, staged, third, fourth, head, devices, group, cols, block_rows):
    period = devices * block_rows // 8
    unit = group * period
    window, unwindow, second, band = staged
    d1, d2, d3, d4 = band.shape[1] // 8, second.shape[1], third.shape[-1], fourth.shape[-1]
    x2, x3 = cols // 4, cols // 8
    x4 = x3 - 1
    width_one = (cols // 2 + 2) * d1
    args = (
        payload,
        head.reshape(16, d4),
        window,
        band,
        second,
        unwindow,
        third.reshape(16 * d2, d3),
        fourth.reshape(16 * d3, d4),
    )
    lanes = payload.shape[1]
    return pl.pallas_call(
        functools.partial(
            disc_kernel, devices=devices, group=group, cols=cols, block_rows=block_rows, period=period
        ),
        out_shape=jax.ShapeDtypeStruct(payload.shape, BF16),
        in_specs=[VM] * 6 + [HBM] * 2,
        out_specs=VM,
        scratch_shapes=[
            pltpu.VMEM((lanes // LANES, payload.shape[0], LANES), F32),
            pltpu.VMEM((16 * d2, d3), BF16),
            pltpu.VMEM((16 * d3, d4), BF16),
            pltpu.VMEM((2, 8 * unit, LANES), F32),
            pltpu.VMEM((6 * unit, width_one), BF16),
            pltpu.VMEM((4 * unit, width_one), F32),
            pltpu.VMEM((x2 * 2 * unit, 16 * d1), BF16),
            pltpu.VMEM((4 * unit, (x2 + 2) * d2), BF16),
            pltpu.VMEM((x2 * 2 * unit, d2), F32),
            pltpu.VMEM((4 * unit, (x3 + 2) * d3), BF16),
            pltpu.VMEM((x4 * unit, 16 * d3), BF16),
            pltpu.VMEM((x4 * unit, 16 * d3), F32),
            pltpu.VMEM((x3 * unit, 16 * d2), F32),
            pltpu.VMEM((x2 * 2 * unit, 16 * d1), F32),
            pltpu.VMEM((lanes // LANES, payload.shape[0], LANES), F32),
            pltpu.SemaphoreType.DMA((5,)),
        ],
        compiler_params=MOST,
        cost_estimate=pl.CostEstimate(flops=4 * 10**9, bytes_accessed=8 * 10**6, transcendentals=10**6),
        name="disc_rows",
    )(*args)


def put_taps(plane, taps_ref, frames, cols, pieces, padded):
    lanes = plane.shape[1]
    column = lax.broadcasted_iota(jnp.int32, plane.shape, 1) % cols
    for b in range(3):
        moved = plane
        if b == 0:
            moved = jnp.where(column == cols - 1, 0.0, pltpu.roll(plane, lanes - 1, 1))
        if b == 2:
            moved = jnp.where(column == 0, 0.0, pltpu.roll(plane, 1, 1))
        for a in range(3):
            turned = moved if a == 2 else pltpu.roll(moved, lanes - (2 - a) * cols, 1)
            for k in range(pieces):
                taps_ref[k, pl.ds((a * 3 + b) * 3 * frames, 3 * frames), :] = turned[:, k * LANES : (k + 1) * LANES]
    for k in range(pieces):
        taps_ref[k, pl.ds(27 * frames, (padded - 27) * frames), :] = jnp.zeros(((padded - 27) * frames, LANES), F32)


def unpack(plane_ref, zin, devices, group):
    lanes = plane_ref.shape[1]
    pitch = plane_ref.shape[0] // devices
    for k in range(lanes // LANES):
        zin[k] = plane_ref[:, k * LANES : (k + 1) * LANES].astype(F32)
    blocks = []
    for o in range(3):
        for part in range(group):
            row = pl.ds(o * group + part, devices, stride=pitch)
            blocks.append(jnp.concatenate([zin[k, row, :] for k in range(lanes // LANES)], axis=1))
    return jnp.concatenate(blocks, axis=0)


def rec_rows(inner_ref, zin, devices, group, cols, block_rows):
    lanes = inner_ref.shape[1]
    pitch = zin.shape[1] // devices
    edges = []
    for i in range(2):
        row = pl.ds(3 * group + i, devices, stride=pitch)
        edges.append(jnp.concatenate([zin[k, row, :] for k in range(lanes // LANES)], axis=1))
    blocks = []
    for i, e in ((0, 0), (1, 0), (1, 1), (0, 1)):
        pieces = [
            edges[i][:, (e * 3 * group + at) * cols : (e * 3 * group + at + 1) * cols] for at in range(3 * group)
        ]
        blocks.append(jnp.concatenate(pieces, axis=0))
    none = lambda count: jnp.zeros((blocks[0].shape[0], count), F32)
    above, first, last, below = blocks
    rest = lanes - (block_rows + 2) * cols
    return inner_ref[...], jnp.concatenate(
        [above, first * loss_scale, none((block_rows - 2) * cols), last * loss_scale, below, none(rest)], axis=1
    )


def both_kernel(
    inner_ref, plane_ref, feat_ref, part_ref, rec_taps, gan_taps, zin, *, frames, devices, group, cols, block_rows
):
    pieces = block_rows * cols // LANES
    put_taps(unpack(plane_ref, zin, devices, group), gan_taps, frames, cols, pieces, 32)
    inner, edges = rec_rows(inner_ref, zin, devices, group, cols, block_rows)
    put_taps(inner + edges, rec_taps, frames, cols, pieces, 32)
    pixels = pieces * LANES
    total = jnp.zeros((64, feat_ref.shape[1]), F32)
    for frame in range(frames):
        rows = pl.ds(slot_of(frame, devices, group), 32, stride=frames)
        taps = jnp.concatenate(
            [
                jnp.concatenate([taps_ref[k, rows, :] for k in range(pieces)], axis=1)
                for taps_ref in (rec_taps, gan_taps)
            ],
            axis=0,
        )
        total = total + mat(taps.astype(BF16), feat_ref[frame * pixels : (frame + 1) * pixels, :])
    blank = jnp.zeros((part_ref.shape[1] - 54, total.shape[1]), F32)
    total = jnp.concatenate([total[0:27], total[32:59], blank], axis=0).astype(BF16)
    for i in range(part_ref.shape[0]):
        part_ref[i] = total


def turn_kernel(
    inner_ref, plane_ref, out_ref, rec_taps, gan_taps, zin, *, frames, devices, group, cols, block_rows
):
    pieces = block_rows * cols // LANES
    pixels = pieces * LANES
    put_taps(unpack(plane_ref, zin, devices, group), gan_taps, frames, cols, pieces, 32)
    inner, edges = rec_rows(inner_ref, zin, devices, group, cols, block_rows)
    put_taps(inner + edges, rec_taps, frames, cols, pieces, 32)
    for pair in range(frames // 2):
        for k in range(pieces):
            parts = []
            for frame in (2 * pair, 2 * pair + 1):
                rows = pl.ds(slot_of(frame, devices, group), 32, stride=frames)
                parts += [rec_taps[k, rows, :], gan_taps[k, rows, :]]
            at = pair * pixels + k * LANES
            out_ref[at : at + LANES, :] = jnp.concatenate(parts, axis=0).T.astype(BF16)


def taps_call(kernel, specs, operands, out, scratch, frames, devices, group, cols, block_rows, flops, name):
    return pl.pallas_call(
        functools.partial(kernel, frames=frames, devices=devices, group=group, cols=cols, block_rows=block_rows),
        out_shape=out,
        in_specs=specs,
        out_specs=jax.tree.map(lambda _: VM, out),
        scratch_shapes=scratch,
        compiler_params=PART,
        cost_estimate=pl.CostEstimate(flops=flops, bytes_accessed=4 * 10**6, transcendentals=0),
        name=name,
    )(*operands)


def final_kernel(
    taps_ref, sums_ref, weight_ref, out_hbm, grad_ref, adapt_ref, weight_scr, both_ref, out_ref, sems, *, pixels, chunk
):
    weight_scr[...] = jnp.zeros_like(weight_scr)
    for a in range(3):
        for b in range(3):
            at = (a * 3 + b) * 3
            weight_scr[at : at + 3, :] = weight_ref[a, b].astype(F32)
    total = sums_ref[0].astype(F32)
    for i in range(1, sums_ref.shape[0]):
        total = total + sums_ref[i].astype(F32)
    rec, gan = total[0:27], total[27:54]
    norm = lambda values: jnp.sqrt(jnp.sum(jnp.sum(values * values, axis=1, keepdims=True), axis=0, keepdims=True))
    adaptive = norm(rec) / (norm(gan) + epsilon)
    grad = (rec + adaptive * gan) / pixels
    for a in range(3):
        for b in range(3):
            at = (a * 3 + b) * 3
            grad_ref[a, b] = grad[at : at + 3, :]
    adapt_ref[...] = adaptive
    weight = weight_scr[...].astype(BF16)
    padded, channels = weight.shape
    scaled = (adaptive * weight.astype(F32)).astype(BF16)
    both_ref[...] = jnp.zeros_like(both_ref)
    both_ref[0:padded, 0:channels] = weight
    both_ref[padded : 2 * padded, 0:channels] = scaled
    both_ref[2 * padded : 3 * padded, channels:] = weight
    both_ref[3 * padded :, channels:] = scaled
    pairs = taps_ref.shape[0] // chunk
    stores = []
    for pair in range(pairs):
        product = mat(taps_ref[pair * chunk : (pair + 1) * chunk], both_ref[...]).astype(BF16)
        for i in range(2):
            at = (2 * pair + i) * chunk
            out_ref[at : at + chunk] = product[:, i * channels : (i + 1) * channels]
            rows = pl.ds(at, chunk)
            stores.append(pltpu.make_async_copy(out_ref.at[rows], out_hbm.at[rows], sems.at[2 * pair + i]))
            stores[-1].start()
    for copy in stores:
        copy.wait()


def final_call(taps, sums, weight, pixels, chunk):
    padded, channels = 32, weight.shape[-1]
    rows = 2 * taps.shape[0]
    return pl.pallas_call(
        functools.partial(final_kernel, pixels=pixels, chunk=chunk),
        out_shape=(
            jax.ShapeDtypeStruct((rows, channels), BF16),
            jax.ShapeDtypeStruct((3, 3, 3, channels), F32),
            jax.ShapeDtypeStruct((1, 1), F32),
        ),
        in_specs=[VM] * 3,
        out_specs=(HBM, VM, VM),
        scratch_shapes=[
            pltpu.VMEM((padded, channels), F32),
            pltpu.VMEM((4 * padded, 2 * channels), BF16),
            pltpu.VMEM((rows, channels), BF16),
            pltpu.SemaphoreType.DMA((rows // chunk,)),
        ],
        compiler_params=PART,
        cost_estimate=pl.CostEstimate(flops=4 * rows * channels * padded, bytes_accessed=4 * rows * channels, transcendentals=0),
        name="feature_pull",
    )(taps, sums, weight)


def per_device(
    features, target, conv_weight, disc_first, disc_second, disc_third, disc_fourth, disc_head
):
    row = ("far", "near")
    devices = lax.axis_size(row)
    clips = lax.axis_size("clip")
    _, frames, block_rows, cols, channels = features.shape
    group = frames // devices
    pixels = clips * devices * frames * block_rows * cols
    lanes = up_to((block_rows + 2) * cols, LANES)
    pitch = up_to(3 * group + 2, 8)
    sizes = (frames, devices, group, cols, block_rows)
    feats = features.reshape(frames * block_rows * cols, channels)
    wanted = target[0].transpose(0, 2, 1, 3)
    payload = forward_call(feats, wanted, conv_weight, frames, devices, group, cols, lanes, pitch)
    trade = lambda values: lax.all_to_all(
        values.reshape(devices, pitch, lanes), row, split_axis=0, concat_axis=0, tiled=True
    ).reshape(devices * pitch, lanes)
    arrived = trade(payload)
    inner = inner_call(payload, wanted, frames, devices, group, block_rows, cols)
    _, disc_first = lax.optimization_barrier((payload, disc_first))
    staged = stage_call(disc_first, disc_second, cols)
    arrived, inner = lax.optimization_barrier((arrived, inner))
    sent = disc_call(arrived, staged, disc_third, disc_fourth, disc_head, devices, group, cols, block_rows)
    returned = trade(sent)
    taps_scratch = pltpu.VMEM((block_rows * cols // LANES, 32 * frames, LANES), F32)
    plane_scratch = pltpu.VMEM((lanes // LANES, devices * pitch, LANES), F32)
    flops = 4 * features.size * 27
    part = taps_call(
        both_kernel, [VM, VM, VM], (inner, returned, feats),
        jax.ShapeDtypeStruct((clips * lax.axis_size("near"), 56, channels), BF16),
        [taps_scratch, taps_scratch, plane_scratch], *sizes, flops, "both_taps",
    )
    share = lambda values, axes: lax.all_to_all(values, axes, split_axis=0, concat_axis=0, tiled=True)
    sums = share(sum_call(share(part, ("clip", "near")), lax.axis_size("far")), "far")
    taps = taps_call(
        turn_kernel, [VM, VM], (inner, returned), jax.ShapeDtypeStruct((feats.shape[0] // 2, LANES), BF16),
        [taps_scratch, taps_scratch, plane_scratch], *sizes, flops, "turn_taps",
    )
    image_back = returned.reshape(devices, pitch, lanes)[:, : 3 * group, cols : (block_rows + 1) * cols]
    image_back = image_back.reshape(devices, 3, group, block_rows, cols).transpose(0, 2, 3, 1, 4)
    image_back = image_back.reshape(1, frames, block_rows, 3, cols)
    feature_grad, weight_grad, adaptive = final_call(taps, sums, conv_weight, pixels, block_rows * cols)
    return (feature_grad.reshape(features.shape), image_back, weight_grad, adaptive[0, 0])


def sum_kernel(parts_ref, out_ref):
    total = parts_ref[0].astype(F32)
    for i in range(1, parts_ref.shape[0]):
        total = total + parts_ref[i].astype(F32)
    total = total.astype(BF16)
    for i in range(out_ref.shape[0]):
        out_ref[i] = total


def sum_call(parts, copies):
    return pl.pallas_call(
        sum_kernel,
        out_shape=jax.ShapeDtypeStruct((copies,) + parts.shape[1:], BF16),
        in_specs=[VM],
        out_specs=VM,
        compiler_params=PART,
        name="sum_parts",
    )(parts)


def solution(mesh):
    clips, devices = mesh.shape["clip"], mesh.shape["row"]
    near = 2 if devices % 2 == 0 else 1
    split = jax.sharding.Mesh(mesh.devices.reshape(clips, devices // near, near), ("clip", "far", "near"))
    rows = P("clip", None, ("far", "near"), None, None)
    return jax.shard_map(
        per_device,
        mesh=split,
        in_specs=(rows, rows, P(), P(), P(), P(), P(), P()),
        out_specs=(rows, rows, P(), P()),
        check_vma=False,
    )
```

```python
import functools

import jax
import jax.numpy as jnp
import numpy as np
from jax import lax
from jax.experimental import pallas as pl
from jax.experimental.pallas import tpu as pltpu
from jax.sharding import PartitionSpec as P

loss_scale = 64.0
epsilon = 0.0001
F32 = jnp.float32
BF16 = jnp.bfloat16
LANES = 128
NN = (((1,), (0,)), ((), ()))
NT = (((1,), (1,)), ((), ()))
TN = (((0,), (0,)), ((), ()))
VM = pl.BlockSpec(memory_space=pltpu.VMEM)
HBM = pl.BlockSpec(memory_space=pl.ANY)
WHOLE = pltpu.CompilerParams(vmem_limit_bytes=60 * 2**20)
MOST = pltpu.CompilerParams(vmem_limit_bytes=48 * 2**20)
PART = pltpu.CompilerParams(vmem_limit_bytes=24 * 2**20)


def up_to(value, step):
    return -(-value // step) * step


def mat(left, right, dims=NN):
    return lax.dot_general(left, right, dims, preferred_element_type=F32)


def slot_of(frame, devices, group):
    return (frame % group) * devices + frame // group


def forward_kernel(
    feat_hbm, target_hbm, weight_hbm, pay_ref, feat_ref, target_ref, weight_ref, weight_scr, target_scr,
    out_ref, sems, *taps_refs, frames, devices, group, cols, lanes, chunks,
):
    pixels = feat_ref.shape[0] // frames
    pieces = pixels // LANES
    pitch = out_ref.shape[1] // devices
    taps = weight_scr.shape[0]
    block_rows = pixels // cols
    copies = [
        pltpu.make_async_copy(weight_hbm, weight_ref, sems.at[frames]),
        pltpu.make_async_copy(target_hbm, target_ref, sems.at[frames + 1]),
    ]
    for slot in range(frames):
        rows = pl.ds((slot % devices * group + slot // devices) * pixels, pixels)
        copies.append(pltpu.make_async_copy(feat_hbm.at[rows, :], feat_ref.at[rows, :], sems.at[slot]))
    for copy in copies[:1] + copies[2:] + copies[1:2]:
        copy.start()
    weight_scr[...] = jnp.zeros_like(weight_scr)
    out_ref[...] = jnp.zeros_like(out_ref)
    copies[0].wait()
    for a in range(3):
        for b in range(3):
            at = (a * 3 + b) * 3
            weight_scr[at : at + 3, :] = weight_ref[a, b].astype(F32)
    weight = weight_scr[...].astype(BF16)
    column = lax.broadcasted_iota(jnp.int32, (devices, pixels), 1) % cols

    def finish(part):
        def tap(a, b, o):
            rows = pl.ds(((a * 3 + b) * 3 + o) * devices, devices)
            return jnp.concatenate([taps_refs[part][k, rows, :] for k in range(pieces)], axis=1)

        for o in range(3):
            total = None
            for a in range(3):
                term = tap(a, 1, o)
                term = term + jnp.where(column == 0, 0.0, pltpu.roll(tap(a, 0, o), 1, 1))
                term = term + jnp.where(column == cols - 1, 0.0, pltpu.roll(tap(a, 2, o), pixels - 1, 1))
                term = jnp.concatenate([term, jnp.zeros((devices, lanes - pixels), F32)], axis=1)
                if a < 2:
                    term = pltpu.roll(term, (2 - a) * cols, 1)
                total = term if total is None else total + term
            for k in range(lanes // LANES):
                rows = pl.ds(o * group + part, devices, stride=pitch)
                out_ref[k, rows, :] = total[:, k * LANES : (k + 1) * LANES]

    def edge_rows():
        target_scr[:, 0:cols] = target_ref[...].reshape(target_scr.shape[0], cols).astype(F32)
        edges = []
        for y in (0, block_rows - 1):
            for o in range(3):
                for part in range(group):
                    rows = pl.ds((part * 3 + o) * block_rows + y, devices, stride=group * 3 * block_rows)
                    edges.append(target_scr[rows, :][:, 0:cols])
        edges.append(jnp.zeros((devices, lanes - len(edges) * cols), F32))
        edges = jnp.concatenate(edges, axis=1)
        for k in range(lanes // LANES):
            out_ref[k, pl.ds(3 * group, devices, stride=pitch), :] = edges[:, k * LANES : (k + 1) * LANES]

    step = frames // chunks
    done = 0
    for chunk in range(chunks):
        for slot in range(chunk * step, (chunk + 1) * step):
            copies[2 + slot].wait()
        if chunk == chunks - 1:
            copies[1].wait()
        for slot in range(chunk * step, (chunk + 1) * step):
            frame = slot % devices * group + slot // devices
            product = mat(weight, feat_ref[frame * pixels : (frame + 1) * pixels, :], NT)
            for k in range(pieces):
                rows = pl.ds(slot % devices, taps, stride=devices)
                taps_refs[slot // devices][k, rows, :] = product[:, k * LANES : (k + 1) * LANES]
        if chunk == chunks - 1:
            edge_rows()
        while (done + 1) * devices <= chunk * step or (chunk == chunks - 1 and done < group):
            finish(done)
            done += 1
    for k in range(lanes // LANES):
        pay_ref[:, k * LANES : (k + 1) * LANES] = out_ref[k].astype(BF16)


def forward_call(features, target, weight, frames, devices, group, cols, lanes, pitch):
    pixels = features.shape[0] // frames
    channels = features.shape[1]
    chunks = 2
    return pl.pallas_call(
        functools.partial(
            forward_kernel, frames=frames, devices=devices, group=group, cols=cols, lanes=lanes, chunks=chunks
        ),
        out_shape=jax.ShapeDtypeStruct((devices * pitch, lanes), BF16),
        in_specs=[HBM, HBM, HBM],
        out_specs=VM,
        scratch_shapes=[
            pltpu.VMEM(features.shape, BF16),
            pltpu.VMEM(target.shape, BF16),
            pltpu.VMEM(weight.shape, BF16),
            pltpu.VMEM((32, channels), F32),
            pltpu.VMEM((3 * pixels // cols * frames, LANES), F32),
            pltpu.VMEM((lanes // LANES, devices * pitch, LANES), F32),
            pltpu.SemaphoreType.DMA((frames + 2,)),
        ]
        + [pltpu.VMEM((pixels // LANES, 32 * devices, LANES), F32)] * group,
        compiler_params=WHOLE,
        cost_estimate=pl.CostEstimate(flops=2 * features.size * 27, bytes_accessed=2 * features.size, transcendentals=0),
        name="forward_taps",
    )(features, target, weight)


def inner_kernel(pay_ref, target_ref, inner_ref, scr, zin, *, frames, devices, group, block_rows, cols):
    scr[:, 0:cols] = target_ref[...].reshape(scr.shape[0], cols).astype(F32)
    stride = group * 3 * block_rows
    lanes = pay_ref.shape[1]
    pitch = pay_ref.shape[0] // devices
    for k in range(lanes // LANES):
        zin[k] = pay_ref[:, k * LANES : (k + 1) * LANES].astype(F32)
    for o in range(3):
        for part in range(group):
            at = o * frames + part * devices
            rows = [jnp.zeros((devices, cols), F32)]
            rows += [
                scr[pl.ds((part * 3 + o) * block_rows + y, devices, stride=stride), :][:, 0:cols]
                for y in range(block_rows)
            ]
            rows.append(jnp.zeros((devices, lanes - (block_rows + 1) * cols), F32))
            wanted = jnp.concatenate(rows, axis=1)
            lane = lax.broadcasted_iota(jnp.int32, wanted.shape, 1)
            inside = (lane >= 2 * cols) & (lane < block_rows * cols)
            row = pl.ds(o * group + part, devices, stride=pitch)
            own = jnp.concatenate([zin[k, row, :] for k in range(lanes // LANES)], axis=1)
            inner_ref[at : at + devices, :] = loss_scale * (jnp.where(inside, own, 0.0) - wanted)


def inner_call(payload, target, frames, devices, group, block_rows, cols):
    lanes = payload.shape[1]
    return pl.pallas_call(
        functools.partial(
            inner_kernel, frames=frames, devices=devices, group=group, block_rows=block_rows, cols=cols
        ),
        out_shape=jax.ShapeDtypeStruct((3 * frames, lanes), F32),
        in_specs=[VM, VM],
        out_specs=VM,
        scratch_shapes=[
            pltpu.VMEM((frames * 3 * block_rows, LANES), F32),
            pltpu.VMEM((lanes // LANES, payload.shape[0], LANES), F32),
        ],
        compiler_params=PART,
        cost_estimate=pl.CostEstimate(flops=10**8, bytes_accessed=10**6, transcendentals=0),
        name="inner_rows",
    )(payload, target)


def shift_rows(values, step, period):
    size = values.shape[0]
    row = lax.broadcasted_iota(jnp.int32, values.shape, 0) % period
    rolled = pltpu.roll(values, step % size, 0)
    source = row - step
    return jnp.where((source >= 0) & (source < period), rolled, 0.0)


def gate_of(values):
    logistic = 0.5 + 0.5 * jnp.tanh(0.5 * values)
    return (values * logistic).astype(BF16), logistic * (1.0 + values * (1.0 - logistic))


def edge_planes(zin, zout, first, last, devices, group, cols, lanes, pitch):
    row = pl.ds(3 * group, devices, stride=pitch)
    target = jnp.concatenate([zin[k, row, :] for k in range(lanes // LANES)], axis=1)
    outer, inner = [], []
    for e, rows, other, move in ((0, first, last, 1), (1, last, first, -1)):
        for o in range(3):
            for part in range(group):
                at = ((1 - e) * 3 * group + o * group + part) * cols
                near = other[part][:, o * cols : (o + 1) * cols] - target[:, at : at + cols]
                outer.append(shift_rows(loss_scale * near, move, devices))
                inner.append(rows[part][:, o * cols : (o + 1) * cols])
    for i, pieces in enumerate((outer, inner)):
        pieces.append(jnp.zeros((devices, lanes - 6 * group * cols), F32))
        plane = jnp.concatenate(pieces, axis=1)
        for k in range(lanes // LANES):
            zout[k, pl.ds(3 * group + i, devices, stride=pitch), :] = plane[:, k * LANES : (k + 1) * LANES]


def disc_kernel(
    pay_ref, head_ref, window, band_ref, second, unwindow, third_hbm, fourth_hbm, out_ref,
    zin, third, fourth, rows_in, act_one, slope_one, cols_two, act_two, slope_two, act_three, cols_four,
    pull_four, pull_three, pull_two, zout, sems, *, devices, group, cols, block_rows, period,
):
    lanes = pay_ref.shape[1]
    pitch = pay_ref.shape[0] // devices
    span = block_rows + 2
    unit = group * period
    wide = 3 * cols
    d1 = (act_one.shape[1]) // (cols // 2 + 2)
    d2, d3, d4 = second.shape[1], third.shape[1], fourth.shape[1]
    x1, x2, x3 = cols // 2, cols // 4, cols // 8
    x4 = x3 - 1
    quarter = fourth.shape[0] // 4
    copies = [
        pltpu.make_async_copy(
            fourth_hbm.at[pl.ds(a * quarter, quarter), :], fourth.at[pl.ds(a * quarter, quarter), :], sems.at[a]
        )
        for a in range(4)
    ]
    copies.append(pltpu.make_async_copy(third_hbm, third, sems.at[4]))
    for i in (4, 0, 1, 2, 3):
        copies[i].start()
    cells = block_rows // 8
    spot = lambda y, part: pl.ds((y % 8 * group + part) * period + y // 8, devices, stride=cells)
    for k in range(lanes // LANES):
        zin[k] = pay_ref[:, k * LANES : (k + 1) * LANES].astype(F32)
    zout[...] = jnp.zeros_like(zout)
    firsts, lasts = [], []
    for part in range(group):
        planes = []
        for o in range(3):
            pieces = [zin[k, pl.ds(o * group + part, devices, stride=pitch), :] for k in range(lanes // LANES)]
            planes.append(jnp.concatenate(pieces, axis=1))
        lines = [
            jnp.concatenate(
                [plane[:, i * cols : (i + 1) * cols] for plane in planes]
                + [jnp.zeros((devices, 2 * LANES - wide), F32)],
                axis=1,
            )
            for i in range(span)
        ]
        lines[1] = lines[1] + shift_rows(lines[span - 1], 1, devices)
        lines[block_rows] = lines[block_rows] + shift_rows(lines[0], -1, devices)
        for y in range(block_rows):
            for k in range(2):
                rows_in[k, spot(y, part), :] = lines[y + 1][:, k * LANES : (k + 1) * LANES]
        firsts.append(lines[1])
        lasts.append(lines[block_rows])
    image = jnp.concatenate([rows_in[0], rows_in[1]], axis=1)[:, :wide].astype(BF16)
    wins = mat(image, window[...])
    ext = [wins[r * unit : (r + 1) * unit] for r in range(8)]
    ext = [shift_rows(ext[7], 1, period)] + ext + [shift_rows(ext[0], -1, period)]
    width_one = act_one.shape[1]
    strip = 8 * d1
    band = band_ref[...]
    for k in range(-(-width_one // strip)):
        low, high = slice(2 * k * LANES, (2 * k + 1) * LANES), slice((2 * k + 1) * LANES, (2 * k + 2) * LANES)
        left = jnp.concatenate(
            [
                jnp.concatenate([ext[2 * p + h][:, low] + ext[2 * p + h + 1][:, high] for p in range(4)], axis=0)
                for h in (0, 2)
            ],
            axis=1,
        ).astype(BF16)
        start, end = k * strip, min((k + 1) * strip, width_one)
        act, slope = gate_of(mat(left, band[:, : end - start]))
        if k == 0 or end == width_one:
            lane = start + lax.broadcasted_iota(jnp.int32, slope.shape, 1)
            inside = (lane >= d1) & (lane < width_one - d1)
            slope = jnp.where(inside, slope, 0.0)
            act = jnp.where(inside, act.astype(F32), 0.0).astype(BF16)
        slope_one[:, start:end] = slope
        act_one[unit : 5 * unit, start:end] = act
        actual = act.astype(F32)
        act_one[0:unit, start:end] = shift_rows(actual[3 * unit :], 1, period).astype(BF16)
        act_one[5 * unit :, start:end] = shift_rows(actual[:unit], -1, period).astype(BF16)
    for x in range(x2):
        for a in range(4):
            for p in range(2):
                cols_two[(x * 2 + p) * unit : (x * 2 + p + 1) * unit, a * 4 * d1 : (a + 1) * 4 * d1] = act_one[
                    (2 * p + a) * unit : (2 * p + a + 1) * unit, 2 * x * d1 : (2 * x + 4) * d1
                ]
    pre = mat(cols_two[...], second[...])
    act, slope = gate_of(pre)
    slope_two[...] = slope
    act_two[:, 0:d2] = jnp.zeros((4 * unit, d2), BF16)
    act_two[:, (x2 + 1) * d2 :] = jnp.zeros((4 * unit, d2), BF16)
    for x in range(x2):
        block = act[x * 2 * unit : (x + 1) * 2 * unit]
        actual = block.astype(F32)
        at = slice((x + 1) * d2, (x + 2) * d2)
        act_two[unit : 3 * unit, at] = block
        act_two[0:unit, at] = shift_rows(actual[unit:], 1, period).astype(BF16)
        act_two[3 * unit :, at] = shift_rows(actual[:unit], -1, period).astype(BF16)
    left = jnp.concatenate(
        [
            jnp.concatenate([act_two[a * unit : (a + 1) * unit, 2 * x * d2 : (2 * x + 4) * d2] for a in range(4)], axis=1)
            for x in range(x3)
        ],
        axis=0,
    )
    copies[4].wait()
    act, slope_three = gate_of(mat(left, third[...]))
    act_three[:, 0:d3] = jnp.zeros((4 * unit, d3), BF16)
    act_three[:, (x3 + 1) * d3 :] = jnp.zeros((4 * unit, d3), BF16)
    for x in range(x3):
        block = act[x * unit : (x + 1) * unit]
        actual = block.astype(F32)
        at = slice((x + 1) * d3, (x + 2) * d3)
        act_three[unit : 2 * unit, at] = block
        for a in (0, 2, 3):
            act_three[a * unit : (a + 1) * unit, at] = shift_rows(actual, 1 - a, period).astype(BF16)
    for x in range(x4):
        for a in range(4):
            cols_four[x * unit : (x + 1) * unit, a * 4 * d3 : (a + 1) * 4 * d3] = act_three[
                a * unit : (a + 1) * unit, x * d3 : (x + 4) * d3
            ]
    edge_planes(zin, zout, firsts, lasts, devices, group, cols, lanes, pitch)
    row = lax.broadcasted_iota(jnp.int32, (unit, d4), 0) % period
    head = head_ref[...].astype(F32) * -loss_scale
    heads = []
    for x in range(x4):
        total = None
        for a in range(4):
            taps = [head[a * 4 + b : a * 4 + b + 1, :] for b in range(4) if 0 <= x - b + 1 < x4 - 1]
            tap = functools.reduce(lambda u, v: u + v, taps)
            inside = (row - a + 1 >= 0) & (row - a + 1 < period - 2) & (row < period - 1)
            term = jnp.where(inside, jnp.broadcast_to(tap, (unit, d4)), 0.0)
            total = term if total is None else total + term
        heads.append(total)
    pre = None
    for a in range(4):
        copies[a].wait()
        term = mat(cols_four[:, a * quarter : (a + 1) * quarter], fourth[a * quarter : (a + 1) * quarter, :])
        pre = term if pre is None else pre + term
    _, slope = gate_of(pre)
    cot = (jnp.concatenate(heads, axis=0) * slope).astype(BF16)
    pull_four[...] = mat(cot, fourth[...], NT)
    cots = []
    for x in range(x3):
        total = None
        for a in range(4):
            term = None
            for b in range(4):
                source = x - b + 1
                if 0 <= source < x4:
                    piece = pull_four[source * unit : (source + 1) * unit, (a * 4 + b) * d3 : (a * 4 + b + 1) * d3]
                    term = piece if term is None else term + piece
            if a != 1:
                term = shift_rows(term, a - 1, period)
            total = term if total is None else total + term
        cots.append((total * slope_three[x * unit : (x + 1) * unit]).astype(BF16))
    pull_three[...] = mat(jnp.concatenate(cots, axis=0), third[...], NT)
    cots = []
    for x in range(x2):
        terms = []
        for a in range(4):
            term = None
            for b in range(4):
                if (x - b + 1) % 2 == 0 and 0 <= (x - b + 1) // 2 < x3:
                    source = (x - b + 1) // 2
                    piece = pull_three[source * unit : (source + 1) * unit, (a * 4 + b) * d2 : (a * 4 + b + 1) * d2]
                    term = piece if term is None else term + piece
            terms.append(term)
        even = terms[1] + shift_rows(terms[3], 1, period)
        odd = terms[2] + shift_rows(terms[0], -1, period)
        both = jnp.concatenate([even, odd], axis=0)
        cots.append((both * slope_two[x * 2 * unit : (x + 1) * 2 * unit]).astype(BF16))
    pull_two[...] = mat(jnp.concatenate(cots, axis=0), second[...], NT)
    strips = []
    for k in range(x2 + 1):
        terms = {}
        for p in range(2):
            for a in range(4):
                term = None
                if k < x2:
                    term = pull_two[(2 * k + p) * unit : (2 * k + p + 1) * unit, a * 4 * d1 : (a * 4 + 2) * d1]
                if k > 0:
                    other = pull_two[(2 * k - 2 + p) * unit : (2 * k - 1 + p) * unit, (a * 4 + 2) * d1 : (a + 1) * 4 * d1]
                    term = other if term is None else term + other
                terms[p, a] = term
        both = jnp.concatenate(
            [
                terms[0, 1] + shift_rows(terms[1, 3], 1, period),
                terms[0, 2] + terms[1, 0],
                terms[0, 3] + terms[1, 1],
                terms[1, 2] + shift_rows(terms[0, 0], -1, period),
            ],
            axis=0,
        )
        strips.append((both * slope_one[:, 2 * k * d1 : (2 * k + 2) * d1]).astype(BF16))
    cot = jnp.concatenate(strips, axis=1)
    sums = []
    for k in range(-(-width_one // strip)):
        start, end = k * strip, min((k + 1) * strip, width_one)
        pulls = mat(cot[:, start:end], band[:, : end - start], NT)
        groups = []
        for m in range(5):
            terms = [
                pulls[p * unit : (p + 1) * unit, (m - p) * LANES : (m - p + 1) * LANES] for p in range(4) if 0 <= m - p < 2
            ]
            groups.append(functools.reduce(lambda u, v: u + v, terms))
        sums.append(jnp.concatenate(groups, axis=0))
    sums = jnp.concatenate(sums, axis=1)
    upper = sums.astype(BF16)
    lower = (sums - upper.astype(F32)).astype(BF16)
    low = lax.broadcasted_iota(jnp.int32, upper.shape, 1) % LANES < LANES // 2
    blank = jnp.zeros_like(upper)
    split = [jnp.where(low, upper, blank), jnp.where(low, lower, blank), jnp.where(low, blank, upper), jnp.where(low, blank, lower)]
    both = mat(jnp.concatenate(split, axis=0), unwindow[...])
    size = 5 * unit
    odd = both[:size] + both[size : 2 * size]
    even = both[2 * size : 3 * size] + both[3 * size :]
    odd = [odd[m * unit : (m + 1) * unit, :] for m in range(5)]
    even = [even[m * unit : (m + 1) * unit, :] for m in range(5)]
    phases = [even[r // 2] if r % 2 == 0 else odd[(r + 1) // 2] for r in range(8)]
    phases[0] = phases[0] + shift_rows(even[4], 1, period)
    phases[7] = phases[7] + shift_rows(odd[0], -1, period)
    image = jnp.concatenate(phases, axis=0)
    image = jnp.concatenate([image, jnp.zeros((image.shape[0], 2 * LANES - wide), F32)], axis=1)
    for k in range(2):
        rows_in[k] = image[:, k * LANES : (k + 1) * LANES]
    for part in range(group):
        lines = [
            jnp.concatenate([rows_in[k, spot(y, part), :] for k in range(2)], axis=1)[:, :wide]
            for y in range(block_rows)
        ]
        lines = [shift_rows(lines[-1], 1, devices)] + lines + [shift_rows(lines[0], -1, devices)]
        for o in range(3):
            plane = [line[:, o * cols : (o + 1) * cols] for line in lines]
            plane.append(jnp.zeros((devices, lanes - span * cols), F32))
            plane = jnp.concatenate(plane, axis=1)
            for k in range(lanes // LANES):
                zout[k, pl.ds(o * group + part, devices, stride=pitch), :] = plane[:, k * LANES : (k + 1) * LANES]
    for k in range(lanes // LANES):
        out_ref[:, k * LANES : (k + 1) * LANES] = zout[k].astype(BF16)


def window_of(at, cols):
    k, rest = at // LANES, at % LANES
    inner = rest % (LANES // 2)
    colour = jnp.where(inner >= 18, 1, 0) + jnp.where(inner >= 36, 1, 0)
    x = 16 * k - 3 + inner - 18 * colour
    inside = (inner < 54) & (x >= 0) & (x < cols)
    return jnp.where(inside, colour * cols + x, -1), rest // (LANES // 2)


def stage_kernel(first_ref, second_hbm, window, unwindow, second, band, scr, sem, *, cols):
    copy = pltpu.make_async_copy(second_hbm, second, sem.at[0])
    copy.start()
    row = lax.broadcasted_iota(jnp.int32, window.shape, 0)
    lane = lax.broadcasted_iota(jnp.int32, window.shape, 1)
    place, half = window_of(lane // (2 * LANES) * LANES + lane % LANES, cols)
    window[...] = jnp.where((place == row) & (half == lane // LANES % 2), 1.0, 0.0).astype(BF16)
    place, _ = window_of(lax.broadcasted_iota(jnp.int32, unwindow.shape, 0), cols)
    column = lax.broadcasted_iota(jnp.int32, unwindow.shape, 1)
    unwindow[...] = jnp.where(place == column, 1.0, 0.0).astype(BF16)
    d1 = first_ref.shape[-1]
    scr[...] = jnp.zeros_like(scr)
    row = lax.broadcasted_iota(jnp.int32, (18, 8 * d1), 0)
    tap = row - 2 * (lax.broadcasted_iota(jnp.int32, (18, 8 * d1), 1) // d1)
    for a in range(4):
        lines = [first_ref[a, b].astype(F32) for b in range(4)]
        for c in range(3):
            block = jnp.zeros((18, 8 * d1), F32)
            for b in range(4):
                line = jnp.concatenate([lines[b][c : c + 1, :]] * 8, axis=1)
                block = jnp.where(tap == b, jnp.broadcast_to(line, block.shape), block)
            at = a * LANES // 2 + c * 18
            scr[at : at + 18, :] = block
    band[...] = scr[...].astype(BF16)
    copy.wait()


def stage_call(first, second, cols):
    d1, d2 = first.shape[-1], second.shape[-1]
    count = -(-(cols // 2 + 2) // 8)
    shapes = [(3 * cols, count * 2 * LANES), (count * LANES, 3 * cols), (16 * d1, d2), (2 * LANES, 8 * d1)]
    return pl.pallas_call(
        functools.partial(stage_kernel, cols=cols),
        out_shape=tuple(jax.ShapeDtypeStruct(shape, BF16) for shape in shapes),
        in_specs=[VM, HBM],
        out_specs=(VM,) * 4,
        scratch_shapes=[pltpu.VMEM((2 * LANES, 8 * d1), F32), pltpu.SemaphoreType.DMA((1,))],
        compiler_params=PART,
        cost_estimate=pl.CostEstimate(flops=10**8, bytes_accessed=4 * 10**6, transcendentals=0),
        name="stage_weights",
    )(first, second.reshape(16 * d1, d2))


def disc_call(payload, staged, third, fourth, head, devices, group, cols, block_rows):
    period = devices * block_rows // 8
    unit = group * period
    window, unwindow, second, band = staged
    d1, d2, d3, d4 = band.shape[1] // 8, second.shape[1], third.shape[-1], fourth.shape[-1]
    x2, x3 = cols // 4, cols // 8
    x4 = x3 - 1
    width_one = (cols // 2 + 2) * d1
    args = (
        payload,
        head.reshape(16, d4),
        window,
        band,
        second,
        unwindow,
        third.reshape(16 * d2, d3),
        fourth.reshape(16 * d3, d4),
    )
    lanes = payload.shape[1]
    return pl.pallas_call(
        functools.partial(
            disc_kernel, devices=devices, group=group, cols=cols, block_rows=block_rows, period=period
        ),
        out_shape=jax.ShapeDtypeStruct(payload.shape, BF16),
        in_specs=[VM] * 6 + [HBM] * 2,
        out_specs=VM,
        scratch_shapes=[
            pltpu.VMEM((lanes // LANES, payload.shape[0], LANES), F32),
            pltpu.VMEM((16 * d2, d3), BF16),
            pltpu.VMEM((16 * d3, d4), BF16),
            pltpu.VMEM((2, 8 * unit, LANES), F32),
            pltpu.VMEM((6 * unit, width_one), BF16),
            pltpu.VMEM((4 * unit, width_one), F32),
            pltpu.VMEM((x2 * 2 * unit, 16 * d1), BF16),
            pltpu.VMEM((4 * unit, (x2 + 2) * d2), BF16),
            pltpu.VMEM((x2 * 2 * unit, d2), F32),
            pltpu.VMEM((4 * unit, (x3 + 2) * d3), BF16),
            pltpu.VMEM((x4 * unit, 16 * d3), BF16),
            pltpu.VMEM((x4 * unit, 16 * d3), F32),
            pltpu.VMEM((x3 * unit, 16 * d2), F32),
            pltpu.VMEM((x2 * 2 * unit, 16 * d1), F32),
            pltpu.VMEM((lanes // LANES, payload.shape[0], LANES), F32),
            pltpu.SemaphoreType.DMA((5,)),
        ],
        compiler_params=MOST,
        cost_estimate=pl.CostEstimate(flops=4 * 10**9, bytes_accessed=8 * 10**6, transcendentals=10**6),
        name="disc_rows",
    )(*args)


def put_taps(plane, taps_ref, frames, cols, pieces, padded):
    lanes = plane.shape[1]
    column = lax.broadcasted_iota(jnp.int32, plane.shape, 1) % cols
    for b in range(3):
        moved = plane
        if b == 0:
            moved = jnp.where(column == cols - 1, 0.0, pltpu.roll(plane, lanes - 1, 1))
        if b == 2:
            moved = jnp.where(column == 0, 0.0, pltpu.roll(plane, 1, 1))
        for a in range(3):
            turned = moved if a == 2 else pltpu.roll(moved, lanes - (2 - a) * cols, 1)
            for k in range(pieces):
                taps_ref[k, pl.ds((a * 3 + b) * 3 * frames, 3 * frames), :] = turned[:, k * LANES : (k + 1) * LANES]
    for k in range(pieces):
        taps_ref[k, pl.ds(27 * frames, (padded - 27) * frames), :] = jnp.zeros(((padded - 27) * frames, LANES), F32)


def unpack(plane_ref, zin, devices, group):
    lanes = plane_ref.shape[1]
    pitch = plane_ref.shape[0] // devices
    for k in range(lanes // LANES):
        zin[k] = plane_ref[:, k * LANES : (k + 1) * LANES].astype(F32)
    blocks = []
    for o in range(3):
        for part in range(group):
            row = pl.ds(o * group + part, devices, stride=pitch)
            blocks.append(jnp.concatenate([zin[k, row, :] for k in range(lanes // LANES)], axis=1))
    return jnp.concatenate(blocks, axis=0)


def edge_blocks(zin, lanes, devices, group, cols):
    pitch = zin.shape[1] // devices
    edges = []
    for i in range(2):
        row = pl.ds(3 * group + i, devices, stride=pitch)
        edges.append(jnp.concatenate([zin[k, row, :] for k in range(lanes // LANES)], axis=1))
    blocks = []
    for i, e in ((0, 0), (1, 0), (1, 1), (0, 1)):
        pieces = [
            edges[i][:, (e * 3 * group + at) * cols : (e * 3 * group + at + 1) * cols] for at in range(3 * group)
        ]
        blocks.append(jnp.concatenate(pieces, axis=0))
    above, first, last, below = blocks
    return above, first * loss_scale, last * loss_scale, below


def weigh(taps_ref, feat_ref, frames, devices, group, pieces, choose):
    total = jnp.zeros((32, feat_ref.shape[1]), F32)
    for frame in range(frames):
        rows = pl.ds(slot_of(frame, devices, group), 32, stride=frames)
        taps = jnp.concatenate([taps_ref[k, rows, :] for k in range(pieces)], axis=1).astype(BF16)
        total = total + mat(taps, choose(frame))
    return total


def rec_kernel(inner_ref, feat_ref, part_ref, taps_ref, *, frames, devices, group, cols, block_rows):
    pixels = block_rows * cols
    put_taps(inner_ref[...], taps_ref, frames, cols, pixels // LANES, 32)
    whole = lambda frame: feat_ref[frame * pixels : (frame + 1) * pixels, :]
    part_ref[...] = weigh(taps_ref, feat_ref, frames, devices, group, pixels // LANES, whole)


def both_kernel(
    rec_ref, plane_ref, feat_ref, part_ref, gan_taps, edge_taps, zin, *, frames, devices, group, cols, block_rows
):
    lanes = plane_ref.shape[1]
    pixels = block_rows * cols
    put_taps(unpack(plane_ref, zin, devices, group), gan_taps, frames, cols, pixels // LANES, 32)
    above, first, last, below = edge_blocks(zin, lanes, devices, group, cols)
    none = jnp.zeros((above.shape[0], 4 * cols), F32)
    plane = jnp.concatenate([above, first, none, last, below], axis=1)
    size = 8 * cols
    lane = lax.broadcasted_iota(jnp.int32, plane.shape, 1)
    for b in range(3):
        moved = plane
        if b == 0:
            moved = jnp.where(lane % cols == cols - 1, 0.0, pltpu.roll(plane, size - 1, 1))
        if b == 2:
            moved = jnp.where(lane % cols == 0, 0.0, pltpu.roll(plane, 1, 1))
        for a in range(3):
            turned = moved if a == 2 else pltpu.roll(moved, size - (2 - a) * cols, 1)
            turned = jnp.where(lane % (4 * cols) < 2 * cols, turned, 0.0)
            for k in range(size // LANES):
                rows = pl.ds((a * 3 + b) * 3 * frames, 3 * frames)
                edge_taps[k, rows, :] = turned[:, k * LANES : (k + 1) * LANES]
    for k in range(size // LANES):
        edge_taps[k, pl.ds(27 * frames, 5 * frames), :] = jnp.zeros((5 * frames, LANES), F32)
    whole = lambda frame: feat_ref[frame * pixels : (frame + 1) * pixels, :]
    gan = weigh(gan_taps, feat_ref, frames, devices, group, pixels // LANES, whole)

    def ends(frame):
        start, end = frame * pixels, (frame + 1) * pixels
        tail = feat_ref[end - 2 * cols : end, :]
        return jnp.concatenate([feat_ref[start : start + 4 * cols, :], tail, tail], axis=0)

    rec = rec_ref[...] + weigh(edge_taps, feat_ref, frames, devices, group, size // LANES, ends)
    blank = jnp.zeros((part_ref.shape[1] - 54, gan.shape[1]), F32)
    total = jnp.concatenate([rec[0:27], gan[0:27], blank], axis=0).astype(BF16)
    for i in range(part_ref.shape[0]):
        part_ref[i] = total


def turn_kernel(
    inner_ref, plane_ref, out_ref, rec_taps, gan_taps, zin, *, frames, devices, group, cols, block_rows
):
    pieces = block_rows * cols // LANES
    pixels = pieces * LANES
    put_taps(unpack(plane_ref, zin, devices, group), gan_taps, frames, cols, pieces, 32)
    lanes = inner_ref.shape[1]
    above, first, last, below = edge_blocks(zin, lanes, devices, group, cols)
    none = lambda count: jnp.zeros((above.shape[0], count), F32)
    edges = jnp.concatenate(
        [above, first, none((block_rows - 2) * cols), last, below, none(lanes - (block_rows + 2) * cols)], axis=1
    )
    put_taps(inner_ref[...] + edges, rec_taps, frames, cols, pieces, 32)
    for pair in range(frames // 2):
        for k in range(pieces):
            parts = []
            for frame in (2 * pair, 2 * pair + 1):
                rows = pl.ds(slot_of(frame, devices, group), 32, stride=frames)
                parts += [rec_taps[k, rows, :], gan_taps[k, rows, :]]
            at = pair * pixels + k * LANES
            out_ref[at : at + LANES, :] = jnp.concatenate(parts, axis=0).T.astype(BF16)


def taps_call(kernel, specs, operands, out, scratch, frames, devices, group, cols, block_rows, flops, name):
    return pl.pallas_call(
        functools.partial(kernel, frames=frames, devices=devices, group=group, cols=cols, block_rows=block_rows),
        out_shape=out,
        in_specs=specs,
        out_specs=jax.tree.map(lambda _: VM, out),
        scratch_shapes=scratch,
        compiler_params=PART,
        cost_estimate=pl.CostEstimate(flops=flops, bytes_accessed=4 * 10**6, transcendentals=0),
        name=name,
    )(*operands)


def final_kernel(
    taps_ref, sums_ref, weight_ref, out_hbm, grad_ref, adapt_ref, weight_scr, both_ref, out_ref, sems, *, pixels, chunk
):
    weight_scr[...] = jnp.zeros_like(weight_scr)
    for a in range(3):
        for b in range(3):
            at = (a * 3 + b) * 3
            weight_scr[at : at + 3, :] = weight_ref[a, b].astype(F32)
    total = sums_ref[0].astype(F32)
    for i in range(1, sums_ref.shape[0]):
        total = total + sums_ref[i].astype(F32)
    rec, gan = total[0:27], total[27:54]
    norm = lambda values: jnp.sqrt(jnp.sum(jnp.sum(values * values, axis=1, keepdims=True), axis=0, keepdims=True))
    adaptive = norm(rec) / (norm(gan) + epsilon)
    grad = (rec + adaptive * gan) / pixels
    for a in range(3):
        for b in range(3):
            at = (a * 3 + b) * 3
            grad_ref[a, b] = grad[at : at + 3, :]
    adapt_ref[...] = adaptive
    weight = weight_scr[...].astype(BF16)
    padded, channels = weight.shape
    scaled = (adaptive * weight.astype(F32)).astype(BF16)
    both_ref[...] = jnp.zeros_like(both_ref)
    both_ref[0:padded, 0:channels] = weight
    both_ref[padded : 2 * padded, 0:channels] = scaled
    both_ref[2 * padded : 3 * padded, channels:] = weight
    both_ref[3 * padded :, channels:] = scaled
    pairs = taps_ref.shape[0] // chunk
    stores = []
    for pair in range(pairs):
        product = mat(taps_ref[pair * chunk : (pair + 1) * chunk], both_ref[...]).astype(BF16)
        rows = pl.ds(2 * pair * chunk, 2 * chunk)
        out_ref[2 * pair * chunk : (2 * pair + 1) * chunk] = product[:, :channels]
        out_ref[(2 * pair + 1) * chunk : (2 * pair + 2) * chunk] = product[:, channels:]
        stores.append(pltpu.make_async_copy(out_ref.at[rows], out_hbm.at[rows], sems.at[pair]))
        stores[-1].start()
    for copy in stores:
        copy.wait()


def final_call(taps, sums, weight, pixels, chunk):
    padded, channels = 32, weight.shape[-1]
    rows = 2 * taps.shape[0]
    return pl.pallas_call(
        functools.partial(final_kernel, pixels=pixels, chunk=chunk),
        out_shape=(
            jax.ShapeDtypeStruct((rows, channels), BF16),
            jax.ShapeDtypeStruct((3, 3, 3, channels), F32),
            jax.ShapeDtypeStruct((1, 1), F32),
        ),
        in_specs=[VM] * 3,
        out_specs=(HBM, VM, VM),
        scratch_shapes=[
            pltpu.VMEM((padded, channels), F32),
            pltpu.VMEM((4 * padded, 2 * channels), BF16),
            pltpu.VMEM((rows, channels), BF16),
            pltpu.SemaphoreType.DMA((rows // (2 * chunk),)),
        ],
        compiler_params=PART,
        cost_estimate=pl.CostEstimate(flops=4 * rows * channels * padded, bytes_accessed=4 * rows * channels, transcendentals=0),
        name="feature_pull",
    )(taps, sums, weight)


def per_device(
    features, target, conv_weight, disc_first, disc_second, disc_third, disc_fourth, disc_head
):
    row = ("far", "near")
    devices = lax.axis_size(row)
    clips = lax.axis_size("clip")
    _, frames, block_rows, cols, channels = features.shape
    group = frames // devices
    pixels = clips * devices * frames * block_rows * cols
    lanes = up_to((block_rows + 2) * cols, LANES)
    pitch = up_to(3 * group + 2, 8)
    sizes = (frames, devices, group, cols, block_rows)
    feats = features.reshape(frames * block_rows * cols, channels)
    wanted = target[0].transpose(0, 2, 1, 3)
    payload = forward_call(feats, wanted, conv_weight, frames, devices, group, cols, lanes, pitch)
    trade = lambda values: lax.all_to_all(
        values.reshape(devices, pitch, lanes), row, split_axis=0, concat_axis=0, tiled=True
    ).reshape(devices * pitch, lanes)
    arrived = trade(payload)
    inner = inner_call(payload, wanted, frames, devices, group, block_rows, cols)
    _, disc_first = lax.optimization_barrier((payload, disc_first))
    staged = stage_call(disc_first, disc_second, cols)
    arrived, inner = lax.optimization_barrier((arrived, inner))
    sent = disc_call(arrived, staged, disc_third, disc_fourth, disc_head, devices, group, cols, block_rows)
    sent, held = lax.optimization_barrier((sent, inner))
    returned = trade(sent)
    taps_scratch = pltpu.VMEM((block_rows * cols // LANES, 32 * frames, LANES), F32)
    plane_scratch = pltpu.VMEM((lanes // LANES, devices * pitch, LANES), F32)
    flops = 4 * features.size * 27
    rec_part = taps_call(
        rec_kernel, [VM, VM], (held, feats), jax.ShapeDtypeStruct((32, channels), F32), [taps_scratch], *sizes, flops, "rec_taps"
    )
    part = taps_call(
        both_kernel, [VM, VM, VM], (rec_part, returned, feats),
        jax.ShapeDtypeStruct((clips * lax.axis_size("near"), 56, channels), BF16),
        [taps_scratch, pltpu.VMEM((8 * cols // LANES, 32 * frames, LANES), F32), plane_scratch], *sizes, flops, "both_taps",
    )
    share = lambda values, axes: lax.all_to_all(values, axes, split_axis=0, concat_axis=0, tiled=True)
    sums = share(sum_call(share(part, ("clip", "near")), lax.axis_size("far")), "far")
    taps = taps_call(
        turn_kernel, [VM, VM], (inner, returned), jax.ShapeDtypeStruct((feats.shape[0] // 2, LANES), BF16),
        [taps_scratch, taps_scratch, plane_scratch], *sizes, flops, "turn_taps",
    )
    image_back = returned.reshape(devices, pitch, lanes)[:, : 3 * group, cols : (block_rows + 1) * cols]
    image_back = image_back.reshape(devices, 3, group, block_rows, cols).transpose(0, 2, 3, 1, 4)
    image_back = image_back.reshape(1, frames, block_rows, 3, cols)
    feature_grad, weight_grad, adaptive = final_call(taps, sums, conv_weight, pixels, block_rows * cols)
    return (feature_grad.reshape(features.shape), image_back, weight_grad, adaptive[0, 0])


def sum_kernel(parts_ref, out_ref):
    total = parts_ref[0].astype(F32)
    for i in range(1, parts_ref.shape[0]):
        total = total + parts_ref[i].astype(F32)
    total = total.astype(BF16)
    for i in range(out_ref.shape[0]):
        out_ref[i] = total


def sum_call(parts, copies):
    return pl.pallas_call(
        sum_kernel,
        out_shape=jax.ShapeDtypeStruct((copies,) + parts.shape[1:], BF16),
        in_specs=[VM],
        out_specs=VM,
        compiler_params=PART,
        name="sum_parts",
    )(parts)


def solution(mesh):
    clips, devices = mesh.shape["clip"], mesh.shape["row"]
    near = 2 if devices % 2 == 0 else 1
    split = jax.sharding.Mesh(mesh.devices.reshape(clips, devices // near, near), ("clip", "far", "near"))
    rows = P("clip", None, ("far", "near"), None, None)
    return jax.shard_map(
        per_device,
        mesh=split,
        in_specs=(rows, rows, P(), P(), P(), P(), P(), P()),
        out_specs=(rows, rows, P(), P()),
        check_vma=False,
    )
```

```python
import functools

import jax
import jax.numpy as jnp
import numpy as np
from jax import lax
from jax.experimental import pallas as pl
from jax.experimental.pallas import tpu as pltpu
from jax.sharding import PartitionSpec as P

loss_scale = 64.0
epsilon = 0.0001
F32 = jnp.float32
BF16 = jnp.bfloat16
LANES = 128
NN = (((1,), (0,)), ((), ()))
NT = (((1,), (1,)), ((), ()))
TN = (((0,), (0,)), ((), ()))
VM = pl.BlockSpec(memory_space=pltpu.VMEM)
HBM = pl.BlockSpec(memory_space=pl.ANY)
WHOLE = pltpu.CompilerParams(vmem_limit_bytes=60 * 2**20)
MOST = pltpu.CompilerParams(vmem_limit_bytes=48 * 2**20)
PART = pltpu.CompilerParams(vmem_limit_bytes=24 * 2**20)


def up_to(value, step):
    return -(-value // step) * step


def mat(left, right, dims=NN):
    return lax.dot_general(left, right, dims, preferred_element_type=F32)


def slot_of(frame, devices, group):
    return (frame % group) * devices + frame // group


def forward_kernel(
    feat_hbm, target_hbm, weight_hbm, pay_ref, feat_ref, target_ref, weight_ref, weight_scr, target_scr,
    out_ref, sems, *taps_refs, frames, devices, group, cols, lanes, chunks,
):
    pixels = feat_ref.shape[0] // frames
    pieces = pixels // LANES
    pitch = out_ref.shape[1] // devices
    taps = weight_scr.shape[0]
    block_rows = pixels // cols
    copies = [
        pltpu.make_async_copy(weight_hbm, weight_ref, sems.at[frames]),
        pltpu.make_async_copy(target_hbm, target_ref, sems.at[frames + 1]),
    ]
    for slot in range(frames):
        rows = pl.ds((slot % devices * group + slot // devices) * pixels, pixels)
        copies.append(pltpu.make_async_copy(feat_hbm.at[rows, :], feat_ref.at[rows, :], sems.at[slot]))
    for copy in copies[:1] + copies[2:] + copies[1:2]:
        copy.start()
    weight_scr[...] = jnp.zeros_like(weight_scr)
    out_ref[...] = jnp.zeros_like(out_ref)
    copies[0].wait()
    for a in range(3):
        for b in range(3):
            at = (a * 3 + b) * 3
            weight_scr[at : at + 3, :] = weight_ref[a, b].astype(F32)
    weight = weight_scr[...].astype(BF16)
    column = lax.broadcasted_iota(jnp.int32, (devices, pixels), 1) % cols

    def finish(part):
        def tap(a, b, o):
            rows = pl.ds(((a * 3 + b) * 3 + o) * devices, devices)
            return jnp.concatenate([taps_refs[part][k, rows, :] for k in range(pieces)], axis=1)

        for o in range(3):
            total = None
            for a in range(3):
                term = tap(a, 1, o)
                term = term + jnp.where(column == 0, 0.0, pltpu.roll(tap(a, 0, o), 1, 1))
                term = term + jnp.where(column == cols - 1, 0.0, pltpu.roll(tap(a, 2, o), pixels - 1, 1))
                term = jnp.concatenate([term, jnp.zeros((devices, lanes - pixels), F32)], axis=1)
                if a < 2:
                    term = pltpu.roll(term, (2 - a) * cols, 1)
                total = term if total is None else total + term
            for k in range(lanes // LANES):
                rows = pl.ds(o * group + part, devices, stride=pitch)
                out_ref[k, rows, :] = total[:, k * LANES : (k + 1) * LANES]

    def edge_rows():
        target_scr[:, 0:cols] = target_ref[...].reshape(target_scr.shape[0], cols).astype(F32)
        edges = []
        for y in (0, block_rows - 1):
            for o in range(3):
                for part in range(group):
                    rows = pl.ds((part * 3 + o) * block_rows + y, devices, stride=group * 3 * block_rows)
                    edges.append(target_scr[rows, :][:, 0:cols])
        edges.append(jnp.zeros((devices, lanes - len(edges) * cols), F32))
        edges = jnp.concatenate(edges, axis=1)
        for k in range(lanes // LANES):
            out_ref[k, pl.ds(3 * group, devices, stride=pitch), :] = edges[:, k * LANES : (k + 1) * LANES]

    step = frames // chunks
    done = 0
    for chunk in range(chunks):
        for slot in range(chunk * step, (chunk + 1) * step):
            copies[2 + slot].wait()
        if chunk == chunks - 1:
            copies[1].wait()
        for slot in range(chunk * step, (chunk + 1) * step):
            frame = slot % devices * group + slot // devices
            product = mat(weight, feat_ref[frame * pixels : (frame + 1) * pixels, :], NT)
            for k in range(pieces):
                rows = pl.ds(slot % devices, taps, stride=devices)
                taps_refs[slot // devices][k, rows, :] = product[:, k * LANES : (k + 1) * LANES]
        if chunk == chunks - 1:
            edge_rows()
        while (done + 1) * devices <= chunk * step or (chunk == chunks - 1 and done < group):
            finish(done)
            done += 1
    for k in range(lanes // LANES):
        pay_ref[:, k * LANES : (k + 1) * LANES] = out_ref[k].astype(BF16)


def forward_call(features, target, weight, frames, devices, group, cols, lanes, pitch):
    pixels = features.shape[0] // frames
    channels = features.shape[1]
    chunks = 2
    return pl.pallas_call(
        functools.partial(
            forward_kernel, frames=frames, devices=devices, group=group, cols=cols, lanes=lanes, chunks=chunks
        ),
        out_shape=jax.ShapeDtypeStruct((devices * pitch, lanes), BF16),
        in_specs=[HBM, HBM, HBM],
        out_specs=VM,
        scratch_shapes=[
            pltpu.VMEM(features.shape, BF16),
            pltpu.VMEM(target.shape, BF16),
            pltpu.VMEM(weight.shape, BF16),
            pltpu.VMEM((32, channels), F32),
            pltpu.VMEM((3 * pixels // cols * frames, LANES), F32),
            pltpu.VMEM((lanes // LANES, devices * pitch, LANES), F32),
            pltpu.SemaphoreType.DMA((frames + 2,)),
        ]
        + [pltpu.VMEM((pixels // LANES, 32 * devices, LANES), F32)] * group,
        compiler_params=WHOLE,
        cost_estimate=pl.CostEstimate(flops=2 * features.size * 27, bytes_accessed=2 * features.size, transcendentals=0),
        name="forward_taps",
    )(features, target, weight)


def inner_kernel(pay_ref, target_ref, inner_ref, scr, zin, *, frames, devices, group, block_rows, cols):
    scr[:, 0:cols] = target_ref[...].reshape(scr.shape[0], cols).astype(F32)
    stride = group * 3 * block_rows
    lanes = pay_ref.shape[1]
    pitch = pay_ref.shape[0] // devices
    for k in range(lanes // LANES):
        zin[k] = pay_ref[:, k * LANES : (k + 1) * LANES].astype(F32)
    for o in range(3):
        for part in range(group):
            at = o * frames + part * devices
            rows = [jnp.zeros((devices, cols), F32)]
            rows += [
                scr[pl.ds((part * 3 + o) * block_rows + y, devices, stride=stride), :][:, 0:cols]
                for y in range(block_rows)
            ]
            rows.append(jnp.zeros((devices, lanes - (block_rows + 1) * cols), F32))
            wanted = jnp.concatenate(rows, axis=1)
            lane = lax.broadcasted_iota(jnp.int32, wanted.shape, 1)
            inside = (lane >= 2 * cols) & (lane < block_rows * cols)
            row = pl.ds(o * group + part, devices, stride=pitch)
            own = jnp.concatenate([zin[k, row, :] for k in range(lanes // LANES)], axis=1)
            inner_ref[at : at + devices, :] = loss_scale * (jnp.where(inside, own, 0.0) - wanted)


def inner_call(payload, target, frames, devices, group, block_rows, cols):
    lanes = payload.shape[1]
    return pl.pallas_call(
        functools.partial(
            inner_kernel, frames=frames, devices=devices, group=group, block_rows=block_rows, cols=cols
        ),
        out_shape=jax.ShapeDtypeStruct((3 * frames, lanes), F32),
        in_specs=[VM, VM],
        out_specs=VM,
        scratch_shapes=[
            pltpu.VMEM((frames * 3 * block_rows, LANES), F32),
            pltpu.VMEM((lanes // LANES, payload.shape[0], LANES), F32),
        ],
        compiler_params=PART,
        cost_estimate=pl.CostEstimate(flops=10**8, bytes_accessed=10**6, transcendentals=0),
        name="inner_rows",
    )(payload, target)


def shift_rows(values, step, period):
    size = values.shape[0]
    row = lax.broadcasted_iota(jnp.int32, values.shape, 0) % period
    rolled = pltpu.roll(values, step % size, 0)
    source = row - step
    return jnp.where((source >= 0) & (source < period), rolled, 0.0)


def gate_of(values):
    logistic = 0.5 + 0.5 * jnp.tanh(0.5 * values)
    return (values * logistic).astype(BF16), logistic * (1.0 + values * (1.0 - logistic))


def edge_planes(zin, zout, first, last, devices, group, cols, lanes, pitch):
    row = pl.ds(3 * group, devices, stride=pitch)
    target = jnp.concatenate([zin[k, row, :] for k in range(lanes // LANES)], axis=1)
    outer, inner = [], []
    for e, rows, other, move in ((0, first, last, 1), (1, last, first, -1)):
        for o in range(3):
            for part in range(group):
                at = ((1 - e) * 3 * group + o * group + part) * cols
                near = other[part][:, o * cols : (o + 1) * cols] - target[:, at : at + cols]
                outer.append(shift_rows(loss_scale * near, move, devices))
                inner.append(rows[part][:, o * cols : (o + 1) * cols])
    for i, pieces in enumerate((outer, inner)):
        pieces.append(jnp.zeros((devices, lanes - 6 * group * cols), F32))
        plane = jnp.concatenate(pieces, axis=1)
        for k in range(lanes // LANES):
            zout[k, pl.ds(3 * group + i, devices, stride=pitch), :] = plane[:, k * LANES : (k + 1) * LANES]


def disc_kernel(
    pay_ref, head_ref, window, band_ref, second, unwindow, third_hbm, fourth_hbm, out_ref,
    zin, third, fourth, rows_in, act_one, slope_one, cols_two, act_two, slope_two, act_three, cols_four,
    pull_four, pull_three, pull_two, zout, sems, *, devices, group, cols, block_rows, period,
):
    lanes = pay_ref.shape[1]
    pitch = pay_ref.shape[0] // devices
    span = block_rows + 2
    unit = group * period
    wide = 3 * cols
    d1 = (act_one.shape[1]) // (cols // 2 + 2)
    d2, d3, d4 = second.shape[1], third.shape[1], fourth.shape[1]
    x1, x2, x3 = cols // 2, cols // 4, cols // 8
    x4 = x3 - 1
    quarter = fourth.shape[0] // 4
    copies = [
        pltpu.make_async_copy(
            fourth_hbm.at[pl.ds(a * quarter, quarter), :], fourth.at[pl.ds(a * quarter, quarter), :], sems.at[a]
        )
        for a in range(4)
    ]
    copies.append(pltpu.make_async_copy(third_hbm, third, sems.at[4]))
    for i in (4, 0, 1, 2, 3):
        copies[i].start()
    cells = block_rows // 8
    spot = lambda y, part: pl.ds((y % 8 * group + part) * period + y // 8, devices, stride=cells)
    for k in range(lanes // LANES):
        zin[k] = pay_ref[:, k * LANES : (k + 1) * LANES].astype(F32)
    zout[...] = jnp.zeros_like(zout)
    firsts, lasts = [], []
    for part in range(group):
        planes = []
        for o in range(3):
            pieces = [zin[k, pl.ds(o * group + part, devices, stride=pitch), :] for k in range(lanes // LANES)]
            planes.append(jnp.concatenate(pieces, axis=1))
        lines = [
            jnp.concatenate(
                [plane[:, i * cols : (i + 1) * cols] for plane in planes]
                + [jnp.zeros((devices, 2 * LANES - wide), F32)],
                axis=1,
            )
            for i in range(span)
        ]
        lines[1] = lines[1] + shift_rows(lines[span - 1], 1, devices)
        lines[block_rows] = lines[block_rows] + shift_rows(lines[0], -1, devices)
        for y in range(block_rows):
            for k in range(2):
                rows_in[k, spot(y, part), :] = lines[y + 1][:, k * LANES : (k + 1) * LANES]
        firsts.append(lines[1])
        lasts.append(lines[block_rows])
    image = jnp.concatenate([rows_in[0], rows_in[1]], axis=1)[:, :wide].astype(BF16)
    wins = mat(image, window[...])
    ext = [wins[r * unit : (r + 1) * unit] for r in range(8)]
    ext = [shift_rows(ext[7], 1, period)] + ext + [shift_rows(ext[0], -1, period)]
    width_one = act_one.shape[1]
    strip = 8 * d1
    band = band_ref[...]
    for k in range(-(-width_one // strip)):
        low, high = slice(2 * k * LANES, (2 * k + 1) * LANES), slice((2 * k + 1) * LANES, (2 * k + 2) * LANES)
        left = jnp.concatenate(
            [
                jnp.concatenate([ext[2 * p + h][:, low] + ext[2 * p + h + 1][:, high] for p in range(4)], axis=0)
                for h in (0, 2)
            ],
            axis=1,
        ).astype(BF16)
        start, end = k * strip, min((k + 1) * strip, width_one)
        act, slope = gate_of(mat(left, band[:, : end - start]))
        if k == 0 or end == width_one:
            lane = start + lax.broadcasted_iota(jnp.int32, slope.shape, 1)
            inside = (lane >= d1) & (lane < width_one - d1)
            slope = jnp.where(inside, slope, 0.0)
            act = jnp.where(inside, act.astype(F32), 0.0).astype(BF16)
        slope_one[:, start:end] = slope
        act_one[unit : 5 * unit, start:end] = act
        actual = act.astype(F32)
        act_one[0:unit, start:end] = shift_rows(actual[3 * unit :], 1, period).astype(BF16)
        act_one[5 * unit :, start:end] = shift_rows(actual[:unit], -1, period).astype(BF16)
    for x in range(x2):
        for a in range(4):
            for p in range(2):
                cols_two[(x * 2 + p) * unit : (x * 2 + p + 1) * unit, a * 4 * d1 : (a + 1) * 4 * d1] = act_one[
                    (2 * p + a) * unit : (2 * p + a + 1) * unit, 2 * x * d1 : (2 * x + 4) * d1
                ]
    pre = mat(cols_two[...], second[...])
    act, slope = gate_of(pre)
    slope_two[...] = slope
    act_two[:, 0:d2] = jnp.zeros((4 * unit, d2), BF16)
    act_two[:, (x2 + 1) * d2 :] = jnp.zeros((4 * unit, d2), BF16)
    for x in range(x2):
        block = act[x * 2 * unit : (x + 1) * 2 * unit]
        actual = block.astype(F32)
        at = slice((x + 1) * d2, (x + 2) * d2)
        act_two[unit : 3 * unit, at] = block
        act_two[0:unit, at] = shift_rows(actual[unit:], 1, period).astype(BF16)
        act_two[3 * unit :, at] = shift_rows(actual[:unit], -1, period).astype(BF16)
    left = jnp.concatenate(
        [
            jnp.concatenate([act_two[a * unit : (a + 1) * unit, 2 * x * d2 : (2 * x + 4) * d2] for a in range(4)], axis=1)
            for x in range(x3)
        ],
        axis=0,
    )
    copies[4].wait()
    act, slope_three = gate_of(mat(left, third[...]))
    act_three[:, 0:d3] = jnp.zeros((4 * unit, d3), BF16)
    act_three[:, (x3 + 1) * d3 :] = jnp.zeros((4 * unit, d3), BF16)
    for x in range(x3):
        block = act[x * unit : (x + 1) * unit]
        actual = block.astype(F32)
        at = slice((x + 1) * d3, (x + 2) * d3)
        act_three[unit : 2 * unit, at] = block
        for a in (0, 2, 3):
            act_three[a * unit : (a + 1) * unit, at] = shift_rows(actual, 1 - a, period).astype(BF16)
    for x in range(x4):
        for a in range(4):
            cols_four[x * unit : (x + 1) * unit, a * 4 * d3 : (a + 1) * 4 * d3] = act_three[
                a * unit : (a + 1) * unit, x * d3 : (x + 4) * d3
            ]
    edge_planes(zin, zout, firsts, lasts, devices, group, cols, lanes, pitch)
    row = lax.broadcasted_iota(jnp.int32, (unit, d4), 0) % period
    head = head_ref[...].astype(F32) * -loss_scale
    heads = []
    for x in range(x4):
        total = None
        for a in range(4):
            taps = [head[a * 4 + b : a * 4 + b + 1, :] for b in range(4) if 0 <= x - b + 1 < x4 - 1]
            tap = functools.reduce(lambda u, v: u + v, taps)
            inside = (row - a + 1 >= 0) & (row - a + 1 < period - 2) & (row < period - 1)
            term = jnp.where(inside, jnp.broadcast_to(tap, (unit, d4)), 0.0)
            total = term if total is None else total + term
        heads.append(total)
    pre = None
    for a in range(4):
        copies[a].wait()
        term = mat(cols_four[:, a * quarter : (a + 1) * quarter], fourth[a * quarter : (a + 1) * quarter, :])
        pre = term if pre is None else pre + term
    _, slope = gate_of(pre)
    cot = (jnp.concatenate(heads, axis=0) * slope).astype(BF16)
    pull_four[...] = mat(cot, fourth[...], NT)
    cots = []
    for x in range(x3):
        total = None
        for a in range(4):
            term = None
            for b in range(4):
                source = x - b + 1
                if 0 <= source < x4:
                    piece = pull_four[source * unit : (source + 1) * unit, (a * 4 + b) * d3 : (a * 4 + b + 1) * d3]
                    term = piece if term is None else term + piece
            if a != 1:
                term = shift_rows(term, a - 1, period)
            total = term if total is None else total + term
        cots.append((total * slope_three[x * unit : (x + 1) * unit]).astype(BF16))
    pull_three[...] = mat(jnp.concatenate(cots, axis=0), third[...], NT)
    cots = []
    for x in range(x2):
        terms = []
        for a in range(4):
            term = None
            for b in range(4):
                if (x - b + 1) % 2 == 0 and 0 <= (x - b + 1) // 2 < x3:
                    source = (x - b + 1) // 2
                    piece = pull_three[source * unit : (source + 1) * unit, (a * 4 + b) * d2 : (a * 4 + b + 1) * d2]
                    term = piece if term is None else term + piece
            terms.append(term)
        even = terms[1] + shift_rows(terms[3], 1, period)
        odd = terms[2] + shift_rows(terms[0], -1, period)
        both = jnp.concatenate([even, odd], axis=0)
        cots.append((both * slope_two[x * 2 * unit : (x + 1) * 2 * unit]).astype(BF16))
    pull_two[...] = mat(jnp.concatenate(cots, axis=0), second[...], NT)
    strips = []
    for k in range(x2 + 1):
        terms = {}
        for p in range(2):
            for a in range(4):
                term = None
                if k < x2:
                    term = pull_two[(2 * k + p) * unit : (2 * k + p + 1) * unit, a * 4 * d1 : (a * 4 + 2) * d1]
                if k > 0:
                    other = pull_two[(2 * k - 2 + p) * unit : (2 * k - 1 + p) * unit, (a * 4 + 2) * d1 : (a + 1) * 4 * d1]
                    term = other if term is None else term + other
                terms[p, a] = term
        both = jnp.concatenate(
            [
                terms[0, 1] + shift_rows(terms[1, 3], 1, period),
                terms[0, 2] + terms[1, 0],
                terms[0, 3] + terms[1, 1],
                terms[1, 2] + shift_rows(terms[0, 0], -1, period),
            ],
            axis=0,
        )
        strips.append((both * slope_one[:, 2 * k * d1 : (2 * k + 2) * d1]).astype(BF16))
    cot = jnp.concatenate(strips, axis=1)
    sums = []
    for k in range(-(-width_one // strip)):
        start, end = k * strip, min((k + 1) * strip, width_one)
        pulls = mat(cot[:, start:end], band[:, : end - start], NT)
        groups = []
        for m in range(5):
            terms = [
                pulls[p * unit : (p + 1) * unit, (m - p) * LANES : (m - p + 1) * LANES] for p in range(4) if 0 <= m - p < 2
            ]
            groups.append(functools.reduce(lambda u, v: u + v, terms))
        sums.append(jnp.concatenate(groups, axis=0))
    sums = jnp.concatenate(sums, axis=1)
    upper = sums.astype(BF16)
    lower = (sums - upper.astype(F32)).astype(BF16)
    low = lax.broadcasted_iota(jnp.int32, upper.shape, 1) % LANES < LANES // 2
    blank = jnp.zeros_like(upper)
    split = [jnp.where(low, upper, blank), jnp.where(low, lower, blank), jnp.where(low, blank, upper), jnp.where(low, blank, lower)]
    both = mat(jnp.concatenate(split, axis=0), unwindow[...])
    size = 5 * unit
    odd = both[:size] + both[size : 2 * size]
    even = both[2 * size : 3 * size] + both[3 * size :]
    odd = [odd[m * unit : (m + 1) * unit, :] for m in range(5)]
    even = [even[m * unit : (m + 1) * unit, :] for m in range(5)]
    phases = [even[r // 2] if r % 2 == 0 else odd[(r + 1) // 2] for r in range(8)]
    phases[0] = phases[0] + shift_rows(even[4], 1, period)
    phases[7] = phases[7] + shift_rows(odd[0], -1, period)
    image = jnp.concatenate(phases, axis=0)
    image = jnp.concatenate([image, jnp.zeros((image.shape[0], 2 * LANES - wide), F32)], axis=1)
    for k in range(2):
        rows_in[k] = image[:, k * LANES : (k + 1) * LANES]
    for part in range(group):
        lines = [
            jnp.concatenate([rows_in[k, spot(y, part), :] for k in range(2)], axis=1)[:, :wide]
            for y in range(block_rows)
        ]
        lines = [shift_rows(lines[-1], 1, devices)] + lines + [shift_rows(lines[0], -1, devices)]
        for o in range(3):
            plane = [line[:, o * cols : (o + 1) * cols] for line in lines]
            plane.append(jnp.zeros((devices, lanes - span * cols), F32))
            plane = jnp.concatenate(plane, axis=1)
            for k in range(lanes // LANES):
                zout[k, pl.ds(o * group + part, devices, stride=pitch), :] = plane[:, k * LANES : (k + 1) * LANES]
    for k in range(lanes // LANES):
        out_ref[:, k * LANES : (k + 1) * LANES] = zout[k].astype(BF16)


def window_of(at, cols):
    k, rest = at // LANES, at % LANES
    inner = rest % (LANES // 2)
    colour = jnp.where(inner >= 18, 1, 0) + jnp.where(inner >= 36, 1, 0)
    x = 16 * k - 3 + inner - 18 * colour
    inside = (inner < 54) & (x >= 0) & (x < cols)
    return jnp.where(inside, colour * cols + x, -1), rest // (LANES // 2)


def stage_kernel(first_ref, second_hbm, window, unwindow, second, band, scr, sem, *, cols):
    copy = pltpu.make_async_copy(second_hbm, second, sem.at[0])
    copy.start()
    row = lax.broadcasted_iota(jnp.int32, window.shape, 0)
    lane = lax.broadcasted_iota(jnp.int32, window.shape, 1)
    place, half = window_of(lane // (2 * LANES) * LANES + lane % LANES, cols)
    window[...] = jnp.where((place == row) & (half == lane // LANES % 2), 1.0, 0.0).astype(BF16)
    place, _ = window_of(lax.broadcasted_iota(jnp.int32, unwindow.shape, 0), cols)
    column = lax.broadcasted_iota(jnp.int32, unwindow.shape, 1)
    unwindow[...] = jnp.where(place == column, 1.0, 0.0).astype(BF16)
    d1 = first_ref.shape[-1]
    scr[...] = jnp.zeros_like(scr)
    row = lax.broadcasted_iota(jnp.int32, (18, 8 * d1), 0)
    tap = row - 2 * (lax.broadcasted_iota(jnp.int32, (18, 8 * d1), 1) // d1)
    for a in range(4):
        lines = [first_ref[a, b].astype(F32) for b in range(4)]
        for c in range(3):
            block = jnp.zeros((18, 8 * d1), F32)
            for b in range(4):
                line = jnp.concatenate([lines[b][c : c + 1, :]] * 8, axis=1)
                block = jnp.where(tap == b, jnp.broadcast_to(line, block.shape), block)
            at = a * LANES // 2 + c * 18
            scr[at : at + 18, :] = block
    band[...] = scr[...].astype(BF16)
    copy.wait()


def stage_call(first, second, cols):
    d1, d2 = first.shape[-1], second.shape[-1]
    count = -(-(cols // 2 + 2) // 8)
    shapes = [(3 * cols, count * 2 * LANES), (count * LANES, 3 * cols), (16 * d1, d2), (2 * LANES, 8 * d1)]
    return pl.pallas_call(
        functools.partial(stage_kernel, cols=cols),
        out_shape=tuple(jax.ShapeDtypeStruct(shape, BF16) for shape in shapes),
        in_specs=[VM, HBM],
        out_specs=(VM,) * 4,
        scratch_shapes=[pltpu.VMEM((2 * LANES, 8 * d1), F32), pltpu.SemaphoreType.DMA((1,))],
        compiler_params=PART,
        cost_estimate=pl.CostEstimate(flops=10**8, bytes_accessed=4 * 10**6, transcendentals=0),
        name="stage_weights",
    )(first, second.reshape(16 * d1, d2))


def disc_call(payload, staged, third, fourth, head, devices, group, cols, block_rows):
    period = devices * block_rows // 8
    unit = group * period
    window, unwindow, second, band = staged
    d1, d2, d3, d4 = band.shape[1] // 8, second.shape[1], third.shape[-1], fourth.shape[-1]
    x2, x3 = cols // 4, cols // 8
    x4 = x3 - 1
    width_one = (cols // 2 + 2) * d1
    args = (
        payload,
        head.reshape(16, d4),
        window,
        band,
        second,
        unwindow,
        third.reshape(16 * d2, d3),
        fourth.reshape(16 * d3, d4),
    )
    lanes = payload.shape[1]
    return pl.pallas_call(
        functools.partial(
            disc_kernel, devices=devices, group=group, cols=cols, block_rows=block_rows, period=period
        ),
        out_shape=jax.ShapeDtypeStruct(payload.shape, BF16),
        in_specs=[VM] * 6 + [HBM] * 2,
        out_specs=VM,
        scratch_shapes=[
            pltpu.VMEM((lanes // LANES, payload.shape[0], LANES), F32),
            pltpu.VMEM((16 * d2, d3), BF16),
            pltpu.VMEM((16 * d3, d4), BF16),
            pltpu.VMEM((2, 8 * unit, LANES), F32),
            pltpu.VMEM((6 * unit, width_one), BF16),
            pltpu.VMEM((4 * unit, width_one), F32),
            pltpu.VMEM((x2 * 2 * unit, 16 * d1), BF16),
            pltpu.VMEM((4 * unit, (x2 + 2) * d2), BF16),
            pltpu.VMEM((x2 * 2 * unit, d2), F32),
            pltpu.VMEM((4 * unit, (x3 + 2) * d3), BF16),
            pltpu.VMEM((x4 * unit, 16 * d3), BF16),
            pltpu.VMEM((x4 * unit, 16 * d3), F32),
            pltpu.VMEM((x3 * unit, 16 * d2), F32),
            pltpu.VMEM((x2 * 2 * unit, 16 * d1), F32),
            pltpu.VMEM((lanes // LANES, payload.shape[0], LANES), F32),
            pltpu.SemaphoreType.DMA((5,)),
        ],
        compiler_params=MOST,
        cost_estimate=pl.CostEstimate(flops=4 * 10**9, bytes_accessed=8 * 10**6, transcendentals=10**6),
        name="disc_rows",
    )(*args)


def put_taps(plane, taps_ref, frames, cols, pieces, padded):
    lanes = plane.shape[1]
    column = lax.broadcasted_iota(jnp.int32, plane.shape, 1) % cols
    for b in range(3):
        moved = plane
        if b == 0:
            moved = jnp.where(column == cols - 1, 0.0, pltpu.roll(plane, lanes - 1, 1))
        if b == 2:
            moved = jnp.where(column == 0, 0.0, pltpu.roll(plane, 1, 1))
        for a in range(3):
            turned = moved if a == 2 else pltpu.roll(moved, lanes - (2 - a) * cols, 1)
            for k in range(pieces):
                taps_ref[k, pl.ds((a * 3 + b) * 3 * frames, 3 * frames), :] = turned[:, k * LANES : (k + 1) * LANES]
    for k in range(pieces):
        taps_ref[k, pl.ds(27 * frames, (padded - 27) * frames), :] = jnp.zeros(((padded - 27) * frames, LANES), F32)


def unpack(plane_ref, zin, devices, group):
    lanes = plane_ref.shape[1]
    pitch = plane_ref.shape[0] // devices
    for k in range(lanes // LANES):
        zin[k] = plane_ref[:, k * LANES : (k + 1) * LANES].astype(F32)
    blocks = []
    for o in range(3):
        for part in range(group):
            row = pl.ds(o * group + part, devices, stride=pitch)
            blocks.append(jnp.concatenate([zin[k, row, :] for k in range(lanes // LANES)], axis=1))
    return jnp.concatenate(blocks, axis=0)


def edge_blocks(zin, lanes, devices, group, cols):
    pitch = zin.shape[1] // devices
    edges = []
    for i in range(2):
        row = pl.ds(3 * group + i, devices, stride=pitch)
        edges.append(jnp.concatenate([zin[k, row, :] for k in range(lanes // LANES)], axis=1))
    blocks = []
    for i, e in ((0, 0), (1, 0), (1, 1), (0, 1)):
        pieces = [
            edges[i][:, (e * 3 * group + at) * cols : (e * 3 * group + at + 1) * cols] for at in range(3 * group)
        ]
        blocks.append(jnp.concatenate(pieces, axis=0))
    above, first, last, below = blocks
    return above, first * loss_scale, last * loss_scale, below


def weigh(taps_ref, feat_ref, frames, devices, group, pieces, choose):
    total = jnp.zeros((32, feat_ref.shape[1]), F32)
    for frame in range(frames):
        rows = pl.ds(slot_of(frame, devices, group), 32, stride=frames)
        taps = jnp.concatenate([taps_ref[k, rows, :] for k in range(pieces)], axis=1).astype(BF16)
        total = total + mat(taps, choose(frame))
    return total


def rec_kernel(after_hbm, inner_ref, feat_ref, part_ref, taps_ref, *, frames, devices, group, cols, block_rows):
    pixels = block_rows * cols
    put_taps(inner_ref[...], taps_ref, frames, cols, pixels // LANES, 32)
    whole = lambda frame: feat_ref[frame * pixels : (frame + 1) * pixels, :]
    part_ref[...] = weigh(taps_ref, feat_ref, frames, devices, group, pixels // LANES, whole)


def both_kernel(
    rec_ref, plane_ref, feat_ref, part_ref, gan_taps, edge_taps, zin, *, frames, devices, group, cols, block_rows
):
    lanes = plane_ref.shape[1]
    pixels = block_rows * cols
    put_taps(unpack(plane_ref, zin, devices, group), gan_taps, frames, cols, pixels // LANES, 32)
    above, first, last, below = edge_blocks(zin, lanes, devices, group, cols)
    none = jnp.zeros((above.shape[0], 4 * cols), F32)
    plane = jnp.concatenate([above, first, none, last, below], axis=1)
    size = 8 * cols
    lane = lax.broadcasted_iota(jnp.int32, plane.shape, 1)
    for b in range(3):
        moved = plane
        if b == 0:
            moved = jnp.where(lane % cols == cols - 1, 0.0, pltpu.roll(plane, size - 1, 1))
        if b == 2:
            moved = jnp.where(lane % cols == 0, 0.0, pltpu.roll(plane, 1, 1))
        for a in range(3):
            turned = moved if a == 2 else pltpu.roll(moved, size - (2 - a) * cols, 1)
            turned = jnp.where(lane % (4 * cols) < 2 * cols, turned, 0.0)
            for k in range(size // LANES):
                rows = pl.ds((a * 3 + b) * 3 * frames, 3 * frames)
                edge_taps[k, rows, :] = turned[:, k * LANES : (k + 1) * LANES]
    for k in range(size // LANES):
        edge_taps[k, pl.ds(27 * frames, 5 * frames), :] = jnp.zeros((5 * frames, LANES), F32)
    whole = lambda frame: feat_ref[frame * pixels : (frame + 1) * pixels, :]
    gan = weigh(gan_taps, feat_ref, frames, devices, group, pixels // LANES, whole)

    def ends(frame):
        start, end = frame * pixels, (frame + 1) * pixels
        tail = feat_ref[end - 2 * cols : end, :]
        return jnp.concatenate([feat_ref[start : start + 4 * cols, :], tail, tail], axis=0)

    rec = rec_ref[...] + weigh(edge_taps, feat_ref, frames, devices, group, size // LANES, ends)
    blank = jnp.zeros((part_ref.shape[1] - 54, gan.shape[1]), F32)
    total = jnp.concatenate([rec[0:27], gan[0:27], blank], axis=0).astype(BF16)
    for i in range(part_ref.shape[0]):
        part_ref[i] = total


def turn_kernel(
    inner_ref, plane_ref, out_ref, rec_taps, gan_taps, zin, *, frames, devices, group, cols, block_rows
):
    pieces = block_rows * cols // LANES
    pixels = pieces * LANES
    put_taps(unpack(plane_ref, zin, devices, group), gan_taps, frames, cols, pieces, 32)
    lanes = inner_ref.shape[1]
    above, first, last, below = edge_blocks(zin, lanes, devices, group, cols)
    none = lambda count: jnp.zeros((above.shape[0], count), F32)
    edges = jnp.concatenate(
        [above, first, none((block_rows - 2) * cols), last, below, none(lanes - (block_rows + 2) * cols)], axis=1
    )
    put_taps(inner_ref[...] + edges, rec_taps, frames, cols, pieces, 32)
    for pair in range(frames // 2):
        for k in range(pieces):
            parts = []
            for frame in (2 * pair, 2 * pair + 1):
                rows = pl.ds(slot_of(frame, devices, group), 32, stride=frames)
                parts += [rec_taps[k, rows, :], gan_taps[k, rows, :]]
            at = pair * pixels + k * LANES
            out_ref[at : at + LANES, :] = jnp.concatenate(parts, axis=0).T.astype(BF16)


def taps_call(kernel, specs, operands, out, scratch, frames, devices, group, cols, block_rows, flops, name):
    return pl.pallas_call(
        functools.partial(kernel, frames=frames, devices=devices, group=group, cols=cols, block_rows=block_rows),
        out_shape=out,
        in_specs=specs,
        out_specs=jax.tree.map(lambda _: VM, out),
        scratch_shapes=scratch,
        compiler_params=PART,
        cost_estimate=pl.CostEstimate(flops=flops, bytes_accessed=4 * 10**6, transcendentals=0),
        name=name,
    )(*operands)


def final_kernel(
    taps_ref, sums_ref, weight_ref, out_hbm, grad_ref, adapt_ref, weight_scr, both_ref, out_ref, sems, *, pixels, chunk
):
    weight_scr[...] = jnp.zeros_like(weight_scr)
    for a in range(3):
        for b in range(3):
            at = (a * 3 + b) * 3
            weight_scr[at : at + 3, :] = weight_ref[a, b].astype(F32)
    total = sums_ref[0].astype(F32)
    for i in range(1, sums_ref.shape[0]):
        total = total + sums_ref[i].astype(F32)
    rec, gan = total[0:27], total[27:54]
    norm = lambda values: jnp.sqrt(jnp.sum(jnp.sum(values * values, axis=1, keepdims=True), axis=0, keepdims=True))
    adaptive = norm(rec) / (norm(gan) + epsilon)
    grad = (rec + adaptive * gan) / pixels
    for a in range(3):
        for b in range(3):
            at = (a * 3 + b) * 3
            grad_ref[a, b] = grad[at : at + 3, :]
    adapt_ref[...] = adaptive
    weight = weight_scr[...].astype(BF16)
    padded, channels = weight.shape
    scaled = (adaptive * weight.astype(F32)).astype(BF16)
    both_ref[...] = jnp.zeros_like(both_ref)
    both_ref[0:padded, 0:channels] = weight
    both_ref[padded : 2 * padded, 0:channels] = scaled
    both_ref[2 * padded : 3 * padded, channels:] = weight
    both_ref[3 * padded :, channels:] = scaled
    pairs = taps_ref.shape[0] // chunk
    stores = []
    for pair in range(pairs):
        product = mat(taps_ref[pair * chunk : (pair + 1) * chunk], both_ref[...]).astype(BF16)
        rows = pl.ds(2 * pair * chunk, 2 * chunk)
        out_ref[2 * pair * chunk : (2 * pair + 1) * chunk] = product[:, :channels]
        out_ref[(2 * pair + 1) * chunk : (2 * pair + 2) * chunk] = product[:, channels:]
        stores.append(pltpu.make_async_copy(out_ref.at[rows], out_hbm.at[rows], sems.at[pair]))
        stores[-1].start()
    for copy in stores:
        copy.wait()


def final_call(taps, sums, weight, pixels, chunk):
    padded, channels = 32, weight.shape[-1]
    rows = 2 * taps.shape[0]
    return pl.pallas_call(
        functools.partial(final_kernel, pixels=pixels, chunk=chunk),
        out_shape=(
            jax.ShapeDtypeStruct((rows, channels), BF16),
            jax.ShapeDtypeStruct((3, 3, 3, channels), F32),
            jax.ShapeDtypeStruct((1, 1), F32),
        ),
        in_specs=[VM] * 3,
        out_specs=(HBM, VM, VM),
        scratch_shapes=[
            pltpu.VMEM((padded, channels), F32),
            pltpu.VMEM((4 * padded, 2 * channels), BF16),
            pltpu.VMEM((rows, channels), BF16),
            pltpu.SemaphoreType.DMA((rows // (2 * chunk),)),
        ],
        compiler_params=PART,
        cost_estimate=pl.CostEstimate(flops=4 * rows * channels * padded, bytes_accessed=4 * rows * channels, transcendentals=0),
        name="feature_pull",
    )(taps, sums, weight)


def per_device(
    features, target, conv_weight, disc_first, disc_second, disc_third, disc_fourth, disc_head
):
    row = ("far", "near")
    devices = lax.axis_size(row)
    clips = lax.axis_size("clip")
    _, frames, block_rows, cols, channels = features.shape
    group = frames // devices
    pixels = clips * devices * frames * block_rows * cols
    lanes = up_to((block_rows + 2) * cols, LANES)
    pitch = up_to(3 * group + 2, 8)
    sizes = (frames, devices, group, cols, block_rows)
    feats = features.reshape(frames * block_rows * cols, channels)
    wanted = target[0].transpose(0, 2, 1, 3)
    payload = forward_call(feats, wanted, conv_weight, frames, devices, group, cols, lanes, pitch)
    trade = lambda values: lax.all_to_all(
        values.reshape(devices, pitch, lanes), row, split_axis=0, concat_axis=0, tiled=True
    ).reshape(devices * pitch, lanes)
    arrived = trade(payload)
    inner = inner_call(payload, wanted, frames, devices, group, block_rows, cols)
    _, disc_first = lax.optimization_barrier((payload, disc_first))
    staged = stage_call(disc_first, disc_second, cols)
    arrived, inner = lax.optimization_barrier((arrived, inner))
    sent = disc_call(arrived, staged, disc_third, disc_fourth, disc_head, devices, group, cols, block_rows)
    returned = trade(sent)
    taps_scratch = pltpu.VMEM((block_rows * cols // LANES, 32 * frames, LANES), F32)
    plane_scratch = pltpu.VMEM((lanes // LANES, devices * pitch, LANES), F32)
    flops = 4 * features.size * 27
    rec_part = taps_call(
        rec_kernel, [HBM, VM, VM], (sent, inner, feats), jax.ShapeDtypeStruct((32, channels), F32),
        [taps_scratch], *sizes, flops, "rec_taps",
    )
    part = taps_call(
        both_kernel, [VM, VM, VM], (rec_part, returned, feats),
        jax.ShapeDtypeStruct((clips * lax.axis_size("near"), 56, channels), BF16),
        [taps_scratch, pltpu.VMEM((8 * cols // LANES, 32 * frames, LANES), F32), plane_scratch], *sizes, flops, "both_taps",
    )
    share = lambda values, axes: lax.all_to_all(values, axes, split_axis=0, concat_axis=0, tiled=True)
    sums = share(sum_call(share(part, ("clip", "near")), lax.axis_size("far")), "far")
    taps = taps_call(
        turn_kernel, [VM, VM], (inner, returned), jax.ShapeDtypeStruct((feats.shape[0] // 2, LANES), BF16),
        [taps_scratch, taps_scratch, plane_scratch], *sizes, flops, "turn_taps",
    )
    image_back = returned.reshape(devices, pitch, lanes)[:, : 3 * group, cols : (block_rows + 1) * cols]
    image_back = image_back.reshape(devices, 3, group, block_rows, cols).transpose(0, 2, 3, 1, 4)
    image_back = image_back.reshape(1, frames, block_rows, 3, cols)
    feature_grad, weight_grad, adaptive = final_call(taps, sums, conv_weight, pixels, block_rows * cols)
    return (feature_grad.reshape(features.shape), image_back, weight_grad, adaptive[0, 0])


def sum_kernel(parts_ref, out_ref):
    total = parts_ref[0].astype(F32)
    for i in range(1, parts_ref.shape[0]):
        total = total + parts_ref[i].astype(F32)
    total = total.astype(BF16)
    for i in range(out_ref.shape[0]):
        out_ref[i] = total


def sum_call(parts, copies):
    return pl.pallas_call(
        sum_kernel,
        out_shape=jax.ShapeDtypeStruct((copies,) + parts.shape[1:], BF16),
        in_specs=[VM],
        out_specs=VM,
        compiler_params=PART,
        name="sum_parts",
    )(parts)


def solution(mesh):
    clips, devices = mesh.shape["clip"], mesh.shape["row"]
    near = 2 if devices % 2 == 0 else 1
    split = jax.sharding.Mesh(mesh.devices.reshape(clips, devices // near, near), ("clip", "far", "near"))
    rows = P("clip", None, ("far", "near"), None, None)
    return jax.shard_map(
        per_device,
        mesh=split,
        in_specs=(rows, rows, P(), P(), P(), P(), P(), P()),
        out_specs=(rows, rows, P(), P()),
        check_vma=False,
    )
```

```python
import functools

import jax
import jax.numpy as jnp
import numpy as np
from jax import lax
from jax.experimental import pallas as pl
from jax.experimental.pallas import tpu as pltpu
from jax.sharding import PartitionSpec as P

loss_scale = 64.0
epsilon = 0.0001
F32 = jnp.float32
BF16 = jnp.bfloat16
LANES = 128
NN = (((1,), (0,)), ((), ()))
NT = (((1,), (1,)), ((), ()))
TN = (((0,), (0,)), ((), ()))
VM = pl.BlockSpec(memory_space=pltpu.VMEM)
HBM = pl.BlockSpec(memory_space=pl.ANY)
WHOLE = pltpu.CompilerParams(vmem_limit_bytes=60 * 2**20)
MOST = pltpu.CompilerParams(vmem_limit_bytes=48 * 2**20)
PART = pltpu.CompilerParams(vmem_limit_bytes=24 * 2**20)


def up_to(value, step):
    return -(-value // step) * step


def mat(left, right, dims=NN):
    return lax.dot_general(left, right, dims, preferred_element_type=F32)


def slot_of(frame, devices, group):
    return (frame % group) * devices + frame // group


def forward_kernel(
    feat_hbm, target_hbm, weight_hbm, pay_ref, feat_ref, target_ref, weight_ref, weight_scr, target_scr,
    taps_ref, out_ref, sems, *, frames, devices, group, cols, lanes, chunks,
):
    pixels = feat_ref.shape[0] // frames
    pieces = pixels // LANES
    pitch = out_ref.shape[1] // devices
    taps = weight_scr.shape[0]
    block_rows = pixels // cols
    copies = [
        pltpu.make_async_copy(weight_hbm, weight_ref, sems.at[frames]),
        pltpu.make_async_copy(target_hbm, target_ref, sems.at[frames + 1]),
    ]
    for slot in range(frames):
        rows = pl.ds((slot % devices * group + slot // devices) * pixels, pixels)
        copies.append(pltpu.make_async_copy(feat_hbm.at[rows, :], feat_ref.at[rows, :], sems.at[slot]))
    for copy in copies:
        copy.start()
    weight_scr[...] = jnp.zeros_like(weight_scr)
    out_ref[...] = jnp.zeros_like(out_ref)
    copies[0].wait()
    for a in range(3):
        for b in range(3):
            at = (a * 3 + b) * 3
            weight_scr[at : at + 3, :] = weight_ref[a, b].astype(F32)
    weight = weight_scr[...].astype(BF16)
    column = lax.broadcasted_iota(jnp.int32, (devices, pixels), 1) % cols

    def finish(part):
        def tap(a, b, o):
            rows = pl.ds(((a * 3 + b) * 3 + o) * frames + part * devices, devices)
            return jnp.concatenate([taps_ref[k, rows, :] for k in range(pieces)], axis=1)

        for o in range(3):
            total = None
            for a in range(3):
                term = tap(a, 1, o)
                term = term + jnp.where(column == 0, 0.0, pltpu.roll(tap(a, 0, o), 1, 1))
                term = term + jnp.where(column == cols - 1, 0.0, pltpu.roll(tap(a, 2, o), pixels - 1, 1))
                term = jnp.concatenate([term, jnp.zeros((devices, lanes - pixels), F32)], axis=1)
                if a < 2:
                    term = pltpu.roll(term, (2 - a) * cols, 1)
                total = term if total is None else total + term
            for k in range(lanes // LANES):
                rows = pl.ds(o * group + part, devices, stride=pitch)
                out_ref[k, rows, :] = total[:, k * LANES : (k + 1) * LANES]

    def edge_rows():
        target_scr[:, 0:cols] = target_ref[...].reshape(target_scr.shape[0], cols).astype(F32)
        edges = []
        for y in (0, block_rows - 1):
            for o in range(3):
                for part in range(group):
                    rows = pl.ds((part * 3 + o) * block_rows + y, devices, stride=group * 3 * block_rows)
                    edges.append(target_scr[rows, :][:, 0:cols])
        edges.append(jnp.zeros((devices, lanes - len(edges) * cols), F32))
        edges = jnp.concatenate(edges, axis=1)
        for k in range(lanes // LANES):
            out_ref[k, pl.ds(3 * group, devices, stride=pitch), :] = edges[:, k * LANES : (k + 1) * LANES]

    copies[1].wait()
    edge_rows()
    step = frames // chunks
    done = 0
    for chunk in range(chunks):
        for slot in range(chunk * step, (chunk + 1) * step):
            copies[2 + slot].wait()
        for slot in range(chunk * step, (chunk + 1) * step):
            frame = slot % devices * group + slot // devices
            product = mat(weight, feat_ref[frame * pixels : (frame + 1) * pixels, :], NT)
            for k in range(pieces):
                taps_ref[k, pl.ds(slot, taps, stride=frames), :] = product[:, k * LANES : (k + 1) * LANES]
        while (done + 1) * devices <= chunk * step or (chunk == chunks - 1 and done < group):
            finish(done)
            done += 1
    for k in range(lanes // LANES):
        pay_ref[:, k * LANES : (k + 1) * LANES] = out_ref[k].astype(BF16)


def forward_call(features, target, weight, frames, devices, group, cols, lanes, pitch):
    pixels = features.shape[0] // frames
    channels = features.shape[1]
    chunks = 2
    return pl.pallas_call(
        functools.partial(
            forward_kernel, frames=frames, devices=devices, group=group, cols=cols, lanes=lanes, chunks=chunks
        ),
        out_shape=jax.ShapeDtypeStruct((devices * pitch, lanes), BF16),
        in_specs=[HBM, HBM, HBM],
        out_specs=VM,
        scratch_shapes=[
            pltpu.VMEM(features.shape, BF16),
            pltpu.VMEM(target.shape, BF16),
            pltpu.VMEM(weight.shape, BF16),
            pltpu.VMEM((32, channels), F32),
            pltpu.VMEM((3 * pixels // cols * frames, LANES), F32),
            pltpu.VMEM((pixels // LANES, 32 * frames, LANES), F32),
            pltpu.VMEM((lanes // LANES, devices * pitch, LANES), F32),
            pltpu.SemaphoreType.DMA((frames + 2,)),
        ],
        compiler_params=WHOLE,
        cost_estimate=pl.CostEstimate(flops=2 * features.size * 27, bytes_accessed=2 * features.size, transcendentals=0),
        name="forward_taps",
    )(features, target, weight)


def inner_kernel(pay_ref, target_ref, inner_ref, scr, zin, *, frames, devices, group, block_rows, cols):
    scr[:, 0:cols] = target_ref[...].reshape(scr.shape[0], cols).astype(F32)
    stride = group * 3 * block_rows
    lanes = pay_ref.shape[1]
    pitch = pay_ref.shape[0] // devices
    for k in range(lanes // LANES):
        zin[k] = pay_ref[:, k * LANES : (k + 1) * LANES].astype(F32)
    for o in range(3):
        for part in range(group):
            at = o * frames + part * devices
            rows = [jnp.zeros((devices, cols), F32)]
            rows += [
                scr[pl.ds((part * 3 + o) * block_rows + y, devices, stride=stride), :][:, 0:cols]
                for y in range(block_rows)
            ]
            rows.append(jnp.zeros((devices, lanes - (block_rows + 1) * cols), F32))
            wanted = jnp.concatenate(rows, axis=1)
            lane = lax.broadcasted_iota(jnp.int32, wanted.shape, 1)
            inside = (lane >= 2 * cols) & (lane < block_rows * cols)
            row = pl.ds(o * group + part, devices, stride=pitch)
            own = jnp.concatenate([zin[k, row, :] for k in range(lanes // LANES)], axis=1)
            inner_ref[at : at + devices, :] = loss_scale * (jnp.where(inside, own, 0.0) - wanted)


def inner_call(payload, target, frames, devices, group, block_rows, cols):
    lanes = payload.shape[1]
    return pl.pallas_call(
        functools.partial(
            inner_kernel, frames=frames, devices=devices, group=group, block_rows=block_rows, cols=cols
        ),
        out_shape=jax.ShapeDtypeStruct((3 * frames, lanes), F32),
        in_specs=[VM, VM],
        out_specs=VM,
        scratch_shapes=[
            pltpu.VMEM((frames * 3 * block_rows, LANES), F32),
            pltpu.VMEM((lanes // LANES, payload.shape[0], LANES), F32),
        ],
        compiler_params=PART,
        cost_estimate=pl.CostEstimate(flops=10**8, bytes_accessed=10**6, transcendentals=0),
        name="inner_rows",
    )(payload, target)


def shift_rows(values, step, period):
    size = values.shape[0]
    row = lax.broadcasted_iota(jnp.int32, values.shape, 0) % period
    rolled = pltpu.roll(values, step % size, 0)
    source = row - step
    return jnp.where((source >= 0) & (source < period), rolled, 0.0)


def gate_of(values):
    logistic = 0.5 + 0.5 * jnp.tanh(0.5 * values)
    return (values * logistic).astype(BF16), logistic * (1.0 + values * (1.0 - logistic))


def edge_planes(zin, zout, first, last, devices, group, cols, lanes, pitch):
    row = pl.ds(3 * group, devices, stride=pitch)
    target = jnp.concatenate([zin[k, row, :] for k in range(lanes // LANES)], axis=1)
    outer, inner = [], []
    for e, rows, other, move in ((0, first, last, 1), (1, last, first, -1)):
        for o in range(3):
            for part in range(group):
                at = ((1 - e) * 3 * group + o * group + part) * cols
                near = other[part][:, o * cols : (o + 1) * cols] - target[:, at : at + cols]
                outer.append(shift_rows(loss_scale * near, move, devices))
                inner.append(rows[part][:, o * cols : (o + 1) * cols])
    for i, pieces in enumerate((outer, inner)):
        pieces.append(jnp.zeros((devices, lanes - 6 * group * cols), F32))
        plane = jnp.concatenate(pieces, axis=1)
        for k in range(lanes // LANES):
            zout[k, pl.ds(3 * group + i, devices, stride=pitch), :] = plane[:, k * LANES : (k + 1) * LANES]


def disc_kernel(
    pay_ref, head_ref, window, band_ref, second, unwindow, third_hbm, fourth_hbm, out_ref,
    zin, third, fourth, rows_in, act_one, slope_one, cols_two, act_two, slope_two, act_three, cols_four,
    pull_four, pull_three, pull_two, zout, sems, *, devices, group, cols, block_rows, period,
):
    lanes = pay_ref.shape[1]
    pitch = pay_ref.shape[0] // devices
    span = block_rows + 2
    unit = group * period
    wide = 3 * cols
    d1 = (act_one.shape[1]) // (cols // 2 + 2)
    d2, d3, d4 = second.shape[1], third.shape[1], fourth.shape[1]
    x1, x2, x3 = cols // 2, cols // 4, cols // 8
    x4 = x3 - 1
    quarter = fourth.shape[0] // 4
    copies = [
        pltpu.make_async_copy(
            fourth_hbm.at[pl.ds(a * quarter, quarter), :], fourth.at[pl.ds(a * quarter, quarter), :], sems.at[a]
        )
        for a in range(4)
    ]
    copies.append(pltpu.make_async_copy(third_hbm, third, sems.at[4]))
    for i in (4, 0, 1, 2, 3):
        copies[i].start()
    cells = block_rows // 8
    spot = lambda y, part: pl.ds((y % 8 * group + part) * period + y // 8, devices, stride=cells)
    for k in range(lanes // LANES):
        zin[k] = pay_ref[:, k * LANES : (k + 1) * LANES].astype(F32)
    zout[...] = jnp.zeros_like(zout)
    firsts, lasts = [], []
    for part in range(group):
        planes = []
        for o in range(3):
            pieces = [zin[k, pl.ds(o * group + part, devices, stride=pitch), :] for k in range(lanes // LANES)]
            planes.append(jnp.concatenate(pieces, axis=1))
        lines = [
            jnp.concatenate(
                [plane[:, i * cols : (i + 1) * cols] for plane in planes]
                + [jnp.zeros((devices, 2 * LANES - wide), F32)],
                axis=1,
            )
            for i in range(span)
        ]
        lines[1] = lines[1] + shift_rows(lines[span - 1], 1, devices)
        lines[block_rows] = lines[block_rows] + shift_rows(lines[0], -1, devices)
        for y in range(block_rows):
            for k in range(2):
                rows_in[k, spot(y, part), :] = lines[y + 1][:, k * LANES : (k + 1) * LANES]
        firsts.append(lines[1])
        lasts.append(lines[block_rows])
    image = jnp.concatenate([rows_in[0], rows_in[1]], axis=1)[:, :wide].astype(BF16)
    wins = mat(image, window[...])
    ext = [wins[r * unit : (r + 1) * unit] for r in range(8)]
    ext = [shift_rows(ext[7], 1, period)] + ext + [shift_rows(ext[0], -1, period)]
    width_one = act_one.shape[1]
    strip = 8 * d1
    band = band_ref[...]
    for k in range(-(-width_one // strip)):
        low, high = slice(2 * k * LANES, (2 * k + 1) * LANES), slice((2 * k + 1) * LANES, (2 * k + 2) * LANES)
        left = jnp.concatenate(
            [
                jnp.concatenate([ext[2 * p + h][:, low] + ext[2 * p + h + 1][:, high] for p in range(4)], axis=0)
                for h in (0, 2)
            ],
            axis=1,
        ).astype(BF16)
        start, end = k * strip, min((k + 1) * strip, width_one)
        act, slope = gate_of(mat(left, band[:, : end - start]))
        if k == 0 or end == width_one:
            lane = start + lax.broadcasted_iota(jnp.int32, slope.shape, 1)
            inside = (lane >= d1) & (lane < width_one - d1)
            slope = jnp.where(inside, slope, 0.0)
            act = jnp.where(inside, act.astype(F32), 0.0).astype(BF16)
        slope_one[:, start:end] = slope
        act_one[unit : 5 * unit, start:end] = act
        actual = act.astype(F32)
        act_one[0:unit, start:end] = shift_rows(actual[3 * unit :], 1, period).astype(BF16)
        act_one[5 * unit :, start:end] = shift_rows(actual[:unit], -1, period).astype(BF16)
    for x in range(x2):
        for a in range(4):
            for p in range(2):
                cols_two[(x * 2 + p) * unit : (x * 2 + p + 1) * unit, a * 4 * d1 : (a + 1) * 4 * d1] = act_one[
                    (2 * p + a) * unit : (2 * p + a + 1) * unit, 2 * x * d1 : (2 * x + 4) * d1
                ]
    pre = mat(cols_two[...], second[...])
    act, slope = gate_of(pre)
    slope_two[...] = slope
    act_two[:, 0:d2] = jnp.zeros((4 * unit, d2), BF16)
    act_two[:, (x2 + 1) * d2 :] = jnp.zeros((4 * unit, d2), BF16)
    for x in range(x2):
        block = act[x * 2 * unit : (x + 1) * 2 * unit]
        actual = block.astype(F32)
        at = slice((x + 1) * d2, (x + 2) * d2)
        act_two[unit : 3 * unit, at] = block
        act_two[0:unit, at] = shift_rows(actual[unit:], 1, period).astype(BF16)
        act_two[3 * unit :, at] = shift_rows(actual[:unit], -1, period).astype(BF16)
    left = jnp.concatenate(
        [
            jnp.concatenate([act_two[a * unit : (a + 1) * unit, 2 * x * d2 : (2 * x + 4) * d2] for a in range(4)], axis=1)
            for x in range(x3)
        ],
        axis=0,
    )
    copies[4].wait()
    act, slope_three = gate_of(mat(left, third[...]))
    act_three[:, 0:d3] = jnp.zeros((4 * unit, d3), BF16)
    act_three[:, (x3 + 1) * d3 :] = jnp.zeros((4 * unit, d3), BF16)
    for x in range(x3):
        block = act[x * unit : (x + 1) * unit]
        actual = block.astype(F32)
        at = slice((x + 1) * d3, (x + 2) * d3)
        act_three[unit : 2 * unit, at] = block
        for a in (0, 2, 3):
            act_three[a * unit : (a + 1) * unit, at] = shift_rows(actual, 1 - a, period).astype(BF16)
    for x in range(x4):
        for a in range(4):
            cols_four[x * unit : (x + 1) * unit, a * 4 * d3 : (a + 1) * 4 * d3] = act_three[
                a * unit : (a + 1) * unit, x * d3 : (x + 4) * d3
            ]
    edge_planes(zin, zout, firsts, lasts, devices, group, cols, lanes, pitch)
    pre = None
    for a in range(4):
        copies[a].wait()
        term = mat(cols_four[:, a * quarter : (a + 1) * quarter], fourth[a * quarter : (a + 1) * quarter, :])
        pre = term if pre is None else pre + term
    _, slope = gate_of(pre)
    row = lax.broadcasted_iota(jnp.int32, (unit, d4), 0) % period
    head = head_ref[...].astype(F32) * -loss_scale
    heads = []
    for x in range(x4):
        total = None
        for a in range(4):
            taps = [head[a * 4 + b : a * 4 + b + 1, :] for b in range(4) if 0 <= x - b + 1 < x4 - 1]
            tap = functools.reduce(lambda u, v: u + v, taps)
            inside = (row - a + 1 >= 0) & (row - a + 1 < period - 2) & (row < period - 1)
            term = jnp.where(inside, jnp.broadcast_to(tap, (unit, d4)), 0.0)
            total = term if total is None else total + term
        heads.append(total)
    cot = (jnp.concatenate(heads, axis=0) * slope).astype(BF16)
    pull_four[...] = mat(cot, fourth[...], NT)
    cots = []
    for x in range(x3):
        total = None
        for a in range(4):
            term = None
            for b in range(4):
                source = x - b + 1
                if 0 <= source < x4:
                    piece = pull_four[source * unit : (source + 1) * unit, (a * 4 + b) * d3 : (a * 4 + b + 1) * d3]
                    term = piece if term is None else term + piece
            if a != 1:
                term = shift_rows(term, a - 1, period)
            total = term if total is None else total + term
        cots.append((total * slope_three[x * unit : (x + 1) * unit]).astype(BF16))
    pull_three[...] = mat(jnp.concatenate(cots, axis=0), third[...], NT)
    cots = []
    for x in range(x2):
        terms = []
        for a in range(4):
            term = None
            for b in range(4):
                if (x - b + 1) % 2 == 0 and 0 <= (x - b + 1) // 2 < x3:
                    source = (x - b + 1) // 2
                    piece = pull_three[source * unit : (source + 1) * unit, (a * 4 + b) * d2 : (a * 4 + b + 1) * d2]
                    term = piece if term is None else term + piece
            terms.append(term)
        even = terms[1] + shift_rows(terms[3], 1, period)
        odd = terms[2] + shift_rows(terms[0], -1, period)
        both = jnp.concatenate([even, odd], axis=0)
        cots.append((both * slope_two[x * 2 * unit : (x + 1) * 2 * unit]).astype(BF16))
    pull_two[...] = mat(jnp.concatenate(cots, axis=0), second[...], NT)
    strips = []
    for k in range(x2 + 1):
        terms = {}
        for p in range(2):
            for a in range(4):
                term = None
                if k < x2:
                    term = pull_two[(2 * k + p) * unit : (2 * k + p + 1) * unit, a * 4 * d1 : (a * 4 + 2) * d1]
                if k > 0:
                    other = pull_two[(2 * k - 2 + p) * unit : (2 * k - 1 + p) * unit, (a * 4 + 2) * d1 : (a + 1) * 4 * d1]
                    term = other if term is None else term + other
                terms[p, a] = term
        both = jnp.concatenate(
            [
                terms[0, 1] + shift_rows(terms[1, 3], 1, period),
                terms[0, 2] + terms[1, 0],
                terms[0, 3] + terms[1, 1],
                terms[1, 2] + shift_rows(terms[0, 0], -1, period),
            ],
            axis=0,
        )
        strips.append((both * slope_one[:, 2 * k * d1 : (2 * k + 2) * d1]).astype(BF16))
    cot = jnp.concatenate(strips, axis=1)
    sums = []
    for k in range(-(-width_one // strip)):
        start, end = k * strip, min((k + 1) * strip, width_one)
        pulls = mat(cot[:, start:end], band[:, : end - start], NT)
        groups = []
        for m in range(5):
            terms = [
                pulls[p * unit : (p + 1) * unit, (m - p) * LANES : (m - p + 1) * LANES] for p in range(4) if 0 <= m - p < 2
            ]
            groups.append(functools.reduce(lambda u, v: u + v, terms))
        sums.append(jnp.concatenate(groups, axis=0))
    sums = jnp.concatenate(sums, axis=1)
    upper = sums.astype(BF16)
    lower = (sums - upper.astype(F32)).astype(BF16)
    low = lax.broadcasted_iota(jnp.int32, upper.shape, 1) % LANES < LANES // 2
    blank = jnp.zeros_like(upper)
    split = [jnp.where(low, upper, blank), jnp.where(low, lower, blank), jnp.where(low, blank, upper), jnp.where(low, blank, lower)]
    both = mat(jnp.concatenate(split, axis=0), unwindow[...])
    size = 5 * unit
    odd = both[:size] + both[size : 2 * size]
    even = both[2 * size : 3 * size] + both[3 * size :]
    odd = [odd[m * unit : (m + 1) * unit, :] for m in range(5)]
    even = [even[m * unit : (m + 1) * unit, :] for m in range(5)]
    phases = [even[r // 2] if r % 2 == 0 else odd[(r + 1) // 2] for r in range(8)]
    phases[0] = phases[0] + shift_rows(even[4], 1, period)
    phases[7] = phases[7] + shift_rows(odd[0], -1, period)
    image = jnp.concatenate(phases, axis=0)
    image = jnp.concatenate([image, jnp.zeros((image.shape[0], 2 * LANES - wide), F32)], axis=1)
    for k in range(2):
        rows_in[k] = image[:, k * LANES : (k + 1) * LANES]
    for part in range(group):
        lines = [
            jnp.concatenate([rows_in[k, spot(y, part), :] for k in range(2)], axis=1)[:, :wide]
            for y in range(block_rows)
        ]
        lines = [shift_rows(lines[-1], 1, devices)] + lines + [shift_rows(lines[0], -1, devices)]
        for o in range(3):
            plane = [line[:, o * cols : (o + 1) * cols] for line in lines]
            plane.append(jnp.zeros((devices, lanes - span * cols), F32))
            plane = jnp.concatenate(plane, axis=1)
            for k in range(lanes // LANES):
                zout[k, pl.ds(o * group + part, devices, stride=pitch), :] = plane[:, k * LANES : (k + 1) * LANES]
    for k in range(lanes // LANES):
        out_ref[:, k * LANES : (k + 1) * LANES] = zout[k].astype(BF16)


def window_of(at, cols):
    k, rest = at // LANES, at % LANES
    inner = rest % (LANES // 2)
    colour = jnp.where(inner >= 18, 1, 0) + jnp.where(inner >= 36, 1, 0)
    x = 16 * k - 3 + inner - 18 * colour
    inside = (inner < 54) & (x >= 0) & (x < cols)
    return jnp.where(inside, colour * cols + x, -1), rest // (LANES // 2)


def stage_kernel(first_ref, second_hbm, window, unwindow, second, band, scr, sem, *, cols):
    copy = pltpu.make_async_copy(second_hbm, second, sem.at[0])
    copy.start()
    row = lax.broadcasted_iota(jnp.int32, window.shape, 0)
    lane = lax.broadcasted_iota(jnp.int32, window.shape, 1)
    place, half = window_of(lane // (2 * LANES) * LANES + lane % LANES, cols)
    window[...] = jnp.where((place == row) & (half == lane // LANES % 2), 1.0, 0.0).astype(BF16)
    place, _ = window_of(lax.broadcasted_iota(jnp.int32, unwindow.shape, 0), cols)
    column = lax.broadcasted_iota(jnp.int32, unwindow.shape, 1)
    unwindow[...] = jnp.where(place == column, 1.0, 0.0).astype(BF16)
    d1 = first_ref.shape[-1]
    scr[...] = jnp.zeros_like(scr)
    row = lax.broadcasted_iota(jnp.int32, (18, 8 * d1), 0)
    tap = row - 2 * (lax.broadcasted_iota(jnp.int32, (18, 8 * d1), 1) // d1)
    for a in range(4):
        lines = [first_ref[a, b].astype(F32) for b in range(4)]
        for c in range(3):
            block = jnp.zeros((18, 8 * d1), F32)
            for b in range(4):
                line = jnp.concatenate([lines[b][c : c + 1, :]] * 8, axis=1)
                block = jnp.where(tap == b, jnp.broadcast_to(line, block.shape), block)
            at = a * LANES // 2 + c * 18
            scr[at : at + 18, :] = block
    band[...] = scr[...].astype(BF16)
    copy.wait()


def stage_call(first, second, cols):
    d1, d2 = first.shape[-1], second.shape[-1]
    count = -(-(cols // 2 + 2) // 8)
    shapes = [(3 * cols, count * 2 * LANES), (count * LANES, 3 * cols), (16 * d1, d2), (2 * LANES, 8 * d1)]
    return pl.pallas_call(
        functools.partial(stage_kernel, cols=cols),
        out_shape=tuple(jax.ShapeDtypeStruct(shape, BF16) for shape in shapes),
        in_specs=[VM, HBM],
        out_specs=(VM,) * 4,
        scratch_shapes=[pltpu.VMEM((2 * LANES, 8 * d1), F32), pltpu.SemaphoreType.DMA((1,))],
        compiler_params=PART,
        cost_estimate=pl.CostEstimate(flops=10**8, bytes_accessed=4 * 10**6, transcendentals=0),
        name="stage_weights",
    )(first, second.reshape(16 * d1, d2))


def disc_call(payload, staged, third, fourth, head, devices, group, cols, block_rows):
    period = devices * block_rows // 8
    unit = group * period
    window, unwindow, second, band = staged
    d1, d2, d3, d4 = band.shape[1] // 8, second.shape[1], third.shape[-1], fourth.shape[-1]
    x2, x3 = cols // 4, cols // 8
    x4 = x3 - 1
    width_one = (cols // 2 + 2) * d1
    args = (
        payload,
        head.reshape(16, d4),
        window,
        band,
        second,
        unwindow,
        third.reshape(16 * d2, d3),
        fourth.reshape(16 * d3, d4),
    )
    lanes = payload.shape[1]
    return pl.pallas_call(
        functools.partial(
            disc_kernel, devices=devices, group=group, cols=cols, block_rows=block_rows, period=period
        ),
        out_shape=jax.ShapeDtypeStruct(payload.shape, BF16),
        in_specs=[VM] * 6 + [HBM] * 2,
        out_specs=VM,
        scratch_shapes=[
            pltpu.VMEM((lanes // LANES, payload.shape[0], LANES), F32),
            pltpu.VMEM((16 * d2, d3), BF16),
            pltpu.VMEM((16 * d3, d4), BF16),
            pltpu.VMEM((2, 8 * unit, LANES), F32),
            pltpu.VMEM((6 * unit, width_one), BF16),
            pltpu.VMEM((4 * unit, width_one), F32),
            pltpu.VMEM((x2 * 2 * unit, 16 * d1), BF16),
            pltpu.VMEM((4 * unit, (x2 + 2) * d2), BF16),
            pltpu.VMEM((x2 * 2 * unit, d2), F32),
            pltpu.VMEM((4 * unit, (x3 + 2) * d3), BF16),
            pltpu.VMEM((x4 * unit, 16 * d3), BF16),
            pltpu.VMEM((x4 * unit, 16 * d3), F32),
            pltpu.VMEM((x3 * unit, 16 * d2), F32),
            pltpu.VMEM((x2 * 2 * unit, 16 * d1), F32),
            pltpu.VMEM((lanes // LANES, payload.shape[0], LANES), F32),
            pltpu.SemaphoreType.DMA((5,)),
        ],
        compiler_params=MOST,
        cost_estimate=pl.CostEstimate(flops=4 * 10**9, bytes_accessed=8 * 10**6, transcendentals=10**6),
        name="disc_rows",
    )(*args)


def put_taps(plane, taps_ref, frames, cols, pieces, padded):
    lanes = plane.shape[1]
    column = lax.broadcasted_iota(jnp.int32, plane.shape, 1) % cols
    for b in range(3):
        moved = plane
        if b == 0:
            moved = jnp.where(column == cols - 1, 0.0, pltpu.roll(plane, lanes - 1, 1))
        if b == 2:
            moved = jnp.where(column == 0, 0.0, pltpu.roll(plane, 1, 1))
        for a in range(3):
            turned = moved if a == 2 else pltpu.roll(moved, lanes - (2 - a) * cols, 1)
            for k in range(pieces):
                taps_ref[k, pl.ds((a * 3 + b) * 3 * frames, 3 * frames), :] = turned[:, k * LANES : (k + 1) * LANES]
    for k in range(pieces):
        taps_ref[k, pl.ds(27 * frames, (padded - 27) * frames), :] = jnp.zeros(((padded - 27) * frames, LANES), F32)


def unpack(plane_ref, zin, devices, group):
    lanes = plane_ref.shape[1]
    pitch = plane_ref.shape[0] // devices
    for k in range(lanes // LANES):
        zin[k] = plane_ref[:, k * LANES : (k + 1) * LANES].astype(F32)
    blocks = []
    for o in range(3):
        for part in range(group):
            row = pl.ds(o * group + part, devices, stride=pitch)
            blocks.append(jnp.concatenate([zin[k, row, :] for k in range(lanes // LANES)], axis=1))
    return jnp.concatenate(blocks, axis=0)


def rec_rows(inner_ref, zin, devices, group, cols, block_rows):
    lanes = inner_ref.shape[1]
    pitch = zin.shape[1] // devices
    edges = []
    for i in range(2):
        row = pl.ds(3 * group + i, devices, stride=pitch)
        edges.append(jnp.concatenate([zin[k, row, :] for k in range(lanes // LANES)], axis=1))
    blocks = []
    for i, e in ((0, 0), (1, 0), (1, 1), (0, 1)):
        pieces = [
            edges[i][:, (e * 3 * group + at) * cols : (e * 3 * group + at + 1) * cols] for at in range(3 * group)
        ]
        blocks.append(jnp.concatenate(pieces, axis=0))
    none = lambda count: jnp.zeros((blocks[0].shape[0], count), F32)
    above, first, last, below = blocks
    rest = lanes - (block_rows + 2) * cols
    return inner_ref[...], jnp.concatenate(
        [above, first * loss_scale, none((block_rows - 2) * cols), last * loss_scale, below, none(rest)], axis=1
    )


def both_kernel(
    inner_ref, plane_ref, feat_ref, part_ref, rec_taps, gan_taps, zin, *, frames, devices, group, cols, block_rows
):
    pieces = block_rows * cols // LANES
    put_taps(unpack(plane_ref, zin, devices, group), gan_taps, frames, cols, pieces, 32)
    inner, edges = rec_rows(inner_ref, zin, devices, group, cols, block_rows)
    put_taps(inner + edges, rec_taps, frames, cols, pieces, 32)
    pixels = pieces * LANES
    total = jnp.zeros((64, feat_ref.shape[1]), F32)
    for frame in range(frames):
        rows = pl.ds(slot_of(frame, devices, group), 32, stride=frames)
        taps = jnp.concatenate(
            [
                jnp.concatenate([taps_ref[k, rows, :] for k in range(pieces)], axis=1)
                for taps_ref in (rec_taps, gan_taps)
            ],
            axis=0,
        )
        total = total + mat(taps.astype(BF16), feat_ref[frame * pixels : (frame + 1) * pixels, :])
    blank = jnp.zeros((part_ref.shape[1] - 54, total.shape[1]), F32)
    total = jnp.concatenate([total[0:27], total[32:59], blank], axis=0).astype(BF16)
    for i in range(part_ref.shape[0]):
        part_ref[i] = total


def turn_kernel(
    inner_ref, plane_ref, out_ref, rec_taps, gan_taps, zin, *, frames, devices, group, cols, block_rows
):
    pieces = block_rows * cols // LANES
    pixels = pieces * LANES
    put_taps(unpack(plane_ref, zin, devices, group), gan_taps, frames, cols, pieces, 32)
    inner, edges = rec_rows(inner_ref, zin, devices, group, cols, block_rows)
    put_taps(inner + edges, rec_taps, frames, cols, pieces, 32)
    for pair in range(frames // 2):
        for k in range(pieces):
            parts = []
            for frame in (2 * pair, 2 * pair + 1):
                rows = pl.ds(slot_of(frame, devices, group), 32, stride=frames)
                parts += [rec_taps[k, rows, :], gan_taps[k, rows, :]]
            at = pair * pixels + k * LANES
            out_ref[at : at + LANES, :] = jnp.concatenate(parts, axis=0).T.astype(BF16)


def taps_call(kernel, specs, operands, out, scratch, frames, devices, group, cols, block_rows, flops, name):
    return pl.pallas_call(
        functools.partial(kernel, frames=frames, devices=devices, group=group, cols=cols, block_rows=block_rows),
        out_shape=out,
        in_specs=specs,
        out_specs=jax.tree.map(lambda _: VM, out),
        scratch_shapes=scratch,
        compiler_params=PART,
        cost_estimate=pl.CostEstimate(flops=flops, bytes_accessed=4 * 10**6, transcendentals=0),
        name=name,
    )(*operands)


def final_kernel(
    taps_ref, sums_ref, weight_ref, out_hbm, grad_ref, adapt_ref, weight_scr, both_ref, out_ref, sems, *, pixels, chunk
):
    weight_scr[...] = jnp.zeros_like(weight_scr)
    for a in range(3):
        for b in range(3):
            at = (a * 3 + b) * 3
            weight_scr[at : at + 3, :] = weight_ref[a, b].astype(F32)
    total = sums_ref[0].astype(F32)
    for i in range(1, sums_ref.shape[0]):
        total = total + sums_ref[i].astype(F32)
    rec, gan = total[0:27], total[27:54]
    norm = lambda values: jnp.sqrt(jnp.sum(jnp.sum(values * values, axis=1, keepdims=True), axis=0, keepdims=True))
    adaptive = norm(rec) / (norm(gan) + epsilon)
    grad = (rec + adaptive * gan) / pixels
    for a in range(3):
        for b in range(3):
            at = (a * 3 + b) * 3
            grad_ref[a, b] = grad[at : at + 3, :]
    adapt_ref[...] = adaptive
    weight = weight_scr[...].astype(BF16)
    padded, channels = weight.shape
    scaled = (adaptive * weight.astype(F32)).astype(BF16)
    both_ref[...] = jnp.zeros_like(both_ref)
    both_ref[0:padded, 0:channels] = weight
    both_ref[padded : 2 * padded, 0:channels] = scaled
    both_ref[2 * padded : 3 * padded, channels:] = weight
    both_ref[3 * padded :, channels:] = scaled
    pairs = taps_ref.shape[0] // chunk
    stores = []
    for pair in range(pairs):
        product = mat(taps_ref[pair * chunk : (pair + 1) * chunk], both_ref[...]).astype(BF16)
        rows = pl.ds(2 * pair * chunk, 2 * chunk)
        out_ref[2 * pair * chunk : (2 * pair + 1) * chunk] = product[:, :channels]
        out_ref[(2 * pair + 1) * chunk : (2 * pair + 2) * chunk] = product[:, channels:]
        stores.append(pltpu.make_async_copy(out_ref.at[rows], out_hbm.at[rows], sems.at[pair]))
        stores[-1].start()
    for copy in stores:
        copy.wait()


def final_call(taps, sums, weight, pixels, chunk):
    padded, channels = 32, weight.shape[-1]
    rows = 2 * taps.shape[0]
    return pl.pallas_call(
        functools.partial(final_kernel, pixels=pixels, chunk=chunk),
        out_shape=(
            jax.ShapeDtypeStruct((rows, channels), BF16),
            jax.ShapeDtypeStruct((3, 3, 3, channels), F32),
            jax.ShapeDtypeStruct((1, 1), F32),
        ),
        in_specs=[VM] * 3,
        out_specs=(HBM, VM, VM),
        scratch_shapes=[
            pltpu.VMEM((padded, channels), F32),
            pltpu.VMEM((4 * padded, 2 * channels), BF16),
            pltpu.VMEM((rows, channels), BF16),
            pltpu.SemaphoreType.DMA((rows // (2 * chunk),)),
        ],
        compiler_params=PART,
        cost_estimate=pl.CostEstimate(flops=4 * rows * channels * padded, bytes_accessed=4 * rows * channels, transcendentals=0),
        name="feature_pull",
    )(taps, sums, weight)


def per_device(
    features, target, conv_weight, disc_first, disc_second, disc_third, disc_fourth, disc_head
):
    row = ("far", "near")
    devices = lax.axis_size(row)
    clips = lax.axis_size("clip")
    _, frames, block_rows, cols, channels = features.shape
    group = frames // devices
    pixels = clips * devices * frames * block_rows * cols
    lanes = up_to((block_rows + 2) * cols, LANES)
    pitch = up_to(3 * group + 2, 8)
    sizes = (frames, devices, group, cols, block_rows)
    feats = features.reshape(frames * block_rows * cols, channels)
    wanted = target[0].transpose(0, 2, 1, 3)
    payload = forward_call(feats, wanted, conv_weight, frames, devices, group, cols, lanes, pitch)
    trade = lambda values: lax.all_to_all(
        values.reshape(devices, pitch, lanes), row, split_axis=0, concat_axis=0, tiled=True
    ).reshape(devices * pitch, lanes)
    arrived = trade(payload)
    inner = inner_call(payload, wanted, frames, devices, group, block_rows, cols)
    _, disc_first = lax.optimization_barrier((payload, disc_first))
    staged = stage_call(disc_first, disc_second, cols)
    arrived, inner = lax.optimization_barrier((arrived, inner))
    sent = disc_call(arrived, staged, disc_third, disc_fourth, disc_head, devices, group, cols, block_rows)
    returned = trade(sent)
    taps_scratch = pltpu.VMEM((block_rows * cols // LANES, 32 * frames, LANES), F32)
    plane_scratch = pltpu.VMEM((lanes // LANES, devices * pitch, LANES), F32)
    flops = 4 * features.size * 27
    part = taps_call(
        both_kernel, [VM, VM, VM], (inner, returned, feats),
        jax.ShapeDtypeStruct((lax.axis_size("far"), 56, channels), BF16),
        [taps_scratch, taps_scratch, plane_scratch], *sizes, flops, "both_taps",
    )
    share = lambda values, axes: lax.all_to_all(values, axes, split_axis=0, concat_axis=0, tiled=True)
    sums = share(sum_call(share(part, "far"), clips * lax.axis_size("near")), ("clip", "near"))
    taps = taps_call(
        turn_kernel, [VM, VM], (inner, returned), jax.ShapeDtypeStruct((feats.shape[0] // 2, LANES), BF16),
        [taps_scratch, taps_scratch, plane_scratch], *sizes, flops, "turn_taps",
    )
    image_back = returned.reshape(devices, pitch, lanes)[:, : 3 * group, cols : (block_rows + 1) * cols]
    image_back = image_back.reshape(devices, 3, group, block_rows, cols).transpose(0, 2, 3, 1, 4)
    image_back = image_back.reshape(1, frames, block_rows, 3, cols)
    feature_grad, weight_grad, adaptive = final_call(taps, sums, conv_weight, pixels, block_rows * cols)
    return (feature_grad.reshape(features.shape), image_back, weight_grad, adaptive[0, 0])


def sum_kernel(parts_ref, out_ref):
    total = parts_ref[0].astype(F32)
    for i in range(1, parts_ref.shape[0]):
        total = total + parts_ref[i].astype(F32)
    total = total.astype(BF16)
    for i in range(out_ref.shape[0]):
        out_ref[i] = total


def sum_call(parts, copies):
    return pl.pallas_call(
        sum_kernel,
        out_shape=jax.ShapeDtypeStruct((copies,) + parts.shape[1:], BF16),
        in_specs=[VM],
        out_specs=VM,
        compiler_params=PART,
        name="sum_parts",
    )(parts)


def solution(mesh):
    clips, devices = mesh.shape["clip"], mesh.shape["row"]
    near = 2 if devices % 2 == 0 else 1
    split = jax.sharding.Mesh(mesh.devices.reshape(clips, devices // near, near), ("clip", "far", "near"))
    rows = P("clip", None, ("far", "near"), None, None)
    return jax.shard_map(
        per_device,
        mesh=split,
        in_specs=(rows, rows, P(), P(), P(), P(), P(), P()),
        out_specs=(rows, rows, P(), P()),
        check_vma=False,
    )
```
